32 devices in a mesh: dp: 16 (over z, y, x), fsdp: 2 (over core).
Axes of the slice: x: 2, y: 2, z: 4, core: 2. Of those that a mesh axis runs over, the one named last changes fastest.
Arguments:
- query_global: bfloat16 [2, 64, 56, 56, 256], P(None, ('dp', 'fsdp')), may hold values from -8 to 8
- small_crop_query: bfloat16 [2, 64, 3, 24, 24, 256], P(None, ('dp', 'fsdp')), may hold values from -8 to 8
- small_count: int32 [2, 64], P(None, ('dp', 'fsdp')), may hold values from 0 to 3
- key_global: bfloat16 [2, 64, 56, 56, 256], P(None, ('dp', 'fsdp')), may hold values from -8 to 8
- shuffle_mask: int32 [2, 2], replicated, may hold values from 0 to 31, as said below
- reduce_weight: float32 [256, 128], P('dp', 'fsdp'), may hold values from -0.375 to 0.375
- spatial_weight: float32 [1152, 128], P('dp', 'fsdp'), may hold values from -0.1875 to 0.1875
- expand_weight: float32 [128, 512], P('dp', 'fsdp'), may hold values from -0.5 to 0.5
- shortcut_weight: float32 [256, 512], P('dp', 'fsdp'), may hold values from -0.375 to 0.375
- norm_gains: float32 [1280], replicated, may hold values from 0.5 to 1.5
- norm_shifts: float32 [1280], replicated, may hold values from -0.5 to 0.5
- lagged_reduce: float32 [256, 128], P('dp', 'fsdp'), may hold values from -0.375 to 0.375
- lagged_spatial: float32 [1152, 128], P('dp', 'fsdp'), may hold values from -0.1875 to 0.1875
- lagged_expand: float32 [128, 512], P('dp', 'fsdp'), may hold values from -0.5 to 0.5
- lagged_shortcut: float32 [256, 512], P('dp', 'fsdp'), may hold values from -0.375 to 0.375
- lagged_gains: float32 [1280], replicated, may hold values from 0.5 to 1.5
- lagged_shifts: float32 [1280], replicated, may hold values from -0.5 to 0.5
Outputs:
- loss: float32 [], replicated
- global_grad: bfloat16 [2, 64, 56, 56, 256], P(None, ('dp', 'fsdp'))
- small_grad: bfloat16 [2, 64, 3, 24, 24, 256], P(None, ('dp', 'fsdp'))
- reduce_grad: float32 [256, 128], P('dp', 'fsdp')
- spatial_grad: float32 [1152, 128], P('dp', 'fsdp')
- expand_grad: float32 [128, 512], P('dp', 'fsdp')
- shortcut_grad: float32 [256, 512], P('dp', 'fsdp')
- gains_grad: float32 [1280], replicated
- shifts_grad: float32 [1280], replicated
The draws below stay inside these ranges and needn't reach their ends.
Inputs may be any that keep to these rules, and one draw needn't show every extreme that they name: The 2 entries of one micro-batch are distinct, and entries come in pairs: shuffle_mask[2 j + 1, s] = shuffle_mask[2 j, s] XOR (31).
All inputs are finite; a program needn't handle non-finite values.
Results may differ from the reference program's by a relative error of at most 0.012.
Values may be sent and summed in bfloat16 or wider, within the bound.
A program may use at most 256 MiB of HBM per device.

```python
import jax
import jax.numpy as jnp
from jax import lax

CIN = 256
CMID = 128
COUT = 512
NORMS = 1280
H = 56
HS = 24
SLOTS = 3
MICRO = 2
IMG_DEV = 2
IMAGE_COUNT = 64
N_DP = 16
N_FSDP = 2


def image_offsets(key):
    return jax.random.normal(key, (MICRO, IMAGE_COUNT, CIN), jnp.float32)


def draw_query_global(key, part):
    offsets = image_offsets(key)
    key = jax.random.fold_in(key, 3)
    shape = (MICRO, IMAGE_COUNT, H, H, CIN)
    noise = jax.random.normal(key, shape, jnp.float32)
    field = offsets[:, :, None, None, :] + noise
    return jnp.clip(field, -8.0, 8.0).astype(jnp.bfloat16)


def draw_small_crop_query(key, part):
    offsets = image_offsets(key)
    key = jax.random.fold_in(key, 5)
    shape = (MICRO, IMAGE_COUNT, SLOTS, HS, HS, CIN)
    noise = jax.random.normal(key, shape, jnp.float32)
    field = offsets[:, :, None, None, None, :] + noise
    return jnp.clip(field, -8.0, 8.0).astype(jnp.bfloat16)


def draw_key_global(key, part):
    offsets = image_offsets(key)
    key = jax.random.fold_in(key, 7)
    shape = (MICRO, IMAGE_COUNT, H, H, CIN)
    noise = jax.random.normal(key, shape, jnp.float32)
    field = offsets[:, :, None, None, :] + noise
    return jnp.clip(field, -8.0, 8.0).astype(jnp.bfloat16)


def draw_shuffle_mask(key, part):
    key = jax.random.fold_in(key, 11)
    groups = N_DP * N_FSDP
    rows = []
    for pair in range(MICRO // 2):
        pair_key = jax.random.fold_in(key, pair)
        order = jax.random.permutation(jax.random.fold_in(pair_key, 1), groups)[:IMG_DEV].astype(jnp.int32)
        pick = jax.random.randint(jax.random.fold_in(pair_key, 2), (), 0, IMG_DEV)
        first = jnp.bitwise_xor(order, order[pick]).astype(jnp.int32)
        second = jnp.bitwise_xor(first, groups - 1).astype(jnp.int32)
        rows += [first, second]
    return jnp.stack(rows, axis=0).astype(jnp.int32)


def with_ends(drawn, stream_key, low, top_value):
    longest = drawn.shape.index(max(drawn.shape))
    spots = []
    for shift in (0, 1):
        where = [jax.random.randint(jax.random.fold_in(stream_key, axis), (), 0, length) for axis, length in enumerate(drawn.shape)]
        where[longest] = (where[longest] + shift) % drawn.shape[longest]
        spots.append(tuple(where))
    return drawn.at[spots[0]].set(low).at[spots[1]].set(top_value)


def steps_of(stream_key, extent, cuts, least, largest):
    factor_of, own = 1.0, jax.random.fold_in(stream_key, 6)
    for position, shards_of in cuts:
        steps = jnp.exp(jax.random.uniform(jax.random.fold_in(own, position), (shards_of,), jnp.float32, least / len(cuts), largest / len(cuts)))
        factor_of = factor_of * jnp.repeat(steps, extent[position] // shards_of).reshape([-1 if axis == position else 1 for axis in range(len(extent))])
    return factor_of


def scatter_about(stream_key, dims, deviation, limit, split=(), held_as=jnp.bfloat16):
    array = jax.random.normal(stream_key, dims, jnp.float32) * deviation
    if len(split) > 0:
        array = steps_of(stream_key, dims, split, -0.22, 0.18) * array
    return jnp.clip(array, min=-limit, max=limit).astype(held_as)


def setup_inputs(seed: int = 0) -> dict:
    splits = jax.random.split(jax.random.key(seed), 18)
    return {
        "query_global": draw_query_global(jax.random.fold_in(splits[17], 71), 0),
        "small_crop_query": draw_small_crop_query(jax.random.fold_in(splits[17], 71), 0),
        "small_count": with_ends(jax.random.randint(splits[2], (MICRO, IMAGE_COUNT), 0, SLOTS + 1), jax.random.fold_in(splits[2], 1), 0, SLOTS).astype(jnp.int32),
        "key_global": draw_key_global(jax.random.fold_in(splits[17], 71), 0),
        "shuffle_mask": draw_shuffle_mask(jax.random.fold_in(splits[17], 71), 0),
        "reduce_weight": scatter_about(splits[5], (CIN, CMID), CIN ** -0.5, 0.375, ((0, 16), (1, 2)), jnp.float32),
        "spatial_weight": scatter_about(splits[6], (9 * CMID, CMID), (9 * CMID) ** -0.5, 0.1875, ((0, 16), (1, 2)), jnp.float32),
        "expand_weight": scatter_about(splits[7], (CMID, COUT), CMID ** -0.5, 0.5, ((0, 16), (1, 2)), jnp.float32),
        "shortcut_weight": scatter_about(splits[8], (CIN, COUT), CIN ** -0.5, 0.375, ((0, 16), (1, 2)), jnp.float32),
        "norm_gains": jnp.clip(1.0 + 0.1 * jax.random.normal(splits[9], (NORMS,), jnp.float32), 0.5, 1.5),
        "norm_shifts": jnp.clip(jax.random.uniform(splits[10], (NORMS,), jnp.float32, -0.5, 0.5), -0.5, 0.5),
        "lagged_reduce": scatter_about(splits[11], (CIN, CMID), CIN ** -0.5, 0.375, ((0, 16), (1, 2)), jnp.float32),
        "lagged_spatial": scatter_about(splits[12], (9 * CMID, CMID), (9 * CMID) ** -0.5, 0.1875, ((0, 16), (1, 2)), jnp.float32),
        "lagged_expand": scatter_about(splits[13], (CMID, COUT), CMID ** -0.5, 0.5, ((0, 16), (1, 2)), jnp.float32),
        "lagged_shortcut": scatter_about(splits[14], (CIN, COUT), CIN ** -0.5, 0.375, ((0, 16), (1, 2)), jnp.float32),
        "lagged_gains": jnp.clip(1.0 + 0.1 * jax.random.normal(splits[15], (NORMS,), jnp.float32), 0.5, 1.5),
        "lagged_shifts": jnp.clip(jax.random.uniform(splits[16], (NORMS,), jnp.float32, -0.5, 0.5), -0.5, 0.5),
    }


@jax.custom_vjp
def low(v):
    return lax.optimization_barrier(v.astype(jnp.bfloat16)).astype(jnp.float32)

@jax.custom_vjp
def low_back(v):
    return v

def low_keep(v):
    return (low(v), None)

def low_pass(kept, grad):
    return (grad,)

def back_keep(v):
    return (v, None)

def back_low(kept, grad):
    return (low(grad),)
low.defvjp(low_keep, low_pass)
low_back.defvjp(back_keep, back_low)
SOFTMAX_TEMP = 0.2
MOMENTUM = 0.999
NORM_EPS = 1e-05
UNIT_EPS = 1e-06

def project(field, weight):
    return jnp.einsum('nhwc,cd->nhwd', field, weight, precision=lax.Precision.HIGHEST)

def spatial(field, weight):
    kernel = weight.reshape(3, 3, field.shape[-1], weight.shape[1])
    return lax.conv_general_dilated(field, kernel, (2, 2), ((1, 1), (1, 1)), dimension_numbers=('NHWC', 'HWIO', 'NHWC'), precision=lax.Precision.HIGHEST)

def normalize(values, lives, gain, shift):
    count = sum((jnp.sum(live) * value.shape[1] * value.shape[2] for value, live in zip(values, lives)))
    total = sum((lax.optimization_barrier(jnp.sum(value * live[:, None, None, None], axis=(0, 1, 2))) for value, live in zip(values, lives)))
    mean = total / count
    spread = sum((lax.optimization_barrier(jnp.sum(jnp.square(value - mean) * live[:, None, None, None], axis=(0, 1, 2))) for value, live in zip(values, lives))) / count
    scale = lax.rsqrt(spread + NORM_EPS) * gain
    return [(value - mean) * scale + shift for value in values]

def slices_of(vector):
    return (vector[:CMID], vector[CMID:2 * CMID], vector[2 * CMID:2 * CMID + COUT], vector[2 * CMID + COUT:])

def unit(embed):
    return embed * lax.rsqrt(lax.optimization_barrier(jnp.sum(embed * embed, axis=-1, keepdims=True)) + UNIT_EPS)

def encode(fields, lives, weights, gains, shifts):
    reduce_w, spatial_w, expand_w, shortcut_matrix = weights
    gain_a, gain_b, gain_c, gain_d = slices_of(gains)
    shift_a, shift_b, shift_c, shift_d = slices_of(shifts)
    first = [low_back(project(f, reduce_w)) for f in fields]
    first = [low(jax.nn.gelu(v, approximate=False)) for v in normalize(first, lives, gain_a, shift_a)]
    second = [low_back(spatial(v, spatial_w)) for v in first]
    second = [low(jax.nn.gelu(v, approximate=False)) for v in normalize(second, lives, gain_b, shift_b)]
    third = [low_back(project(v, expand_w)) for v in second]
    side = [low_back(project(f[:, ::2, ::2, :], shortcut_matrix)) for f in fields]
    third = normalize(third, lives, gain_c, shift_c)
    side = normalize(side, lives, gain_d, shift_d)
    merged = [jax.nn.gelu(u + v, approximate=False) for u, v in zip(third, side)]
    return [unit(lax.optimization_barrier(jnp.mean(v, axis=(1, 2)))) for v in merged]

def key_embeddings(block, mask, weights, gains, shifts):
    groups = N_DP * N_FSDP
    grouped = block.reshape(groups, IMG_DEV, H, H, CIN)
    sources = jnp.bitwise_xor(jnp.arange(groups, dtype=jnp.int32)[:, None], mask[None, :].astype(jnp.int32))
    slot_index = jnp.arange(IMG_DEV, dtype=jnp.int32)

    def one(source):
        images = grouped[source, slot_index]
        live = jnp.ones((IMG_DEV,), jnp.float32)
        return encode([images], [live], weights, gains, shifts)[0]
    return lax.map(one, sources).reshape(IMAGE_COUNT, COUT)

def group_loss(weights, gains, shifts, key_vectors, mask, pieces):
    fields_g, fields_s, counts, index = pieces
    live_g = jnp.ones((IMG_DEV,), jnp.float32)
    live_s = (jnp.arange(SLOTS, dtype=jnp.int32)[None, :] < counts[:, None]).astype(jnp.float32).reshape(-1)
    small = fields_s.reshape(IMG_DEV * SLOTS, HS, HS, CIN)
    embed_g, embed_s = encode([fields_g, small], [live_g, live_s], weights, gains, shifts)
    embedding_rows = jnp.concatenate([embed_g, embed_s], axis=0)
    lives = jnp.concatenate([live_g, live_s], axis=0)
    owner = jnp.concatenate([jnp.arange(IMG_DEV, dtype=jnp.int32), jnp.repeat(jnp.arange(IMG_DEV, dtype=jnp.int32), SLOTS)])
    positive = jnp.bitwise_xor(index, mask[owner]) * IMG_DEV + owner
    similarity_logits = jnp.dot(embedding_rows, key_vectors.T, precision=lax.Precision.HIGHEST) / SOFTMAX_TEMP
    top = lax.optimization_barrier(jnp.max(similarity_logits, axis=-1, keepdims=True))
    total = top[:, 0] + jnp.log(lax.optimization_barrier(jnp.sum(jnp.exp(similarity_logits - top), axis=-1)))
    chosen = lax.optimization_barrier(jnp.sum(jnp.where(jnp.arange(IMAGE_COUNT, dtype=jnp.int32)[None, :] == positive[:, None], similarity_logits, 0.0), axis=-1))
    return jnp.sum((total - chosen) * lives)

def reference(query_global, small_crop_query, small_count, key_global, shuffle_mask, reduce_weight, spatial_weight, expand_weight, shortcut_weight, norm_gains, norm_shifts, lagged_reduce, lagged_spatial, lagged_expand, lagged_shortcut, lagged_gains, lagged_shifts):
    current = (reduce_weight, spatial_weight, expand_weight, shortcut_weight, norm_gains, norm_shifts)
    lagged = (lagged_reduce, lagged_spatial, lagged_expand, lagged_shortcut, lagged_gains, lagged_shifts)
    fresh = [MOMENTUM * old + (1.0 - MOMENTUM) * new for old, new in zip(lagged, current)]
    key_weights = [low(w) for w in fresh[:4]]
    key_list = [key_embeddings(key_global[m].astype(jnp.float32), shuffle_mask[m], key_weights, fresh[4], fresh[5]) for m in range(MICRO)]
    groups = N_DP * N_FSDP
    checked = jax.checkpoint(group_loss)

    def total_loss(globals_in, smalls_in, first_w, second_w, third_w, fourth_w, gains, shifts):
        weights = [low(w) for w in (first_w, second_w, third_w, fourth_w)]
        loss = jnp.zeros((), jnp.float32)
        for m in range(MICRO):
            grouped = (globals_in[m].reshape(groups, IMG_DEV, H, H, CIN), smalls_in[m].reshape(groups, IMG_DEV, SLOTS, HS, HS, CIN), small_count[m].reshape(groups, IMG_DEV), jnp.arange(groups, dtype=jnp.int32))
            key_vectors = key_list[m]
            mask = shuffle_mask[m].astype(jnp.int32)
            losses = lax.map(lambda pieces: checked(weights, gains, shifts, key_vectors, mask, pieces), grouped)
            loss = loss + jnp.sum(losses)
        return loss
    loss, pull = jax.vjp(total_loss, query_global.astype(jnp.float32), small_crop_query.astype(jnp.float32), reduce_weight, spatial_weight, expand_weight, shortcut_weight, norm_gains, norm_shifts)
    grads = pull(jnp.ones((), jnp.float32))
    return (loss, grads[0].astype(jnp.bfloat16), grads[1].astype(jnp.bfloat16), grads[2], grads[3], grads[4], grads[5], grads[6], grads[7])
```

```python
import functools
import jax
import jax.numpy as jnp
from jax import lax
from jax.experimental import pallas as pl
from jax.experimental.pallas import tpu as pltpu
from jax.sharding import PartitionSpec as P

f32, bf16 = jnp.float32, jnp.bfloat16
CIN, CMID, COUT, NORMS = 256, 128, 512, 1280
SIDE, SMALL = 56, 24
BLOCKS = COUT // 128
TEMP, NORM_EPS, UNIT_EPS = 0.2, 1e-05, 1e-06
ROOT_HALF = 0.7071067811865476
DENSITY = 0.3989422804014327


class Field:
    def __init__(self, count, side, row, out_row, ahead):
        self.count, self.side, self.row, self.out_row = count, side, row, out_row
        self.ahead = ahead
        self.half = side // 2
        self.wide = -(-self.half // 16) * 16
        self.area, self.out_area = side * side, (side // 2) ** 2


def field_pair(images, slots):
    big = Field(images, SIDE, 0, 0, 0)
    small = Field(images * slots, SMALL, images * big.area, images * big.out_area, images)
    return big, small


def at(start, size, align=16):
    return pl.ds(pl.multiple_of(start, align), size)


def folded(x):
    return x.reshape(x.shape[0] // 8, 8, x.shape[1]).sum(0)


def dot(a, b):
    return jnp.dot(a, b, preferred_element_type=f32)


def dot_rows(a, b):
    return lax.dot_general(a, b, (((0,), (0,)), ((), ())), preferred_element_type=f32)


def dot_exact(a, b, dims):
    return lax.dot_general(a, b, (dims, ((), ())), precision=lax.Precision.HIGHEST, preferred_element_type=f32)


def gelu_pair(v):
    share = 0.5 + 0.5 * lax.erf(v * ROOT_HALF)
    return v * share, share + v * (DENSITY * jnp.exp(v * v * -0.5))


def gelu_only(v):
    return v * (0.5 + 0.5 * lax.erf(v * ROOT_HALF))


def each_crop(fields, body):
    for field in fields:
        step = 1 if field.side == SIDE else 2

        def turn(c, _, field=field, step=step):
            for k in range(step):
                crop = c * step + k
                body(field, crop)
            return 0

        lax.fori_loop(0, field.count // step, turn, 0)


def each_part(fields, body):
    for field in fields:
        if field.side == SIDE:

            def turn(c, _, field=field):
                body(field, c // 2, (c % 2) * (field.half // 2), field.half // 2)
                return 0

            lax.fori_loop(0, field.count * 2, turn, 0)
        else:

            def turn(c, _, field=field):
                for k in range(2):
                    body(field, c * 2 + k, 0, field.half)
                return 0

            lax.fori_loop(0, field.count // 2, turn, 0)


def line(vector, start):
    return vector[pl.ds(start, 128)].reshape(1, 128)


def moments(ref, pick, start, size, step, pivot):
    total = jnp.zeros((8, 128), f32)
    square = jnp.zeros((8, 128), f32)
    for k in range(size // step):
        x = ref[pick(start + k * step, step)] - pivot
        total += folded(x)
        square += folded(x * x)
    return total, square


def closed(total, square, pivot, count):
    off = total.sum(0, keepdims=True) / count
    spread = jnp.maximum(square.sum(0, keepdims=True) / count - off * off, 0.0)
    return pivot + off, lax.rsqrt(spread + NORM_EPS)


def patches(planes, field, crop, first, rows):
    size = rows * field.wide
    above = planes[1, crop, pl.ds(first, rows)].reshape(size, 3 * CMID)
    level = planes[0, crop, pl.ds(first, rows)].reshape(size, 3 * CMID)
    below = planes[1, crop, pl.ds(first + 1, rows)].reshape(size, 3 * CMID)
    return jnp.concatenate([above, level, below], axis=1)


def split_planes(hidden, stage, planes, field, crop, line, slot):
    side, wide = field.side, field.wide
    for odd in range(2):
        stage[slot, odd, 8 : 8 + side] = hidden[odd * side : (odd + 1) * side]
    for odd in range(2):
        for tap in range(3):
            column = stage[slot, odd, pl.ds(7 + tap, wide, stride=2)]
            planes[odd, crop, line + odd, :, tap * CMID : (tap + 1) * CMID] = column.astype(bf16)


def even_cells(field_ref, wide_stage, dense_stage, even, field, crop):
    side, half = field.side, field.half
    for block in range(CIN // 128):
        lanes = slice(block * 128, (block + 1) * 128)

        def turn(y, _):
            for k in range(2):
                line = y * 2 + k
                x = field_ref[at(crop * field.area + line * 2 * side, 2 * side), lanes].astype(f32)
                wide_stage[k, 0:side] = x[0:side]
                dense_stage[pl.ds(line * half, half)] = wide_stage[k, pl.ds(0, half, stride=2)]
            return 0

        lax.fori_loop(0, half // 2, turn, 0)
        even[at(field.out_row + crop * field.out_area, field.out_area), lanes] = dense_stage[
            0 : field.out_area
        ].astype(bf16)


def query_kernel(
    slots,
    big_ref, small_ref, counts, device, w1, w2, w3, w4, gains, shifts, keys,
    big_out, small_out, loss_out, g1_out, g2_out, g3_out, g4_out, gain_out, shift_out,
    a1, slope1, planes_big, planes_small, a2, slope2, h2, even, a3, ap, slope3,
    back_big, back_small, gy2, stage_big, stage_small, wide_stage, dense_stage, d3, dp, pieces,
    w1t, w3t, w4t, wt0, wt1, sums, vec, rows_e, rows_c,
):
    micro = pl.program_id(0)
    images = counts.shape[1]
    fields = field_pair(images, slots)
    big, small = fields
    field_refs = {0: big_ref, images: small_ref}
    out_refs = {0: big_out, images: small_out}
    planes_of = {0: planes_big, images: planes_small}
    back_of = {0: back_big, images: back_small}
    stage_of = {0: stage_big, images: stage_small}
    crops = images * (1 + slots)
    out_total = small.out_row + small.count * small.out_area

    def living(field, crop):
        if field is big:
            return jnp.float32(1.0)
        return jnp.where(lax.rem(crop, slots) < counts[micro, crop // slots], 1.0, 0.0)

    alive = sum(counts[micro, i] for i in range(images)).astype(f32)
    count1 = images * big.area + small.area * alive
    count2 = images * big.out_area + small.out_area * alive

    @pl.when(micro == 0)
    def _():
        w1t[...] = w1[...].T
        w3t[...] = w3[...].T
        w4t[...] = w4[...].T
        wt0[...] = jnp.zeros_like(wt0)
        wt1[...] = jnp.zeros_like(wt1)

        def tap(ky, kx):
            start = (3 * ky + kx) * CMID
            return w2[start : start + CMID, :].T

        wt0[0:128, 0:128] = tap(1, 1)
        wt0[0:128, 128:256] = tap(1, 2)
        wt0[128:256, 128:256] = tap(1, 0)
        wt1[0:128, 0:128] = tap(2, 1)
        wt1[0:128, 128:256] = tap(2, 2)
        wt1[128:256, 128:256] = tap(2, 0)
        wt1[256:384, 0:128] = tap(0, 1)
        wt1[256:384, 128:256] = tap(0, 2)
        wt1[384:512, 128:256] = tap(0, 0)
        for ref in (loss_out, g1_out, g2_out, g3_out, g4_out, gain_out, shift_out):
            ref[...] = jnp.zeros_like(ref)
        for ref in (planes_big, planes_small, back_big, back_small, stage_big, stage_small):
            ref[...] = jnp.zeros_like(ref)
        gy2[...] = jnp.zeros_like(gy2)

    def flat(start, size):
        return at(start, size, 8)

    def blocked(block):
        return lambda start, size: at(block * out_total + start, size, 8)

    sums[...] = jnp.zeros_like(sums)

    def reduce_part(field, crop, first, rows):
        size = rows * 2 * field.side
        inside = crop * field.area + first * 2 * field.side
        start = field.row + inside
        a1[at(start, size)] = dot(field_refs[field.ahead][at(inside, size)], w1[...])
        if field is big:

            @pl.when(inside == 0)
            def _():
                total, _ = moments(a1, flat, start, size, 2 * field.side, 0.0)
                vec[0:1] = total.sum(0, keepdims=True) / size

        total, square = moments(a1, flat, start, size, 2 * field.side, vec[0:1])
        sums[0] += total * living(field, crop)
        sums[1] += square * living(field, crop)

    each_part(fields, reduce_part)
    mean1, root1 = closed(sums[0], sums[1], vec[0:1], count1)
    gain1, shift1 = line(gains, 0), line(shifts, 0)
    scale1 = root1 * gain1
    bias1 = shift1 - mean1 * scale1
    vec[1:2], vec[2:3], vec[3:4], vec[4:5] = mean1, root1, scale1, bias1

    def hidden_part(field, crop, first, rows):
        scale, bias = vec[3:4], vec[4:5]
        for k in range(rows):
            start = field.row + crop * field.area + (first + k) * 2 * field.side
            v = a1[at(start, 2 * field.side)] * scale + bias
            hidden, slope = gelu_pair(v)
            slope1[at(start, 2 * field.side)] = slope.astype(bf16)
            split_planes(hidden, stage_of[field.ahead], planes_of[field.ahead], field, crop, first + k, k % 2)

    each_part(fields, hidden_part)

    def spatial_part(field, crop, first, rows):
        half, wide = field.half, field.wide
        value = dot(patches(planes_of[field.ahead], field, crop, first, rows), w2[...])
        start = field.out_row + crop * field.out_area + first * half
        for k in range(rows):
            a2[pl.ds(start + k * half, half)] = value[k * wide : k * wide + half]

    each_part(fields, spatial_part)
    sums[...] = jnp.zeros_like(sums)

    def out_step(field):
        return 4 * field.half

    def spatial_moments(field, crop):
        start = field.out_row + crop * field.out_area
        if field is big:

            @pl.when(crop == 0)
            def _():
                total, _ = moments(a2, flat, start, field.out_area, out_step(field), 0.0)
                vec[0:1] = total.sum(0, keepdims=True) / field.out_area

        total, square = moments(a2, flat, start, field.out_area, out_step(field), vec[0:1])
        sums[0] += total * living(field, crop)
        sums[1] += square * living(field, crop)

    each_crop(fields, spatial_moments)
    mean2, root2 = closed(sums[0], sums[1], vec[0:1], count2)
    gain2, shift2 = line(gains, CMID), line(shifts, CMID)
    scale2 = root2 * gain2
    bias2 = shift2 - mean2 * scale2
    vec[5:6], vec[6:7], vec[7:8], vec[8:9] = mean2, root2, scale2, bias2

    sums[...] = jnp.zeros_like(sums)

    def expand_crop(field, crop):
        even_cells(field_refs[field.ahead], wide_stage, dense_stage, even, field, crop)
        start = field.out_row + crop * field.out_area
        step = out_step(field)
        scale, bias = vec[7:8], vec[8:9]
        for k in range(field.out_area // step):
            here = at(start + k * step, step)
            hidden, slope = gelu_pair(a2[here] * scale + bias)
            h2[here] = hidden.astype(bf16)
            slope2[here] = slope.astype(bf16)
        here = at(start, field.out_area)
        third = dot(h2[here], w3[...])
        for block in range(BLOCKS):
            a3[at(block * out_total + start, field.out_area)] = third[:, block * 128 : (block + 1) * 128]
        third = dot(even[here], w4[...])
        for block in range(BLOCKS):
            ap[at(block * out_total + start, field.out_area)] = third[:, block * 128 : (block + 1) * 128]
        for which, ref in ((0, a3), (1, ap)):
            for block in range(BLOCKS):
                row = 16 + which * 4 + block
                if field is big:

                    @pl.when(crop == 0)
                    def _():
                        total, _ = moments(ref, blocked(block), start, field.out_area, step, 0.0)
                        vec[row : row + 1] = total.sum(0, keepdims=True) / field.out_area

                total, square = moments(ref, blocked(block), start, field.out_area, step, vec[row : row + 1])
                place = which * 8 + block * 2
                sums[place] += total * living(field, crop)
                sums[place + 1] += square * living(field, crop)

    each_crop(fields, expand_crop)
    for which in range(2):
        for block in range(BLOCKS):
            row = which * 4 + block
            place = which * 8 + block * 2
            first = 2 * CMID + row * 128
            mean, root = closed(sums[place], sums[place + 1], vec[16 + row : 17 + row], count2)
            scale = root * line(gains, first)
            bias = line(shifts, first) - mean * scale
            vec[24 + row : 25 + row], vec[32 + row : 33 + row] = mean, root
            vec[40 + row : 41 + row] = scale
            if which == 0:
                vec[48 + block : 49 + block] = bias
            else:
                vec[48 + block : 49 + block] += bias

    def embed_crop(field, crop):
        start = field.out_row + crop * field.out_area
        step = out_step(field)
        for block in range(BLOCKS):
            mean3, mean4 = vec[24 + block : 25 + block], vec[28 + block : 29 + block]
            scale3, scale4 = vec[40 + block : 41 + block], vec[44 + block : 45 + block]
            bias = vec[48 + block : 49 + block]
            zero = jnp.zeros((8, 128), f32)
            e, s0, s3, s4 = zero, zero, zero, zero
            for k in range(field.out_area // step):
                here = at(block * out_total + start + k * step, step)
                x3, x4 = a3[here], ap[here]
                value, slope = gelu_pair(x3 * scale3 + x4 * scale4 + bias)
                slope3[here] = slope.astype(bf16)
                e += folded(value)
                s0 += folded(slope)
                s3 += folded(slope * (x3 - mean3))
                s4 += folded(slope * (x4 - mean4))
            row = field.ahead + crop
            for place, value in enumerate((e / field.out_area, s0, s3, s4)):
                rows_e[place, block, pl.ds(row, 1)] = value.sum(0, keepdims=True)

    each_crop(fields, embed_crop)

    def joined(place):
        return jnp.concatenate([rows_e[place, block] for block in range(BLOCKS)], axis=1)

    e = joined(0)
    inverse = lax.rsqrt(jnp.sum(e * e, axis=-1, keepdims=True) + UNIT_EPS)
    row = lax.broadcasted_iota(jnp.int32, (crops, 1), 0)
    owner = jnp.where(row < images, row, (row - images) // slots)
    live = jnp.where(row < images, 1.0, 0.0)
    for i in range(images):
        for slot in range(slots):
            here = row == images + i * slots + slot
            live = jnp.where(here, jnp.where(slot < counts[micro, i], 1.0, 0.0), live)
    embedding = e * inverse
    count = keys.shape[0] // BLOCKS
    key_blocks = [keys[pl.ds(block, count, stride=BLOCKS)] for block in range(BLOCKS)]
    logits = sum(
        dot_exact(embedding[:, block * 128 : (block + 1) * 128], key_blocks[block], ((1,), (1,)))
        for block in range(BLOCKS)
    )
    logits = logits / TEMP
    top = jnp.max(logits, axis=-1, keepdims=True)
    powers = jnp.exp(logits - top)
    total = jnp.sum(powers, axis=-1, keepdims=True)
    column = lax.broadcasted_iota(jnp.int32, logits.shape, 1)
    mine = column == device[0] * images + owner
    chosen = jnp.sum(jnp.where(mine, logits, 0.0), axis=-1, keepdims=True)
    ce = (top + jnp.log(total) - chosen) * live
    loss_out[...] += jnp.sum(ce, axis=0, keepdims=True)
    toward = (powers / total - jnp.where(mine, 1.0, 0.0)) * (live / TEMP)
    back = jnp.concatenate([dot_exact(toward, block, ((1,), (0,))) for block in key_blocks], axis=1)
    de = inverse * back - e * (inverse * inverse * inverse * jnp.sum(e * back, axis=-1, keepdims=True))
    de = de * jnp.where(row < images, 1.0 / big.out_area, 1.0 / small.out_area)
    sum0 = jnp.sum(de * joined(1), axis=0, keepdims=True)
    for which in range(2):
        reach = jnp.sum(de * joined(2 + which), axis=0, keepdims=True)
        for block in range(BLOCKS):
            row = which * 4 + block
            here = slice(block * 128, (block + 1) * 128)
            lanes = slice(2 * CMID + row * 128, 2 * CMID + (row + 1) * 128)
            mean, root, scale = vec[24 + row : 25 + row], vec[32 + row : 33 + row], vec[40 + row : 41 + row]
            along = reach[:, here] * root
            gain_out[:, lanes] += along
            shift_out[:, lanes] += sum0[:, here]
            tilt = scale * root * along / count2
            vec[52 + row : 53 + row] = tilt
            vec[60 + row : 61 + row] = scale * sum0[:, here] / count2 - tilt * mean
            rows_c[which, block] = de[:, here] * scale

    sums[...] = jnp.zeros_like(sums)

    def head_back(field, crop):
        start = field.out_row + crop * field.out_area
        size = field.out_area
        step = out_step(field)
        alive = living(field, crop)
        row = pl.ds(field.ahead + crop, 1)
        for which, ref, store in ((0, a3, d3), (1, ap, dp)):
            for block in range(BLOCKS):
                lanes = slice(block * 128, (block + 1) * 128)
                place = which * 4 + block
                rise = rows_c[which, block, row]
                tilt, level = vec[52 + place : 53 + place] * alive, vec[60 + place : 61 + place] * alive
                for k in range(size // step):
                    here = at(block * out_total + start + k * step, step)
                    grad = slope3[here].astype(f32) * rise - (ref[here] * tilt + level)
                    store[k * step : (k + 1) * step, lanes] = grad.astype(bf16)
        here = at(start, size)
        grad3, gradp = d3[0:size], dp[0:size]
        gy2[here] = dot(grad3, w3t[...])
        gradient = dot(gradp, w4t[...])
        for block in range(2):
            ap[at(block * out_total + start, size)] = gradient[:, block * 128 : (block + 1) * 128]
        g3_out[...] += dot_rows(h2[here], grad3)
        g4_out[...] += dot_rows(even[here], gradp)
        mean = vec[5:6]
        level, reach = jnp.zeros((8, 128), f32), jnp.zeros((8, 128), f32)
        for k in range(size // step):
            here = at(start + k * step, step)
            gy = gy2[here] * slope2[here].astype(f32)
            gy2[here] = gy
            level += folded(gy)
            reach += folded(gy * (a2[here] - mean))
        sums[0] += level
        sums[1] += reach

    each_crop(fields, head_back)

    def norm_back(place, lanes, count):
        mean, root, scale = vec[place : place + 1], vec[place + 1 : place + 2], vec[place + 2 : place + 3]
        level = sums[0].sum(0, keepdims=True)
        along = sums[1].sum(0, keepdims=True) * root
        gain_out[:, lanes] += along
        shift_out[:, lanes] += level
        tilt = scale * root * along / count
        vec[68:69] = scale
        vec[69:70] = tilt
        vec[70:71] = scale * level / count - tilt * mean

    norm_back(5, slice(CMID, 2 * CMID), count2)

    def spatial_grad_crop(field, crop):
        start = field.out_row + crop * field.out_area
        step = out_step(field)
        alive = living(field, crop)
        tilt, level = vec[69:70] * alive, vec[70:71] * alive
        for k in range(field.out_area // step):
            here = at(start + k * step, step)
            gy2[here] = gy2[here] * vec[68:69] - (a2[here] * tilt + level)

    each_crop(fields, spatial_grad_crop)

    def spread_part(field, crop, first, rows):
        half, wide = field.half, field.wide
        start = field.out_row + crop * field.out_area + first * half
        column = lax.broadcasted_iota(jnp.int32, (wide, 128), 0)
        store = back_of[field.ahead]
        for k in range(rows):
            own = jnp.where(column < half, gy2[pl.ds(start + k * half, wide)], 0.0)
            following = jnp.where(column < half - 1, gy2[pl.ds(start + k * half + 1, wide)], 0.0)
            store[crop, first + k, :, 0:128] = own.astype(bf16)
            store[crop, first + k, :, 128:256] = following.astype(bf16)

    each_part(fields, spread_part)

    sums[...] = jnp.zeros_like(sums)
    gy1 = a3

    def spatial_back(field, crop, first, rows):
        half, wide, side = field.half, field.wide, field.side
        store = back_of[field.ahead]
        near = store[crop, pl.ds(first, rows)].reshape(rows * wide, 256)
        beyond = store[crop, pl.ds(first + 1, rows)].reshape(rows * wide, 256)
        g2_out[...] += dot_rows(near[:, 0:128], patches(planes_of[field.ahead], field, crop, first, rows))
        upper = dot(near, wt0[...])
        lower = dot(near, wt1[0:256]) + dot(beyond, wt1[256:512])
        start = field.row + crop * field.area + first * 2 * side
        for k in range(rows):
            here = slice(k * wide, k * wide + half)
            line = start + k * 2 * side
            for odd, value in ((0, upper), (1, lower)):
                gy1[pl.ds(line + odd * side, half, stride=2)] = value[here, 0:128]
                gy1[pl.ds(line + odd * side + 1, half, stride=2)] = value[here, 128:256]
        mean = vec[1:2]
        level, reach = jnp.zeros((8, 128), f32), jnp.zeros((8, 128), f32)
        for k in range(rows):
            here = at(start + k * 2 * side, 2 * side)
            gy = gy1[here] * slope1[here].astype(f32)
            gy1[here] = gy
            level += folded(gy)
            reach += folded(gy * (a1[here] - mean))
        sums[0] += level
        sums[1] += reach

    each_part(fields, spatial_back)
    norm_back(1, slice(0, CMID), count1)

    out_stage = ap

    def reduce_back(field, crop, first, rows):
        half, side = field.half, field.side
        size = rows * 2 * side
        inside = crop * field.area + first * 2 * side
        start = field.row + inside
        alive = living(field, crop)
        rise, tilt, level = vec[68:69], vec[69:70] * alive, vec[70:71] * alive
        for k in range(rows):
            here = at(start + k * 2 * side, 2 * side)
            grad = gy1[here] * rise - (a1[here] * tilt + level)
            pieces[k * 2 * side : (k + 1) * 2 * side] = grad.astype(bf16)
        grad = pieces[0:size]
        g1_out[...] += dot_rows(grad, field_refs[field.ahead][at(inside, size)])
        whole = dot(grad, w1t[...])
        out_start = field.out_row + crop * field.out_area + first * half
        for block in range(2):
            lanes = slice(block * 128, (block + 1) * 128)
            base = 2 * out_total + block * (big.area // 2)
            out_stage[base : base + size] = whole[:, lanes]
            for k in range(rows):
                here = pl.ds(base + k * 2 * side, half, stride=2)
                out_stage[here] += ap[pl.ds(block * out_total + out_start + k * half, half)]
            out_refs[field.ahead][at(inside, size), lanes] = out_stage[base : base + size].astype(bf16)

    each_part(fields, reduce_back)


def query_pass(big, small, counts, device, weights, gains, shifts, keys, slots):
    micro, images = counts.shape
    one, two = field_pair(images, slots)
    rows = two.row + two.count * two.area
    outs = two.out_row + two.count * two.out_area
    crops = images * (1 + slots)
    vmem = pl.BlockSpec(memory_space=pltpu.VMEM)
    smem = pl.BlockSpec(memory_space=pltpu.SMEM)

    def block(shape):
        return pl.BlockSpec((None,) + shape, lambda m: (m,) + (0,) * len(shape))

    def total(shape):
        return pl.BlockSpec(shape, lambda m: (0,) * len(shape))

    totals = [(1, 1), (CMID, CIN), (CMID, 9 * CMID), (CMID, COUT), (CIN, COUT), (1, NORMS), (1, NORMS)]
    half, wide = one.half, one.wide
    scratch = [
        pltpu.VMEM((rows, 128), f32),
        pltpu.VMEM((rows, 128), bf16),
        pltpu.VMEM((2, one.count, one.half + 1, one.wide, 384), bf16),
        pltpu.VMEM((2, two.count, two.half + 1, two.wide, 384), bf16),
        pltpu.VMEM((outs, 128), f32),
        pltpu.VMEM((outs, 128), bf16),
        pltpu.VMEM((outs, 128), bf16),
        pltpu.VMEM((outs, CIN), bf16),
        pltpu.VMEM((BLOCKS * outs, 128), f32),
        pltpu.VMEM((BLOCKS * outs, 128), f32),
        pltpu.VMEM((BLOCKS * outs, 128), bf16),
        pltpu.VMEM((one.count, one.half + 1, one.wide, 256), bf16),
        pltpu.VMEM((two.count, two.half + 1, two.wide, 256), bf16),
        pltpu.VMEM((outs + 16, 128), f32),
        pltpu.VMEM((2, 2, 80, 128), f32),
        pltpu.VMEM((2, 2, 48, 128), f32),
        pltpu.VMEM((2, 56, 128), f32),
        pltpu.VMEM((one.out_area, 128), f32),
        pltpu.VMEM((one.out_area, COUT), bf16),
        pltpu.VMEM((one.out_area, COUT), bf16),
        pltpu.VMEM((one.area // 2, 128), bf16),
        pltpu.VMEM((CMID, CIN), bf16),
        pltpu.VMEM((COUT, CMID), bf16),
        pltpu.VMEM((COUT, CIN), bf16),
        pltpu.VMEM((256, 256), bf16),
        pltpu.VMEM((512, 256), bf16),
        pltpu.VMEM((16, 8, 128), f32),
        pltpu.VMEM((80, 128), f32),
        pltpu.VMEM((4, BLOCKS, crops, 128), f32),
        pltpu.VMEM((2, BLOCKS, crops, 128), f32),
    ]
    return pl.pallas_call(
        functools.partial(query_kernel, slots),
        grid=(micro,),
        out_shape=[jax.ShapeDtypeStruct(big.shape, bf16), jax.ShapeDtypeStruct(small.shape, bf16)]
        + [jax.ShapeDtypeStruct(shape, f32) for shape in totals],
        in_specs=[block(big.shape[1:]), block(small.shape[1:]), smem, smem]
        + [vmem] * 6
        + [block(keys.shape[1:])],
        out_specs=[block(big.shape[1:]), block(small.shape[1:])] + [total(shape) for shape in totals],
        scratch_shapes=scratch,
        compiler_params=pltpu.CompilerParams(vmem_limit_bytes=63 * 2**20, dimension_semantics=("arbitrary",)),
        name="query",
    )(big, small, counts, device, *weights, gains, shifts, keys)


MOMENTUM = 0.999
MESH = pl.DeviceIdType.MESH
PACK = 192
HALF_PACK = PACK // 2


def flipped(index, mask):
    bit = 1
    while bit <= mask:
        if mask & bit:
            index = index + bit * (1 - 2 * lax.rem(lax.div(index, bit), 2))
        bit *= 2
    return index


def packed_shards(shards, core, store, which):
    first, second, third, fourth = shards
    zero = jnp.zeros
    second = jnp.concatenate([second, zero((second.shape[0], 56), f32)], axis=1)
    second = jnp.concatenate([second, zero((64, 128), f32)], axis=0).T[0:72, 0:64]
    for start, part in ((0, first), (16, second)):
        rows, lanes = part.shape
        left = jnp.concatenate([part, zero((rows, lanes), f32)], axis=1)
        right = jnp.concatenate([zero((rows, lanes), f32), part], axis=1)
        value = jnp.where(core == 0, left, right)
        if rows % 16:
            value = jnp.concatenate([value, zero((16 - rows % 16, 128), f32)], axis=0)
        store[which, start : start + value.shape[0]] = value.astype(bf16)
    for pair in range(2):
        value = jnp.concatenate([third[:, 0:128], third[:, 128:256]], axis=0)
        value = jnp.where(core == pair, value, 0.0)
        store[which, 96 + pair * 16 : 112 + pair * 16] = value.astype(bf16)
        for block in range(2):
            value = jnp.where(core == pair, fourth[:, block * 128 : (block + 1) * 128], 0.0)
            start = 128 + (pair * 2 + block) * 16
            store[which, start : start + 16] = value.astype(bf16)


def unpacked(gathered, which, chips, w1, w2, w3, w4, stage):
    def turn(i, _):
        w1[at(i * 16, 16)] = gathered[which, i, 0:16]
        stage[at(i * 72, 72, 8)] = gathered[which, i, 16:96].astype(f32)[0:72]
        for block in range(BLOCKS):
            lanes = slice(block * 128, (block + 1) * 128)
            w4[at(i * 16, 16), lanes] = gathered[which, i, 128 + block * 16 : 144 + block * 16]
        return 0

    lax.fori_loop(0, chips, turn, 0)
    w2[...] = stage[0 : 9 * CMID].astype(bf16)

    def pairs(i, _):
        a = gathered[which, i * 2, 96:128].astype(f32)
        b = gathered[which, i * 2 + 1, 96:128].astype(f32)
        for block in range(BLOCKS):
            rows = slice(block * 8, (block + 1) * 8)
            w3[at(i * 16, 16), block * 128 : (block + 1) * 128] = jnp.concatenate([a[rows], b[rows]], axis=0).astype(bf16)
        return 0

    lax.fori_loop(0, chips // 2, pairs, 0)


def key_kernel(
    axes, gather,
    field_hbm, mask,
    r0, s0, e0, p0, r1, s1, e1, p1, gains, shifts, gains1, shifts1,
    w1q, w2q, w3q, w4q, keys_out,
    field, a1, planes, a2, h2, even, a3, ap, stage, wide_stage, dense_stage, vec,
    first_low, first_high, embed, sent, swapped_in, gathered, unpack_stage, w1, w2, w3, w4,
    load_sem, low_send, low_recv, high_send, high_recv, core_send, core_recv,
    wide_send, wide_recv, join_send, join_recv, key_send, key_recv,
):
    chips, cores = axes
    devices = chips * cores
    bits = devices.bit_length() - 1
    lows = 1 << (bits + 1) // 2
    highs = devices // lows
    micro = field_hbm.shape[0]
    big = Field(2, SIDE, 0, 0, 0)
    chip, core = lax.axis_index("dp"), lax.axis_index("fsdp")
    me = chip * cores + core

    def place(device):
        return (lax.div(device, cores), lax.rem(device, cores))

    loads = [
        pltpu.make_async_copy(field_hbm.at[m, pl.ds(c * big.area, big.area)], field.at[m, pl.ds(c * big.area, big.area)], load_sem.at[m, c])
        for m in range(micro)
        for c in range(2)
    ]
    for load in loads:
        load.start()

    barrier = pltpu.get_barrier_semaphore()

    def greet(k, _):
        pl.semaphore_signal(barrier, inc=1, device_id=place(lax.rem(me + k, devices)), device_id_type=MESH)
        return 0

    lax.fori_loop(1, devices, greet, 0)

    if gather:
        packed_shards([r[...] for r in (r0, s0, e0, p0)], core, sent, 1)
        fresh = [MOMENTUM * b[...] + (1.0 - MOMENTUM) * a[...] for a, b in ((r0, r1), (s0, s1), (e0, e1), (p0, p1))]
        packed_shards(fresh, core, sent, 0)
    planes[...] = jnp.zeros_like(planes)
    stage[...] = jnp.zeros_like(stage)
    pl.semaphore_wait(barrier, devices - 1)

    own_half = pl.ds(pl.multiple_of(core * HALF_PACK, HALF_PACK), HALF_PACK)

    def core_copy(which):
        return pltpu.make_async_remote_copy(
            src_ref=sent.at[which], dst_ref=swapped_in.at[which], send_sem=core_send.at[which],
            recv_sem=core_recv.at[which], device_id=(chip, 1 - core), device_id_type=MESH)

    def wide_copy(which, k):
        return pltpu.make_async_remote_copy(
            src_ref=gathered.at[which, chip, own_half], dst_ref=gathered.at[which, chip, own_half],
            send_sem=wide_send.at[which, k], recv_sem=wide_recv.at[which, k],
            device_id=(lax.rem(chip + k, chips), core), device_id_type=MESH)

    def join_copy(which):
        return pltpu.make_async_remote_copy(
            src_ref=gathered.at[which, :, own_half], dst_ref=gathered.at[which, :, own_half],
            send_sem=join_send.at[which], recv_sem=join_recv.at[which],
            device_id=(chip, 1 - core), device_id_type=MESH)

    def spread_start(which):
        core_copy(which).wait()
        gathered[which, chip, own_half] = sent[which, own_half] + swapped_in[which, own_half]

        def turn(k, _):
            wide_copy(which, k).start()
            return 0

        lax.fori_loop(1, chips, turn, 0)

    def spread_join(which):
        def turn(k, _):
            wide_copy(which, k).wait()
            return 0

        lax.fori_loop(1, chips, turn, 0)
        join_copy(which).start()

    if gather:
        for which in range(2):
            core_copy(which).start()
        for which in range(2):
            spread_start(which)

    for load in loads:
        load.wait()
    for m in range(micro):
        for c in range(2):
            even_cells(field.at[m], wide_stage, dense_stage, even.at[m], big, c)

    if gather:
        spread_join(0)
        join_copy(0).wait()
        unpacked(gathered, 0, chips, w1, w2, w3, w4, unpack_stage)
    else:
        for source, target in ((r1, w1), (s1, w2), (e1, w3), (p1, w4)):
            target[...] = source[...]

    def low_copy(m, turn, k, rows):
        return pltpu.make_async_remote_copy(
            src_ref=first_low[m * 3 + turn].at[0, pl.ds(0, rows)], dst_ref=first_low[m * 3 + turn].at[k, pl.ds(0, rows)],
            send_sem=low_send.at[m, turn, k], recv_sem=low_recv.at[m, turn, k],
            device_id=place(flipped(me, k)), device_id_type=MESH)

    def high_copy(m, turn, k, rows):
        return pltpu.make_async_remote_copy(
            src_ref=first_high[m * 3 + turn].at[0, pl.ds(0, rows)], dst_ref=first_high[m * 3 + turn].at[k, pl.ds(0, rows)],
            send_sem=high_send.at[m, turn, k], recv_sem=high_recv.at[m, turn, k],
            device_id=place(flipped(me, k * lows)), device_id_type=MESH)

    ROWS = (24, 8, 16)

    def exchange_start(m, turn):
        for k in range(1, lows):
            low_copy(m, turn, k, ROWS[turn]).start()

    def exchange_middle(m, turn):
        for k in range(1, lows):
            low_copy(m, turn, k, ROWS[turn]).wait()
        pick = lax.rem(jnp.bitwise_xor(mask[m, 0], mask[m, 1]), lows)
        first_high[m * 3 + turn][0] = first_low[m * 3 + turn][pick]
        for k in range(1, highs):
            high_copy(m, turn, k, ROWS[turn]).start()

    def exchange_end(m, turn):
        for k in range(1, highs):
            high_copy(m, turn, k, ROWS[turn]).wait()

    def put_moments(m, turn, row, total, square, pivot, count):
        off = total.sum(0, keepdims=True) / count
        first_low[m * 3 + turn][0, row : row + 1] = pivot + off
        first_low[m * 3 + turn][0, row + 1 : row + 2] = jnp.maximum(square.sum(0, keepdims=True) - off * off * count, 0.0)

    def combined(m, turn, crop, blocks, block, base, count):
        pick = lax.div(jnp.bitwise_xor(mask[m, 0], mask[m, 1]), lows)
        row = base + (crop * blocks + block) * 2
        other = base + ((1 - crop) * blocks + block) * 2
        theirs = first_high[m * 3 + turn][pick]
        mean, spread = first_low[m * 3 + turn][0, row : row + 1], first_low[m * 3 + turn][0, row + 1 : row + 2]
        mean2, spread2 = theirs[other : other + 1], theirs[other + 1 : other + 2]
        apart = mean - mean2
        variance = (spread + spread2 + apart * apart * (count * 0.5)) / (2.0 * count)
        return (mean + mean2) * 0.5, lax.rsqrt(variance + NORM_EPS)

    def affine(mean, root, start):
        new_gain = MOMENTUM * line(gains1, start) + (1.0 - MOMENTUM) * line(gains, start)
        new_shift = MOMENTUM * line(shifts1, start) + (1.0 - MOMENTUM) * line(shifts, start)
        scale = root * new_gain
        return scale, new_shift - mean * scale

    def crop_moments(ref, m, start, size, step):
        pivot = folded(ref[m, at(start, step, 8)]).sum(0, keepdims=True) / step
        total, square = jnp.zeros((8, 128), f32), jnp.zeros((8, 128), f32)
        for k in range(size // step):
            x = ref[m, at(start + k * step, step, 8)] - pivot
            total += folded(x)
            square += folded(x * x)
        return total, square, pivot

    step_out = 4 * big.half

    def stage_a(m, c):
        for part in range(2):
            here = at(c * big.area + part * (big.area // 2), big.area // 2)
            a1[m, here] = dot(field[m, here], w1[...])
        total, square, pivot = crop_moments(a1, m, c * big.area, big.area, 2 * SIDE)
        put_moments(m, 0, c * 2, total, square, pivot, big.area)
        here = at(c * big.out_area, big.out_area)
        value = dot(even[m, here], w4[...])
        for block in range(BLOCKS):
            start = block * 2 * big.out_area + c * big.out_area
            ap[m, at(start, big.out_area)] = value[:, block * 128 : (block + 1) * 128]
            total, square, pivot = crop_moments(ap, m, start, big.out_area, step_out)
            put_moments(m, 0, 8 + (c * BLOCKS + block) * 2, total, square, pivot, big.out_area)

    def stage_b(m, c):
        scale, bias = affine(*combined(m, 0, c, 1, 0, 0, float(big.area)), 0)

        def turn(y, _):
            for k in range(2):
                line = y * 2 + k
                v = a1[m, at(c * big.area + line * 2 * SIDE, 2 * SIDE)] * scale + bias
                split_planes(gelu_only(v), stage, planes.at[m], big, c, line, k)
            return 0

        lax.fori_loop(0, big.half // 2, turn, 0)
        for part in range(2):
            rows = big.half // 2
            value = dot(patches(planes.at[m], big, c, part * rows, rows), w2[...])
            for k in range(rows):
                start = c * big.out_area + (part * rows + k) * big.half
                a2[m, pl.ds(start, big.half)] = value[k * big.wide : k * big.wide + big.half]
        total, square, pivot = crop_moments(a2, m, c * big.out_area, big.out_area, step_out)
        put_moments(m, 1, c * 2, total, square, pivot, big.out_area)

    def stage_c(m, c):
        scale, bias = affine(*combined(m, 1, c, 1, 0, 0, float(big.out_area)), CMID)
        for k in range(big.out_area // step_out):
            here = at(c * big.out_area + k * step_out, step_out)
            h2[m, here] = gelu_only(a2[m, here] * scale + bias).astype(bf16)
        value = dot(h2[m, at(c * big.out_area, big.out_area)], w3[...])
        for block in range(BLOCKS):
            start = block * 2 * big.out_area + c * big.out_area
            a3[m, at(start, big.out_area)] = value[:, block * 128 : (block + 1) * 128]
            total, square, pivot = crop_moments(a3, m, start, big.out_area, step_out)
            put_moments(m, 2, (c * BLOCKS + block) * 2, total, square, pivot, big.out_area)

    def stage_d(m):
        for c in range(2):
            parts = []
            for block in range(BLOCKS):
                lanes = 2 * CMID + block * 128
                scale3, bias3 = affine(*combined(m, 2, c, BLOCKS, block, 0, float(big.out_area)), lanes)
                scale4, bias4 = affine(*combined(m, 0, c, BLOCKS, block, 8, float(big.out_area)), lanes + COUT)
                bias = bias3 + bias4
                e = jnp.zeros((8, 128), f32)
                for k in range(big.out_area // step_out):
                    here = at(block * 2 * big.out_area + c * big.out_area + k * step_out, step_out)
                    e += folded(gelu_only(a3[m, here] * scale3 + ap[m, here] * scale4 + bias))
                parts.append(e.sum(0, keepdims=True) / big.out_area)
            length = sum(jnp.sum(part * part, axis=1, keepdims=True) for part in parts)
            inverse = lax.rsqrt(length + UNIT_EPS)
            for block in range(BLOCKS):
                embed[m, c * BLOCKS + block : c * BLOCKS + block + 1] = parts[block] * inverse
        keys_out[m, me] = embed[m]

    def key_copy(m, k):
        return pltpu.make_async_remote_copy(
            src_ref=embed.at[m], dst_ref=keys_out.at[m, me], send_sem=key_send.at[m, k], recv_sem=key_recv.at[m, k],
            device_id=place(lax.rem(me + k, devices)), device_id_type=MESH)

    def share_start(m):
        def turn(k, _):
            key_copy(m, k).start()
            return 0

        lax.fori_loop(1, devices, turn, 0)

    def share_end(m):
        def turn(k, _):
            key_copy(m, k).wait()
            return 0

        lax.fori_loop(1, devices, turn, 0)

    lead, lag = 0, 1
    stage_a(lead, 0)
    stage_a(lead, 1)
    exchange_start(lead, 0)
    stage_a(lag, 0)
    exchange_middle(lead, 0)
    stage_a(lag, 1)
    exchange_start(lag, 0)
    exchange_end(lead, 0)
    stage_b(lead, 0)
    exchange_middle(lag, 0)
    stage_b(lead, 1)
    exchange_start(lead, 1)
    exchange_end(lag, 0)
    stage_b(lag, 0)
    exchange_middle(lead, 1)
    stage_b(lag, 1)
    exchange_start(lag, 1)
    exchange_end(lead, 1)
    stage_c(lead, 0)
    exchange_middle(lag, 1)
    stage_c(lead, 1)
    exchange_start(lead, 2)
    exchange_end(lag, 1)
    stage_c(lag, 0)
    exchange_middle(lead, 2)
    stage_c(lag, 1)
    exchange_start(lag, 2)
    if gather:
        spread_join(1)
    exchange_end(lead, 2)
    stage_d(lead)
    share_start(lead)
    exchange_middle(lag, 2)
    if gather:
        join_copy(1).wait()
        unpacked(gathered, 1, chips, w1q, w2q, w3q, w4q, unpack_stage)
    exchange_end(lag, 2)
    stage_d(lag)
    share_start(lag)
    share_end(lead)
    share_end(lag)


def key_pass(axes, gather, field, mask, current, lagged, gains, shifts, gains1, shifts1):
    chips, cores = axes
    devices = chips * cores
    bits = devices.bit_length() - 1
    lows = 1 << (bits + 1) // 2
    highs = devices // lows
    micro = field.shape[0]
    big = Field(2, SIDE, 0, 0, 0)
    vmem = pl.BlockSpec(memory_space=pltpu.VMEM)
    smem = pl.BlockSpec(memory_space=pltpu.SMEM)
    hbm = pl.BlockSpec(memory_space=pl.ANY)
    dma = pltpu.SemaphoreType.DMA
    weights = [(CIN, CMID), (9 * CMID, CMID), (CMID, COUT), (CIN, COUT)]
    rows, outs = 2 * big.area, 2 * big.out_area
    scratch = [
        pltpu.VMEM((micro, rows, CIN), bf16),
        pltpu.VMEM((micro, rows, 128), f32),
        pltpu.VMEM((micro, 2, 2, big.half + 1, big.wide, 384), bf16),
        pltpu.VMEM((micro, outs, 128), f32),
        pltpu.VMEM((micro, outs, 128), bf16),
        pltpu.VMEM((micro, outs, CIN), bf16),
        pltpu.VMEM((micro, BLOCKS * outs, 128), f32),
        pltpu.VMEM((micro, BLOCKS * outs, 128), f32),
        pltpu.VMEM((2, 2, 80, 128), f32),
        pltpu.VMEM((2, 56, 128), f32),
        pltpu.VMEM((big.out_area, 128), f32),
        pltpu.VMEM((8, 128), f32),
        [pltpu.VMEM((lows, rows_of, 128), f32) for _ in range(micro) for rows_of in (24, 8, 16)],
        [pltpu.VMEM((highs, rows_of, 128), f32) for _ in range(micro) for rows_of in (24, 8, 16)],
        pltpu.VMEM((micro, 8, 128), f32),
        pltpu.VMEM((2, PACK, 128), bf16),
        pltpu.VMEM((2, PACK, 128), bf16),
        pltpu.VMEM((2, chips, PACK, 128) if gather else (1, 1, 16, 128), bf16),
        pltpu.VMEM((9 * CMID, 128), f32),
    ]
    scratch += [pltpu.VMEM(shape, bf16) for shape in weights]
    scratch += [dma((micro, 2)), dma((micro, 3, lows)), dma((micro, 3, lows)), dma((micro, 3, highs)), dma((micro, 3, highs))]
    scratch += [dma((2,)), dma((2,)), dma((2, chips)), dma((2, chips)), dma((2,)), dma((2,))]
    scratch += [dma((micro, devices)), dma((micro, devices))]
    out = pl.pallas_call(
        functools.partial(key_kernel, axes, gather),
        out_shape=[jax.ShapeDtypeStruct(shape if gather else (16, 128), bf16) for shape in weights]
        + [jax.ShapeDtypeStruct((micro, devices, 8, 128), f32)],
        in_specs=[hbm, smem] + [vmem] * 12,
        out_specs=[vmem] * 5,
        scratch_shapes=scratch,
        compiler_params=pltpu.CompilerParams(vmem_limit_bytes=60 * 2**20, collective_id=0, has_side_effects=True),
        name="keys",
    )(field, mask, *current, *lagged, gains, shifts, gains1, shifts1)
    return out[4], out[:4]


STAT = 16
CHUNK = 4


def reduce_kernel(
    axes,
    g1, g2, g3, g4, loss, gains, shifts, out,
    whole, parts, stats, arrived, stats_in, sending, landed,
    swap_send, swap_recv, wide_send, wide_recv, join_send, join_recv,
):
    chips, _ = axes
    chip, core = lax.axis_index("dp"), lax.axis_index("fsdp")
    sibling = (chip, 1 - core)
    barrier = pltpu.get_barrier_semaphore()
    pl.semaphore_signal(barrier, inc=1, device_id=sibling, device_id_type=MESH)

    def greet(k, _):
        pl.semaphore_signal(barrier, inc=1, device_id=(lax.rem(chip + k, chips), core), device_id_type=MESH)
        return 0

    lax.fori_loop(1, chips, greet, 0)

    stats[...] = jnp.zeros_like(stats)
    for row in range(NORMS // 128):
        lanes = slice(row * 128, (row + 1) * 128)
        stats[0, row : row + 1] = gains[:, lanes]
        stats[1, row : row + 1] = shifts[:, lanes]
    column = lax.broadcasted_iota(jnp.int32, (1, 128), 1)
    stats[0, 10:11] = jnp.where(column == 0, loss[...], 0.0)

    def fill(i, _):
        for block in range(BLOCKS):
            lanes = slice(block * 128, (block + 1) * 128)
            parts[1, i, block * 8 : (block + 1) * 8] = g3[at(i * 8, 8, 8), lanes]
            parts[1, i, 32 + block * 16 : 48 + block * 16] = g4[at(i * 16, 16), lanes]
        parts[0, i, 0:16] = whole[at(i * 16, 16)]
        parts[0, i, 16:88] = whole[at(CIN + i * 72, 72, 8)]
        parts[0, i, 88:96] = jnp.zeros((8, 128), f32)
        return 0

    for tile in range(2):
        whole[tile * 128 : (tile + 1) * 128] = g1[:, tile * 128 : (tile + 1) * 128].T
    for tile in range(9):
        start = CIN + tile * 128
        whole[start : start + 128] = g2[:, tile * 128 : (tile + 1) * 128].T
    lax.fori_loop(0, chips, fill, 0)
    pl.semaphore_wait(barrier, chips)

    def chunk_of(turn):
        return pl.multiple_of(lax.rem(lax.div(chip, CHUNK) + turn, chips // CHUNK) * CHUNK, CHUNK)

    def swap_copy(turn, start):
        here = pl.ds(start, CHUNK)
        return pltpu.make_async_remote_copy(
            src_ref=parts.at[1 - core, here], dst_ref=arrived.at[here], send_sem=swap_send.at[turn],
            recv_sem=swap_recv.at[turn], device_id=sibling, device_id_type=MESH)

    stat_copy = pltpu.make_async_remote_copy(
        src_ref=stats.at[1 - core], dst_ref=stats_in, send_sem=swap_send.at[chips // CHUNK],
        recv_sem=swap_recv.at[chips // CHUNK], device_id=sibling, device_id_type=MESH)
    stat_copy.start()
    for turn in range(chips // CHUNK):
        swap_copy(turn, chunk_of(turn)).start()
    stat_copy.wait()
    both = stats[core] + stats_in[...]
    coarse = both.astype(bf16)
    fine = (both - coarse.astype(f32)).astype(bf16)

    def wide_copy(target, source):
        return pltpu.make_async_remote_copy(
            src_ref=sending.at[target], dst_ref=landed.at[source], send_sem=wide_send.at[target],
            recv_sem=wide_recv.at[source], device_id=(target, core), device_id_type=MESH)

    for turn in range(chips // CHUNK):
        start = chunk_of(turn)
        swap_copy(turn, start).wait()
        for k in range(CHUNK):
            target = start + lax.rem(chip + k, CHUNK)
            sending[target, 0:HALF_PACK] = (parts[core, target] + arrived[target]).astype(bf16)
            sending[target, HALF_PACK : HALF_PACK + STAT] = coarse
            sending[target, HALF_PACK + STAT : HALF_PACK + 2 * STAT] = fine

            @pl.when(target != chip)
            def _():
                wide_copy(target, chip).start()

    total = sending[chip].astype(f32)

    def add(k, total):
        source = lax.rem(chip + chips - k, chips)
        wide_copy(source, source).wait_recv()
        return total + landed[source].astype(f32)

    total = lax.fori_loop(1, chips, add, total)
    out[core, 0:HALF_PACK] = total[0:HALF_PACK]
    out[core, HALF_PACK : HALF_PACK + STAT] = total[HALF_PACK : HALF_PACK + STAT] + total[HALF_PACK + STAT :]
    join = pltpu.make_async_remote_copy(
        src_ref=out.at[core], dst_ref=out.at[core], send_sem=join_send, recv_sem=join_recv,
        device_id=sibling, device_id_type=MESH)
    join.start()

    def drain(k, _):
        target = lax.rem(chip + k, chips)
        wide_copy(target, chip).wait_send()
        return 0

    lax.fori_loop(1, chips, drain, 0)
    join.wait()


def finish_kernel(device, packed, loss, reduce_out, spatial_out, expand_out, shortcut_out, gains, shifts):
    core = lax.rem(device[0], 2)
    here = core == 0
    reduce_out[...] = jnp.where(here, packed[0, 0:16, 0:64], packed[0, 0:16, 64:128])
    wide = jnp.concatenate([packed[0, 16:88], jnp.zeros((56, 128), f32)], axis=0).T
    spatial_out[...] = jnp.where(here, wide[0:64, 0:72], wide[64:128, 0:72])
    for block in range(2):
        lanes = slice(block * 128, (block + 1) * 128)
        first, second = block, block + 2
        expand_out[:, lanes] = jnp.where(
            here, packed[1, first * 8 : first * 8 + 8], packed[1, second * 8 : second * 8 + 8])
        shortcut_out[:, lanes] = jnp.where(
            here, packed[1, 32 + first * 16 : 48 + first * 16], packed[1, 32 + second * 16 : 48 + second * 16])
    for row in range(NORMS // 128):
        lanes = pl.ds(row * 128, 128)
        gains[lanes] = packed[0, HALF_PACK + row]
        shifts[lanes] = packed[1, HALF_PACK + row]
    loss[...] = packed[0, HALF_PACK + 10 : HALF_PACK + 11, 0:1]


def reduce_pass(axes, device, totals):
    chips, _ = axes
    vmem = pl.BlockSpec(memory_space=pltpu.VMEM)
    smem = pl.BlockSpec(memory_space=pltpu.SMEM)
    dma = pltpu.SemaphoreType.DMA
    rows = HALF_PACK + 2 * STAT
    packed = pl.pallas_call(
        functools.partial(reduce_kernel, axes),
        out_shape=jax.ShapeDtypeStruct((2, HALF_PACK + STAT, 128), f32),
        in_specs=[vmem] * 7,
        out_specs=vmem,
        scratch_shapes=[
            pltpu.VMEM((CIN + 9 * CMID, 128), f32),
            pltpu.VMEM((2, chips, HALF_PACK, 128), f32),
            pltpu.VMEM((2, STAT, 128), f32),
            pltpu.VMEM((chips, HALF_PACK, 128), f32),
            pltpu.VMEM((STAT, 128), f32),
            pltpu.VMEM((chips, rows, 128), bf16),
            pltpu.VMEM((chips, rows, 128), bf16),
            dma((chips // CHUNK + 1,)), dma((chips // CHUNK + 1,)), dma((chips,)), dma((chips,)), dma(()), dma(()),
        ],
        compiler_params=pltpu.CompilerParams(vmem_limit_bytes=40 * 2**20, collective_id=1, has_side_effects=True),
        name="reduce",
    )(*totals)
    shapes = [(1, 1), (16, 64), (64, 72), (8, 256), (16, 256), (NORMS,), (NORMS,)]
    return pl.pallas_call(
        finish_kernel,
        out_shape=[jax.ShapeDtypeStruct(shape, f32) for shape in shapes],
        in_specs=[smem, vmem],
        out_specs=[vmem] * 7,
        name="finish",
    )(device, packed)


def gather_weights(shards):
    rows = [lax.all_gather(part, "dp", axis=0, tiled=True) for part in shards]
    return [lax.all_gather(part, "fsdp", axis=1, tiled=True) for part in rows]


def per_device(axes, *args):
    query_global, small_crop_query, small_count, key_global, shuffle_mask = args[:5]
    current, (norm_gains, norm_shifts) = args[5:9], args[9:11]
    lagged, (lagged_gains, lagged_shifts) = args[11:15], args[15:17]
    micro, images = query_global.shape[:2]
    slots = small_crop_query.shape[2]
    chips, cores = axes
    gather = chips == 16 and cores == 2
    device = (lax.axis_index("dp") * cores + lax.axis_index("fsdp")).astype(jnp.int32).reshape(1)
    vectors = [norm_gains, norm_shifts, lagged_gains, lagged_shifts]
    sources, targets = current, lagged
    if not gather:
        fresh = [MOMENTUM * old + (1.0 - MOMENTUM) * new for old, new in zip(lagged, current)]
        sources = gather_weights([w.astype(bf16) for w in current])
        targets = gather_weights([w.astype(bf16) for w in fresh])
    else:
        sources = [w.T if i == 1 else w for i, w in enumerate(sources)]
        targets = [w.T if i == 1 else w for i, w in enumerate(targets)]
    keys, weights = key_pass(
        axes, gather, key_global.reshape(micro, -1, CIN), shuffle_mask, sources, targets, *vectors
    )
    out = query_pass(
        query_global.reshape(micro, -1, CIN), small_crop_query.reshape(micro, -1, CIN), small_count, device,
        weights if gather else sources, vectors[0], vectors[1], keys.reshape(micro, -1, 128), slots,
    )
    fields = (out[0].reshape(query_global.shape), out[1].reshape(small_crop_query.shape))
    if gather:
        loss, first, second, third, fourth, gains_grad, shifts_grad = reduce_pass(axes, device, (*out[3:7], out[2], *out[7:]))
        return (loss.reshape(()), *fields, first, second.T, third, fourth, gains_grad, shifts_grad)
    totals = (out[3].T, out[4].T, out[5], out[6])
    summed = lax.psum_scatter(totals, "dp", scatter_dimension=0, tiled=True)
    owned = lax.psum_scatter(summed, "fsdp", scatter_dimension=1, tiled=True)
    loss, gains_grad, shifts_grad = lax.psum((out[2], out[7], out[8]), ("dp", "fsdp"))
    return (
        loss.reshape(()),
        *fields,
        *owned,
        gains_grad.reshape(NORMS),
        shifts_grad.reshape(NORMS),
    )


def solution(mesh):
    whole, split = P(), P("dp", "fsdp")
    images, crops = P(None, ("dp", "fsdp"), None, None, None), P(None, ("dp", "fsdp"), None, None, None, None)
    axes = (mesh.shape["dp"], mesh.shape["fsdp"])
    return jax.shard_map(
        functools.partial(per_device, axes),
        mesh=mesh,
        in_specs=(images, crops, P(None, ("dp", "fsdp")), images, whole)
        + (split,) * 4 + (whole,) * 2 + (split,) * 4 + (whole,) * 2,
        out_specs=(whole, images, crops) + (split,) * 4 + (whole,) * 2,
        check_vma=False,
    )
```

```python
import functools
import types
import jax
import jax.numpy as jnp
from jax import lax
from jax.experimental import pallas as pl
from jax.experimental.pallas import tpu as pltpu
from jax.sharding import PartitionSpec as P

f32, bf16 = jnp.float32, jnp.bfloat16
CIN, CMID, COUT, NORMS = 256, 128, 512, 1280
SIDE, SMALL = 56, 24
BLOCKS = COUT // 128
TEMP, NORM_EPS, UNIT_EPS = 0.2, 1e-05, 1e-06
ROOT_HALF = 0.7071067811865476
DENSITY = 0.3989422804014327


class Field:
    def __init__(self, count, side, row, out_row, ahead):
        self.count, self.side, self.row, self.out_row = count, side, row, out_row
        self.ahead = ahead
        self.half = side // 2
        self.wide = -(-self.half // 16) * 16
        self.area, self.out_area = side * side, (side // 2) ** 2


def field_pair(images, slots):
    big = Field(images, SIDE, 0, 0, 0)
    small = Field(images * slots, SMALL, images * big.area, images * big.out_area, images)
    return big, small


def at(start, size, align=16):
    return pl.ds(pl.multiple_of(start, align), size)


def folded(x):
    return x.reshape(x.shape[0] // 8, 8, x.shape[1]).sum(0)


def dot(a, b):
    return jnp.dot(a, b, preferred_element_type=f32)


def dot_rows(a, b):
    return lax.dot_general(a, b, (((0,), (0,)), ((), ())), preferred_element_type=f32)


def dot_exact(a, b, dims):
    return lax.dot_general(a, b, (dims, ((), ())), precision=lax.Precision.HIGHEST, preferred_element_type=f32)


def gelu_pair(v):
    share = 0.5 + 0.5 * lax.erf(v * ROOT_HALF)
    return v * share, share + v * (DENSITY * jnp.exp(v * v * -0.5))


def gelu_only(v):
    return v * (0.5 + 0.5 * lax.erf(v * ROOT_HALF))


MOMENTUM = 0.999
MESH = pl.DeviceIdType.MESH
PACK = 192
HALF_PACK = PACK // 2
JOB = 48
TURN_ROWS = (48, 16, 32)


def line(vector, start):
    return vector[pl.ds(start, 128)].reshape(1, 128)


def moments(ref, start, size, step, pivot):
    total = jnp.zeros((8, 128), f32)
    square = jnp.zeros((8, 128), f32)
    for k in range(size // step):
        x = ref[at(start + k * step, step, 8)] - pivot
        total += folded(x)
        square += folded(x * x)
    return total, square


def closed(total, square, pivot, count):
    off = total.sum(0, keepdims=True) / count
    spread = jnp.maximum(square.sum(0, keepdims=True) / count - off * off, 0.0)
    return pivot + off, lax.rsqrt(spread + NORM_EPS)


def patches(planes, field, first, crops):
    size = crops * field.half * field.wide
    here = pl.ds(first, crops)
    above = planes[1, here, 0 : field.half].reshape(size, 3 * CMID)
    level = planes[0, here, 0 : field.half].reshape(size, 3 * CMID)
    below = planes[1, here, 1 : field.half + 1].reshape(size, 3 * CMID)
    return jnp.concatenate([above, level, below], axis=1)


def split_planes(hidden, stage, planes, field, crop, row, slot):
    side, wide = field.side, field.wide
    for odd in range(2):
        stage[slot, odd, 8 : 8 + side] = hidden[odd * side : (odd + 1) * side]
    for odd in range(2):
        for tap in range(3):
            column = stage[slot, odd, pl.ds(7 + tap, wide, stride=2)]
            planes[odd, crop, row + odd, :, tap * CMID : (tap + 1) * CMID] = column.astype(bf16)


def even_cells(source, base, field, wide_stage, dense_stage, put):
    side, half = field.side, field.half
    for y in range(half):
        for block in range(CIN // 128):
            slot = y % 4 * 2 + block
            x = source[at(base + y * 2 * side, 2 * side), block * 128 : (block + 1) * 128]
            wide_stage[slot, 0:side] = x.astype(f32)[0:side]
            dense_stage[block, y * half : (y + 1) * half] = wide_stage[slot, pl.ds(0, half, stride=2)]
    for block in range(CIN // 128):
        put(block, dense_stage[block, 0 : field.out_area].astype(bf16))


def flipped(index, mask):
    bit = 1
    while bit <= mask:
        if mask & bit:
            index = index + bit * (1 - 2 * lax.rem(lax.div(index, bit), 2))
        bit *= 2
    return index


def packed_shards(shards, core, store, which):
    first, second, third, fourth = shards
    zero = jnp.zeros
    second = jnp.concatenate([second, zero((second.shape[0], 56), f32)], axis=1)
    second = jnp.concatenate([second, zero((64, 128), f32)], axis=0).T[0:72, 0:64]
    for start, part in ((0, first), (16, second)):
        rows, lanes = part.shape
        left = jnp.concatenate([part, zero((rows, lanes), f32)], axis=1)
        right = jnp.concatenate([zero((rows, lanes), f32), part], axis=1)
        value = jnp.where(core == 0, left, right)
        if rows % 16:
            value = jnp.concatenate([value, zero((16 - rows % 16, 128), f32)], axis=0)
        store[which, start : start + value.shape[0]] = value.astype(bf16)
    for pair in range(2):
        value = jnp.concatenate([third[:, 0:128], third[:, 128:256]], axis=0)
        value = jnp.where(core == pair, value, 0.0)
        store[which, 96 + pair * 16 : 112 + pair * 16] = value.astype(bf16)
        for block in range(2):
            value = jnp.where(core == pair, fourth[:, block * 128 : (block + 1) * 128], 0.0)
            start = 128 + (pair * 2 + block) * 16
            store[which, start : start + 16] = value.astype(bf16)


def unpacked(gathered, which, chips, weights, stage):
    w1, w2, w3, w4 = weights

    def turn(i, _):
        w1[at(i * 16, 16)] = gathered[which, i, 0:16]
        stage[at(i * 72, 72, 8)] = gathered[which, i, 16:96].astype(f32)[0:72]
        for block in range(BLOCKS):
            lanes = slice(block * 128, (block + 1) * 128)
            w4[at(i * 16, 16), lanes] = gathered[which, i, 128 + block * 16 : 144 + block * 16]
        return 0

    lax.fori_loop(0, chips, turn, 0)
    w2[...] = stage[0 : 9 * CMID].astype(bf16)

    def pairs(i, _):
        a = gathered[which, i * 2, 96:128].astype(f32)
        b = gathered[which, i * 2 + 1, 96:128].astype(f32)
        for block in range(BLOCKS):
            rows = slice(block * 8, (block + 1) * 8)
            w3[at(i * 16, 16), block * 128 : (block + 1) * 128] = jnp.concatenate([a[rows], b[rows]], axis=0).astype(bf16)
        return 0

    lax.fori_loop(0, chips // 2, pairs, 0)


def step_kernel(axes, own, slots, names, *refs):
    r = types.SimpleNamespace(**dict(zip(names, refs)))
    chips, cores = axes
    devices = chips * cores
    lows = 1 << (devices.bit_length() // 2)
    highs = devices // lows
    counts, mask = r.counts, r.mask
    micros, images = counts.shape
    fields = field_pair(images, slots)
    big, small = fields
    crops = images * (1 + slots)
    field_rows = small.row + small.count * small.area
    outs = small.out_row + small.count * small.out_area
    chip, core = lax.axis_index("dp"), lax.axis_index("fsdp")
    me = chip * cores + core
    sibling = (chip, 1 - core)
    field, a1, slope1, a2, even, wide, slope3 = (r.field, r.a1, r.slope1, r.a2, r.even, r.wide, r.slope3)
    thin, gy2, vec, sums, keys = (r.thin, r.gy2, r.vec, r.sums, r.keys)
    planes_of = {0: r.planes_big, images: r.planes_small}
    back_of = {0: r.back_big, images: r.back_small}
    stage_of = {0: r.stage_big, images: r.stage_small}
    wide_stage, dense_stage = r.wide_stage, r.dense_stage
    wq = [r.w1q, r.w2q, r.w3q, r.w4q]
    wk = [r.w1k, r.w2k, r.w3k, r.w4k]
    grads = [r.g1, r.g2, r.g3, r.g4]
    gains, shifts, gains1, shifts1 = (r.gains, r.shifts, r.gains1, r.shifts1)
    gain_sum, shift_sum, loss_sum = r.gain_sum, r.shift_sum, r.loss_sum
    A3, AP, H2, SLOPE2 = 0, BLOCKS * outs, 0, outs

    def place(device):
        return (lax.div(device, cores), lax.rem(device, cores))

    def remote(source, target, send, receive, device):
        return pltpu.make_async_remote_copy(
            src_ref=source, dst_ref=target, send_sem=send, recv_sem=receive, device_id=device, device_id_type=MESH)

    def repeat(first, last, body):
        lax.fori_loop(first, last, lambda k, _: (body(k), 0)[1], 0)

    key_base = field_rows
    key_loads = [
        pltpu.make_async_copy(
            r.key_hbm.at[i // 2, pl.ds(i % 2 * big.area, big.area)],
            field.at[pl.ds(key_base + i * big.area, big.area)], r.key_load.at[i])
        for i in range(2 * micros)
    ]

    def query_loads(m):
        return [
            pltpu.make_async_copy(
                r.big_hbm.at[m], field.at[pl.ds(m * field_rows, small.row)], r.query_load.at[m, 0]),
            pltpu.make_async_copy(
                r.small_hbm.at[m], field.at[pl.ds(m * field_rows + small.row, field_rows - small.row)],
                r.query_load.at[m, 1]),
        ]

    def store_big(m, c):
        return pltpu.make_async_copy(
            field.at[pl.ds(m * field_rows + c * big.area, big.area)],
            r.big_out.at[m, pl.ds(c * big.area, big.area)], r.store.at[m, c])

    def store_small(m):
        return pltpu.make_async_copy(
            field.at[pl.ds(m * field_rows + small.row, field_rows - small.row)], r.small_out.at[m],
            r.store.at[m, images])

    own_half = pl.ds(pl.multiple_of(core * HALF_PACK, HALF_PACK), HALF_PACK)

    def core_copy(which):
        return remote(r.sent.at[which], r.swapped_in.at[which], r.core_send.at[which], r.core_recv.at[which], sibling)

    def wide_copy(which, k):
        here = r.gathered.at[which, chip, own_half]
        return remote(here, here, r.wide_send.at[which, k], r.wide_recv.at[which, k], (lax.rem(chip + k, chips), core))

    def join_copy(which):
        here = r.gathered.at[which, :, own_half]
        return remote(here, here, r.join_send.at[which], r.join_recv.at[which], sibling)

    def spread_start(which):
        core_copy(which).wait()
        r.gathered[which, chip, own_half] = r.sent[which, own_half] + r.swapped_in[which, own_half]
        repeat(1, chips, lambda k: wide_copy(which, k).start())

    def spread_join(which):
        repeat(1, chips, lambda k: wide_copy(which, k).wait())
        join_copy(which).start()

    lower, upper = r.lower, r.upper

    def low_copy(turn, k):
        return remote(
            lower[turn].at[0], lower[turn].at[k], r.low_send.at[turn, k], r.low_recv.at[turn, k], place(flipped(me, k)))

    def high_copy(turn, k):
        return remote(
            upper[turn].at[0], upper[turn].at[k], r.high_send.at[turn, k], r.high_recv.at[turn, k],
            place(flipped(me, k * lows)))

    def exchange_start(turn):
        for k in range(1, lows):
            low_copy(turn, k).start()

    def exchange_middle(turn):
        for k in range(1, lows):
            low_copy(turn, k).wait()
        half = TURN_ROWS[turn] // micros
        for m in range(micros):
            pick = lax.rem(jnp.bitwise_xor(mask[m, 0], mask[m, 1]), lows)
            upper[turn][0, m * half : (m + 1) * half] = lower[turn][pick, m * half : (m + 1) * half]
        for k in range(1, highs):
            high_copy(turn, k).start()

    def exchange_end(turn):
        for k in range(1, highs):
            high_copy(turn, k).wait()

    def put_moments(turn, row, start, size, step):
        pivot = folded(wide[at(start, step, 8)]).sum(0, keepdims=True) / step
        total, square = moments(wide, start, size, step, pivot)
        off = total.sum(0, keepdims=True) / size
        lower[turn][0, pl.ds(row, 1)] = pivot + off
        lower[turn][0, pl.ds(row + 1, 1)] = jnp.maximum(square.sum(0, keepdims=True) - off * off * size, 0.0)

    def combined(turn, m, row, other, count):
        pick = lax.div(jnp.bitwise_xor(mask[m, 0], mask[m, 1]), lows)
        mean, spread = lower[turn][0, pl.ds(row, 1)], lower[turn][0, pl.ds(row + 1, 1)]
        mean2, spread2 = upper[turn][pick, pl.ds(other, 1)], upper[turn][pick, pl.ds(other + 1, 1)]
        apart = mean - mean2
        variance = (spread + spread2 + apart * apart * (count * 0.5)) / (2.0 * count)
        return (mean + mean2) * 0.5, lax.rsqrt(variance + NORM_EPS)

    def affine(group, start):
        mean, root = group
        new_gain = MOMENTUM * line(gains1, start) + (1.0 - MOMENTUM) * line(gains, start)
        new_shift = MOMENTUM * line(shifts1, start) + (1.0 - MOMENTUM) * line(shifts, start)
        scale = root * new_gain
        return scale, new_shift - mean * scale

    area, out_area = float(big.area), float(big.out_area)
    first_row = BLOCKS * outs
    spare = 2 * big.area

    def key_even(i):
        def put(block, value):
            slope3[at((i * 2 + block) * big.out_area, big.out_area)] = value

        even_cells(field, key_base + i * big.area, big, wide_stage, dense_stage, put)

    def key_side(i, start):
        cells = [slope3[at((i * 2 + block) * big.out_area, big.out_area)] for block in range(2)]
        value = dot(jnp.concatenate(cells, axis=1), wk[3][...])
        for block in range(BLOCKS):
            wide[at(start + block * big.out_area, big.out_area)] = value[:, block * 128 : (block + 1) * 128]

    def key_third(m, c, start):
        value = dot(thin[at(m * outs + c * big.out_area, big.out_area)], wk[2][...])
        for block in range(BLOCKS):
            wide[at(start + block * big.out_area, big.out_area)] = value[:, block * 128 : (block + 1) * 128]

    def key_a(i):
        m, c = lax.div(i, 2), lax.rem(i, 2)
        start = m * first_row + c * big.area
        wide[at(start, big.area)] = dot(field[at(key_base + i * big.area, big.area)], wk[0][...])
        put_moments(0, m * 24 + c * 2, start, big.area, 112)
        start = m * first_row + spare
        key_side(i, start)
        for block in range(BLOCKS):
            put_moments(0, m * 24 + 8 + (c * BLOCKS + block) * 2, start + block * big.out_area, big.out_area, 112)

    def key_b(i):
        m, c = lax.div(i, 2), lax.rem(i, 2)
        scale, bias = affine(combined(0, m, m * 24 + c * 2, m * 24 + (1 - c) * 2, area), 0)

        def rows_of(y):
            for k in range(4):
                row = y * 4 + k
                v = wide[at(m * first_row + c * big.area + row * 2 * SIDE, 2 * SIDE)] * scale + bias
                split_planes(gelu_only(v), stage_of[0], planes_of[0], big, c, row, k % 2)

        repeat(0, big.half // 4, rows_of)
        value = dot(patches(planes_of[0], big, c, 1), wk[1][...])
        start = m * first_row + spare + c * big.out_area
        for k in range(big.half):
            wide[pl.ds(start + k * big.half, big.half)] = value[k * big.wide : k * big.wide + big.half]
        put_moments(1, m * 8 + c * 2, start, big.out_area, 112)

    def key_c(i):
        m, c = lax.div(i, 2), lax.rem(i, 2)
        scale, bias = affine(combined(1, m, m * 8 + c * 2, m * 8 + (1 - c) * 2, out_area), CMID)
        for k in range(big.out_area // 112):
            v = wide[at(m * first_row + spare + c * big.out_area + k * 112, 112)] * scale + bias
            thin[at(m * outs + c * big.out_area + k * 112, 112)] = gelu_only(v).astype(bf16)
        start = m * first_row
        key_third(m, c, start)
        for block in range(BLOCKS):
            put_moments(2, m * 16 + (c * BLOCKS + block) * 2, start + block * big.out_area, big.out_area, 112)

    def key_d(i):
        m, c = lax.div(i, 2), lax.rem(i, 2)
        start = m * first_row
        key_third(m, c, start)
        key_side(i, start + BLOCKS * big.out_area)
        parts = []
        for block in range(BLOCKS):
            lanes = 2 * CMID + block * 128
            row, other = (c * BLOCKS + block) * 2, ((1 - c) * BLOCKS + block) * 2
            scale3, bias3 = affine(combined(2, m, m * 16 + row, m * 16 + other, out_area), lanes)
            scale4, bias4 = affine(combined(0, m, m * 24 + 8 + row, m * 24 + 8 + other, out_area), lanes + COUT)
            bias = bias3 + bias4
            e = jnp.zeros((8, 128), f32)
            for k in range(big.out_area // 112):
                x3 = wide[at(start + block * big.out_area + k * 112, 112)]
                x4 = wide[at(start + (BLOCKS + block) * big.out_area + k * 112, 112)]
                e += folded(gelu_only(x3 * scale3 + x4 * scale4 + bias))
            parts.append(e.sum(0, keepdims=True) / out_area)
        length = sum(jnp.sum(part * part, axis=1, keepdims=True) for part in parts)
        inverse = lax.rsqrt(length + UNIT_EPS)
        for block in range(BLOCKS):
            r.embed[pl.ds(m * 8 + c * BLOCKS + block, 1)] = parts[block] * inverse

    def key_copy(k):
        mine = keys.at[pl.ds(pl.multiple_of(me * 16, 16), 16)]
        return remote(r.embed, mine, r.key_send.at[k], r.key_recv.at[k], place(lax.rem(me + k, devices)))

    def share_start():
        keys[at(me * 16, 16)] = r.embed[...]
        repeat(1, devices, lambda k: key_copy(k).start())

    def share_end():
        repeat(1, devices, lambda k: key_copy(k).wait())

    def swap_copy(job):
        return remote(
            r.parts.at[job, 1 - core], r.arrived.at[job], r.swap_send.at[job], r.swap_recv.at[job], sibling)

    def row_copy(job, target, source):
        return remote(
            r.sending.at[job, target], r.landed.at[job, source], r.row_send.at[job, target],
            r.row_recv.at[job, source], (target, core))

    def result_copy(job):
        here = r.packed.at[job, core]
        return remote(here, here, r.result_send.at[job], r.result_recv.at[job], sibling)

    def job_send(job):
        swap_copy(job).wait()

        def turn(k):
            target = lax.rem(chip + k, chips)
            r.sending[job, target] = (r.parts[job, core, target] + r.arrived[job, target]).astype(bf16)
            row_copy(job, target, chip).start()

        repeat(1, chips, turn)
        r.sending[job, chip] = (r.parts[job, core, chip] + r.arrived[job, chip]).astype(bf16)

    def job_sum(job):
        def add(k, total):
            source = lax.rem(chip + chips - k, chips)
            row_copy(job, source, source).wait_recv()
            return total + r.landed[job, source].astype(f32)

        r.packed[job, core] = lax.fori_loop(1, chips, add, r.sending[job, chip].astype(f32))
        result_copy(job).start()

    def job_end(job):
        repeat(1, chips, lambda k: row_copy(job, lax.rem(chip + k, chips), chip).wait_send())
        result_copy(job).wait()

    def fill_head():
        parts, third, fourth = r.parts, grads[2], grads[3]

        def turn(i):
            for block in range(BLOCKS):
                lanes = slice(block * 128, (block + 1) * 128)
                parts[0, 0, i, block * 8 : (block + 1) * 8] = third[at(i * 8, 8, 8), lanes]
                half, row = (0, 32) if block == 0 else (1, (block - 1) * 16)
                parts[0, half, i, row : row + 16] = fourth[at(i * 16, 16), lanes]

        repeat(0, chips, turn)
        swap_copy(0).start()

    def fill_spatial():
        parts = r.parts
        for tile in range(9):
            lanes = slice(tile * 128, (tile + 1) * 128)
            gy2[lanes] = grads[1][:, lanes].T

        def turn(i):
            parts[1, 0, i] = gy2[at(i * 72, JOB, 8)]
            parts[1, 1, i, 0:24] = gy2[at(i * 72 + JOB, 24, 8)]
            parts[1, 1, i, 24:JOB] = jnp.zeros((JOB - 24, 128), f32)

        repeat(0, chips, turn)
        swap_copy(1).start()

    def fill_rest():
        parts = r.parts
        for tile in range(2):
            lanes = slice(tile * 128, (tile + 1) * 128)
            gy2[lanes] = grads[0][:, lanes].T
        column = lax.broadcasted_iota(jnp.int32, (1, 128), 1)
        filler = jnp.zeros((5, 128), f32)
        both = [
            [gain_sum[:, k * 128 : (k + 1) * 128] for k in range(10)] + [jnp.where(column == 0, loss_sum[...], 0.0), filler],
            [shift_sum[:, k * 128 : (k + 1) * 128] for k in range(10)] + [jnp.zeros((1, 128), f32), filler],
        ]
        both = [jnp.concatenate(rows, axis=0) for rows in both]

        def turn(i):
            parts[2, 0, i, 0:16] = gy2[at(i * 16, 16)]
            parts[2, 1, i, 0:16] = jnp.zeros((16, 128), f32)
            for half in range(2):
                parts[2, half, i, 16:32] = both[half]
                parts[2, half, i, 32:48] = jnp.zeros((16, 128), f32)

        repeat(0, chips, turn)
        swap_copy(2).start()

    def rest_send():
        swap_copy(2).wait()

        def value_for(target):
            value = r.parts[2, core, target] + r.arrived[2, target]
            fine = value[16:32] - value[16:32].astype(bf16).astype(f32)
            return jnp.concatenate([value[0:32], fine], axis=0).astype(bf16)

        def turn(k):
            target = lax.rem(chip + k, chips)
            r.sending[2, target] = value_for(target)
            row_copy(2, target, chip).start()

        repeat(1, chips, turn)
        r.sending[2, chip] = value_for(chip)

    for load in query_loads(0) + key_loads:
        load.start()
    barrier = pltpu.get_barrier_semaphore()
    repeat(1, devices, lambda k: pl.semaphore_signal(
        barrier, inc=1, device_id=place(lax.rem(me + k, devices)), device_id_type=MESH))
    if own:
        current = [r.r0[...], r.s0[...], r.e0[...], r.p0[...]]
        lagged = [r.r1[...], r.s1[...], r.e1[...], r.p1[...]]
        packed_shards([MOMENTUM * old + (1.0 - MOMENTUM) * new for old, new in zip(lagged, current)], core, r.sent, 0)
        packed_shards(current, core, r.sent, 1)
    else:
        for shard, w in zip((r.r0, r.s0, r.e0, r.p0, r.r1, r.s1, r.e1, r.p1), wq + wk):
            w[...] = shard[...]
    for ref in list(planes_of.values()) + list(back_of.values()) + list(stage_of.values()) + grads + [
        r.raised, gain_sum, shift_sum, loss_sum, gy2, lower[0], lower[1], lower[2]]:
        ref[...] = jnp.zeros_like(ref)
    pl.semaphore_wait(barrier, devices - 1)
    if own:
        for which in range(2):
            core_copy(which).start()
        for which in range(2):
            spread_start(which)

    def micro_step(m):
        opening, closing = m == 0, m == micros - 1
        base = m * field_rows
        w1, w2, w3, w4 = wq
        w1t, w3t, w4t, wt0, wt1 = (r.w1t, r.w3t, r.w4t, r.wt0, r.wt1)
        alive_count = sum(counts[m, i] for i in range(images)).astype(f32)
        count1 = images * big.area + small.area * alive_count
        count2 = images * big.out_area + small.out_area * alive_count

        def living(kind, crop):
            if kind is big:
                return jnp.float32(1.0)
            return jnp.where(lax.rem(crop, slots) < counts[m, lax.div(crop, slots)], 1.0, 0.0)

        def step_of(kind):
            return 112 if kind is big else 144

        def over_big(body):
            repeat(0, big.count, lambda c: body(big, c, 1))

        def over_small(body):
            body(small, 0, small.count)

        def add_moments(ref, offset, kind, first, count, row0, size, row, where, opener):
            start = offset + row0 + first * size
            if kind is big:

                @pl.when(first == 0)
                def _():
                    vec[row : row + 1] = folded(ref[at(start, opener, 8)]).sum(0, keepdims=True) / opener

            for c in range(count):
                total, square = moments(ref, start + c * size, size, step_of(kind), vec[row : row + 1])
                alive = living(kind, first + c)
                sums[where] += total * alive
                sums[where + 1] += square * alive

        for load in query_loads(m):
            load.wait()

        def even_batch(kind, first, count):
            for c in range(count):
                start = kind.out_row + (first + c) * kind.out_area

                def put(block, value):
                    even[at(start, kind.out_area), block * 128 : (block + 1) * 128] = value

                even_cells(field, base + kind.row + (first + c) * kind.area, kind, wide_stage, dense_stage, put)

        over_big(even_batch)
        over_small(even_batch)

        @pl.when(opening)
        def _():
            for load in key_loads:
                load.wait()
            repeat(0, 2 * micros, key_even)
            if own:
                spread_join(0)
                join_copy(0).wait()
                unpacked(r.gathered, 0, chips, wk, gy2)
            repeat(0, 2 * micros, key_a)
            exchange_start(0)
            for load in query_loads(1):
                load.start()
            if own:
                spread_join(1)
                join_copy(1).wait()
                unpacked(r.gathered, 1, chips, wq, gy2)
            w1t[...] = w1[...].T
            w3t[...] = w3[...].T
            w4t[...] = w4[...].T
            wt0[...] = jnp.zeros_like(wt0)
            wt1[...] = jnp.zeros_like(wt1)

            def tap(ky, kx):
                start = (3 * ky + kx) * CMID
                return w2[start : start + CMID, :].T

            wt0[0:128, 0:128] = tap(1, 1)
            wt0[0:128, 128:256] = tap(1, 2)
            wt0[128:256, 128:256] = tap(1, 0)
            wt1[0:128, 0:128] = tap(2, 1)
            wt1[0:128, 128:256] = tap(2, 2)
            wt1[128:256, 128:256] = tap(2, 0)
            wt1[256:384, 0:128] = tap(0, 1)
            wt1[256:384, 128:256] = tap(0, 2)
            wt1[384:512, 128:256] = tap(0, 0)

        sums[...] = jnp.zeros_like(sums)

        def reduce_batch(kind, first, count):
            start = kind.row + first * kind.area
            size = count * kind.area
            a1[at(start, size)] = dot(field[at(base + start, size)], w1[...])
            add_moments(a1, 0, kind, first, count, kind.row, kind.area, 0, 0, 784)

        over_big(reduce_batch)

        @pl.when(opening)
        def _():
            exchange_middle(0)

        over_small(reduce_batch)
        mean1, root1 = closed(sums[0], sums[1], vec[0:1], count1)
        scale1 = root1 * line(gains, 0)
        bias1 = line(shifts, 0) - mean1 * scale1
        vec[1:2], vec[2:3], vec[3:4], vec[4:5] = mean1, root1, scale1, bias1

        @pl.when(opening)
        def _():
            exchange_end(0)
            repeat(0, 2 * micros, key_b)
            exchange_start(1)

        sums[...] = jnp.zeros_like(sums)

        def hidden_batch(kind, first, count):
            scale, bias = vec[3:4], vec[4:5]
            for c in range(count):
                for k in range(kind.half):
                    start = kind.row + (first + c) * kind.area + k * 2 * kind.side
                    v = a1[at(start, 2 * kind.side)] * scale + bias
                    hidden, slope = gelu_pair(v)
                    slope1[at(start, 2 * kind.side)] = slope.astype(bf16)
                    split_planes(hidden, stage_of[kind.ahead], planes_of[kind.ahead], kind, first + c, k, k % 2)

        over_big(hidden_batch)

        @pl.when(opening)
        def _():
            exchange_middle(1)

        over_small(hidden_batch)

        @pl.when(opening)
        def _():
            exchange_end(1)
            repeat(0, 2 * micros, key_c)
            exchange_start(2)

        def spatial_batch(kind, first, count):
            half, lanes = kind.half, kind.wide
            value = dot(patches(planes_of[kind.ahead], kind, first, count), w2[...])
            start = kind.out_row + first * kind.out_area
            for k in range(count * half):
                a2[pl.ds(start + k * half, half)] = value[k * lanes : k * lanes + half]
            add_moments(a2, 0, kind, first, count, kind.out_row, kind.out_area, 0, 16, 784)

        over_big(spatial_batch)

        @pl.when(opening)
        def _():
            exchange_middle(2)

        over_small(spatial_batch)
        mean2, root2 = closed(sums[16], sums[17], vec[0:1], count2)
        scale2 = root2 * line(gains, CMID)
        bias2 = line(shifts, CMID) - mean2 * scale2
        vec[5:6], vec[6:7], vec[7:8], vec[8:9] = mean2, root2, scale2, bias2

        @pl.when(opening)
        def _():
            exchange_end(2)
            repeat(0, 2 * micros, key_d)
            share_start()

        def head_product(which, source, weight, kind, first, count):
            start = kind.out_row + first * kind.out_area
            size = count * kind.out_area
            value = dot(source, weight[...])
            for block in range(BLOCKS):
                offset = (which * BLOCKS + block) * outs
                wide[at(offset + start, size)] = value[:, block * 128 : (block + 1) * 128]
            for block in range(BLOCKS):
                offset = (which * BLOCKS + block) * outs
                add_moments(
                    wide, offset, kind, first, count, kind.out_row, kind.out_area,
                    16 + which * 4 + block, which * 8 + block * 2, 784)

        def expand_batch(kind, first, count):
            start = kind.out_row + first * kind.out_area
            size, step = count * kind.out_area, step_of(kind)
            scale, bias = vec[7:8], vec[8:9]
            head_product(1, even[at(start, size)], w4, kind, first, count)
            for k in range(size // step):
                hidden, slope = gelu_pair(a2[at(start + k * step, step)] * scale + bias)
                thin[at(H2 + start + k * step, step)] = hidden.astype(bf16)
                thin[at(SLOPE2 + start + k * step, step)] = slope.astype(bf16)
            head_product(0, thin[at(H2 + start, size)], w3, kind, first, count)

        over_big(expand_batch)
        over_small(expand_batch)
        for which in range(2):
            for block in range(BLOCKS):
                row = which * 4 + block
                where = which * 8 + block * 2
                lanes = 2 * CMID + row * 128
                mean, root = closed(sums[where], sums[where + 1], vec[16 + row : 17 + row], count2)
                scale = root * line(gains, lanes)
                bias = line(shifts, lanes) - mean * scale
                vec[24 + row : 25 + row], vec[32 + row : 33 + row] = mean, root
                vec[40 + row : 41 + row] = scale
                if which == 0:
                    vec[48 + block : 49 + block] = bias
                else:
                    vec[48 + block : 49 + block] += bias

        rows_e, rows_c = r.rows_e, r.rows_c

        def embed_batch(kind, first, count):
            step = step_of(kind)
            for c in range(count):
                start = kind.out_row + (first + c) * kind.out_area
                for block in range(BLOCKS):
                    mean3, mean4 = vec[24 + block : 25 + block], vec[28 + block : 29 + block]
                    scale3, scale4 = vec[40 + block : 41 + block], vec[44 + block : 45 + block]
                    bias = vec[48 + block : 49 + block]
                    zero = jnp.zeros((8, 128), f32)
                    e, s0, s3, s4 = zero, zero, zero, zero
                    for k in range(kind.out_area // step):
                        inside = block * outs + start + k * step
                        x3, x4 = wide[at(A3 + inside, step)], wide[at(AP + inside, step)]
                        value, slope = gelu_pair(x3 * scale3 + x4 * scale4 + bias)
                        slope3[at(inside, step)] = slope.astype(bf16)
                        e += folded(value)
                        s0 += folded(slope)
                        s3 += folded(slope * (x3 - mean3))
                        s4 += folded(slope * (x4 - mean4))
                    row = kind.ahead + first + c
                    for which, value in enumerate((e / kind.out_area, s0, s3, s4)):
                        rows_e[which, block, pl.ds(row, 1)] = value.sum(0, keepdims=True)

        over_big(embed_batch)
        over_small(embed_batch)

        @pl.when(opening)
        def _():
            share_end()

        def joined(which):
            return jnp.concatenate([rows_e[which, block] for block in range(BLOCKS)], axis=1)

        e = joined(0)
        inverse = lax.rsqrt(jnp.sum(e * e, axis=-1, keepdims=True) + UNIT_EPS)
        row = lax.broadcasted_iota(jnp.int32, (crops, 1), 0)
        owner = jnp.zeros((crops, 1), jnp.int32)
        live = jnp.where(row < images, 1.0, 0.0)
        for i in range(images):
            owner = jnp.where(row == i, i, owner)
            for slot in range(slots):
                here = row == images + i * slots + slot
                owner = jnp.where(here, i, owner)
                live = jnp.where(here, jnp.where(slot < counts[m, i], 1.0, 0.0), live)
        embedding = e * inverse
        key_blocks = [
            jnp.concatenate(
                [keys[pl.ds(m * 8 + c * BLOCKS + block, devices, stride=16)] for c in range(images)], axis=0)
            for block in range(BLOCKS)
        ]
        logits = sum(
            dot_exact(embedding[:, block * 128 : (block + 1) * 128], key_blocks[block], ((1,), (1,)))
            for block in range(BLOCKS)
        )
        logits = logits / TEMP
        top = jnp.max(logits, axis=-1, keepdims=True)
        powers = jnp.exp(logits - top)
        total = jnp.sum(powers, axis=-1, keepdims=True)
        column = lax.broadcasted_iota(jnp.int32, logits.shape, 1)
        mine = column == owner * devices + me
        chosen = jnp.sum(jnp.where(mine, logits, 0.0), axis=-1, keepdims=True)
        ce = (top + jnp.log(total) - chosen) * live
        loss_sum[...] += jnp.sum(ce, axis=0, keepdims=True)
        toward = (powers / total - jnp.where(mine, 1.0, 0.0)) * (live / TEMP)
        back = jnp.concatenate([dot_exact(toward, block, ((1,), (0,))) for block in key_blocks], axis=1)
        de = inverse * back - e * (inverse * inverse * inverse * jnp.sum(e * back, axis=-1, keepdims=True))
        de = de * jnp.where(row < images, 1.0 / big.out_area, 1.0 / small.out_area)
        sum0 = jnp.sum(de * joined(1), axis=0, keepdims=True)
        for which in range(2):
            reach = jnp.sum(de * joined(2 + which), axis=0, keepdims=True)
            for block in range(BLOCKS):
                row = which * 4 + block
                here = slice(block * 128, (block + 1) * 128)
                lanes = slice(2 * CMID + row * 128, 2 * CMID + (row + 1) * 128)
                mean, root, scale = vec[24 + row : 25 + row], vec[32 + row : 33 + row], vec[40 + row : 41 + row]
                along = reach[:, here] * root
                gain_sum[:, lanes] += along
                shift_sum[:, lanes] += sum0[:, here]
                tilt = scale * root * along / count2
                vec[52 + row : 53 + row] = tilt
                vec[60 + row : 61 + row] = scale * sum0[:, here] / count2 - tilt * mean
                rows_c[which, block] = de[:, here] * scale

        sums[...] = jnp.zeros_like(sums)
        d3, dp = r.d3, r.dp

        def head_back(kind, first, count):
            start = kind.out_row + first * kind.out_area
            size, step = count * kind.out_area, step_of(kind)
            for which, store in ((0, d3), (1, dp)):
                for block in range(BLOCKS):
                    lanes = slice(block * 128, (block + 1) * 128)
                    where = which * 4 + block
                    for c in range(count):
                        rise = rows_c[which, block, pl.ds(kind.ahead + first + c, 1)]
                        alive = living(kind, first + c)
                        tilt, level = vec[52 + where : 53 + where] * alive, vec[60 + where : 61 + where] * alive
                        for k in range(kind.out_area // step):
                            inside = c * kind.out_area + k * step
                            here = block * outs + start + inside
                            x = wide[at(which * BLOCKS * outs + here, step)]
                            grad = slope3[at(here, step)].astype(f32) * rise - (x * tilt + level)
                            store[inside : inside + step, lanes] = grad.astype(bf16)
            grad3, gradp = d3[0:size], dp[0:size]
            gy2[at(start, size)] = dot(grad3, w3t[...])
            gradient = dot(gradp, w4t[...])
            for block in range(2):
                wide[at(AP + block * outs + start, size)] = gradient[:, block * 128 : (block + 1) * 128]
            grads[2][...] += dot_rows(thin[at(H2 + start, size)], grad3)
            grads[3][...] += dot_rows(even[at(start, size)], gradp)
            mean = vec[5:6]
            level, reach = jnp.zeros((8, 128), f32), jnp.zeros((8, 128), f32)
            for k in range(size // step):
                here = at(start + k * step, step)
                gy = gy2[here] * thin[at(SLOPE2 + start + k * step, step)].astype(f32)
                gy2[here] = gy
                level += folded(gy)
                reach += folded(gy * (a2[here] - mean))
            sums[0] += level
            sums[1] += reach

        over_big(head_back)
        over_small(head_back)

        if own:

            @pl.when(closing)
            def _():
                fill_head()

        def norm_back(where, lanes, count):
            mean, root, scale = vec[where : where + 1], vec[where + 1 : where + 2], vec[where + 2 : where + 3]
            level = sums[0].sum(0, keepdims=True)
            along = sums[1].sum(0, keepdims=True) * root
            gain_sum[:, lanes] += along
            shift_sum[:, lanes] += level
            tilt = scale * root * along / count
            vec[68:69] = scale
            vec[69:70] = tilt
            vec[70:71] = scale * level / count - tilt * mean

        norm_back(5, slice(CMID, 2 * CMID), count2)
        sums[...] = jnp.zeros_like(sums)

        def spatial_back(kind, first, count):
            half, lanes, side, step = kind.half, kind.wide, kind.side, step_of(kind)
            out_start = kind.out_row + first * kind.out_area
            for c in range(count):
                alive = living(kind, first + c)
                tilt, level = vec[69:70] * alive, vec[70:71] * alive
                for k in range(kind.out_area // step):
                    here = at(out_start + c * kind.out_area + k * step, step)
                    gy2[here] = gy2[here] * vec[68:69] - (a2[here] * tilt + level)
            column = lax.broadcasted_iota(jnp.int32, (lanes, 128), 0)
            store = back_of[kind.ahead]
            for k in range(count * half):
                here = jnp.where(column < half, gy2[pl.ds(out_start + k * half, lanes)], 0.0)
                following = jnp.where(column < half - 1, gy2[pl.ds(out_start + k * half + 1, lanes)], 0.0)
                store[first + k // half, k % half, :, 0:128] = here.astype(bf16)
                store[first + k // half, k % half, :, 128:256] = following.astype(bf16)
            size = count * half * lanes
            near = store[pl.ds(first, count), 0:half].reshape(size, 256)
            beyond = store[pl.ds(first, count), 1 : half + 1].reshape(size, 256)
            upper_rows = dot(near, wt0[...])
            lower_rows = dot(jnp.concatenate([near, beyond], axis=1), wt1[...])
            start = kind.row + first * kind.area
            for k in range(count * half):
                here = slice(k * lanes, k * lanes + half)
                row = start + k * 2 * side
                for odd, value in ((0, upper_rows), (1, lower_rows)):
                    wide[pl.ds(row + odd * side, half, stride=2)] = value[here, 0:128]
                    wide[pl.ds(row + odd * side + 1, half, stride=2)] = value[here, 128:256]
            grads[1][...] += dot_rows(near[:, 0:128], patches(planes_of[kind.ahead], kind, first, count))
            mean = vec[1:2]
            level, reach = jnp.zeros((8, 128), f32), jnp.zeros((8, 128), f32)
            for k in range(count * kind.area // step):
                here = at(start + k * step, step)
                gy = wide[here] * slope1[here].astype(f32)
                wide[here] = gy
                level += folded(gy)
                reach += folded(gy * (a1[here] - mean))
            sums[0] += level
            sums[1] += reach

        over_big(spatial_back)

        if own:

            @pl.when(closing)
            def _():
                job_send(0)

        over_small(spatial_back)
        norm_back(1, slice(0, CMID), count1)

        if own:

            @pl.when(closing)
            def _():
                fill_spatial()

        def reduce_back(kind, first, count):
            step = step_of(kind)
            size = count * kind.area
            start = kind.row + first * kind.area
            rise = vec[68:69]
            for c in range(count):
                alive = living(kind, first + c)
                tilt, level = vec[69:70] * alive, vec[70:71] * alive
                for k in range(kind.area // step):
                    here = at(start + c * kind.area + k * step, step)
                    grad = wide[here] * rise - (a1[here] * tilt + level)
                    slope1[here] = grad.astype(bf16)
            grads[0][...] += dot_rows(slope1[at(start, size)], field[at(base + start, size)])

        over_big(reduce_back)

        if own:

            @pl.when(closing)
            def _():
                job_send(1)

        over_small(reduce_back)

        if own:

            @pl.when(closing)
            def _():
                fill_rest()
                job_sum(0)

        raised = r.raised

        def field_back(kind, first, count):
            half, side = kind.half, kind.side
            size = count * kind.area
            start = kind.row + first * kind.area
            whole = dot(slope1[at(start, size)], w1t[...])
            out_start = kind.out_row + first * kind.out_area
            for k in range(count * half):
                row = k * 2 * side
                for block in range(2):
                    lanes = slice(block * 128, (block + 1) * 128)
                    slot = k % 4 * 2 + block
                    raised[slot, pl.ds(0, half, stride=2)] = wide[pl.ds(AP + block * outs + out_start + k * half, half)]
                    top_row = whole[row : row + side, lanes] + raised[slot, 0:side]
                    both = jnp.concatenate([top_row, whole[row + side : row + 2 * side, lanes]], axis=0)
                    field[at(base + start + row, 2 * side), lanes] = both.astype(bf16)
            if kind is big:
                store_big(m, first).start()
            else:
                store_small(m).start()

        over_big(field_back)

        if own:

            @pl.when(closing)
            def _():
                rest_send()
                job_sum(1)

        over_small(field_back)

    repeat(0, micros, micro_step)
    if own:
        job_sum(2)
        for job in range(3):
            job_end(job)
    for m in range(micros):
        for c in range(images):
            store_big(m, c).wait()
        store_small(m).wait()


def step_pass(axes, own, slots, big, small, key, counts, mask, current, lagged, vectors):
    chips, cores = axes
    devices = chips * cores
    lows = 1 << (devices.bit_length() // 2)
    highs = devices // lows
    micros, images = counts.shape
    one, two = field_pair(images, slots)
    rows = two.row + two.count * two.area
    outs = two.out_row + two.count * two.out_area
    crops = images * (1 + slots)
    vmem = pl.BlockSpec(memory_space=pltpu.VMEM)
    smem = pl.BlockSpec(memory_space=pltpu.SMEM)
    hbm = pl.BlockSpec(memory_space=pl.ANY)
    weights = [(CIN, CMID), (9 * CMID, CMID), (CMID, COUT), (CIN, COUT)]
    totals = dict(
        g1=(CMID, CIN), g2=(CMID, 9 * CMID), g3=(CMID, COUT), g4=(CIN, COUT),
        gain_sum=(1, NORMS), shift_sum=(1, NORMS), loss_sum=(1, 1))
    r0, s0, e0, p0 = ((w, vmem) for w in current)
    r1, s1, e1, p1 = ((w, vmem) for w in lagged)
    gains, shifts, gains1, shifts1 = ((v, vmem) for v in vectors)
    inputs = dict(
        big_hbm=(big, hbm), small_hbm=(small, hbm), key_hbm=(key, hbm), counts=(counts, smem), mask=(mask, smem),
        r0=r0, s0=s0, e0=e0, p0=p0, r1=r1, s1=s1, e1=e1, p1=p1, gains=gains, shifts=shifts, gains1=gains1, shifts1=shifts1)
    outputs = dict(
        big_out=(jax.ShapeDtypeStruct(big.shape, bf16), hbm), small_out=(jax.ShapeDtypeStruct(small.shape, bf16), hbm))
    if own:
        outputs |= dict(packed=(jax.ShapeDtypeStruct((3, 2, JOB, 128), f32), vmem))
    else:
        outputs |= {n: (jax.ShapeDtypeStruct(shape, f32), vmem) for n, shape in totals.items()}

    def buf(dtype, *shape):
        return pltpu.VMEM(shape, dtype)

    def dma(*shape):
        return pltpu.SemaphoreType.DMA(shape)

    scratch = dict(
        field=buf(bf16, rows + 2 * micros * one.area, CIN),
        a1=buf(f32, rows, 128), slope1=buf(bf16, rows, 128),
        planes_big=buf(bf16, 2, one.count, one.half + 1, one.wide, 384),
        planes_small=buf(bf16, 2, two.count, two.half + 1, two.wide, 384),
        a2=buf(f32, outs, 128), thin=buf(bf16, 2 * outs, 128), even=buf(bf16, outs, CIN),
        wide=buf(f32, 2 * BLOCKS * outs, 128), slope3=buf(bf16, BLOCKS * outs, 128),
        back_big=buf(bf16, one.count, one.half + 1, one.wide, 256),
        back_small=buf(bf16, two.count, two.half + 1, two.wide, 256),
        gy2=buf(f32, outs + 16, 128), stage_big=buf(f32, 2, 2, 80, 128), stage_small=buf(f32, 2, 2, 48, 128),
        wide_stage=buf(f32, 8, SIDE, 128), dense_stage=buf(f32, 2, one.out_area, 128), raised=buf(f32, 8, SIDE, 128),
        d3=buf(bf16, two.count * two.out_area, COUT), dp=buf(bf16, two.count * two.out_area, COUT),
        w1t=buf(bf16, CMID, CIN), w3t=buf(bf16, COUT, CMID), w4t=buf(bf16, COUT, CIN),
        wt0=buf(bf16, 256, 256), wt1=buf(bf16, 512, 256), sums=buf(f32, 18, 8, 128), vec=buf(f32, 80, 128),
        rows_e=buf(f32, 4, BLOCKS, crops, 128), rows_c=buf(f32, 2, BLOCKS, crops, 128),
        keys=buf(f32, devices * 16, 128), embed=buf(f32, 16, 128),
        lower=[buf(f32, lows, n, 128) for n in TURN_ROWS], upper=[buf(f32, highs, n, 128) for n in TURN_ROWS],
        key_load=dma(2 * micros), query_load=dma(micros, 2), store=dma(micros, images + 1),
        low_send=dma(3, lows), low_recv=dma(3, lows), high_send=dma(3, highs), high_recv=dma(3, highs),
        key_send=dma(devices), key_recv=dma(devices),
    )
    first, second, third, fourth = (buf(bf16, *shape) for shape in weights)
    scratch |= dict(w1q=first, w2q=second, w3q=third, w4q=fourth, w1k=first, w2k=second, w3k=third, w4k=fourth)
    if own:
        scratch |= {n: buf(f32, *shape) for n, shape in totals.items()}
        scratch |= dict(
            sent=buf(bf16, 2, PACK, 128), swapped_in=buf(bf16, 2, PACK, 128), gathered=buf(bf16, 2, chips, PACK, 128),
            parts=buf(f32, 3, 2, chips, JOB, 128), arrived=buf(f32, 3, chips, JOB, 128),
            sending=buf(bf16, 3, chips, JOB, 128), landed=buf(bf16, 3, chips, JOB, 128),
            core_send=dma(2), core_recv=dma(2), wide_send=dma(2, chips), wide_recv=dma(2, chips),
            join_send=dma(2), join_recv=dma(2), swap_send=dma(3), swap_recv=dma(3),
            row_send=dma(3, chips), row_recv=dma(3, chips), result_send=dma(3), result_recv=dma(3),
        )
    names = list(inputs) + list(outputs) + list(scratch)
    out = pl.pallas_call(
        functools.partial(step_kernel, axes, own, slots, names),
        out_shape=[shape for shape, _ in outputs.values()],
        in_specs=[spec for _, spec in inputs.values()],
        out_specs=[spec for _, spec in outputs.values()],
        scratch_shapes=list(scratch.values()),
        compiler_params=pltpu.CompilerParams(vmem_limit_bytes=63 * 2**20, collective_id=0, has_side_effects=True),
        name="step",
    )(*[array for array, _ in inputs.values()])
    return types.SimpleNamespace(**dict(zip(outputs, out)))


def finish_kernel(device, packed, loss, reduce_out, spatial_out, expand_out, shortcut_out, gains, shifts):
    here = lax.rem(device[0], 2) == 0
    reduce_out[...] = jnp.where(here, packed[2, 0, 0:16, 0:64], packed[2, 0, 0:16, 64:128])
    rows = jnp.concatenate([packed[1, 0], packed[1, 1, 0:24], jnp.zeros((56, 128), f32)], axis=0).T
    spatial_out[...] = jnp.where(here, rows[0:64, 0:72], rows[64:128, 0:72])
    shortcut = [packed[0, 0, 32:48]] + [packed[0, 1, k * 16 : (k + 1) * 16] for k in range(3)]
    for block in range(2):
        lanes = slice(block * 128, (block + 1) * 128)
        first, second = block, block + 2
        expand_out[:, lanes] = jnp.where(
            here, packed[0, 0, first * 8 : first * 8 + 8], packed[0, 0, second * 8 : second * 8 + 8])
        shortcut_out[:, lanes] = jnp.where(here, shortcut[first], shortcut[second])
    for half, ref in enumerate((gains, shifts)):
        for row in range(NORMS // 128):
            ref[pl.ds(row * 128, 128)] = packed[2, half, 16 + row] + packed[2, half, 32 + row]
    loss[...] = packed[2, 0, 26:27, 0:1] + packed[2, 0, 42:43, 0:1]


def finish_pass(device, packed):
    vmem = pl.BlockSpec(memory_space=pltpu.VMEM)
    smem = pl.BlockSpec(memory_space=pltpu.SMEM)
    shapes = [(1, 1), (16, 64), (64, 72), (8, 256), (16, 256), (NORMS,), (NORMS,)]
    return pl.pallas_call(
        finish_kernel,
        out_shape=[jax.ShapeDtypeStruct(shape, f32) for shape in shapes],
        in_specs=[smem, vmem],
        out_specs=[vmem] * 7,
        name="finish",
    )(device, packed)


def gather_weights(shards):
    rows = [lax.all_gather(part, "dp", axis=0, tiled=True) for part in shards]
    return [lax.all_gather(part, "fsdp", axis=1, tiled=True) for part in rows]


def per_device(axes, *args):
    query_global, small_crop_query, small_count, key_global, shuffle_mask = args[:5]
    current, lagged = args[5:9], args[11:15]
    vectors = (args[9], args[10], args[15], args[16])
    micros = query_global.shape[0]
    slots = small_crop_query.shape[2]
    chips, cores = axes
    own = chips == 16 and cores == 2
    if own:
        current = [w.T if i == 1 else w for i, w in enumerate(current)]
        lagged = [w.T if i == 1 else w for i, w in enumerate(lagged)]
    else:
        fresh = [MOMENTUM * old + (1.0 - MOMENTUM) * new for old, new in zip(lagged, current)]
        current = gather_weights([w.astype(bf16) for w in current])
        lagged = gather_weights([w.astype(bf16) for w in fresh])
    out = step_pass(
        axes, own, slots, query_global.reshape(micros, -1, CIN), small_crop_query.reshape(micros, -1, CIN),
        key_global.reshape(micros, -1, CIN), small_count, shuffle_mask, current, lagged, vectors,
    )
    fields = (out.big_out.reshape(query_global.shape), out.small_out.reshape(small_crop_query.shape))
    if own:
        device = (lax.axis_index("dp") * cores + lax.axis_index("fsdp")).astype(jnp.int32).reshape(1)
        loss, first, second, third, fourth, gains_grad, shifts_grad = finish_pass(device, out.packed)
        return (loss.reshape(()), *fields, first, second.T, third, fourth, gains_grad, shifts_grad)
    totals = (out.g1.T, out.g2.T, out.g3, out.g4)
    summed = lax.psum_scatter(totals, "dp", scatter_dimension=0, tiled=True)
    owned = lax.psum_scatter(summed, "fsdp", scatter_dimension=1, tiled=True)
    sums = lax.psum((out.loss_sum, out.gain_sum, out.shift_sum), ("dp", "fsdp"))
    return (sums[0].reshape(()), *fields, *owned, sums[1].reshape(NORMS), sums[2].reshape(NORMS))


def solution(mesh):
    whole, split = P(), P("dp", "fsdp")
    images, crops = P(None, ("dp", "fsdp"), None, None, None), P(None, ("dp", "fsdp"), None, None, None, None)
    axes = (mesh.shape["dp"], mesh.shape["fsdp"])
    return jax.shard_map(
        functools.partial(per_device, axes),
        mesh=mesh,
        in_specs=(images, crops, P(None, ("dp", "fsdp")), images, whole)
        + (split,) * 4 + (whole,) * 2 + (split,) * 4 + (whole,) * 2,
        out_specs=(whole, images, crops) + (split,) * 4 + (whole,) * 2,
        check_vma=False,
    )
```

```python
import functools
import types
import jax
import jax.numpy as jnp
from jax import lax
from jax.experimental import pallas as pl
from jax.experimental.pallas import tpu as pltpu
from jax.sharding import PartitionSpec as P

f32, bf16 = jnp.float32, jnp.bfloat16
CIN, CMID, COUT, NORMS = 256, 128, 512, 1280
SIDE, SMALL = 56, 24
BLOCKS = COUT // 128
TEMP, NORM_EPS, UNIT_EPS = 0.2, 1e-05, 1e-06
ROOT_HALF = 0.7071067811865476
DENSITY = 0.3989422804014327


class Field:
    def __init__(self, count, side, row, out_row, ahead):
        self.count, self.side, self.row, self.out_row = count, side, row, out_row
        self.ahead = ahead
        self.half = side // 2
        self.wide = -(-self.half // 16) * 16
        self.area, self.out_area = side * side, (side // 2) ** 2


def field_pair(images, slots):
    big = Field(images, SIDE, 0, 0, 0)
    small = Field(images * slots, SMALL, images * big.area, images * big.out_area, images)
    return big, small


def at(start, size, align=16):
    return pl.ds(pl.multiple_of(start, align), size)


def folded(x):
    return x.reshape(x.shape[0] // 8, 8, x.shape[1]).sum(0)


def dot(a, b):
    return jnp.dot(a, b, preferred_element_type=f32)


def dot_rows(a, b):
    return lax.dot_general(a, b, (((0,), (0,)), ((), ())), preferred_element_type=f32)


def dot_exact(a, b, dims):
    return lax.dot_general(a, b, (dims, ((), ())), precision=lax.Precision.HIGHEST, preferred_element_type=f32)


def gelu_pair(v):
    share = 0.5 + 0.5 * lax.erf(v * ROOT_HALF)
    return v * share, share + v * (DENSITY * jnp.exp(v * v * -0.5))


def gelu_only(v):
    return v * (0.5 + 0.5 * lax.erf(v * ROOT_HALF))


MOMENTUM = 0.999
MESH = pl.DeviceIdType.MESH
PACK = 96
JOB_ROWS = (48, 48, 32)
TURN_ROWS = (48, 16, 32)


def line(vector, start):
    return vector[pl.ds(start, 128)].reshape(1, 128)


def moments(ref, start, size, step, pivot):
    total = jnp.zeros((8, 128), f32)
    square = jnp.zeros((8, 128), f32)
    for k in range(size // step):
        x = ref[at(start + k * step, step, 8)] - pivot
        total += folded(x)
        square += folded(x * x)
    return total, square


def closed(total, square, pivot, count):
    off = total.sum(0, keepdims=True) / count
    spread = jnp.maximum(square.sum(0, keepdims=True) / count - off * off, 0.0)
    return pivot + off, lax.rsqrt(spread + NORM_EPS)


def patches(planes, field, first, crops):
    size = crops * field.half * field.wide
    here = pl.ds(first, crops)
    above = planes[1, here, 0 : field.half].reshape(size, 3 * CMID)
    level = planes[0, here, 0 : field.half].reshape(size, 3 * CMID)
    below = planes[1, here, 1 : field.half + 1].reshape(size, 3 * CMID)
    return jnp.concatenate([above, level, below], axis=1)


def split_planes(hidden, stage, planes, field, crop, row, slot):
    side, wide = field.side, field.wide
    for odd in range(2):
        stage[slot, odd, 8 : 8 + side] = hidden[odd * side : (odd + 1) * side]
    for odd in range(2):
        for tap in range(3):
            column = stage[slot, odd, pl.ds(7 + tap, wide, stride=2)]
            planes[odd, crop, row + odd, :, tap * CMID : (tap + 1) * CMID] = column.astype(bf16)


def even_cells(source, base, field, wide_stage, dense_stage, put):
    side, half = field.side, field.half
    for y in range(half):
        for block in range(CIN // 128):
            slot = y % 4 * 2 + block
            x = source[at(base + y * 2 * side, 2 * side), block * 128 : (block + 1) * 128]
            wide_stage[slot, 0:side] = x.astype(f32)[0:side]
            dense_stage[block, y * half : (y + 1) * half] = wide_stage[slot, pl.ds(0, half, stride=2)]
    for block in range(CIN // 128):
        put(block, dense_stage[block, 0 : field.out_area].astype(bf16))


def flipped(index, mask):
    bit = 1
    while bit <= mask:
        if mask & bit:
            index = index + bit * (1 - 2 * lax.rem(lax.div(index, bit), 2))
        bit *= 2
    return index


def side_by_side(top, bottom, core):
    left = lax.broadcasted_iota(jnp.int32, top.shape, 1) < 64
    if core == 0:
        return jnp.where(left, top, pltpu.roll(bottom, 64, 1))
    return jnp.where(left, pltpu.roll(top, 64, 1), bottom)


def packed_shards(shards, store, which):
    first, second, third, fourth = shards
    zero = jnp.zeros
    second = jnp.concatenate([second, zero((second.shape[0], 56), f32)], axis=1)
    second = jnp.concatenate([second, zero((64, 128), f32)], axis=0).T[0:80, 0:64]
    rows = [jnp.concatenate([first[0:8], first[8:16]], axis=1), jnp.concatenate([second[0:40], second[40:80]], axis=1)]
    rows += [third[:, 0:128], third[:, 128:256], fourth[:, 0:128], fourth[:, 128:256]]
    store[which] = jnp.concatenate(rows, axis=0).astype(bf16)


def unpacked(gathered, which, chips, weights, stage):
    w1, w2, w3, w4 = weights

    def turn(i, _):
        z, xy = lax.div(i, 4), lax.rem(i, 4)
        ours = [gathered[which, core, xy, z] for core in range(2)]
        first, second = (rows[0:48].astype(f32) for rows in ours)
        left = lax.broadcasted_iota(jnp.int32, (48, 128), 1) < 64
        top = jnp.where(left, first, pltpu.roll(second, 64, 1))
        bottom = jnp.where(left, pltpu.roll(first, 64, 1), second)
        w1[at(i * 16, 16)] = jnp.concatenate([top[0:8], bottom[0:8]], axis=0).astype(bf16)
        stage[at(i * 72, 40, 8)] = top[8:48]
        stage[at(i * 72 + 40, 32, 8)] = bottom[8:40]
        for block in range(BLOCKS):
            start = 64 + block % 2 * 16
            w4[at(i * 16, 16), block * 128 : (block + 1) * 128] = ours[block // 2][start : start + 16]
        return 0

    lax.fori_loop(0, chips, turn, 0)
    w2[...] = stage[0 : 9 * CMID].astype(bf16)

    def pairs(i, _):
        z, xy = lax.div(i, 2), lax.rem(i, 2) * 2
        for block in range(BLOCKS):
            rows = slice(block % 2 * 8, block % 2 * 8 + 8)
            both = [gathered[which, block // 2, xy + k, z, 48:64].astype(f32)[rows] for k in range(2)]
            w3[at(i * 16, 16), block * 128 : (block + 1) * 128] = jnp.concatenate(both, axis=0).astype(bf16)
        return 0

    lax.fori_loop(0, chips // 2, pairs, 0)


def stage_widths(devices):
    bits = devices.bit_length() - 1
    return (bits + 2) // 3, (bits + 1) // 3, bits // 3


def step_kernel(axes, own, slots, names, *refs):
    r = types.SimpleNamespace(**dict(zip(names, refs)))
    chips, cores = axes
    devices = chips * cores
    widths = stage_widths(devices)
    shifts_of = (0, widths[0], widths[0] + widths[1])
    counts, mask = r.counts, r.mask
    micros, images = counts.shape
    fields = field_pair(images, slots)
    big, small = fields
    crops = images * (1 + slots)
    field_rows = small.row + small.count * small.area
    outs = small.out_row + small.count * small.out_area
    chip, core = lax.axis_index("dp"), lax.axis_index("fsdp")
    me = chip * cores + core
    xy, z = lax.rem(chip, 4), lax.div(chip, 4)
    field, a1, slope1, a2, even, wide, slope3 = (r.field, r.a1, r.slope1, r.a2, r.even, r.wide, r.slope3)
    thin, gy2, vec, sums, keys = (r.thin, r.gy2, r.vec, r.sums, r.keys)
    planes_of = {0: r.planes_big, images: r.planes_small}
    back_of = {0: r.back_big, images: r.back_small}
    stage_of = {0: r.stage_big, images: r.stage_small}
    wide_stage, dense_stage = r.wide_stage, r.dense_stage
    wq = [r.w1q, r.w2q, r.w3q, r.w4q]
    wk = [r.w1k, r.w2k, r.w3k, r.w4k]
    grads = [r.g1, r.g2, r.g3, r.g4]
    gains, shifts, gains1, shifts1 = (r.gains, r.shifts, r.gains1, r.shifts1)
    gain_sum, shift_sum, loss_sum = r.gain_sum, r.shift_sum, r.loss_sum
    A3, AP, H2, SLOPE2 = 0, BLOCKS * outs, 0, outs

    def place(device):
        return (lax.div(device, cores), lax.rem(device, cores))

    def remote(source, target, send, receive, device):
        return pltpu.make_async_remote_copy(
            src_ref=source, dst_ref=target, send_sem=send, recv_sem=receive, device_id=device, device_id_type=MESH)

    def repeat(first, last, body):
        lax.fori_loop(first, last, lambda k, _: (body(k), 0)[1], 0)

    key_base = field_rows
    key_loads = [
        pltpu.make_async_copy(
            r.key_hbm.at[i // 2, pl.ds(i % 2 * big.area, big.area)],
            field.at[pl.ds(key_base + i * big.area, big.area)], r.key_load.at[i])
        for i in range(2 * micros)
    ]

    def query_loads(m):
        return [
            pltpu.make_async_copy(
                r.big_hbm.at[m], field.at[pl.ds(m * field_rows, small.row)], r.query_load.at[m, 0]),
            pltpu.make_async_copy(
                r.small_hbm.at[m], field.at[pl.ds(m * field_rows + small.row, field_rows - small.row)],
                r.query_load.at[m, 1]),
        ]

    def store_big(m, c):
        return pltpu.make_async_copy(
            field.at[pl.ds(m * field_rows + c * big.area, big.area)],
            r.big_out.at[m, pl.ds(c * big.area, big.area)], r.store.at[m, c])

    def store_small(m):
        return pltpu.make_async_copy(
            field.at[pl.ds(m * field_rows + small.row, field_rows - small.row)], r.small_out.at[m],
            r.store.at[m, images])

    def partner(flip):
        return place(flipped(me, flip))

    def gather_copies(which, stage):
        if stage == 0:
            here = r.gathered.at[which, core, xy, z]
            flips = [8 * k for k in range(1, chips // 4)]
        elif stage == 1:
            here = r.gathered.at[which, core, xy]
            flips = [2 * k for k in range(1, 4)]
        else:
            here = r.gathered.at[which, core]
            flips = [1]
        return [
            remote(here, here, r.gather_send.at[which, stage, k], r.gather_recv.at[which, stage, k], partner(flip))
            for k, flip in enumerate(flips)
        ]

    def gather_start(which, stage):
        for copy in gather_copies(which, stage):
            copy.start()

    def gather_end(which, stage):
        for copy in gather_copies(which, stage):
            copy.wait()

    moved = r.moved

    def exchange_copies(turn, stage):
        ref = moved[turn][stage]
        return [
            remote(
                ref.at[0], ref.at[k], r.move_send.at[turn, stage, k], r.move_recv.at[turn, stage, k],
                partner(k << shifts_of[stage]))
            for k in range(1, 1 << widths[stage])
        ]

    def picked(m, stage):
        return lax.rem(lax.div(jnp.bitwise_xor(mask[m, 0], mask[m, 1]), 1 << shifts_of[stage]), 1 << widths[stage])

    def exchange_start(turn):
        for copy in exchange_copies(turn, 0):
            copy.start()

    def exchange_next(turn, stage):
        for copy in exchange_copies(turn, stage - 1):
            copy.wait()
        half = TURN_ROWS[turn] // micros
        for m in range(micros):
            rows = slice(m * half, (m + 1) * half)
            moved[turn][stage][0, rows] = moved[turn][stage - 1][picked(m, stage - 1), rows]
        for copy in exchange_copies(turn, stage):
            copy.start()

    def exchange_end(turn):
        for copy in exchange_copies(turn, 2):
            copy.wait()

    def put_moments(turn, row, start, size, step):
        pivot = folded(wide[at(start, step, 8)]).sum(0, keepdims=True) / step
        total, square = moments(wide, start, size, step, pivot)
        off = total.sum(0, keepdims=True) / size
        moved[turn][0][0, pl.ds(row, 1)] = pivot + off
        moved[turn][0][0, pl.ds(row + 1, 1)] = jnp.maximum(square.sum(0, keepdims=True) - off * off * size, 0.0)

    def combined(turn, m, row, other, count):
        pick = picked(m, 2)
        mean, spread = moved[turn][0][0, pl.ds(row, 1)], moved[turn][0][0, pl.ds(row + 1, 1)]
        mean2, spread2 = moved[turn][2][pick, pl.ds(other, 1)], moved[turn][2][pick, pl.ds(other + 1, 1)]
        apart = mean - mean2
        variance = (spread + spread2 + apart * apart * (count * 0.5)) / (2.0 * count)
        return (mean + mean2) * 0.5, lax.rsqrt(variance + NORM_EPS)

    def affine(group, start):
        mean, root = group
        new_gain = MOMENTUM * line(gains1, start) + (1.0 - MOMENTUM) * line(gains, start)
        new_shift = MOMENTUM * line(shifts1, start) + (1.0 - MOMENTUM) * line(shifts, start)
        scale = root * new_gain
        return scale, new_shift - mean * scale

    area, out_area = float(big.area), float(big.out_area)
    first_row = BLOCKS * outs
    spare = 2 * big.area

    def key_even(i):
        def put(block, value):
            slope3[at((i * 2 + block) * big.out_area, big.out_area)] = value

        even_cells(field, key_base + i * big.area, big, wide_stage, dense_stage, put)

    def key_side(i, start):
        cells = [slope3[at((i * 2 + block) * big.out_area, big.out_area)] for block in range(2)]
        value = dot(jnp.concatenate(cells, axis=1), wk[3][...])
        for block in range(BLOCKS):
            wide[at(start + block * big.out_area, big.out_area)] = value[:, block * 128 : (block + 1) * 128]

    def key_third(m, c, start):
        value = dot(thin[at(m * outs + c * big.out_area, big.out_area)], wk[2][...])
        for block in range(BLOCKS):
            wide[at(start + block * big.out_area, big.out_area)] = value[:, block * 128 : (block + 1) * 128]

    def key_a(i):
        m, c = lax.div(i, 2), lax.rem(i, 2)
        start = m * first_row + c * big.area
        wide[at(start, big.area)] = dot(field[at(key_base + i * big.area, big.area)], wk[0][...])
        put_moments(0, m * 24 + c * 2, start, big.area, 112)
        start = m * first_row + spare
        key_side(i, start)
        for block in range(BLOCKS):
            put_moments(0, m * 24 + 8 + (c * BLOCKS + block) * 2, start + block * big.out_area, big.out_area, 112)

    def key_b(i):
        m, c = lax.div(i, 2), lax.rem(i, 2)
        scale, bias = affine(combined(0, m, m * 24 + c * 2, m * 24 + (1 - c) * 2, area), 0)

        def rows_of(y):
            for k in range(4):
                row = y * 4 + k
                v = wide[at(m * first_row + c * big.area + row * 2 * SIDE, 2 * SIDE)] * scale + bias
                split_planes(gelu_only(v), stage_of[0], planes_of[0], big, c, row, k % 2)

        repeat(0, big.half // 4, rows_of)
        value = dot(patches(planes_of[0], big, c, 1), wk[1][...])
        start = m * first_row + spare + c * big.out_area
        for k in range(big.half):
            wide[pl.ds(start + k * big.half, big.half)] = value[k * big.wide : k * big.wide + big.half]
        put_moments(1, m * 8 + c * 2, start, big.out_area, 112)

    def key_c(i):
        m, c = lax.div(i, 2), lax.rem(i, 2)
        scale, bias = affine(combined(1, m, m * 8 + c * 2, m * 8 + (1 - c) * 2, out_area), CMID)
        for k in range(big.out_area // 112):
            v = wide[at(m * first_row + spare + c * big.out_area + k * 112, 112)] * scale + bias
            thin[at(m * outs + c * big.out_area + k * 112, 112)] = gelu_only(v).astype(bf16)
        start = m * first_row
        key_third(m, c, start)
        for block in range(BLOCKS):
            put_moments(2, m * 16 + (c * BLOCKS + block) * 2, start + block * big.out_area, big.out_area, 112)

    def key_d(i):
        m, c = lax.div(i, 2), lax.rem(i, 2)
        start = m * first_row
        key_third(m, c, start)
        key_side(i, start + BLOCKS * big.out_area)
        parts = []
        for block in range(BLOCKS):
            lanes = 2 * CMID + block * 128
            row, other = (c * BLOCKS + block) * 2, ((1 - c) * BLOCKS + block) * 2
            scale3, bias3 = affine(combined(2, m, m * 16 + row, m * 16 + other, out_area), lanes)
            scale4, bias4 = affine(combined(0, m, m * 24 + 8 + row, m * 24 + 8 + other, out_area), lanes + COUT)
            bias = bias3 + bias4
            e = jnp.zeros((8, 128), f32)
            for k in range(big.out_area // 112):
                x3 = wide[at(start + block * big.out_area + k * 112, 112)]
                x4 = wide[at(start + (BLOCKS + block) * big.out_area + k * 112, 112)]
                e += folded(gelu_only(x3 * scale3 + x4 * scale4 + bias))
            parts.append(e.sum(0, keepdims=True) / out_area)
        length = sum(jnp.sum(part * part, axis=1, keepdims=True) for part in parts)
        inverse = lax.rsqrt(length + UNIT_EPS)
        for block in range(BLOCKS):
            r.embed[pl.ds(m * 8 + c * BLOCKS + block, 1)] = parts[block] * inverse

    def share_copies(stage):
        size = 16 << shifts_of[stage]
        here = keys.at[pl.ds(pl.multiple_of(lax.div(me, 1 << shifts_of[stage]) * size, 16), size)]
        return [
            remote(here, here, r.key_send.at[stage, k], r.key_recv.at[stage, k], partner(k << shifts_of[stage]))
            for k in range(1, 1 << widths[stage])
        ]

    def share_start(stage):
        if stage == 0:
            keys[at(me * 16, 16)] = r.embed[...]
        for copy in share_copies(stage):
            copy.start()

    def share_end(stage):
        for copy in share_copies(stage):
            copy.wait()

    def core_copy(job):
        return remote(
            r.parts[job].at[1 - core], r.arrived[job], r.sum_send.at[job, 0, 0], r.sum_recv.at[job, 0, 0], partner(1))

    def plane_copies(job):
        return [
            remote(
                r.plane_out[job].at[k], r.plane_in[job].at[k], r.sum_send.at[job, 1, k], r.sum_recv.at[job, 1, k],
                partner(2 * k))
            for k in range(1, 4)
        ]

    def column_copies(job):
        return [
            remote(
                r.column_out[job].at[k], r.column_in[job].at[k], r.sum_send.at[job, 2, k], r.sum_recv.at[job, 2, k],
                partner(8 * k))
            for k in range(1, 4)
        ]

    def job_plane(job):
        core_copy(job).wait()
        own_part, wire = r.parts[job], r.plane_out[job].dtype
        for k in range(1, 4):
            far = flipped(xy, k)
            r.plane_out[job][k] = (own_part[core, far] + r.arrived[job][far]).astype(wire)
        for copy in plane_copies(job):
            copy.start()
        r.arrived[job][xy] = own_part[core, xy] + r.arrived[job][xy]

    def job_column(job):
        for copy in plane_copies(job):
            copy.wait()
        held, wire = r.arrived[job], r.column_out[job].dtype
        for far in range(4):
            held[xy, far] += sum(r.plane_in[job][k, far].astype(f32) for k in range(1, 4))
        for k in range(1, 4):
            r.column_out[job][k] = held[xy, flipped(z, k)].astype(wire)
        for copy in column_copies(job):
            copy.start()

    def job_end(job):
        for copy in column_copies(job):
            copy.wait()
        start = sum(JOB_ROWS[:job])
        total = r.arrived[job][xy, z] + sum(r.column_in[job][k].astype(f32) for k in range(1, 4))
        r.packed[start : start + JOB_ROWS[job]] = total

    def each_chip(body):
        def turn(i):
            body(i, lax.rem(i, 4), lax.div(i, 4))

        repeat(0, chips, turn)

    def fill_head():
        part, third, fourth = r.parts[0], grads[2], grads[3]

        def turn(i, to_xy, to_z):
            for block in range(BLOCKS):
                half, row = block // 2, block % 2
                lanes = slice(block * 128, (block + 1) * 128)
                part[half, to_xy, to_z, row * 8 : row * 8 + 8] = third[at(i * 8, 8, 8), lanes]
                part[half, to_xy, to_z, 16 + row * 16 : 32 + row * 16] = fourth[at(i * 16, 16), lanes]

        each_chip(turn)
        core_copy(0).start()

    def fill_spatial():
        part = r.parts[1]
        for tile in range(9):
            lanes = slice(tile * 128, (tile + 1) * 128)
            gy2[lanes] = grads[1][:, lanes].T
        filler = jnp.zeros((8, 128), f32)

        def turn(i, to_xy, to_z):
            top = gy2[at(i * 72, 40, 8)]
            bottom = jnp.concatenate([gy2[at(i * 72 + 40, 32, 8)], filler], axis=0)
            for half in range(2):
                part[half, to_xy, to_z, 0:40] = side_by_side(top, bottom, half)
                part[half, to_xy, to_z, 40:48] = filler

        each_chip(turn)
        core_copy(1).start()

    def fill_rest():
        part = r.parts[2]
        for tile in range(2):
            lanes = slice(tile * 128, (tile + 1) * 128)
            gy2[lanes] = grads[0][:, lanes].T
        column = lax.broadcasted_iota(jnp.int32, (1, 128), 1)
        filler = jnp.zeros((1, 128), f32)
        rows = [gain_sum[:, k * 128 : (k + 1) * 128] for k in range(10)]
        rows += [jnp.where(column == 0, loss_sum[...], 0.0), filler]
        rows += [shift_sum[:, k * 128 : (k + 1) * 128] for k in range(10)] + [filler, filler]
        rows = jnp.concatenate(rows, axis=0)

        def turn(i, to_xy, to_z):
            for half in range(2):
                value = side_by_side(gy2[at(i * 16, 8, 8)], gy2[at(i * 16 + 8, 8, 8)], half)
                part[half, to_xy, to_z] = jnp.concatenate([value, rows], axis=0)

        each_chip(turn)
        core_copy(2).start()

    for load in query_loads(0) + key_loads:
        load.start()
    flips = {k << shift for width, shift in zip(widths, shifts_of) for k in range(1, 1 << width)}
    if own:
        flips |= {1} | {2 * k for k in range(1, 4)} | {8 * k for k in range(1, 4)}
    barrier = pltpu.get_barrier_semaphore()
    for flip in sorted(flips):
        pl.semaphore_signal(barrier, inc=1, device_id=partner(flip), device_id_type=MESH)
    if own:
        current = [r.r0[...], r.s0[...], r.e0[...], r.p0[...]]
        lagged = [r.r1[...], r.s1[...], r.e1[...], r.p1[...]]
        packed_shards([MOMENTUM * old + (1.0 - MOMENTUM) * new for old, new in zip(lagged, current)], r.sent, 0)
        packed_shards(current, r.sent, 1)
        for which in range(2):
            r.gathered[which, core, xy, z] = r.sent[which]
    else:
        for shard, w in zip((r.r0, r.s0, r.e0, r.p0, r.r1, r.s1, r.e1, r.p1), wq + wk):
            w[...] = shard[...]
    if flips:
        pl.semaphore_wait(barrier, len(flips))
    if own:
        for which in range(2):
            gather_start(which, 0)
    for ref in list(planes_of.values()) + list(back_of.values()) + list(stage_of.values()) + grads + [
        r.raised, gain_sum, shift_sum, loss_sum, gy2, moved[0][0], moved[1][0], moved[2][0]]:
        ref[...] = jnp.zeros_like(ref)
    if own:
        for which in range(2):
            gather_end(which, 0)
            gather_start(which, 1)

    def micro_step(m):
        opening, closing = m == 0, m == micros - 1
        base = m * field_rows
        w1, w2, w3, w4 = wq
        w1t, w3t, w4t, wt0, wt1 = (r.w1t, r.w3t, r.w4t, r.wt0, r.wt1)
        alive_count = sum(counts[m, i] for i in range(images)).astype(f32)
        count1 = images * big.area + small.area * alive_count
        count2 = images * big.out_area + small.out_area * alive_count

        def living(kind, crop):
            if kind is big:
                return jnp.float32(1.0)
            return jnp.where(lax.rem(crop, slots) < counts[m, lax.div(crop, slots)], 1.0, 0.0)

        def step_of(kind):
            return 112 if kind is big else 144

        def over_big(body, *hooks):
            def turn(c):
                body(big, c, 1)
                for k, (when, hook) in enumerate(hooks):

                    @pl.when(jnp.logical_and(when, c == k))
                    def _():
                        hook()

            repeat(0, big.count, turn)

        def over_small(body):
            body(small, 0, small.count)

        def add_moments(ref, offset, kind, first, count, row0, size, row, where, opener):
            start = offset + row0 + first * size
            if kind is big:

                @pl.when(first == 0)
                def _():
                    vec[row : row + 1] = folded(ref[at(start, opener, 8)]).sum(0, keepdims=True) / opener

            for c in range(count):
                total, square = moments(ref, start + c * size, size, step_of(kind), vec[row : row + 1])
                alive = living(kind, first + c)
                sums[where] += total * alive
                sums[where + 1] += square * alive

        for load in query_loads(m):
            load.wait()

        def even_batch(kind, first, count):
            for c in range(count):
                start = kind.out_row + (first + c) * kind.out_area

                def put(block, value):
                    even[at(start, kind.out_area), block * 128 : (block + 1) * 128] = value

                even_cells(field, base + kind.row + (first + c) * kind.area, kind, wide_stage, dense_stage, put)

        over_big(even_batch)
        over_small(even_batch)

        @pl.when(opening)
        def _():
            for load in key_loads:
                load.wait()
            repeat(0, 2 * micros, key_even)
            if own:
                gather_end(0, 1)
                gather_start(0, 2)
                gather_end(1, 1)
                gather_start(1, 2)
                gather_end(0, 2)
                unpacked(r.gathered, 0, chips, wk, gy2)
            repeat(0, 2 * micros, key_a)
            exchange_start(0)
            for load in query_loads(1):
                load.start()
            if own:
                gather_end(1, 2)
                unpacked(r.gathered, 1, chips, wq, gy2)
            w1t[...] = w1[...].T
            w3t[...] = w3[...].T
            w4t[...] = w4[...].T
            wt0[...] = jnp.zeros_like(wt0)
            wt1[...] = jnp.zeros_like(wt1)

            def tap(ky, kx):
                start = (3 * ky + kx) * CMID
                return w2[start : start + CMID, :].T

            wt0[0:128, 0:128] = tap(1, 1)
            wt0[0:128, 128:256] = tap(1, 2)
            wt0[128:256, 128:256] = tap(1, 0)
            wt1[0:128, 0:128] = tap(2, 1)
            wt1[0:128, 128:256] = tap(2, 2)
            wt1[128:256, 128:256] = tap(2, 0)
            wt1[256:384, 0:128] = tap(0, 1)
            wt1[256:384, 128:256] = tap(0, 2)
            wt1[384:512, 128:256] = tap(0, 0)

        sums[...] = jnp.zeros_like(sums)

        def reduce_batch(kind, first, count):
            start = kind.row + first * kind.area
            size = count * kind.area
            a1[at(start, size)] = dot(field[at(base + start, size)], w1[...])
            add_moments(a1, 0, kind, first, count, kind.row, kind.area, 0, 0, 784)

        over_big(reduce_batch, (opening, lambda: exchange_next(0, 1)), (opening, lambda: exchange_next(0, 2)))
        over_small(reduce_batch)
        mean1, root1 = closed(sums[0], sums[1], vec[0:1], count1)
        scale1 = root1 * line(gains, 0)
        bias1 = line(shifts, 0) - mean1 * scale1
        vec[1:2], vec[2:3], vec[3:4], vec[4:5] = mean1, root1, scale1, bias1

        @pl.when(opening)
        def _():
            exchange_end(0)
            repeat(0, 2 * micros, key_b)
            exchange_start(1)

        sums[...] = jnp.zeros_like(sums)

        def hidden_batch(kind, first, count):
            scale, bias = vec[3:4], vec[4:5]
            for c in range(count):
                for k in range(kind.half):
                    start = kind.row + (first + c) * kind.area + k * 2 * kind.side
                    v = a1[at(start, 2 * kind.side)] * scale + bias
                    hidden, slope = gelu_pair(v)
                    slope1[at(start, 2 * kind.side)] = slope.astype(bf16)
                    split_planes(hidden, stage_of[kind.ahead], planes_of[kind.ahead], kind, first + c, k, k % 2)

        over_big(hidden_batch, (opening, lambda: exchange_next(1, 1)), (opening, lambda: exchange_next(1, 2)))
        over_small(hidden_batch)

        @pl.when(opening)
        def _():
            exchange_end(1)
            repeat(0, 2 * micros, key_c)
            exchange_start(2)

        def spatial_batch(kind, first, count):
            half, lanes = kind.half, kind.wide
            value = dot(patches(planes_of[kind.ahead], kind, first, count), w2[...])
            start = kind.out_row + first * kind.out_area
            for k in range(count * half):
                a2[pl.ds(start + k * half, half)] = value[k * lanes : k * lanes + half]
            add_moments(a2, 0, kind, first, count, kind.out_row, kind.out_area, 0, 16, 784)

        over_big(spatial_batch, (opening, lambda: exchange_next(2, 1)), (opening, lambda: exchange_next(2, 2)))
        over_small(spatial_batch)
        mean2, root2 = closed(sums[16], sums[17], vec[0:1], count2)
        scale2 = root2 * line(gains, CMID)
        bias2 = line(shifts, CMID) - mean2 * scale2
        vec[5:6], vec[6:7], vec[7:8], vec[8:9] = mean2, root2, scale2, bias2

        @pl.when(opening)
        def _():
            exchange_end(2)
            repeat(0, 2 * micros, key_d)
            share_start(0)

        def head_product(which, source, weight, kind, first, count):
            start = kind.out_row + first * kind.out_area
            size = count * kind.out_area
            value = dot(source, weight[...])
            for block in range(BLOCKS):
                offset = (which * BLOCKS + block) * outs
                wide[at(offset + start, size)] = value[:, block * 128 : (block + 1) * 128]
            for block in range(BLOCKS):
                offset = (which * BLOCKS + block) * outs
                add_moments(
                    wide, offset, kind, first, count, kind.out_row, kind.out_area,
                    16 + which * 4 + block, which * 8 + block * 2, 784)

        def expand_batch(kind, first, count):
            start = kind.out_row + first * kind.out_area
            size, step = count * kind.out_area, step_of(kind)
            scale, bias = vec[7:8], vec[8:9]
            head_product(1, even[at(start, size)], w4, kind, first, count)
            for k in range(size // step):
                hidden, slope = gelu_pair(a2[at(start + k * step, step)] * scale + bias)
                thin[at(H2 + start + k * step, step)] = hidden.astype(bf16)
                thin[at(SLOPE2 + start + k * step, step)] = slope.astype(bf16)
            head_product(0, thin[at(H2 + start, size)], w3, kind, first, count)

        def share_next(stage):
            share_end(stage - 1)
            share_start(stage)

        over_big(expand_batch, (opening, lambda: None), (opening, lambda: share_next(1)))
        over_small(expand_batch)

        @pl.when(opening)
        def _():
            share_next(2)

        for which in range(2):
            for block in range(BLOCKS):
                row = which * 4 + block
                where = which * 8 + block * 2
                lanes = 2 * CMID + row * 128
                mean, root = closed(sums[where], sums[where + 1], vec[16 + row : 17 + row], count2)
                scale = root * line(gains, lanes)
                bias = line(shifts, lanes) - mean * scale
                vec[24 + row : 25 + row], vec[32 + row : 33 + row] = mean, root
                vec[40 + row : 41 + row] = scale
                if which == 0:
                    vec[48 + block : 49 + block] = bias
                else:
                    vec[48 + block : 49 + block] += bias

        rows_e, rows_c = r.rows_e, r.rows_c

        def embed_batch(kind, first, count):
            step = step_of(kind)
            for c in range(count):
                start = kind.out_row + (first + c) * kind.out_area
                for block in range(BLOCKS):
                    mean3, mean4 = vec[24 + block : 25 + block], vec[28 + block : 29 + block]
                    scale3, scale4 = vec[40 + block : 41 + block], vec[44 + block : 45 + block]
                    bias = vec[48 + block : 49 + block]
                    zero = jnp.zeros((8, 128), f32)
                    e, s0, s3, s4 = zero, zero, zero, zero
                    for k in range(kind.out_area // step):
                        inside = block * outs + start + k * step
                        x3, x4 = wide[at(A3 + inside, step)], wide[at(AP + inside, step)]
                        value, slope = gelu_pair(x3 * scale3 + x4 * scale4 + bias)
                        slope3[at(inside, step)] = slope.astype(bf16)
                        e += folded(value)
                        s0 += folded(slope)
                        s3 += folded(slope * (x3 - mean3))
                        s4 += folded(slope * (x4 - mean4))
                    row = kind.ahead + first + c
                    for which, value in enumerate((e / kind.out_area, s0, s3, s4)):
                        rows_e[which, block, pl.ds(row, 1)] = value.sum(0, keepdims=True)

        over_big(embed_batch)
        over_small(embed_batch)

        @pl.when(opening)
        def _():
            share_end(2)

        def joined(which):
            return jnp.concatenate([rows_e[which, block] for block in range(BLOCKS)], axis=1)

        e = joined(0)
        inverse = lax.rsqrt(jnp.sum(e * e, axis=-1, keepdims=True) + UNIT_EPS)
        row = lax.broadcasted_iota(jnp.int32, (crops, 1), 0)
        owner = jnp.zeros((crops, 1), jnp.int32)
        live = jnp.where(row < images, 1.0, 0.0)
        for i in range(images):
            owner = jnp.where(row == i, i, owner)
            for slot in range(slots):
                here = row == images + i * slots + slot
                owner = jnp.where(here, i, owner)
                live = jnp.where(here, jnp.where(slot < counts[m, i], 1.0, 0.0), live)
        embedding = e * inverse
        key_blocks = [
            jnp.concatenate(
                [keys[pl.ds(m * 8 + c * BLOCKS + block, devices, stride=16)] for c in range(images)], axis=0)
            for block in range(BLOCKS)
        ]
        logits = sum(
            dot_exact(embedding[:, block * 128 : (block + 1) * 128], key_blocks[block], ((1,), (1,)))
            for block in range(BLOCKS)
        )
        logits = logits / TEMP
        top = jnp.max(logits, axis=-1, keepdims=True)
        powers = jnp.exp(logits - top)
        total = jnp.sum(powers, axis=-1, keepdims=True)
        column = lax.broadcasted_iota(jnp.int32, logits.shape, 1)
        mine = column == owner * devices + me
        chosen = jnp.sum(jnp.where(mine, logits, 0.0), axis=-1, keepdims=True)
        ce = (top + jnp.log(total) - chosen) * live
        loss_sum[...] += jnp.sum(ce, axis=0, keepdims=True)
        toward = (powers / total - jnp.where(mine, 1.0, 0.0)) * (live / TEMP)
        back = jnp.concatenate([dot_exact(toward, block, ((1,), (0,))) for block in key_blocks], axis=1)
        de = inverse * back - e * (inverse * inverse * inverse * jnp.sum(e * back, axis=-1, keepdims=True))
        de = de * jnp.where(row < images, 1.0 / big.out_area, 1.0 / small.out_area)
        sum0 = jnp.sum(de * joined(1), axis=0, keepdims=True)
        for which in range(2):
            reach = jnp.sum(de * joined(2 + which), axis=0, keepdims=True)
            for block in range(BLOCKS):
                row = which * 4 + block
                here = slice(block * 128, (block + 1) * 128)
                lanes = slice(2 * CMID + row * 128, 2 * CMID + (row + 1) * 128)
                mean, root, scale = vec[24 + row : 25 + row], vec[32 + row : 33 + row], vec[40 + row : 41 + row]
                along = reach[:, here] * root
                gain_sum[:, lanes] += along
                shift_sum[:, lanes] += sum0[:, here]
                tilt = scale * root * along / count2
                vec[52 + row : 53 + row] = tilt
                vec[60 + row : 61 + row] = scale * sum0[:, here] / count2 - tilt * mean
                rows_c[which, block] = de[:, here] * scale

        sums[...] = jnp.zeros_like(sums)
        d3, dp = r.d3, r.dp

        def head_back(kind, first, count):
            start = kind.out_row + first * kind.out_area
            size, step = count * kind.out_area, step_of(kind)
            for which, store in ((0, d3), (1, dp)):
                for block in range(BLOCKS):
                    lanes = slice(block * 128, (block + 1) * 128)
                    where = which * 4 + block
                    for c in range(count):
                        rise = rows_c[which, block, pl.ds(kind.ahead + first + c, 1)]
                        alive = living(kind, first + c)
                        tilt, level = vec[52 + where : 53 + where] * alive, vec[60 + where : 61 + where] * alive
                        for k in range(kind.out_area // step):
                            inside = c * kind.out_area + k * step
                            here = block * outs + start + inside
                            x = wide[at(which * BLOCKS * outs + here, step)]
                            grad = slope3[at(here, step)].astype(f32) * rise - (x * tilt + level)
                            store[inside : inside + step, lanes] = grad.astype(bf16)
            grad3, gradp = d3[0:size], dp[0:size]
            gy2[at(start, size)] = dot(grad3, w3t[...])
            gradient = dot(gradp, w4t[...])
            for block in range(2):
                wide[at(AP + block * outs + start, size)] = gradient[:, block * 128 : (block + 1) * 128]
            grads[2][...] += dot_rows(thin[at(H2 + start, size)], grad3)
            grads[3][...] += dot_rows(even[at(start, size)], gradp)
            mean = vec[5:6]
            level, reach = jnp.zeros((8, 128), f32), jnp.zeros((8, 128), f32)
            for k in range(size // step):
                here = at(start + k * step, step)
                gy = gy2[here] * thin[at(SLOPE2 + start + k * step, step)].astype(f32)
                gy2[here] = gy
                level += folded(gy)
                reach += folded(gy * (a2[here] - mean))
            sums[0] += level
            sums[1] += reach

        over_big(head_back)
        over_small(head_back)

        if own:

            @pl.when(closing)
            def _():
                fill_head()

        def norm_back(where, lanes, count):
            mean, root, scale = vec[where : where + 1], vec[where + 1 : where + 2], vec[where + 2 : where + 3]
            level = sums[0].sum(0, keepdims=True)
            along = sums[1].sum(0, keepdims=True) * root
            gain_sum[:, lanes] += along
            shift_sum[:, lanes] += level
            tilt = scale * root * along / count
            vec[68:69] = scale
            vec[69:70] = tilt
            vec[70:71] = scale * level / count - tilt * mean

        norm_back(5, slice(CMID, 2 * CMID), count2)
        sums[...] = jnp.zeros_like(sums)

        def spatial_back(kind, first, count):
            half, lanes, side, step = kind.half, kind.wide, kind.side, step_of(kind)
            out_start = kind.out_row + first * kind.out_area
            for c in range(count):
                alive = living(kind, first + c)
                tilt, level = vec[69:70] * alive, vec[70:71] * alive
                for k in range(kind.out_area // step):
                    here = at(out_start + c * kind.out_area + k * step, step)
                    gy2[here] = gy2[here] * vec[68:69] - (a2[here] * tilt + level)
            column = lax.broadcasted_iota(jnp.int32, (lanes, 128), 0)
            store = back_of[kind.ahead]
            for k in range(count * half):
                here = jnp.where(column < half, gy2[pl.ds(out_start + k * half, lanes)], 0.0)
                following = jnp.where(column < half - 1, gy2[pl.ds(out_start + k * half + 1, lanes)], 0.0)
                store[first + k // half, k % half, :, 0:128] = here.astype(bf16)
                store[first + k // half, k % half, :, 128:256] = following.astype(bf16)
            size = count * half * lanes
            near = store[pl.ds(first, count), 0:half].reshape(size, 256)
            beyond = store[pl.ds(first, count), 1 : half + 1].reshape(size, 256)
            upper_rows = dot(near, wt0[...])
            lower_rows = dot(jnp.concatenate([near, beyond], axis=1), wt1[...])
            start = kind.row + first * kind.area
            for k in range(count * half):
                here = slice(k * lanes, k * lanes + half)
                row = start + k * 2 * side
                for odd, value in ((0, upper_rows), (1, lower_rows)):
                    wide[pl.ds(row + odd * side, half, stride=2)] = value[here, 0:128]
                    wide[pl.ds(row + odd * side + 1, half, stride=2)] = value[here, 128:256]
            grads[1][...] += dot_rows(near[:, 0:128], patches(planes_of[kind.ahead], kind, first, count))
            mean = vec[1:2]
            level, reach = jnp.zeros((8, 128), f32), jnp.zeros((8, 128), f32)
            for k in range(count * kind.area // step):
                here = at(start + k * step, step)
                gy = wide[here] * slope1[here].astype(f32)
                wide[here] = gy
                level += folded(gy)
                reach += folded(gy * (a1[here] - mean))
            sums[0] += level
            sums[1] += reach

        def job_hooks(job):
            return ((closing, lambda: job_plane(job)), (closing, lambda: job_column(job))) if own else ()

        over_big(spatial_back, *job_hooks(0))
        over_small(spatial_back)
        norm_back(1, slice(0, CMID), count1)

        if own:

            @pl.when(closing)
            def _():
                fill_spatial()
                job_end(0)

        def reduce_back(kind, first, count):
            step = step_of(kind)
            size = count * kind.area
            start = kind.row + first * kind.area
            rise = vec[68:69]
            for c in range(count):
                alive = living(kind, first + c)
                tilt, level = vec[69:70] * alive, vec[70:71] * alive
                for k in range(kind.area // step):
                    here = at(start + c * kind.area + k * step, step)
                    grad = wide[here] * rise - (a1[here] * tilt + level)
                    slope1[here] = grad.astype(bf16)
            grads[0][...] += dot_rows(slope1[at(start, size)], field[at(base + start, size)])

        over_big(reduce_back, *job_hooks(1))
        over_small(reduce_back)

        if own:

            @pl.when(closing)
            def _():
                fill_rest()
                job_end(1)

        raised = r.raised

        def field_back(kind, first, count):
            half, side = kind.half, kind.side
            size = count * kind.area
            start = kind.row + first * kind.area
            whole = dot(slope1[at(start, size)], w1t[...])
            out_start = kind.out_row + first * kind.out_area
            for k in range(count * half):
                row = k * 2 * side
                for block in range(2):
                    lanes = slice(block * 128, (block + 1) * 128)
                    slot = k % 4 * 2 + block
                    raised[slot, pl.ds(0, half, stride=2)] = wide[pl.ds(AP + block * outs + out_start + k * half, half)]
                    top_row = whole[row : row + side, lanes] + raised[slot, 0:side]
                    both = jnp.concatenate([top_row, whole[row + side : row + 2 * side, lanes]], axis=0)
                    field[at(base + start + row, 2 * side), lanes] = both.astype(bf16)
            if kind is big:
                store_big(m, first).start()
            else:
                store_small(m).start()

        over_big(field_back, *job_hooks(2))
        over_small(field_back)

    repeat(0, micros, micro_step)
    if own:
        job_end(2)
    for m in range(micros):
        for c in range(images):
            store_big(m, c).wait()
        store_small(m).wait()


def step_pass(axes, own, slots, big, small, key, counts, mask, current, lagged, vectors):
    chips, cores = axes
    devices = chips * cores
    widths = stage_widths(devices)
    micros, images = counts.shape
    one, two = field_pair(images, slots)
    rows = two.row + two.count * two.area
    outs = two.out_row + two.count * two.out_area
    crops = images * (1 + slots)
    vmem = pl.BlockSpec(memory_space=pltpu.VMEM)
    smem = pl.BlockSpec(memory_space=pltpu.SMEM)
    hbm = pl.BlockSpec(memory_space=pl.ANY)
    weights = [(CIN, CMID), (9 * CMID, CMID), (CMID, COUT), (CIN, COUT)]
    totals = dict(
        g1=(CMID, CIN), g2=(CMID, 9 * CMID), g3=(CMID, COUT), g4=(CIN, COUT),
        gain_sum=(1, NORMS), shift_sum=(1, NORMS), loss_sum=(1, 1))
    r0, s0, e0, p0 = ((w, vmem) for w in current)
    r1, s1, e1, p1 = ((w, vmem) for w in lagged)
    gains, shifts, gains1, shifts1 = ((v, vmem) for v in vectors)
    inputs = dict(
        big_hbm=(big, hbm), small_hbm=(small, hbm), key_hbm=(key, hbm), counts=(counts, smem), mask=(mask, smem),
        r0=r0, s0=s0, e0=e0, p0=p0, r1=r1, s1=s1, e1=e1, p1=p1, gains=gains, shifts=shifts, gains1=gains1, shifts1=shifts1)
    outputs = dict(
        big_out=(jax.ShapeDtypeStruct(big.shape, bf16), hbm), small_out=(jax.ShapeDtypeStruct(small.shape, bf16), hbm))
    if own:
        outputs |= dict(packed=(jax.ShapeDtypeStruct((sum(JOB_ROWS), 128), f32), vmem))
    else:
        outputs |= {n: (jax.ShapeDtypeStruct(shape, f32), vmem) for n, shape in totals.items()}

    def buf(dtype, *shape):
        return pltpu.VMEM(shape, dtype)

    def dma(*shape):
        return pltpu.SemaphoreType.DMA(shape)

    scratch = dict(
        field=buf(bf16, rows + 2 * micros * one.area, CIN),
        a1=buf(f32, rows, 128), slope1=buf(bf16, rows, 128),
        planes_big=buf(bf16, 2, one.count, one.half + 1, one.wide, 384),
        planes_small=buf(bf16, 2, two.count, two.half + 1, two.wide, 384),
        a2=buf(f32, outs, 128), thin=buf(bf16, 2 * outs, 128), even=buf(bf16, outs, CIN),
        wide=buf(f32, 2 * BLOCKS * outs, 128), slope3=buf(bf16, BLOCKS * outs, 128),
        back_big=buf(bf16, one.count, one.half + 1, one.wide, 256),
        back_small=buf(bf16, two.count, two.half + 1, two.wide, 256),
        gy2=buf(f32, outs + 16, 128), stage_big=buf(f32, 2, 2, 80, 128), stage_small=buf(f32, 2, 2, 48, 128),
        wide_stage=buf(f32, 8, SIDE, 128), dense_stage=buf(f32, 2, one.out_area, 128), raised=buf(f32, 8, SIDE, 128),
        d3=buf(bf16, two.count * two.out_area, COUT), dp=buf(bf16, two.count * two.out_area, COUT),
        w1t=buf(bf16, CMID, CIN), w3t=buf(bf16, COUT, CMID), w4t=buf(bf16, COUT, CIN),
        wt0=buf(bf16, 256, 256), wt1=buf(bf16, 512, 256), sums=buf(f32, 18, 8, 128), vec=buf(f32, 80, 128),
        rows_e=buf(f32, 4, BLOCKS, crops, 128), rows_c=buf(f32, 2, BLOCKS, crops, 128),
        keys=buf(f32, devices * 16, 128), embed=buf(f32, 16, 128),
        moved=[[buf(f32, 1 << width, n, 128) for width in widths] for n in TURN_ROWS],
        key_load=dma(2 * micros), query_load=dma(micros, 2), store=dma(micros, images + 1),
        move_send=dma(3, 3, 1 << widths[0]), move_recv=dma(3, 3, 1 << widths[0]),
        key_send=dma(3, 1 << widths[0]), key_recv=dma(3, 1 << widths[0]),
    )
    first, second, third, fourth = (buf(bf16, *shape) for shape in weights)
    scratch |= dict(w1q=first, w2q=second, w3q=third, w4q=fourth, w1k=first, w2k=second, w3k=third, w4k=fourth)
    wires = (bf16, bf16, f32)
    if own:
        scratch |= {n: buf(f32, *shape) for n, shape in totals.items()}
        scratch |= dict(
            sent=buf(bf16, 2, PACK, 128), gathered=buf(bf16, 2, 2, 4, 4, PACK, 128),
            parts=[buf(f32, 2, 4, 4, n, 128) for n in JOB_ROWS], arrived=[buf(f32, 4, 4, n, 128) for n in JOB_ROWS],
            plane_out=[buf(t, 4, 4, n, 128) for n, t in zip(JOB_ROWS, wires)],
            plane_in=[buf(t, 4, 4, n, 128) for n, t in zip(JOB_ROWS, wires)],
            column_out=[buf(t, 4, n, 128) for n, t in zip(JOB_ROWS, wires)],
            column_in=[buf(t, 4, n, 128) for n, t in zip(JOB_ROWS, wires)],
            gather_send=dma(2, 3, 3), gather_recv=dma(2, 3, 3), sum_send=dma(3, 3, 4), sum_recv=dma(3, 3, 4),
        )
    names = list(inputs) + list(outputs) + list(scratch)
    out = pl.pallas_call(
        functools.partial(step_kernel, axes, own, slots, names),
        out_shape=[shape for shape, _ in outputs.values()],
        in_specs=[spec for _, spec in inputs.values()],
        out_specs=[spec for _, spec in outputs.values()],
        scratch_shapes=list(scratch.values()),
        compiler_params=pltpu.CompilerParams(vmem_limit_bytes=63 * 2**20, collective_id=0, has_side_effects=True),
        name="step",
    )(*[array for array, _ in inputs.values()])
    return types.SimpleNamespace(**dict(zip(outputs, out)))


def finish_kernel(packed, loss, reduce_out, spatial_out, expand_out, shortcut_out, gains, shifts):
    reduce_out[0:8] = packed[96:104, 0:64]
    reduce_out[8:16] = packed[96:104, 64:128]
    rows = jnp.concatenate([packed[48:88], jnp.zeros((88, 128), f32)], axis=0).T
    spatial_out[...] = jnp.concatenate([rows[0:64, 0:40], rows[64:128, 0:32]], axis=1)
    for block in range(2):
        lanes = slice(block * 128, (block + 1) * 128)
        expand_out[:, lanes] = packed[block * 8 : block * 8 + 8]
        shortcut_out[:, lanes] = packed[16 + block * 16 : 32 + block * 16]
    for row in range(NORMS // 128):
        gains[pl.ds(row * 128, 128)] = packed[104 + row]
        shifts[pl.ds(row * 128, 128)] = packed[116 + row]
    loss[...] = packed[114:115, 0:1]


def finish_pass(packed):
    vmem = pl.BlockSpec(memory_space=pltpu.VMEM)
    shapes = [(1, 1), (16, 64), (64, 72), (8, 256), (16, 256), (NORMS,), (NORMS,)]
    return pl.pallas_call(
        finish_kernel,
        out_shape=[jax.ShapeDtypeStruct(shape, f32) for shape in shapes],
        in_specs=[vmem],
        out_specs=[vmem] * 7,
        name="finish",
    )(packed)


def gather_weights(shards):
    rows = [lax.all_gather(part, "dp", axis=0, tiled=True) for part in shards]
    return [lax.all_gather(part, "fsdp", axis=1, tiled=True) for part in rows]


def per_device(axes, *args):
    query_global, small_crop_query, small_count, key_global, shuffle_mask = args[:5]
    current, lagged = args[5:9], args[11:15]
    vectors = (args[9], args[10], args[15], args[16])
    micros = query_global.shape[0]
    slots = small_crop_query.shape[2]
    chips, cores = axes
    own = chips == 16 and cores == 2
    if own:
        current = [w.T if i == 1 else w for i, w in enumerate(current)]
        lagged = [w.T if i == 1 else w for i, w in enumerate(lagged)]
    else:
        fresh = [MOMENTUM * old + (1.0 - MOMENTUM) * new for old, new in zip(lagged, current)]
        current = gather_weights([w.astype(bf16) for w in current])
        lagged = gather_weights([w.astype(bf16) for w in fresh])
    out = step_pass(
        axes, own, slots, query_global.reshape(micros, -1, CIN), small_crop_query.reshape(micros, -1, CIN),
        key_global.reshape(micros, -1, CIN), small_count, shuffle_mask, current, lagged, vectors,
    )
    fields = (out.big_out.reshape(query_global.shape), out.small_out.reshape(small_crop_query.shape))
    if own:
        loss, first, second, third, fourth, gains_grad, shifts_grad = finish_pass(out.packed)
        return (loss.reshape(()), *fields, first, second.T, third, fourth, gains_grad, shifts_grad)
    totals = (out.g1.T, out.g2.T, out.g3, out.g4)
    summed = lax.psum_scatter(totals, "dp", scatter_dimension=0, tiled=True)
    owned = lax.psum_scatter(summed, "fsdp", scatter_dimension=1, tiled=True)
    sums = lax.psum((out.loss_sum, out.gain_sum, out.shift_sum), ("dp", "fsdp"))
    return (sums[0].reshape(()), *fields, *owned, sums[1].reshape(NORMS), sums[2].reshape(NORMS))


def solution(mesh):
    whole, split = P(), P("dp", "fsdp")
    images, crops = P(None, ("dp", "fsdp"), None, None, None), P(None, ("dp", "fsdp"), None, None, None, None)
    axes = (mesh.shape["dp"], mesh.shape["fsdp"])
    return jax.shard_map(
        functools.partial(per_device, axes),
        mesh=mesh,
        in_specs=(images, crops, P(None, ("dp", "fsdp")), images, whole)
        + (split,) * 4 + (whole,) * 2 + (split,) * 4 + (whole,) * 2,
        out_specs=(whole, images, crops) + (split,) * 4 + (whole,) * 2,
        check_vma=False,
    )
```

```python
import functools
import types
import jax
import jax.numpy as jnp
from jax import lax
from jax.experimental import pallas as pl
from jax.experimental.pallas import tpu as pltpu
from jax.sharding import PartitionSpec as P

f32, bf16 = jnp.float32, jnp.bfloat16
CIN, CMID, COUT, NORMS = 256, 128, 512, 1280
SIDE, SMALL = 56, 24
BLOCKS = COUT // 128
TEMP, NORM_EPS, UNIT_EPS = 0.2, 1e-05, 1e-06
ROOT_HALF = 0.7071067811865476
DENSITY = 0.3989422804014327


class Field:
    def __init__(self, count, side, row, out_row, ahead):
        self.count, self.side, self.row, self.out_row = count, side, row, out_row
        self.ahead = ahead
        self.half = side // 2
        self.wide = -(-self.half // 16) * 16
        self.area, self.out_area = side * side, (side // 2) ** 2


def field_pair(images, slots):
    big = Field(images, SIDE, 0, 0, 0)
    small = Field(images * slots, SMALL, images * big.area, images * big.out_area, images)
    return big, small


def at(start, size, align=16):
    return pl.ds(pl.multiple_of(start, align), size)


def folded(x):
    return x.reshape(x.shape[0] // 8, 8, x.shape[1]).sum(0)


def dot(a, b):
    return jnp.dot(a, b, preferred_element_type=f32)


def dot_rows(a, b):
    return lax.dot_general(a, b, (((0,), (0,)), ((), ())), preferred_element_type=f32)


def dot_exact(a, b, dims):
    return lax.dot_general(a, b, (dims, ((), ())), precision=lax.Precision.HIGHEST, preferred_element_type=f32)


def gelu_pair(v):
    share = 0.5 + 0.5 * lax.erf(v * ROOT_HALF)
    return v * share, share + v * (DENSITY * jnp.exp(v * v * -0.5))


def gelu_only(v):
    return v * (0.5 + 0.5 * lax.erf(v * ROOT_HALF))


MOMENTUM = 0.999
MESH = pl.DeviceIdType.MESH
PACK = 96
JOB_ROWS = (48, 48, 24, 8)
TURN_ROWS = (24, 8, 16)


def line(vector, start):
    return vector[pl.ds(start, 128)].reshape(1, 128)


def moments(ref, start, size, step, pivot):
    total = jnp.zeros((8, 128), f32)
    square = jnp.zeros((8, 128), f32)
    for k in range(size // step):
        x = ref[at(start + k * step, step, 8)] - pivot
        total += folded(x)
        square += folded(x * x)
    return total, square


def closed(total, square, pivot, count):
    off = total.sum(0, keepdims=True) / count
    spread = jnp.maximum(square.sum(0, keepdims=True) / count - off * off, 0.0)
    return pivot + off, lax.rsqrt(spread + NORM_EPS)


def patches(planes, field, first, crops):
    size = crops * field.half * field.wide
    here = pl.ds(first, crops)
    above = planes[1, here, 0 : field.half].reshape(size, 3 * CMID)
    level = planes[0, here, 0 : field.half].reshape(size, 3 * CMID)
    below = planes[1, here, 1 : field.half + 1].reshape(size, 3 * CMID)
    return jnp.concatenate([above, level, below], axis=1)


def split_planes(hidden, stage, planes, field, crop, row, slot):
    side, wide = field.side, field.wide
    for odd in range(2):
        stage[slot, odd, 8 : 8 + side] = hidden[odd * side : (odd + 1) * side]
    for odd in range(2):
        for tap in range(3):
            column = stage[slot, odd, pl.ds(7 + tap, wide, stride=2)]
            planes[odd, crop, row + odd, :, tap * CMID : (tap + 1) * CMID] = column.astype(bf16)


def even_cells(source, base, field, wide_stage, dense_stage, put):
    side, half = field.side, field.half
    for y in range(half):
        for block in range(CIN // 128):
            slot = y % 4 * 2 + block
            x = source[at(base + y * 2 * side, 2 * side), block * 128 : (block + 1) * 128]
            wide_stage[slot, 0:side] = x.astype(f32)[0:side]
            dense_stage[block, y * half : (y + 1) * half] = wide_stage[slot, pl.ds(0, half, stride=2)]
    for block in range(CIN // 128):
        put(block, dense_stage[block, 0 : field.out_area].astype(bf16))


def flipped(index, mask):
    bit = 1
    while bit <= mask:
        if mask & bit:
            index = index + bit * (1 - 2 * lax.rem(lax.div(index, bit), 2))
        bit *= 2
    return index


def side_by_side(top, bottom, core):
    left = lax.broadcasted_iota(jnp.int32, top.shape, 1) < 64
    if core == 0:
        return jnp.where(left, top, pltpu.roll(bottom, 64, 1))
    return jnp.where(left, pltpu.roll(top, 64, 1), bottom)


def packed_shards(shards, store, which):
    first, second, third, fourth = shards
    zero = jnp.zeros
    second = jnp.concatenate([second, zero((second.shape[0], 56), f32)], axis=1)
    second = jnp.concatenate([second, zero((64, 128), f32)], axis=0).T[0:80, 0:64]
    rows = [jnp.concatenate([first[0:8], first[8:16]], axis=1), jnp.concatenate([second[0:40], second[40:80]], axis=1)]
    rows += [third[:, 0:128], third[:, 128:256], fourth[:, 0:128], fourth[:, 128:256]]
    store[which] = jnp.concatenate(rows, axis=0).astype(bf16)


def unpacked(gathered, which, chips, weights, stage):
    w1, w2, w3, w4 = weights

    def turn(i, _):
        z, xy = lax.div(i, 4), lax.rem(i, 4)
        ours = [gathered[which, core, xy, z] for core in range(2)]
        first, second = (rows[0:48].astype(f32) for rows in ours)
        left = lax.broadcasted_iota(jnp.int32, (48, 128), 1) < 64
        top = jnp.where(left, first, pltpu.roll(second, 64, 1))
        bottom = jnp.where(left, pltpu.roll(first, 64, 1), second)
        w1[at(i * 16, 16)] = jnp.concatenate([top[0:8], bottom[0:8]], axis=0).astype(bf16)
        stage[at(i * 72, 40, 8)] = top[8:48]
        stage[at(i * 72 + 40, 32, 8)] = bottom[8:40]
        for block in range(BLOCKS):
            start = 64 + block % 2 * 16
            w4[at(i * 16, 16), block * 128 : (block + 1) * 128] = ours[block // 2][start : start + 16]
        return 0

    lax.fori_loop(0, chips, turn, 0)
    w2[...] = stage[0 : 9 * CMID].astype(bf16)

    def pairs(i, _):
        z, xy = lax.div(i, 2), lax.rem(i, 2) * 2
        for block in range(BLOCKS):
            rows = slice(block % 2 * 8, block % 2 * 8 + 8)
            both = [gathered[which, block // 2, xy + k, z, 48:64].astype(f32)[rows] for k in range(2)]
            w3[at(i * 16, 16), block * 128 : (block + 1) * 128] = jnp.concatenate(both, axis=0).astype(bf16)
        return 0

    lax.fori_loop(0, chips // 2, pairs, 0)


def stage_widths(devices):
    bits = devices.bit_length() - 1
    return (bits + 1) // 2, bits // 2


def step_kernel(axes, own, slots, names, *refs):
    r = types.SimpleNamespace(**dict(zip(names, refs)))
    chips, cores = axes
    devices = chips * cores
    widths = stage_widths(devices)
    shifts_of = (0, widths[0])
    counts, mask = r.counts, r.mask
    micros, images = counts.shape
    fields = field_pair(images, slots)
    big, small = fields
    crops = images * (1 + slots)
    field_rows = small.row + small.count * small.area
    outs = small.out_row + small.count * small.out_area
    chip, core = lax.axis_index("dp"), lax.axis_index("fsdp")
    me = chip * cores + core
    xy, z = lax.rem(chip, 4), lax.div(chip, 4)
    field, a1, slope1, a2, even, wide, slope3 = (r.field, r.a1, r.slope1, r.a2, r.even, r.wide, r.slope3)
    thin, gy2, vec, sums, keys = (r.thin, r.gy2, r.vec, r.sums, r.keys)
    planes_of = {0: r.planes_big, images: r.planes_small}
    back_of = {0: r.back_big, images: r.back_small}
    stage_of = {0: r.stage_big, images: r.stage_small}
    wide_stage, dense_stage = r.wide_stage, r.dense_stage
    wq = [r.w1q, r.w2q, r.w3q, r.w4q]
    wk = [r.w1k, r.w2k, r.w3k, r.w4k]
    grads = [r.g1, r.g2, r.g3, r.g4]
    gains, shifts, gains1, shifts1 = (r.gains, r.shifts, r.gains1, r.shifts1)
    gain_sum, shift_sum, loss_sum = r.gain_sum, r.shift_sum, r.loss_sum
    A3, AP, H2, SLOPE2 = 0, BLOCKS * outs, 0, outs

    def place(device):
        return (lax.div(device, cores), lax.rem(device, cores))

    def remote(source, target, send, receive, device):
        return pltpu.make_async_remote_copy(
            src_ref=source, dst_ref=target, send_sem=send, recv_sem=receive, device_id=device, device_id_type=MESH)

    def repeat(first, last, body):
        lax.fori_loop(first, last, lambda k, _: (body(k), 0)[1], 0)

    key_base = field_rows
    key_loads = [
        pltpu.make_async_copy(
            r.key_hbm.at[i // 2, pl.ds(i % 2 * big.area, big.area)],
            field.at[pl.ds(key_base + i * big.area, big.area)], r.key_load.at[i])
        for i in range(2 * micros)
    ]

    def query_loads(m):
        return [
            pltpu.make_async_copy(
                r.big_hbm.at[m], field.at[pl.ds(m * field_rows, small.row)], r.query_load.at[m, 0]),
            pltpu.make_async_copy(
                r.small_hbm.at[m], field.at[pl.ds(m * field_rows + small.row, field_rows - small.row)],
                r.query_load.at[m, 1]),
        ]

    def store_big(m, c):
        return pltpu.make_async_copy(
            field.at[pl.ds(m * field_rows + c * big.area, big.area)],
            r.big_out.at[m, pl.ds(c * big.area, big.area)], r.store.at[m, c])

    def store_small(m):
        return pltpu.make_async_copy(
            field.at[pl.ds(m * field_rows + small.row, field_rows - small.row)], r.small_out.at[m],
            r.store.at[m, images])

    def partner(flip):
        return place(flipped(me, flip))

    def gather_copies(which, stage):
        if stage == 0:
            here = r.gathered.at[which, core, xy, z]
            flips = [8 * k for k in range(1, chips // 4)]
        elif stage == 1:
            here = r.gathered.at[which, core, xy]
            flips = [2 * k for k in range(1, 4)]
        else:
            here = r.gathered.at[which, core]
            flips = [1]
        return [
            remote(here, here, r.gather_send.at[which, stage, k], r.gather_recv.at[which, stage, k], partner(flip))
            for k, flip in enumerate(flips)
        ]

    def gather_start(which, stage):
        for copy in gather_copies(which, stage):
            copy.start()

    def gather_end(which, stage):
        for copy in gather_copies(which, stage):
            copy.wait()

    moved = r.moved

    def exchange_copies(m, turn, stage):
        ref, which = moved[m * 3 + turn][stage], m * 3 + turn
        return [
            remote(
                ref.at[0], ref.at[k], r.move_send.at[which, stage, k], r.move_recv.at[which, stage, k],
                partner(k << shifts_of[stage]))
            for k in range(1, 1 << widths[stage])
        ]

    def picked(m, stage):
        return lax.rem(lax.div(jnp.bitwise_xor(mask[m, 0], mask[m, 1]), 1 << shifts_of[stage]), 1 << widths[stage])

    def exchange_start(m, turn):
        for copy in exchange_copies(m, turn, 0):
            copy.start()

    def exchange_next(m, turn):
        for copy in exchange_copies(m, turn, 0):
            copy.wait()
        first, second = moved[m * 3 + turn]
        second[0] = first[picked(m, 0)]
        for copy in exchange_copies(m, turn, 1):
            copy.start()

    def exchange_end(m, turn):
        for copy in exchange_copies(m, turn, 1):
            copy.wait()

    def put_moments(m, turn, row, start, size, step):
        pivot = folded(wide[at(start, step, 8)]).sum(0, keepdims=True) / step
        total, square = moments(wide, start, size, step, pivot)
        off = total.sum(0, keepdims=True) / size
        moved[m * 3 + turn][0][0, pl.ds(row, 1)] = pivot + off
        moved[m * 3 + turn][0][0, pl.ds(row + 1, 1)] = jnp.maximum(square.sum(0, keepdims=True) - off * off * size, 0.0)

    def combined(m, turn, row, other, count):
        pick = picked(m, 1)
        mean, spread = moved[m * 3 + turn][0][0, pl.ds(row, 1)], moved[m * 3 + turn][0][0, pl.ds(row + 1, 1)]
        mean2, spread2 = moved[m * 3 + turn][1][pick, pl.ds(other, 1)], moved[m * 3 + turn][1][pick, pl.ds(other + 1, 1)]
        apart = mean - mean2
        variance = (spread + spread2 + apart * apart * (count * 0.5)) / (2.0 * count)
        return (mean + mean2) * 0.5, lax.rsqrt(variance + NORM_EPS)

    def affine(group, start):
        mean, root = group
        new_gain = MOMENTUM * line(gains1, start) + (1.0 - MOMENTUM) * line(gains, start)
        new_shift = MOMENTUM * line(shifts1, start) + (1.0 - MOMENTUM) * line(shifts, start)
        scale = root * new_gain
        return scale, new_shift - mean * scale

    area, out_area = float(big.area), float(big.out_area)
    first_row = BLOCKS * outs
    spare = 2 * big.area

    def key_even(i):
        def put(block, value):
            slope3[at((i * 2 + block) * big.out_area, big.out_area)] = value

        even_cells(field, key_base + i * big.area, big, wide_stage, dense_stage, put)

    def key_side(i, start):
        cells = [slope3[at((i * 2 + block) * big.out_area, big.out_area)] for block in range(2)]
        value = dot(jnp.concatenate(cells, axis=1), wk[3][...])
        for block in range(BLOCKS):
            wide[at(start + block * big.out_area, big.out_area)] = value[:, block * 128 : (block + 1) * 128]

    def key_third(m, c, start):
        value = dot(thin[at(m * outs + c * big.out_area, big.out_area)], wk[2][...])
        for block in range(BLOCKS):
            wide[at(start + block * big.out_area, big.out_area)] = value[:, block * 128 : (block + 1) * 128]

    def key_a(m, c):
        start = m * first_row + c * big.area
        wide[at(start, big.area)] = dot(field[at(key_base + (2 * m + c) * big.area, big.area)], wk[0][...])
        put_moments(m, 0, c * 2, start, big.area, 112)
        start = m * first_row + spare
        key_side(2 * m + c, start)
        for block in range(BLOCKS):
            put_moments(m, 0, 8 + (c * BLOCKS + block) * 2, start + block * big.out_area, big.out_area, 112)

    def key_b(m, c):
        scale, bias = affine(combined(m, 0, c * 2, (1 - c) * 2, area), 0)

        def rows_of(y):
            for k in range(4):
                row = y * 4 + k
                v = wide[at(m * first_row + c * big.area + row * 2 * SIDE, 2 * SIDE)] * scale + bias
                split_planes(gelu_only(v), stage_of[0], planes_of[0], big, c, row, k % 2)

        repeat(0, big.half // 4, rows_of)
        value = dot(patches(planes_of[0], big, c, 1), wk[1][...])
        start = m * first_row + spare + c * big.out_area
        for k in range(big.half):
            wide[pl.ds(start + k * big.half, big.half)] = value[k * big.wide : k * big.wide + big.half]
        put_moments(m, 1, c * 2, start, big.out_area, 112)

    def key_c(m, c):
        scale, bias = affine(combined(m, 1, c * 2, (1 - c) * 2, out_area), CMID)
        for k in range(big.out_area // 112):
            v = wide[at(m * first_row + spare + c * big.out_area + k * 112, 112)] * scale + bias
            thin[at(m * outs + c * big.out_area + k * 112, 112)] = gelu_only(v).astype(bf16)
        start = m * first_row
        key_third(m, c, start)
        for block in range(BLOCKS):
            put_moments(m, 2, (c * BLOCKS + block) * 2, start + block * big.out_area, big.out_area, 112)

    def key_d(m, c):
        start = m * first_row
        key_third(m, c, start)
        key_side(2 * m + c, start + BLOCKS * big.out_area)
        parts = []
        for block in range(BLOCKS):
            lanes = 2 * CMID + block * 128
            row, other = (c * BLOCKS + block) * 2, ((1 - c) * BLOCKS + block) * 2
            scale3, bias3 = affine(combined(m, 2, row, other, out_area), lanes)
            scale4, bias4 = affine(combined(m, 0, 8 + row, 8 + other, out_area), lanes + COUT)
            bias = bias3 + bias4
            e = jnp.zeros((8, 128), f32)
            for k in range(big.out_area // 112):
                x3 = wide[at(start + block * big.out_area + k * 112, 112)]
                x4 = wide[at(start + (BLOCKS + block) * big.out_area + k * 112, 112)]
                e += folded(gelu_only(x3 * scale3 + x4 * scale4 + bias))
            parts.append(e.sum(0, keepdims=True) / out_area)
        length = sum(jnp.sum(part * part, axis=1, keepdims=True) for part in parts)
        inverse = lax.rsqrt(length + UNIT_EPS)
        for block in range(BLOCKS):
            r.embed[pl.ds(m * 8 + c * BLOCKS + block, 1)] = parts[block] * inverse

    def key_copy(m, k):
        mine = keys.at[pl.ds(pl.multiple_of((m * devices + me) * 8, 8), 8)]
        return remote(
            r.embed.at[pl.ds(m * 8, 8)], mine, r.key_send.at[m, k], r.key_recv.at[m, k], place(lax.rem(me + k, devices)))

    def share_start(m):
        keys[at((m * devices + me) * 8, 8, 8)] = r.embed[m * 8 : (m + 1) * 8]
        repeat(1, devices, lambda k: key_copy(m, k).start())

    def share_end(m):
        repeat(1, devices, lambda k: key_copy(m, k).wait())

    def core_copy(job):
        return remote(r.parts[job].at[1 - core], r.arrived[job], r.core_send.at[job], r.core_recv.at[job], partner(1))

    def row_copy(job, target, source):
        return remote(
            r.outward[job].at[target], r.inward[job].at[source], r.row_send.at[job, target], r.row_recv.at[job, source],
            (target, core))

    def job_send(job):
        core_copy(job).wait()

        def turn(k):
            target = lax.rem(chip + k, chips)
            value = r.parts[job][core, target] + r.arrived[job][target]
            r.outward[job][target] = value.astype(r.outward[job].dtype)
            row_copy(job, target, chip).start()

        repeat(1, chips, turn)

    def job_end(job):
        def add(k, total):
            source = lax.rem(chip + chips - k, chips)
            row_copy(job, source, source).wait_recv()
            return total + r.inward[job][source].astype(f32)

        total = lax.fori_loop(1, chips, add, r.parts[job][core, chip] + r.arrived[job][chip])
        start = sum(JOB_ROWS[:job])
        r.packed[start : start + JOB_ROWS[job]] = total
        repeat(1, chips, lambda k: row_copy(job, lax.rem(chip + k, chips), chip).wait_send())

    def fill_head():
        part, third, fourth = r.parts[0], grads[2], grads[3]

        def turn(i):
            for block in range(BLOCKS):
                half, row = block // 2, block % 2
                lanes = slice(block * 128, (block + 1) * 128)
                part[half, i, row * 8 : row * 8 + 8] = third[at(i * 8, 8, 8), lanes]
                part[half, i, 16 + row * 16 : 32 + row * 16] = fourth[at(i * 16, 16), lanes]

        repeat(0, chips, turn)
        core_copy(0).start()

    def fill_spatial():
        part = r.parts[1]
        for tile in range(9):
            lanes = slice(tile * 128, (tile + 1) * 128)
            gy2[lanes] = grads[1][:, lanes].T
        filler = jnp.zeros((8, 128), f32)

        def turn(i):
            top = gy2[at(i * 72, 40, 8)]
            bottom = jnp.concatenate([gy2[at(i * 72 + 40, 32, 8)], filler], axis=0)
            for half in range(2):
                part[half, i, 0:40] = side_by_side(top, bottom, half)
                part[half, i, 40:48] = filler

        repeat(0, chips, turn)
        core_copy(1).start()

    def fill_sums():
        part = r.parts[2]
        column = lax.broadcasted_iota(jnp.int32, (1, 128), 1)
        filler = jnp.zeros((1, 128), f32)
        rows = [gain_sum[:, k * 128 : (k + 1) * 128] for k in range(10)]
        rows += [jnp.where(column == 0, loss_sum[...], 0.0), filler]
        rows += [shift_sum[:, k * 128 : (k + 1) * 128] for k in range(10)] + [filler, filler]
        rows = jnp.concatenate(rows, axis=0)

        def turn(i):
            for half in range(2):
                part[half, i] = rows

        repeat(0, chips, turn)
        core_copy(2).start()

    def fill_reduce():
        part = r.parts[3]
        for tile in range(2):
            lanes = slice(tile * 128, (tile + 1) * 128)
            gy2[lanes] = grads[0][:, lanes].T

        def turn(i):
            for half in range(2):
                part[half, i] = side_by_side(gy2[at(i * 16, 8, 8)], gy2[at(i * 16 + 8, 8, 8)], half)

        repeat(0, chips, turn)
        core_copy(3).start()

    for load in query_loads(0) + key_loads:
        load.start()
    barrier = pltpu.get_barrier_semaphore()
    repeat(1, devices, lambda k: pl.semaphore_signal(
        barrier, inc=1, device_id=place(lax.rem(me + k, devices)), device_id_type=MESH))
    if own:
        current = [r.r0[...], r.s0[...], r.e0[...], r.p0[...]]
        lagged = [r.r1[...], r.s1[...], r.e1[...], r.p1[...]]
        packed_shards([MOMENTUM * old + (1.0 - MOMENTUM) * new for old, new in zip(lagged, current)], r.sent, 0)
        packed_shards(current, r.sent, 1)
        for which in range(2):
            r.gathered[which, core, xy, z] = r.sent[which]
    else:
        for shard, w in zip((r.r0, r.s0, r.e0, r.p0, r.r1, r.s1, r.e1, r.p1), wq + wk):
            w[...] = shard[...]
    if devices > 1:
        pl.semaphore_wait(barrier, devices - 1)
    if own:
        gather_start(0, 0)
    for ref in list(planes_of.values()) + list(back_of.values()) + list(stage_of.values()) + grads + [
        r.raised, gain_sum, shift_sum, loss_sum, gy2] + [pair[0] for pair in moved]:
        ref[...] = jnp.zeros_like(ref)
    if own:
        gather_end(0, 0)
        gather_start(0, 1)
        gather_start(1, 0)

    def micro_step(m):
        opening, closing = m == 0, m == micros - 1
        base = m * field_rows
        w1, w2, w3, w4 = wq
        w1t, w3t, w4t, wt0, wt1 = (r.w1t, r.w3t, r.w4t, r.wt0, r.wt1)
        alive_count = sum(counts[m, i] for i in range(images)).astype(f32)
        count1 = images * big.area + small.area * alive_count
        count2 = images * big.out_area + small.out_area * alive_count

        def living(kind, crop):
            if kind is big:
                return jnp.float32(1.0)
            return jnp.where(lax.rem(crop, slots) < counts[m, lax.div(crop, slots)], 1.0, 0.0)

        def step_of(kind):
            return 112 if kind is big else 144

        def over_big(body, *hooks):
            def turn(c):
                body(big, c, 1)
                for k, (when, hook) in enumerate(hooks):

                    @pl.when(jnp.logical_and(when, c == k))
                    def _():
                        hook()

            repeat(0, big.count, turn)

        def over_small(body):
            body(small, 0, small.count)

        def add_moments(ref, offset, kind, first, count, row0, size, row, where, opener):
            start = offset + row0 + first * size
            if kind is big:

                @pl.when(first == 0)
                def _():
                    vec[row : row + 1] = folded(ref[at(start, opener, 8)]).sum(0, keepdims=True) / opener

            for c in range(count):
                total, square = moments(ref, start + c * size, size, step_of(kind), vec[row : row + 1])
                alive = living(kind, first + c)
                sums[where] += total * alive
                sums[where + 1] += square * alive

        for load in query_loads(m):
            load.wait()

        def even_batch(kind, first, count):
            for c in range(count):
                start = kind.out_row + (first + c) * kind.out_area

                def put(block, value):
                    even[at(start, kind.out_area), block * 128 : (block + 1) * 128] = value

                even_cells(field, base + kind.row + (first + c) * kind.area, kind, wide_stage, dense_stage, put)

        over_big(even_batch)
        over_small(even_batch)

        @pl.when(opening)
        def _():
            for load in key_loads:
                load.wait()
            repeat(0, 2 * micros, key_even)
            if own:
                gather_end(0, 1)
                gather_start(0, 2)
                gather_end(1, 0)
                gather_start(1, 1)
                gather_end(0, 2)
                unpacked(r.gathered, 0, chips, wk, gy2)
            repeat(0, 2, lambda c: key_a(0, c))
            exchange_start(0, 0)
            if own:
                gather_end(1, 1)
                gather_start(1, 2)
            repeat(0, 2, lambda c: key_a(1, c))
            exchange_start(1, 0)
            for load in query_loads(1):
                load.start()
            if own:
                gather_end(1, 2)
                unpacked(r.gathered, 1, chips, wq, gy2)
            w1t[...] = w1[...].T
            w3t[...] = w3[...].T
            w4t[...] = w4[...].T
            wt0[...] = jnp.zeros_like(wt0)
            wt1[...] = jnp.zeros_like(wt1)

            def tap(ky, kx):
                start = (3 * ky + kx) * CMID
                return w2[start : start + CMID, :].T

            wt0[0:128, 0:128] = tap(1, 1)
            wt0[0:128, 128:256] = tap(1, 2)
            wt0[128:256, 128:256] = tap(1, 0)
            wt1[0:128, 0:128] = tap(2, 1)
            wt1[0:128, 128:256] = tap(2, 2)
            wt1[128:256, 128:256] = tap(2, 0)
            wt1[256:384, 0:128] = tap(0, 1)
            wt1[256:384, 128:256] = tap(0, 2)
            wt1[384:512, 128:256] = tap(0, 0)

        sums[...] = jnp.zeros_like(sums)

        def reduce_batch(kind, first, count):
            start = kind.row + first * kind.area
            size = count * kind.area
            a1[at(start, size)] = dot(field[at(base + start, size)], w1[...])
            add_moments(a1, 0, kind, first, count, kind.row, kind.area, 0, 0, 784)

        over_big(reduce_batch, (opening, lambda: exchange_next(0, 0)), (opening, lambda: exchange_next(1, 0)))
        over_small(reduce_batch)
        mean1, root1 = closed(sums[0], sums[1], vec[0:1], count1)
        scale1 = root1 * line(gains, 0)
        bias1 = line(shifts, 0) - mean1 * scale1
        vec[1:2], vec[2:3], vec[3:4], vec[4:5] = mean1, root1, scale1, bias1

        @pl.when(opening)
        def _():
            for k in range(2):
                exchange_end(k, 0)
                repeat(0, 2, lambda c: key_b(k, c))
                exchange_start(k, 1)

        sums[...] = jnp.zeros_like(sums)

        def hidden_batch(kind, first, count):
            scale, bias = vec[3:4], vec[4:5]
            for c in range(count):
                for k in range(kind.half):
                    start = kind.row + (first + c) * kind.area + k * 2 * kind.side
                    v = a1[at(start, 2 * kind.side)] * scale + bias
                    hidden, slope = gelu_pair(v)
                    slope1[at(start, 2 * kind.side)] = slope.astype(bf16)
                    split_planes(hidden, stage_of[kind.ahead], planes_of[kind.ahead], kind, first + c, k, k % 2)

        over_big(hidden_batch, (opening, lambda: exchange_next(0, 1)), (opening, lambda: exchange_next(1, 1)))
        over_small(hidden_batch)

        @pl.when(opening)
        def _():
            for k in range(2):
                exchange_end(k, 1)
                repeat(0, 2, lambda c: key_c(k, c))
                exchange_start(k, 2)

        def spatial_batch(kind, first, count):
            half, lanes = kind.half, kind.wide
            value = dot(patches(planes_of[kind.ahead], kind, first, count), w2[...])
            start = kind.out_row + first * kind.out_area
            for k in range(count * half):
                a2[pl.ds(start + k * half, half)] = value[k * lanes : k * lanes + half]
            add_moments(a2, 0, kind, first, count, kind.out_row, kind.out_area, 0, 16, 784)

        over_big(spatial_batch, (opening, lambda: exchange_next(0, 2)), (opening, lambda: exchange_next(1, 2)))
        over_small(spatial_batch)
        mean2, root2 = closed(sums[16], sums[17], vec[0:1], count2)
        scale2 = root2 * line(gains, CMID)
        bias2 = line(shifts, CMID) - mean2 * scale2
        vec[5:6], vec[6:7], vec[7:8], vec[8:9] = mean2, root2, scale2, bias2

        @pl.when(opening)
        def _():
            for k in range(2):
                exchange_end(k, 2)
                repeat(0, 2, lambda c: key_d(k, c))
                share_start(k)

        def head_product(which, source, weight, kind, first, count):
            start = kind.out_row + first * kind.out_area
            size = count * kind.out_area
            value = dot(source, weight[...])
            for block in range(BLOCKS):
                offset = (which * BLOCKS + block) * outs
                wide[at(offset + start, size)] = value[:, block * 128 : (block + 1) * 128]
            for block in range(BLOCKS):
                offset = (which * BLOCKS + block) * outs
                add_moments(
                    wide, offset, kind, first, count, kind.out_row, kind.out_area,
                    16 + which * 4 + block, which * 8 + block * 2, 784)

        def expand_batch(kind, first, count):
            start = kind.out_row + first * kind.out_area
            size, step = count * kind.out_area, step_of(kind)
            scale, bias = vec[7:8], vec[8:9]
            head_product(1, even[at(start, size)], w4, kind, first, count)
            for k in range(size // step):
                hidden, slope = gelu_pair(a2[at(start + k * step, step)] * scale + bias)
                thin[at(H2 + start + k * step, step)] = hidden.astype(bf16)
                thin[at(SLOPE2 + start + k * step, step)] = slope.astype(bf16)
            head_product(0, thin[at(H2 + start, size)], w3, kind, first, count)

        over_big(expand_batch)
        over_small(expand_batch)
        for which in range(2):
            for block in range(BLOCKS):
                row = which * 4 + block
                where = which * 8 + block * 2
                lanes = 2 * CMID + row * 128
                mean, root = closed(sums[where], sums[where + 1], vec[16 + row : 17 + row], count2)
                scale = root * line(gains, lanes)
                bias = line(shifts, lanes) - mean * scale
                vec[24 + row : 25 + row], vec[32 + row : 33 + row] = mean, root
                vec[40 + row : 41 + row] = scale
                if which == 0:
                    vec[48 + block : 49 + block] = bias
                else:
                    vec[48 + block : 49 + block] += bias

        rows_e, rows_c = r.rows_e, r.rows_c

        def embed_batch(kind, first, count):
            step = step_of(kind)
            for c in range(count):
                start = kind.out_row + (first + c) * kind.out_area
                for block in range(BLOCKS):
                    mean3, mean4 = vec[24 + block : 25 + block], vec[28 + block : 29 + block]
                    scale3, scale4 = vec[40 + block : 41 + block], vec[44 + block : 45 + block]
                    bias = vec[48 + block : 49 + block]
                    zero = jnp.zeros((8, 128), f32)
                    e, s0, s3, s4 = zero, zero, zero, zero
                    for k in range(kind.out_area // step):
                        inside = block * outs + start + k * step
                        x3, x4 = wide[at(A3 + inside, step)], wide[at(AP + inside, step)]
                        value, slope = gelu_pair(x3 * scale3 + x4 * scale4 + bias)
                        slope3[at(inside, step)] = slope.astype(bf16)
                        e += folded(value)
                        s0 += folded(slope)
                        s3 += folded(slope * (x3 - mean3))
                        s4 += folded(slope * (x4 - mean4))
                    row = kind.ahead + first + c
                    for which, value in enumerate((e / kind.out_area, s0, s3, s4)):
                        rows_e[which, block, pl.ds(row, 1)] = value.sum(0, keepdims=True)

        over_big(embed_batch)
        over_small(embed_batch)

        share_end(m)

        def joined(which):
            return jnp.concatenate([rows_e[which, block] for block in range(BLOCKS)], axis=1)

        e = joined(0)
        inverse = lax.rsqrt(jnp.sum(e * e, axis=-1, keepdims=True) + UNIT_EPS)
        row = lax.broadcasted_iota(jnp.int32, (crops, 1), 0)
        owner = jnp.zeros((crops, 1), jnp.int32)
        live = jnp.where(row < images, 1.0, 0.0)
        for i in range(images):
            owner = jnp.where(row == i, i, owner)
            for slot in range(slots):
                here = row == images + i * slots + slot
                owner = jnp.where(here, i, owner)
                live = jnp.where(here, jnp.where(slot < counts[m, i], 1.0, 0.0), live)
        embedding = e * inverse
        key_blocks = [
            jnp.concatenate(
                [keys[pl.ds(m * devices * 8 + c * BLOCKS + block, devices, stride=8)] for c in range(images)], axis=0)
            for block in range(BLOCKS)
        ]
        logits = sum(
            dot_exact(embedding[:, block * 128 : (block + 1) * 128], key_blocks[block], ((1,), (1,)))
            for block in range(BLOCKS)
        )
        logits = logits / TEMP
        top = jnp.max(logits, axis=-1, keepdims=True)
        powers = jnp.exp(logits - top)
        total = jnp.sum(powers, axis=-1, keepdims=True)
        column = lax.broadcasted_iota(jnp.int32, logits.shape, 1)
        mine = column == owner * devices + me
        chosen = jnp.sum(jnp.where(mine, logits, 0.0), axis=-1, keepdims=True)
        ce = (top + jnp.log(total) - chosen) * live
        loss_sum[...] += jnp.sum(ce, axis=0, keepdims=True)
        toward = (powers / total - jnp.where(mine, 1.0, 0.0)) * (live / TEMP)
        back = jnp.concatenate([dot_exact(toward, block, ((1,), (0,))) for block in key_blocks], axis=1)
        de = inverse * back - e * (inverse * inverse * inverse * jnp.sum(e * back, axis=-1, keepdims=True))
        de = de * jnp.where(row < images, 1.0 / big.out_area, 1.0 / small.out_area)
        sum0 = jnp.sum(de * joined(1), axis=0, keepdims=True)
        for which in range(2):
            reach = jnp.sum(de * joined(2 + which), axis=0, keepdims=True)
            for block in range(BLOCKS):
                row = which * 4 + block
                here = slice(block * 128, (block + 1) * 128)
                lanes = slice(2 * CMID + row * 128, 2 * CMID + (row + 1) * 128)
                mean, root, scale = vec[24 + row : 25 + row], vec[32 + row : 33 + row], vec[40 + row : 41 + row]
                along = reach[:, here] * root
                gain_sum[:, lanes] += along
                shift_sum[:, lanes] += sum0[:, here]
                tilt = scale * root * along / count2
                vec[52 + row : 53 + row] = tilt
                vec[60 + row : 61 + row] = scale * sum0[:, here] / count2 - tilt * mean
                rows_c[which, block] = de[:, here] * scale

        sums[...] = jnp.zeros_like(sums)
        d3, dp = r.d3, r.dp

        def head_back(kind, first, count):
            start = kind.out_row + first * kind.out_area
            size, step = count * kind.out_area, step_of(kind)
            for which, store in ((0, d3), (1, dp)):
                for block in range(BLOCKS):
                    lanes = slice(block * 128, (block + 1) * 128)
                    where = which * 4 + block
                    for c in range(count):
                        rise = rows_c[which, block, pl.ds(kind.ahead + first + c, 1)]
                        alive = living(kind, first + c)
                        tilt, level = vec[52 + where : 53 + where] * alive, vec[60 + where : 61 + where] * alive
                        for k in range(kind.out_area // step):
                            inside = c * kind.out_area + k * step
                            here = block * outs + start + inside
                            x = wide[at(which * BLOCKS * outs + here, step)]
                            grad = slope3[at(here, step)].astype(f32) * rise - (x * tilt + level)
                            store[inside : inside + step, lanes] = grad.astype(bf16)
            grad3, gradp = d3[0:size], dp[0:size]
            gy2[at(start, size)] = dot(grad3, w3t[...])
            gradient = dot(gradp, w4t[...])
            for block in range(2):
                wide[at(AP + block * outs + start, size)] = gradient[:, block * 128 : (block + 1) * 128]
            grads[2][...] += dot_rows(thin[at(H2 + start, size)], grad3)
            grads[3][...] += dot_rows(even[at(start, size)], gradp)
            mean = vec[5:6]
            level, reach = jnp.zeros((8, 128), f32), jnp.zeros((8, 128), f32)
            for k in range(size // step):
                here = at(start + k * step, step)
                gy = gy2[here] * thin[at(SLOPE2 + start + k * step, step)].astype(f32)
                gy2[here] = gy
                level += folded(gy)
                reach += folded(gy * (a2[here] - mean))
            sums[0] += level
            sums[1] += reach

        over_big(head_back)
        over_small(head_back)

        if own:

            @pl.when(closing)
            def _():
                fill_head()

        def norm_back(where, lanes, count):
            mean, root, scale = vec[where : where + 1], vec[where + 1 : where + 2], vec[where + 2 : where + 3]
            level = sums[0].sum(0, keepdims=True)
            along = sums[1].sum(0, keepdims=True) * root
            gain_sum[:, lanes] += along
            shift_sum[:, lanes] += level
            tilt = scale * root * along / count
            vec[68:69] = scale
            vec[69:70] = tilt
            vec[70:71] = scale * level / count - tilt * mean

        norm_back(5, slice(CMID, 2 * CMID), count2)
        sums[...] = jnp.zeros_like(sums)

        def spatial_back(kind, first, count):
            half, lanes, side, step = kind.half, kind.wide, kind.side, step_of(kind)
            out_start = kind.out_row + first * kind.out_area
            for c in range(count):
                alive = living(kind, first + c)
                tilt, level = vec[69:70] * alive, vec[70:71] * alive
                for k in range(kind.out_area // step):
                    here = at(out_start + c * kind.out_area + k * step, step)
                    gy2[here] = gy2[here] * vec[68:69] - (a2[here] * tilt + level)
            column = lax.broadcasted_iota(jnp.int32, (lanes, 128), 0)
            store = back_of[kind.ahead]
            for k in range(count * half):
                here = jnp.where(column < half, gy2[pl.ds(out_start + k * half, lanes)], 0.0)
                following = jnp.where(column < half - 1, gy2[pl.ds(out_start + k * half + 1, lanes)], 0.0)
                store[first + k // half, k % half, :, 0:128] = here.astype(bf16)
                store[first + k // half, k % half, :, 128:256] = following.astype(bf16)
            size = count * half * lanes
            near = store[pl.ds(first, count), 0:half].reshape(size, 256)
            beyond = store[pl.ds(first, count), 1 : half + 1].reshape(size, 256)
            upper_rows = dot(near, wt0[...])
            lower_rows = dot(jnp.concatenate([near, beyond], axis=1), wt1[...])
            start = kind.row + first * kind.area
            for k in range(count * half):
                here = slice(k * lanes, k * lanes + half)
                row = start + k * 2 * side
                for odd, value in ((0, upper_rows), (1, lower_rows)):
                    wide[pl.ds(row + odd * side, half, stride=2)] = value[here, 0:128]
                    wide[pl.ds(row + odd * side + 1, half, stride=2)] = value[here, 128:256]
            grads[1][...] += dot_rows(near[:, 0:128], patches(planes_of[kind.ahead], kind, first, count))
            mean = vec[1:2]
            level, reach = jnp.zeros((8, 128), f32), jnp.zeros((8, 128), f32)
            for k in range(count * kind.area // step):
                here = at(start + k * step, step)
                gy = wide[here] * slope1[here].astype(f32)
                wide[here] = gy
                level += folded(gy)
                reach += folded(gy * (a1[here] - mean))
            sums[0] += level
            sums[1] += reach

        def job_hooks(*jobs):
            def sends(some):
                return lambda: [job_send(job) for job in some]

            return [(closing, sends(some)) for some in jobs] if own else []

        over_big(spatial_back, *job_hooks((0,)))
        over_small(spatial_back)
        norm_back(1, slice(0, CMID), count1)

        if own:

            @pl.when(closing)
            def _():
                fill_spatial()
                fill_sums()

        def reduce_back(kind, first, count):
            step = step_of(kind)
            size = count * kind.area
            start = kind.row + first * kind.area
            rise = vec[68:69]
            for c in range(count):
                alive = living(kind, first + c)
                tilt, level = vec[69:70] * alive, vec[70:71] * alive
                for k in range(kind.area // step):
                    here = at(start + c * kind.area + k * step, step)
                    grad = wide[here] * rise - (a1[here] * tilt + level)
                    slope1[here] = grad.astype(bf16)
            grads[0][...] += dot_rows(slope1[at(start, size)], field[at(base + start, size)])

        over_big(reduce_back, *job_hooks((1,), (2,)))
        over_small(reduce_back)

        if own:

            @pl.when(closing)
            def _():
                fill_reduce()
                job_end(0)

        raised = r.raised

        def field_back(kind, first, count):
            half, side = kind.half, kind.side
            size = count * kind.area
            start = kind.row + first * kind.area
            whole = dot(slope1[at(start, size)], w1t[...])
            out_start = kind.out_row + first * kind.out_area
            for k in range(count * half):
                row = k * 2 * side
                for block in range(2):
                    lanes = slice(block * 128, (block + 1) * 128)
                    slot = k % 4 * 2 + block
                    raised[slot, pl.ds(0, half, stride=2)] = wide[pl.ds(AP + block * outs + out_start + k * half, half)]
                    top_row = whole[row : row + side, lanes] + raised[slot, 0:side]
                    both = jnp.concatenate([top_row, whole[row + side : row + 2 * side, lanes]], axis=0)
                    field[at(base + start + row, 2 * side), lanes] = both.astype(bf16)
            if kind is big:
                store_big(m, first).start()
            else:
                store_small(m).start()

        over_big(field_back, *job_hooks((), (3,)))
        over_small(field_back)

    repeat(0, micros, micro_step)
    if own:
        for job in range(1, 4):
            job_end(job)
    for m in range(micros):
        for c in range(images):
            store_big(m, c).wait()
        store_small(m).wait()


def step_pass(axes, own, slots, big, small, key, counts, mask, current, lagged, vectors):
    chips, cores = axes
    devices = chips * cores
    widths = stage_widths(devices)
    micros, images = counts.shape
    one, two = field_pair(images, slots)
    rows = two.row + two.count * two.area
    outs = two.out_row + two.count * two.out_area
    crops = images * (1 + slots)
    vmem = pl.BlockSpec(memory_space=pltpu.VMEM)
    smem = pl.BlockSpec(memory_space=pltpu.SMEM)
    hbm = pl.BlockSpec(memory_space=pl.ANY)
    weights = [(CIN, CMID), (9 * CMID, CMID), (CMID, COUT), (CIN, COUT)]
    totals = dict(
        g1=(CMID, CIN), g2=(CMID, 9 * CMID), g3=(CMID, COUT), g4=(CIN, COUT),
        gain_sum=(1, NORMS), shift_sum=(1, NORMS), loss_sum=(1, 1))
    r0, s0, e0, p0 = ((w, vmem) for w in current)
    r1, s1, e1, p1 = ((w, vmem) for w in lagged)
    gains, shifts, gains1, shifts1 = ((v, vmem) for v in vectors)
    inputs = dict(
        big_hbm=(big, hbm), small_hbm=(small, hbm), key_hbm=(key, hbm), counts=(counts, smem), mask=(mask, smem),
        r0=r0, s0=s0, e0=e0, p0=p0, r1=r1, s1=s1, e1=e1, p1=p1, gains=gains, shifts=shifts, gains1=gains1, shifts1=shifts1)
    outputs = dict(
        big_out=(jax.ShapeDtypeStruct(big.shape, bf16), hbm), small_out=(jax.ShapeDtypeStruct(small.shape, bf16), hbm))
    if own:
        outputs |= dict(packed=(jax.ShapeDtypeStruct((sum(JOB_ROWS), 128), f32), vmem))
    else:
        outputs |= {n: (jax.ShapeDtypeStruct(shape, f32), vmem) for n, shape in totals.items()}

    def buf(dtype, *shape):
        return pltpu.VMEM(shape, dtype)

    def dma(*shape):
        return pltpu.SemaphoreType.DMA(shape)

    scratch = dict(
        field=buf(bf16, rows + 2 * micros * one.area, CIN),
        a1=buf(f32, rows, 128), slope1=buf(bf16, rows, 128),
        planes_big=buf(bf16, 2, one.count, one.half + 1, one.wide, 384),
        planes_small=buf(bf16, 2, two.count, two.half + 1, two.wide, 384),
        a2=buf(f32, outs, 128), thin=buf(bf16, 2 * outs, 128), even=buf(bf16, outs, CIN),
        wide=buf(f32, 2 * BLOCKS * outs, 128), slope3=buf(bf16, BLOCKS * outs, 128),
        back_big=buf(bf16, one.count, one.half + 1, one.wide, 256),
        back_small=buf(bf16, two.count, two.half + 1, two.wide, 256),
        gy2=buf(f32, outs + 16, 128), stage_big=buf(f32, 2, 2, 80, 128), stage_small=buf(f32, 2, 2, 48, 128),
        wide_stage=buf(f32, 8, SIDE, 128), dense_stage=buf(f32, 2, one.out_area, 128), raised=buf(f32, 8, SIDE, 128),
        d3=buf(bf16, two.count * two.out_area, COUT), dp=buf(bf16, two.count * two.out_area, COUT),
        w1t=buf(bf16, CMID, CIN), w3t=buf(bf16, COUT, CMID), w4t=buf(bf16, COUT, CIN),
        wt0=buf(bf16, 256, 256), wt1=buf(bf16, 512, 256), sums=buf(f32, 18, 8, 128), vec=buf(f32, 80, 128),
        rows_e=buf(f32, 4, BLOCKS, crops, 128), rows_c=buf(f32, 2, BLOCKS, crops, 128),
        keys=buf(f32, devices * 16, 128), embed=buf(f32, 16, 128),
        moved=[[buf(f32, 1 << width, n, 128) for width in widths] for _ in range(micros) for n in TURN_ROWS],
        key_load=dma(2 * micros), query_load=dma(micros, 2), store=dma(micros, images + 1),
        move_send=dma(3 * micros, 2, 1 << widths[0]), move_recv=dma(3 * micros, 2, 1 << widths[0]),
        key_send=dma(micros, devices), key_recv=dma(micros, devices),
    )
    first, second, third, fourth = (buf(bf16, *shape) for shape in weights)
    scratch |= dict(w1q=first, w2q=second, w3q=third, w4q=fourth, w1k=first, w2k=second, w3k=third, w4k=fourth)
    wires = (bf16, bf16, f32, f32)
    if own:
        scratch |= {n: buf(f32, *shape) for n, shape in totals.items()}
        scratch |= dict(
            sent=buf(bf16, 2, PACK, 128), gathered=buf(bf16, 2, 2, 4, 4, PACK, 128),
            parts=[buf(f32, 2, chips, n, 128) for n in JOB_ROWS], arrived=[buf(f32, chips, n, 128) for n in JOB_ROWS],
            outward=[buf(t, chips, n, 128) for n, t in zip(JOB_ROWS, wires)],
            inward=[buf(t, chips, n, 128) for n, t in zip(JOB_ROWS, wires)],
            gather_send=dma(2, 3, 3), gather_recv=dma(2, 3, 3), core_send=dma(4), core_recv=dma(4),
            row_send=dma(4, chips), row_recv=dma(4, chips),
        )
    names = list(inputs) + list(outputs) + list(scratch)
    out = pl.pallas_call(
        functools.partial(step_kernel, axes, own, slots, names),
        out_shape=[shape for shape, _ in outputs.values()],
        in_specs=[spec for _, spec in inputs.values()],
        out_specs=[spec for _, spec in outputs.values()],
        scratch_shapes=list(scratch.values()),
        compiler_params=pltpu.CompilerParams(vmem_limit_bytes=63 * 2**20, collective_id=0, has_side_effects=True),
        name="step",
    )(*[array for array, _ in inputs.values()])
    return types.SimpleNamespace(**dict(zip(outputs, out)))


def finish_kernel(packed, loss, reduce_out, spatial_out, expand_out, shortcut_out, gains, shifts):
    reduce_out[0:8] = packed[120:128, 0:64]
    reduce_out[8:16] = packed[120:128, 64:128]
    rows = jnp.concatenate([packed[48:88], jnp.zeros((88, 128), f32)], axis=0).T
    spatial_out[...] = jnp.concatenate([rows[0:64, 0:40], rows[64:128, 0:32]], axis=1)
    for block in range(2):
        lanes = slice(block * 128, (block + 1) * 128)
        expand_out[:, lanes] = packed[block * 8 : block * 8 + 8]
        shortcut_out[:, lanes] = packed[16 + block * 16 : 32 + block * 16]
    for row in range(NORMS // 128):
        gains[pl.ds(row * 128, 128)] = packed[96 + row]
        shifts[pl.ds(row * 128, 128)] = packed[108 + row]
    loss[...] = packed[106:107, 0:1]


def finish_pass(packed):
    vmem = pl.BlockSpec(memory_space=pltpu.VMEM)
    shapes = [(1, 1), (16, 64), (64, 72), (8, 256), (16, 256), (NORMS,), (NORMS,)]
    return pl.pallas_call(
        finish_kernel,
        out_shape=[jax.ShapeDtypeStruct(shape, f32) for shape in shapes],
        in_specs=[vmem],
        out_specs=[vmem] * 7,
        name="finish",
    )(packed)


def gather_weights(shards):
    rows = [lax.all_gather(part, "dp", axis=0, tiled=True) for part in shards]
    return [lax.all_gather(part, "fsdp", axis=1, tiled=True) for part in rows]


def per_device(axes, *args):
    query_global, small_crop_query, small_count, key_global, shuffle_mask = args[:5]
    current, lagged = args[5:9], args[11:15]
    vectors = (args[9], args[10], args[15], args[16])
    micros = query_global.shape[0]
    slots = small_crop_query.shape[2]
    chips, cores = axes
    own = chips == 16 and cores == 2
    if own:
        current = [w.T if i == 1 else w for i, w in enumerate(current)]
        lagged = [w.T if i == 1 else w for i, w in enumerate(lagged)]
    else:
        fresh = [MOMENTUM * old + (1.0 - MOMENTUM) * new for old, new in zip(lagged, current)]
        current = gather_weights([w.astype(bf16) for w in current])
        lagged = gather_weights([w.astype(bf16) for w in fresh])
    out = step_pass(
        axes, own, slots, query_global.reshape(micros, -1, CIN), small_crop_query.reshape(micros, -1, CIN),
        key_global.reshape(micros, -1, CIN), small_count, shuffle_mask, current, lagged, vectors,
    )
    fields = (out.big_out.reshape(query_global.shape), out.small_out.reshape(small_crop_query.shape))
    if own:
        loss, first, second, third, fourth, gains_grad, shifts_grad = finish_pass(out.packed)
        return (loss.reshape(()), *fields, first, second.T, third, fourth, gains_grad, shifts_grad)
    totals = (out.g1.T, out.g2.T, out.g3, out.g4)
    summed = lax.psum_scatter(totals, "dp", scatter_dimension=0, tiled=True)
    owned = lax.psum_scatter(summed, "fsdp", scatter_dimension=1, tiled=True)
    sums = lax.psum((out.loss_sum, out.gain_sum, out.shift_sum), ("dp", "fsdp"))
    return (sums[0].reshape(()), *fields, *owned, sums[1].reshape(NORMS), sums[2].reshape(NORMS))


def solution(mesh):
    whole, split = P(), P("dp", "fsdp")
    images, crops = P(None, ("dp", "fsdp"), None, None, None), P(None, ("dp", "fsdp"), None, None, None, None)
    axes = (mesh.shape["dp"], mesh.shape["fsdp"])
    return jax.shard_map(
        functools.partial(per_device, axes),
        mesh=mesh,
        in_specs=(images, crops, P(None, ("dp", "fsdp")), images, whole)
        + (split,) * 4 + (whole,) * 2 + (split,) * 4 + (whole,) * 2,
        out_specs=(whole, images, crops) + (split,) * 4 + (whole,) * 2,
        check_vma=False,
    )
```

```python
import functools
import types
import jax
import jax.numpy as jnp
from jax import lax
from jax.experimental import pallas as pl
from jax.experimental.pallas import tpu as pltpu
from jax.sharding import PartitionSpec as P

f32, bf16 = jnp.float32, jnp.bfloat16
CIN, CMID, COUT, NORMS = 256, 128, 512, 1280
SIDE, SMALL = 56, 24
BLOCKS = COUT // 128
TEMP, NORM_EPS, UNIT_EPS = 0.2, 1e-05, 1e-06
ROOT_HALF = 0.7071067811865476
DENSITY = 0.3989422804014327


class Field:
    def __init__(self, count, side, row, out_row, ahead):
        self.count, self.side, self.row, self.out_row = count, side, row, out_row
        self.ahead = ahead
        self.half = side // 2
        self.wide = -(-self.half // 16) * 16
        self.area, self.out_area = side * side, (side // 2) ** 2


def field_pair(images, slots):
    big = Field(images, SIDE, 0, 0, 0)
    small = Field(images * slots, SMALL, images * big.area, images * big.out_area, images)
    return big, small


def at(start, size, align=16):
    if isinstance(start, int):
        return pl.ds(start, size)
    return pl.ds(pl.multiple_of(start, align), size)


def folded(x):
    return x.reshape(x.shape[0] // 8, 8, x.shape[1]).sum(0)


def dot(a, b):
    return jnp.dot(a, b, preferred_element_type=f32)


def dot_rows(a, b):
    return lax.dot_general(a, b, (((0,), (0,)), ((), ())), preferred_element_type=f32)


def gelu_pair(v):
    share = 0.5 + 0.5 * lax.erf(v * ROOT_HALF)
    return v * share, share + v * (DENSITY * jnp.exp(v * v * -0.5))


def gelu_only(v):
    return v * (0.5 + 0.5 * lax.erf(v * ROOT_HALF))


MOMENTUM = 0.999
MESH = pl.DeviceIdType.MESH
PACK = 96
JOB_ROWS = (48, 48, 24, 8)
TURN_ROWS = (24, 8, 16)


def line(vector, start):
    return vector[pl.ds(start, 128)].reshape(1, 128)


def two_parts(x):
    high = x.astype(bf16)
    return high, (x - high.astype(f32)).astype(bf16)


def moments(ref, start, size, step, pivot):
    total = jnp.zeros((8, 128), f32)
    square = jnp.zeros((8, 128), f32)
    for k in range(size // step):
        x = ref[at(start + k * step, step, 8)] - pivot
        total += folded(x)
        square += folded(x * x)
    return total, square


def closed(total, square, pivot, count):
    off = total.sum(0, keepdims=True) / count
    spread = jnp.maximum(square.sum(0, keepdims=True) / count - off * off, 0.0)
    return pivot + off, lax.rsqrt(spread + NORM_EPS)


def patches(planes, field, first, crops):
    size = crops * field.half * field.wide
    here = pl.ds(first, crops)
    above = planes[1, here, 0 : field.half].reshape(size, 3 * CMID)
    level = planes[0, here, 0 : field.half].reshape(size, 3 * CMID)
    below = planes[1, here, 1 : field.half + 1].reshape(size, 3 * CMID)
    return jnp.concatenate([above, level, below], axis=1)


def split_planes(hidden, stage, planes, field, crop, row, slot):
    side, wide = field.side, field.wide
    for odd in range(2):
        stage[slot, odd, 8 : 8 + side] = hidden[odd * side : (odd + 1) * side]
    for odd in range(2):
        for tap in range(3):
            column = stage[slot, odd, pl.ds(7 + tap, wide, stride=2)]
            planes[odd, crop, row + odd, :, tap * CMID : (tap + 1) * CMID] = column.astype(bf16)


def even_cells(source, base, field, wide_stage, dense_stage, put):
    side, half = field.side, field.half
    for y in range(half):
        for block in range(CIN // 128):
            slot = y % 4 * 2 + block
            x = source[at(base + y * 2 * side, 2 * side), block * 128 : (block + 1) * 128]
            wide_stage[slot, 0:side] = x.astype(f32)[0:side]
            dense_stage[block, y * half : (y + 1) * half] = wide_stage[slot, pl.ds(0, half, stride=2)]
    for block in range(CIN // 128):
        put(block, dense_stage[block, 0 : field.out_area].astype(bf16))


def flipped(index, mask):
    bit = 1
    while bit <= mask:
        if mask & bit:
            index = index + bit * (1 - 2 * lax.rem(lax.div(index, bit), 2))
        bit *= 2
    return index


def side_by_side(top, bottom, core):
    left = lax.broadcasted_iota(jnp.int32, top.shape, 1) < 64
    if core == 0:
        return jnp.where(left, top, pltpu.roll(bottom, 64, 1))
    return jnp.where(left, pltpu.roll(top, 64, 1), bottom)


def packed_shards(shards, store, which):
    first, second, third, fourth = shards
    zero = jnp.zeros
    second = jnp.concatenate([second, zero((second.shape[0], 56), f32)], axis=1)
    second = jnp.concatenate([second, zero((64, 128), f32)], axis=0).T[0:80, 0:64]
    rows = [jnp.concatenate([first[0:8], first[8:16]], axis=1), jnp.concatenate([second[0:40], second[40:80]], axis=1)]
    rows += [third[:, 0:128], third[:, 128:256], fourth[:, 0:128], fourth[:, 128:256]]
    store[which] = jnp.concatenate(rows, axis=0).astype(bf16)


def unpacked(gathered, which, chips, weights, stage):
    w1, w2, w3, w4 = weights

    def turn(i, _):
        z, xy = lax.div(i, 4), lax.rem(i, 4)
        ours = [gathered[which, core, xy, z] for core in range(2)]
        first, second = (rows[0:48].astype(f32) for rows in ours)
        left = lax.broadcasted_iota(jnp.int32, (48, 128), 1) < 64
        top = jnp.where(left, first, pltpu.roll(second, 64, 1))
        bottom = jnp.where(left, pltpu.roll(first, 64, 1), second)
        w1[at(i * 16, 16)] = jnp.concatenate([top[0:8], bottom[0:8]], axis=0).astype(bf16)
        stage[at(i * 72, 40, 8)] = top[8:48]
        stage[at(i * 72 + 40, 32, 8)] = bottom[8:40]
        for block in range(BLOCKS):
            start = 64 + block % 2 * 16
            w4[at(i * 16, 16), block * 128 : (block + 1) * 128] = ours[block // 2][start : start + 16]
        return 0

    lax.fori_loop(0, chips, turn, 0)
    w2[...] = stage[0 : 9 * CMID].astype(bf16)

    def pairs(i, _):
        z, xy = lax.div(i, 2), lax.rem(i, 2) * 2
        for block in range(BLOCKS):
            rows = slice(block % 2 * 8, block % 2 * 8 + 8)
            both = [gathered[which, block // 2, xy + k, z, 48:64].astype(f32)[rows] for k in range(2)]
            w3[at(i * 16, 16), block * 128 : (block + 1) * 128] = jnp.concatenate(both, axis=0).astype(bf16)
        return 0

    lax.fori_loop(0, chips // 2, pairs, 0)


def stage_widths(devices):
    bits = devices.bit_length() - 1
    return (bits + 1) // 2, bits // 2


def step_kernel(axes, own, slots, names, *refs):
    r = types.SimpleNamespace(**dict(zip(names, refs)))
    chips, cores = axes
    devices = chips * cores
    widths = stage_widths(devices)
    shifts_of = (0, widths[0])
    counts, mask = r.counts, r.mask
    micros, images = counts.shape
    fields = field_pair(images, slots)
    big, small = fields
    crops = images * (1 + slots)
    field_rows = small.row + small.count * small.area
    outs = small.out_row + small.count * small.out_area
    chip, core = lax.axis_index("dp"), lax.axis_index("fsdp")
    me = chip * cores + core
    xy, z = lax.rem(chip, 4), lax.div(chip, 4)
    field, a1, slope1, a2, even, wide, slope3 = (r.field, r.a1, r.slope1, r.a2, r.even, r.wide, r.slope3)
    thin, gy2, vec, sums, keys = (r.thin, r.gy2, r.vec, r.sums, r.keys)
    planes_of = {0: r.planes_big, images: r.planes_small}
    back_of = {0: r.back_big, images: r.back_small}
    stage_of = {0: r.stage_big, images: r.stage_small}
    wide_stage, dense_stage = r.wide_stage, r.dense_stage
    wq = [r.w1q, r.w2q, r.w3q, r.w4q]
    wk = [r.w1k, r.w2k, r.w3k, r.w4k]
    grads = [r.g1, r.g2, r.g3, r.g4]
    gains, shifts, gains1, shifts1 = (r.gains, r.shifts, r.gains1, r.shifts1)
    gain_sum, shift_sum, loss_sum = r.gain_sum, r.shift_sum, r.loss_sum
    A3, AP, H2, SLOPE2 = 0, BLOCKS * outs, 0, outs

    def place(device):
        return (lax.div(device, cores), lax.rem(device, cores))

    def remote(source, target, send, receive, device):
        return pltpu.make_async_remote_copy(
            src_ref=source, dst_ref=target, send_sem=send, recv_sem=receive, device_id=device, device_id_type=MESH)

    def repeat(first, last, body):
        lax.fori_loop(first, last, lambda k, _: (body(k), 0)[1], 0)

    key_base = field_rows
    key_loads = [
        pltpu.make_async_copy(
            r.key_hbm.at[i // 2, pl.ds(i % 2 * big.area, big.area)],
            field.at[pl.ds(key_base + i * big.area, big.area)], r.key_load.at[i])
        for i in range(2 * micros)
    ]

    def query_loads(m):
        return [
            pltpu.make_async_copy(
                r.big_hbm.at[m], field.at[pl.ds(m * field_rows, small.row)], r.query_load.at[m, 0]),
            pltpu.make_async_copy(
                r.small_hbm.at[m], field.at[pl.ds(m * field_rows + small.row, field_rows - small.row)],
                r.query_load.at[m, 1]),
        ]

    def store_big(m, c):
        return pltpu.make_async_copy(
            field.at[pl.ds(m * field_rows + c * big.area, big.area)],
            r.big_out.at[m, pl.ds(c * big.area, big.area)], r.store.at[m, c])

    def store_small(m):
        return pltpu.make_async_copy(
            field.at[pl.ds(m * field_rows + small.row, field_rows - small.row)], r.small_out.at[m],
            r.store.at[m, images])

    def partner(flip):
        return place(flipped(me, flip))

    def gather_copies(which, stage):
        if stage == 0:
            here = r.gathered.at[which, core, xy, z]
            flips = [8 * k for k in range(1, chips // 4)]
        elif stage == 1:
            here = r.gathered.at[which, core, xy]
            flips = [2 * k for k in range(1, 4)]
        else:
            here = r.gathered.at[which, core]
            flips = [1]
        return [
            remote(here, here, r.gather_send.at[which, stage, k], r.gather_recv.at[which, stage, k], partner(flip))
            for k, flip in enumerate(flips)
        ]

    def gather_start(which, stage):
        for copy in gather_copies(which, stage):
            copy.start()

    def gather_end(which, stage):
        for copy in gather_copies(which, stage):
            copy.wait()

    moved = r.moved

    def exchange_copies(m, turn, stage):
        ref, which = moved[m * 3 + turn][stage], m * 3 + turn
        return [
            remote(
                ref.at[0], ref.at[k], r.move_send.at[which, stage, k], r.move_recv.at[which, stage, k],
                partner(k << shifts_of[stage]))
            for k in range(1, 1 << widths[stage])
        ]

    def picked(m, stage):
        return lax.rem(lax.div(jnp.bitwise_xor(mask[m, 0], mask[m, 1]), 1 << shifts_of[stage]), 1 << widths[stage])

    def exchange_start(m, turn):
        for copy in exchange_copies(m, turn, 0):
            copy.start()

    def exchange_next(m, turn):
        for copy in exchange_copies(m, turn, 0):
            copy.wait()
        first, second = moved[m * 3 + turn]
        second[0] = first[picked(m, 0)]
        for copy in exchange_copies(m, turn, 1):
            copy.start()

    def exchange_end(m, turn):
        for copy in exchange_copies(m, turn, 1):
            copy.wait()

    def put_moments(m, turn, row, start, size, step):
        pivot = folded(wide[at(start, step, 8)]).sum(0, keepdims=True) / step
        total, square = moments(wide, start, size, step, pivot)
        off = total.sum(0, keepdims=True) / size
        moved[m * 3 + turn][0][0, pl.ds(row, 1)] = pivot + off
        moved[m * 3 + turn][0][0, pl.ds(row + 1, 1)] = jnp.maximum(square.sum(0, keepdims=True) - off * off * size, 0.0)

    def combined(m, turn, row, other, count):
        pick = picked(m, 1)
        mean, spread = moved[m * 3 + turn][0][0, pl.ds(row, 1)], moved[m * 3 + turn][0][0, pl.ds(row + 1, 1)]
        mean2, spread2 = moved[m * 3 + turn][1][pick, pl.ds(other, 1)], moved[m * 3 + turn][1][pick, pl.ds(other + 1, 1)]
        apart = mean - mean2
        variance = (spread + spread2 + apart * apart * (count * 0.5)) / (2.0 * count)
        return (mean + mean2) * 0.5, lax.rsqrt(variance + NORM_EPS)

    def affine(group, start):
        mean, root = group
        new_gain = MOMENTUM * line(gains1, start) + (1.0 - MOMENTUM) * line(gains, start)
        new_shift = MOMENTUM * line(shifts1, start) + (1.0 - MOMENTUM) * line(shifts, start)
        scale = root * new_gain
        return scale, new_shift - mean * scale

    area, out_area = float(big.area), float(big.out_area)
    first_row = BLOCKS * outs
    spare = 2 * big.area

    def key_even(i):
        def put(block, value):
            slope3[at((i * 2 + block) * big.out_area, big.out_area)] = value

        even_cells(field, key_base + i * big.area, big, wide_stage, dense_stage, put)

    def key_side(i, start):
        cells = [slope3[at((i * 2 + block) * big.out_area, big.out_area)] for block in range(2)]
        value = dot(jnp.concatenate(cells, axis=1), wk[3][...])
        for block in range(BLOCKS):
            wide[at(start + block * big.out_area, big.out_area)] = value[:, block * 128 : (block + 1) * 128]

    def key_third(m, c, start):
        value = dot(thin[at(m * outs + c * big.out_area, big.out_area)], wk[2][...])
        for block in range(BLOCKS):
            wide[at(start + block * big.out_area, big.out_area)] = value[:, block * 128 : (block + 1) * 128]

    def key_a(m, c):
        start = m * first_row + c * big.area
        wide[at(start, big.area)] = dot(field[at(key_base + (2 * m + c) * big.area, big.area)], wk[0][...])
        put_moments(m, 0, c * 2, start, big.area, 112)
        start = m * first_row + spare
        key_side(2 * m + c, start)
        for block in range(BLOCKS):
            put_moments(m, 0, 8 + (c * BLOCKS + block) * 2, start + block * big.out_area, big.out_area, 112)

    def key_b(m, c):
        scale, bias = affine(combined(m, 0, c * 2, (1 - c) * 2, area), 0)

        def rows_of(y):
            for k in range(4):
                row = y * 4 + k
                v = wide[at(m * first_row + c * big.area + row * 2 * SIDE, 2 * SIDE)] * scale + bias
                split_planes(gelu_only(v), stage_of[0], planes_of[0], big, c, row, k % 2)

        repeat(0, big.half // 4, rows_of)
        value = dot(patches(planes_of[0], big, c, 1), wk[1][...])
        start = m * first_row + spare + c * big.out_area
        for k in range(big.half):
            wide[pl.ds(start + k * big.half, big.half)] = value[k * big.wide : k * big.wide + big.half]
        put_moments(m, 1, c * 2, start, big.out_area, 112)

    def key_c(m, c):
        scale, bias = affine(combined(m, 1, c * 2, (1 - c) * 2, out_area), CMID)
        for k in range(big.out_area // 112):
            v = wide[at(m * first_row + spare + c * big.out_area + k * 112, 112)] * scale + bias
            thin[at(m * outs + c * big.out_area + k * 112, 112)] = gelu_only(v).astype(bf16)
        start = m * first_row + c * BLOCKS * big.out_area
        key_third(m, c, start)
        for block in range(BLOCKS):
            put_moments(m, 2, (c * BLOCKS + block) * 2, start + block * big.out_area, big.out_area, 112)

    def key_d(m, c):
        start = m * first_row + c * BLOCKS * big.out_area
        side = m * first_row + spare
        key_side(2 * m + c, side)
        parts = []
        for block in range(BLOCKS):
            lanes = 2 * CMID + block * 128
            row, other = (c * BLOCKS + block) * 2, ((1 - c) * BLOCKS + block) * 2
            scale3, bias3 = affine(combined(m, 2, row, other, out_area), lanes)
            scale4, bias4 = affine(combined(m, 0, 8 + row, 8 + other, out_area), lanes + COUT)
            bias = bias3 + bias4
            e = jnp.zeros((8, 128), f32)
            for k in range(big.out_area // 112):
                x3 = wide[at(start + block * big.out_area + k * 112, 112)]
                x4 = wide[at(side + block * big.out_area + k * 112, 112)]
                e += folded(gelu_only(x3 * scale3 + x4 * scale4 + bias))
            parts.append(e.sum(0, keepdims=True) / out_area)
        length = sum(jnp.sum(part * part, axis=1, keepdims=True) for part in parts)
        inverse = lax.rsqrt(length + UNIT_EPS)
        for block in range(BLOCKS):
            r.embed[pl.ds(m * 8 + c * BLOCKS + block, 1)] = parts[block] * inverse

    def key_copy(m, k):
        mine = keys.at[pl.ds(pl.multiple_of((m * devices + me) * 8, 8), 8)]
        return remote(
            r.embed.at[pl.ds(m * 8, 8)], mine, r.key_send.at[m, k], r.key_recv.at[m, k], place(lax.rem(me + k, devices)))

    def share_start(m):
        keys[at((m * devices + me) * 8, 8, 8)] = r.embed[m * 8 : (m + 1) * 8]
        repeat(1, devices, lambda k: key_copy(m, k).start())

    def share_end(m):
        repeat(1, devices, lambda k: key_copy(m, k).wait())

    def core_copy(job):
        return remote(r.parts[job].at[1 - core], r.arrived[job], r.core_send.at[job], r.core_recv.at[job], partner(1))

    def row_copy(job, target, source):
        return remote(
            r.outward[job].at[target], r.inward[job].at[source], r.row_send.at[job, target], r.row_recv.at[job, source],
            (target, core))

    def job_send(job):
        core_copy(job).wait()

        for k in range(1, chips):
            target = lax.rem(chip + k, chips)
            value = r.parts[job][core, target] + r.arrived[job][target]
            r.outward[job][target] = value.astype(r.outward[job].dtype)
            row_copy(job, target, chip).start()

    def job_end(job):
        total = r.parts[job][core, chip] + r.arrived[job][chip]
        for k in range(1, chips):
            row_copy(job, chip, lax.rem(chip + k, chips)).wait_recv()
        for k in range(1, chips):
            total += r.inward[job][lax.rem(chip + k, chips)].astype(f32)
        start = sum(JOB_ROWS[:job])
        r.packed[start : start + JOB_ROWS[job]] = total
        for k in range(1, chips):
            row_copy(job, lax.rem(chip + k, chips), chip).wait_send()

    def fill_head():
        part, third, fourth = r.parts[0], grads[2], grads[3]

        def turn(i):
            for block in range(BLOCKS):
                half, row = block // 2, block % 2
                lanes = slice(block * 128, (block + 1) * 128)
                part[half, i, row * 8 : row * 8 + 8] = third[at(i * 8, 8, 8), lanes]
                part[half, i, 16 + row * 16 : 32 + row * 16] = fourth[at(i * 16, 16), lanes]

        for i in range(chips):
            turn(i)
        core_copy(0).start()

    def fill_spatial():
        part = r.parts[1]
        for tile in range(9):
            lanes = slice(tile * 128, (tile + 1) * 128)
            gy2[lanes] = grads[1][:, lanes].T
        filler = jnp.zeros((8, 128), f32)

        def turn(i):
            top = gy2[at(i * 72, 40, 8)]
            bottom = jnp.concatenate([gy2[at(i * 72 + 40, 32, 8)], filler], axis=0)
            for half in range(2):
                part[half, i, 0:40] = side_by_side(top, bottom, half)
                part[half, i, 40:48] = filler

        for i in range(chips):
            turn(i)
        core_copy(1).start()

    def fill_sums():
        part = r.parts[2]
        column = lax.broadcasted_iota(jnp.int32, (1, 128), 1)
        filler = jnp.zeros((1, 128), f32)
        rows = [gain_sum[:, k * 128 : (k + 1) * 128] for k in range(10)]
        rows += [jnp.where(column == 0, loss_sum[...], 0.0), filler]
        rows += [shift_sum[:, k * 128 : (k + 1) * 128] for k in range(10)] + [filler, filler]
        rows = jnp.concatenate(rows, axis=0)

        def turn(i):
            for half in range(2):
                part[half, i] = rows

        for i in range(chips):
            turn(i)
        core_copy(2).start()

    def fill_reduce():
        part = r.parts[3]
        for tile in range(2):
            lanes = slice(tile * 128, (tile + 1) * 128)
            gy2[lanes] = grads[0][:, lanes].T

        def turn(i):
            for half in range(2):
                part[half, i] = side_by_side(gy2[at(i * 16, 8, 8)], gy2[at(i * 16 + 8, 8, 8)], half)

        for i in range(chips):
            turn(i)
        core_copy(3).start()

    for load in query_loads(0) + key_loads:
        load.start()
    barrier = pltpu.get_barrier_semaphore()
    repeat(1, devices, lambda k: pl.semaphore_signal(
        barrier, inc=1, device_id=place(lax.rem(me + k, devices)), device_id_type=MESH))
    if own:
        current = [r.r0[...], r.s0[...], r.e0[...], r.p0[...]]
        lagged = [r.r1[...], r.s1[...], r.e1[...], r.p1[...]]
        packed_shards([MOMENTUM * old + (1.0 - MOMENTUM) * new for old, new in zip(lagged, current)], r.sent, 0)
        packed_shards(current, r.sent, 1)
        for which in range(2):
            r.gathered[which, core, xy, z] = r.sent[which]
    else:
        for shard, w in zip((r.r0, r.s0, r.e0, r.p0, r.r1, r.s1, r.e1, r.p1), wq + wk):
            w[...] = shard[...]
    if devices > 1:
        pl.semaphore_wait(barrier, devices - 1)
    if own:
        gather_start(0, 0)
    for ref in list(planes_of.values()) + list(back_of.values()) + list(stage_of.values()) + grads + [
        r.raised, gain_sum, shift_sum, loss_sum, gy2] + [pair[0] for pair in moved]:
        ref[...] = jnp.zeros_like(ref)
    if own:
        gather_end(0, 0)
        gather_start(0, 1)
        gather_start(1, 0)

    def micro_step(m):
        opening, closing = m == 0, m == micros - 1
        base = m * field_rows
        w1, w2, w3, w4 = wq
        w1t, w3t, w4t, wt0, wt1 = (r.w1t, r.w3t, r.w4t, r.wt0, r.wt1)
        alive_count = sum(counts[m, i] for i in range(images)).astype(f32)
        count1 = images * big.area + small.area * alive_count
        count2 = images * big.out_area + small.out_area * alive_count

        def living(kind, crop):
            if kind is big:
                return jnp.float32(1.0)
            return jnp.where(lax.rem(crop, slots) < counts[m, lax.div(crop, slots)], 1.0, 0.0)

        def step_of(kind):
            return 112 if kind is big else 144

        def over_big(body, *hooks):
            def turn(c):
                body(big, c, 1)
                for k, (when, hook) in enumerate(hooks):

                    @pl.when(jnp.logical_and(when, c == k))
                    def _():
                        hook()

            repeat(0, big.count, turn)

        def over_small(body):
            body(small, 0, small.count)

        def add_moments(ref, offset, kind, first, count, row0, size, row, where, opener):
            start = offset + row0 + first * size
            if kind is big:

                @pl.when(first == 0)
                def _():
                    vec[row : row + 1] = folded(ref[at(start, opener, 8)]).sum(0, keepdims=True) / opener

            for c in range(count):
                total, square = moments(ref, start + c * size, size, step_of(kind), vec[row : row + 1])
                alive = living(kind, first + c)
                sums[where] += total * alive
                sums[where + 1] += square * alive

        for load in query_loads(m):
            load.wait()

        def even_batch(kind, first, count):
            for c in range(count):
                start = kind.out_row + (first + c) * kind.out_area

                def put(block, value):
                    even[at(start, kind.out_area), block * 128 : (block + 1) * 128] = value

                even_cells(field, base + kind.row + (first + c) * kind.area, kind, wide_stage, dense_stage, put)

        over_big(even_batch)
        over_small(even_batch)

        @pl.when(opening)
        def _():
            for load in key_loads:
                load.wait()
            repeat(0, 2 * micros, key_even)
            if own:
                gather_end(0, 1)
                gather_start(0, 2)
                gather_end(1, 0)
                gather_start(1, 1)
                gather_end(0, 2)
                unpacked(r.gathered, 0, chips, wk, gy2)
            repeat(0, 2, lambda c: key_a(0, c))
            exchange_start(0, 0)
            if own:
                gather_end(1, 1)
                gather_start(1, 2)
            repeat(0, 2, lambda c: key_a(1, c))
            exchange_start(1, 0)
            for load in query_loads(1):
                load.start()
            if own:
                gather_end(1, 2)
                unpacked(r.gathered, 1, chips, wq, gy2)
            w1t[...] = w1[...].T
            w3t[...] = w3[...].T
            w4t[...] = w4[...].T
            wt0[...] = jnp.zeros_like(wt0)
            wt1[...] = jnp.zeros_like(wt1)

            def tap(ky, kx):
                start = (3 * ky + kx) * CMID
                return w2[start : start + CMID, :].T

            wt0[0:128, 0:128] = tap(1, 1)
            wt0[0:128, 128:256] = tap(1, 2)
            wt0[128:256, 128:256] = tap(1, 0)
            wt1[0:128, 0:128] = tap(2, 1)
            wt1[0:128, 128:256] = tap(2, 2)
            wt1[128:256, 128:256] = tap(2, 0)
            wt1[256:384, 0:128] = tap(0, 1)
            wt1[256:384, 128:256] = tap(0, 2)
            wt1[384:512, 128:256] = tap(0, 0)

        sums[...] = jnp.zeros_like(sums)

        def reduce_batch(kind, first, count):
            start = kind.row + first * kind.area
            size = count * kind.area
            a1[at(start, size)] = dot(field[at(base + start, size)], w1[...])
            add_moments(a1, 0, kind, first, count, kind.row, kind.area, 0, 0, 784)

        over_big(reduce_batch, (opening, lambda: exchange_next(0, 0)), (opening, lambda: exchange_next(1, 0)))
        over_small(reduce_batch)
        mean1, root1 = closed(sums[0], sums[1], vec[0:1], count1)
        scale1 = root1 * line(gains, 0)
        bias1 = line(shifts, 0) - mean1 * scale1
        vec[1:2], vec[2:3], vec[3:4], vec[4:5] = mean1, root1, scale1, bias1

        @pl.when(opening)
        def _():
            for k in range(2):
                exchange_end(k, 0)
                repeat(0, 2, lambda c: key_b(k, c))
                exchange_start(k, 1)

        sums[...] = jnp.zeros_like(sums)

        def hidden_batch(kind, first, count):
            scale, bias = vec[3:4], vec[4:5]
            for c in range(count):
                for k in range(kind.half):
                    start = kind.row + (first + c) * kind.area + k * 2 * kind.side
                    v = a1[at(start, 2 * kind.side)] * scale + bias
                    hidden, slope = gelu_pair(v)
                    slope1[at(start, 2 * kind.side)] = slope.astype(bf16)
                    split_planes(hidden, stage_of[kind.ahead], planes_of[kind.ahead], kind, first + c, k, k % 2)

        over_big(hidden_batch, (opening, lambda: exchange_next(0, 1)), (opening, lambda: exchange_next(1, 1)))
        over_small(hidden_batch)

        @pl.when(opening)
        def _():
            for k in range(2):
                exchange_end(k, 1)
                repeat(0, 2, lambda c: key_c(k, c))
                exchange_start(k, 2)

        def spatial_batch(kind, first, count):
            half, lanes = kind.half, kind.wide
            value = dot(patches(planes_of[kind.ahead], kind, first, count), w2[...])
            start = kind.out_row + first * kind.out_area
            for k in range(count * half):
                a2[pl.ds(start + k * half, half)] = value[k * lanes : k * lanes + half]
            add_moments(a2, 0, kind, first, count, kind.out_row, kind.out_area, 0, 16, 784)

        over_big(spatial_batch, (opening, lambda: exchange_next(0, 2)), (opening, lambda: exchange_next(1, 2)))
        over_small(spatial_batch)
        mean2, root2 = closed(sums[16], sums[17], vec[0:1], count2)
        scale2 = root2 * line(gains, CMID)
        bias2 = line(shifts, CMID) - mean2 * scale2
        vec[5:6], vec[6:7], vec[7:8], vec[8:9] = mean2, root2, scale2, bias2

        @pl.when(opening)
        def _():
            for k in range(2):
                exchange_end(k, 2)
                repeat(0, 2, lambda c: key_d(k, c))
                share_start(k)

        def head_product(which, source, weight, kind, first, count):
            start = kind.out_row + first * kind.out_area
            size = count * kind.out_area
            value = dot(source, weight[...])
            for block in range(BLOCKS):
                offset = (which * BLOCKS + block) * outs
                wide[at(offset + start, size)] = value[:, block * 128 : (block + 1) * 128]
            for block in range(BLOCKS):
                offset = (which * BLOCKS + block) * outs
                add_moments(
                    wide, offset, kind, first, count, kind.out_row, kind.out_area,
                    16 + which * 4 + block, which * 8 + block * 2, 784)

        def expand_batch(kind, first, count):
            start = kind.out_row + first * kind.out_area
            size, step = count * kind.out_area, step_of(kind)
            scale, bias = vec[7:8], vec[8:9]
            head_product(1, even[at(start, size)], w4, kind, first, count)
            for k in range(size // step):
                hidden, slope = gelu_pair(a2[at(start + k * step, step)] * scale + bias)
                thin[at(H2 + start + k * step, step)] = hidden.astype(bf16)
                thin[at(SLOPE2 + start + k * step, step)] = slope.astype(bf16)
            head_product(0, thin[at(H2 + start, size)], w3, kind, first, count)

        over_big(expand_batch)
        over_small(expand_batch)
        for which in range(2):
            for block in range(BLOCKS):
                row = which * 4 + block
                where = which * 8 + block * 2
                lanes = 2 * CMID + row * 128
                mean, root = closed(sums[where], sums[where + 1], vec[16 + row : 17 + row], count2)
                scale = root * line(gains, lanes)
                bias = line(shifts, lanes) - mean * scale
                vec[24 + row : 25 + row], vec[32 + row : 33 + row] = mean, root
                vec[40 + row : 41 + row] = scale
                if which == 0:
                    vec[48 + block : 49 + block] = bias
                else:
                    vec[48 + block : 49 + block] += bias

        rows_e, rows_c = r.rows_e, r.rows_c

        def embed_batch(kind, first, count):
            step = step_of(kind)
            for c in range(count):
                start = kind.out_row + (first + c) * kind.out_area
                for block in range(BLOCKS):
                    mean3, mean4 = vec[24 + block : 25 + block], vec[28 + block : 29 + block]
                    scale3, scale4 = vec[40 + block : 41 + block], vec[44 + block : 45 + block]
                    bias = vec[48 + block : 49 + block]
                    zero = jnp.zeros((8, 128), f32)
                    e, s0, s3, s4 = zero, zero, zero, zero
                    for k in range(kind.out_area // step):
                        inside = block * outs + start + k * step
                        x3, x4 = wide[at(A3 + inside, step)], wide[at(AP + inside, step)]
                        value, slope = gelu_pair(x3 * scale3 + x4 * scale4 + bias)
                        slope3[at(inside, step)] = slope.astype(bf16)
                        e += folded(value)
                        s0 += folded(slope)
                        s3 += folded(slope * (x3 - mean3))
                        s4 += folded(slope * (x4 - mean4))
                    row = kind.ahead + first + c
                    for which, value in enumerate((e / kind.out_area, s0, s3, s4)):
                        rows_e[which, block, pl.ds(row, 1)] = value.sum(0, keepdims=True)

        over_big(embed_batch)
        over_small(embed_batch)

        share_end(m)

        def joined(which):
            return jnp.concatenate([rows_e[which, block] for block in range(BLOCKS)], axis=1)

        e = joined(0)
        inverse = lax.rsqrt(jnp.sum(e * e, axis=-1, keepdims=True) + UNIT_EPS)
        row = lax.broadcasted_iota(jnp.int32, (crops, 1), 0)
        owner = jnp.zeros((crops, 1), jnp.int32)
        live = jnp.where(row < images, 1.0, 0.0)
        for i in range(images):
            owner = jnp.where(row == i, i, owner)
            for slot in range(slots):
                here = row == images + i * slots + slot
                owner = jnp.where(here, i, owner)
                live = jnp.where(here, jnp.where(slot < counts[m, i], 1.0, 0.0), live)
        key_rows = [
            jnp.concatenate(
                [keys[pl.ds(m * devices * 8 + c * BLOCKS + block, devices, stride=8)] for c in range(images)], axis=0)
            for block in range(BLOCKS)
        ]
        key_high, key_low = two_parts(jnp.concatenate(key_rows, axis=1))
        logits = lax.dot_general(
            jnp.concatenate(two_parts(e * inverse), axis=0), jnp.concatenate([key_high, key_low], axis=0),
            (((1,), (1,)), ((), ())), preferred_element_type=f32)
        count = devices * images
        logits = logits[0:crops] + logits[crops:]
        logits = (logits[:, 0:count] + logits[:, count:]) / TEMP
        top = jnp.max(logits, axis=-1, keepdims=True)
        powers = jnp.exp(logits - top)
        total = jnp.sum(powers, axis=-1, keepdims=True)
        column = lax.broadcasted_iota(jnp.int32, logits.shape, 1)
        mine = column == owner * devices + me
        chosen = jnp.sum(jnp.where(mine, logits, 0.0), axis=-1, keepdims=True)
        ce = (top + jnp.log(total) - chosen) * live
        loss_sum[...] += jnp.sum(ce, axis=0, keepdims=True)
        toward = (powers / total - jnp.where(mine, 1.0, 0.0)) * (live / TEMP)
        back = dot(jnp.concatenate(two_parts(toward), axis=0), jnp.concatenate([key_high, key_low], axis=1))
        back = back[0:crops] + back[crops:]
        back = back[:, 0:COUT] + back[:, COUT:]
        de = inverse * back - e * (inverse * inverse * inverse * jnp.sum(e * back, axis=-1, keepdims=True))
        de = de * jnp.where(row < images, 1.0 / big.out_area, 1.0 / small.out_area)
        sum0 = jnp.sum(de * joined(1), axis=0, keepdims=True)
        for which in range(2):
            reach = jnp.sum(de * joined(2 + which), axis=0, keepdims=True)
            for block in range(BLOCKS):
                row = which * 4 + block
                here = slice(block * 128, (block + 1) * 128)
                lanes = slice(2 * CMID + row * 128, 2 * CMID + (row + 1) * 128)
                mean, root, scale = vec[24 + row : 25 + row], vec[32 + row : 33 + row], vec[40 + row : 41 + row]
                along = reach[:, here] * root
                gain_sum[:, lanes] += along
                shift_sum[:, lanes] += sum0[:, here]
                tilt = scale * root * along / count2
                vec[52 + row : 53 + row] = tilt
                vec[60 + row : 61 + row] = scale * sum0[:, here] / count2 - tilt * mean
                rows_c[which, block] = de[:, here] * scale

        sums[...] = jnp.zeros_like(sums)
        d3, dp = r.d3, r.dp

        def head_back(kind, first, count):
            start = kind.out_row + first * kind.out_area
            size, step = count * kind.out_area, step_of(kind)
            for which, store in ((0, d3), (1, dp)):
                for block in range(BLOCKS):
                    lanes = slice(block * 128, (block + 1) * 128)
                    where = which * 4 + block
                    for c in range(count):
                        rise = rows_c[which, block, pl.ds(kind.ahead + first + c, 1)]
                        alive = living(kind, first + c)
                        tilt, level = vec[52 + where : 53 + where] * alive, vec[60 + where : 61 + where] * alive
                        for k in range(kind.out_area // step):
                            inside = c * kind.out_area + k * step
                            here = block * outs + start + inside
                            x = wide[at(which * BLOCKS * outs + here, step)]
                            grad = slope3[at(here, step)].astype(f32) * rise - (x * tilt + level)
                            store[inside : inside + step, lanes] = grad.astype(bf16)
            grad3, gradp = d3[0:size], dp[0:size]
            gy2[at(start, size)] = dot(grad3, w3t[...])
            gradient = dot(gradp, w4t[...])
            for block in range(2):
                wide[at(AP + block * outs + start, size)] = gradient[:, block * 128 : (block + 1) * 128]
            grads[2][...] += dot_rows(thin[at(H2 + start, size)], grad3)
            grads[3][...] += dot_rows(even[at(start, size)], gradp)
            mean = vec[5:6]
            level, reach = jnp.zeros((8, 128), f32), jnp.zeros((8, 128), f32)
            for k in range(size // step):
                here = at(start + k * step, step)
                gy = gy2[here] * thin[at(SLOPE2 + start + k * step, step)].astype(f32)
                gy2[here] = gy
                level += folded(gy)
                reach += folded(gy * (a2[here] - mean))
            sums[0] += level
            sums[1] += reach

        over_big(head_back)
        over_small(head_back)

        if own:

            @pl.when(closing)
            def _():
                fill_head()

        def norm_back(where, lanes, count):
            mean, root, scale = vec[where : where + 1], vec[where + 1 : where + 2], vec[where + 2 : where + 3]
            level = sums[0].sum(0, keepdims=True)
            along = sums[1].sum(0, keepdims=True) * root
            gain_sum[:, lanes] += along
            shift_sum[:, lanes] += level
            tilt = scale * root * along / count
            vec[68:69] = scale
            vec[69:70] = tilt
            vec[70:71] = scale * level / count - tilt * mean

        norm_back(5, slice(CMID, 2 * CMID), count2)
        sums[...] = jnp.zeros_like(sums)

        def spatial_back(kind, first, count):
            half, lanes, side, step = kind.half, kind.wide, kind.side, step_of(kind)
            out_start = kind.out_row + first * kind.out_area
            for c in range(count):
                alive = living(kind, first + c)
                tilt, level = vec[69:70] * alive, vec[70:71] * alive
                for k in range(kind.out_area // step):
                    here = at(out_start + c * kind.out_area + k * step, step)
                    gy2[here] = gy2[here] * vec[68:69] - (a2[here] * tilt + level)
            column = lax.broadcasted_iota(jnp.int32, (lanes, 128), 0)
            store = back_of[kind.ahead]
            for k in range(count * half):
                here = jnp.where(column < half, gy2[pl.ds(out_start + k * half, lanes)], 0.0)
                following = jnp.where(column < half - 1, gy2[pl.ds(out_start + k * half + 1, lanes)], 0.0)
                store[first + k // half, k % half, :, 0:128] = here.astype(bf16)
                store[first + k // half, k % half, :, 128:256] = following.astype(bf16)
            size = count * half * lanes
            near = store[pl.ds(first, count), 0:half].reshape(size, 256)
            beyond = store[pl.ds(first, count), 1 : half + 1].reshape(size, 256)
            upper_rows = dot(near, wt0[...])
            lower_rows = dot(jnp.concatenate([near, beyond], axis=1), wt1[...])
            start = kind.row + first * kind.area
            for k in range(count * half):
                here = slice(k * lanes, k * lanes + half)
                row = start + k * 2 * side
                for odd, value in ((0, upper_rows), (1, lower_rows)):
                    wide[pl.ds(row + odd * side, half, stride=2)] = value[here, 0:128]
                    wide[pl.ds(row + odd * side + 1, half, stride=2)] = value[here, 128:256]
            grads[1][...] += dot_rows(near[:, 0:128], patches(planes_of[kind.ahead], kind, first, count))
            mean = vec[1:2]
            level, reach = jnp.zeros((8, 128), f32), jnp.zeros((8, 128), f32)
            for k in range(count * kind.area // step):
                here = at(start + k * step, step)
                gy = wide[here] * slope1[here].astype(f32)
                wide[here] = gy
                level += folded(gy)
                reach += folded(gy * (a1[here] - mean))
            sums[0] += level
            sums[1] += reach

        def job_hooks(*jobs):
            def sends(some):
                return lambda: [job_send(job) for job in some]

            return [(closing, sends(some)) for some in jobs] if own else []

        over_big(spatial_back, *job_hooks((0,)))
        over_small(spatial_back)
        norm_back(1, slice(0, CMID), count1)

        if own:

            @pl.when(closing)
            def _():
                fill_spatial()
                fill_sums()

        def reduce_back(kind, first, count):
            step = step_of(kind)
            size = count * kind.area
            start = kind.row + first * kind.area
            rise = vec[68:69]
            for c in range(count):
                alive = living(kind, first + c)
                tilt, level = vec[69:70] * alive, vec[70:71] * alive
                for k in range(kind.area // step):
                    here = at(start + c * kind.area + k * step, step)
                    grad = wide[here] * rise - (a1[here] * tilt + level)
                    slope1[here] = grad.astype(bf16)
            grads[0][...] += dot_rows(slope1[at(start, size)], field[at(base + start, size)])

        over_big(reduce_back, *job_hooks((1,), (2,)))
        over_small(reduce_back)

        if own:

            @pl.when(closing)
            def _():
                fill_reduce()
                job_end(0)

        raised = r.raised

        def field_back(kind, first, count):
            half, side = kind.half, kind.side
            size = count * kind.area
            start = kind.row + first * kind.area
            whole = dot(slope1[at(start, size)], w1t[...])
            out_start = kind.out_row + first * kind.out_area
            for k in range(count * half):
                row = k * 2 * side
                for block in range(2):
                    lanes = slice(block * 128, (block + 1) * 128)
                    slot = k % 4 * 2 + block
                    raised[slot, pl.ds(0, half, stride=2)] = wide[pl.ds(AP + block * outs + out_start + k * half, half)]
                    top_row = whole[row : row + side, lanes] + raised[slot, 0:side]
                    both = jnp.concatenate([top_row, whole[row + side : row + 2 * side, lanes]], axis=0)
                    field[at(base + start + row, 2 * side), lanes] = both.astype(bf16)
            if kind is big:
                store_big(m, first).start()
            else:
                store_small(m).start()

        over_big(field_back, *job_hooks((), (3,)))
        over_small(field_back)

    repeat(0, micros, micro_step)
    if own:
        for job in range(1, 4):
            job_end(job)
    for m in range(micros):
        for c in range(images):
            store_big(m, c).wait()
        store_small(m).wait()


def step_pass(axes, own, slots, big, small, key, counts, mask, current, lagged, vectors):
    chips, cores = axes
    devices = chips * cores
    widths = stage_widths(devices)
    micros, images = counts.shape
    one, two = field_pair(images, slots)
    rows = two.row + two.count * two.area
    outs = two.out_row + two.count * two.out_area
    crops = images * (1 + slots)
    vmem = pl.BlockSpec(memory_space=pltpu.VMEM)
    smem = pl.BlockSpec(memory_space=pltpu.SMEM)
    hbm = pl.BlockSpec(memory_space=pl.ANY)
    weights = [(CIN, CMID), (9 * CMID, CMID), (CMID, COUT), (CIN, COUT)]
    totals = dict(
        g1=(CMID, CIN), g2=(CMID, 9 * CMID), g3=(CMID, COUT), g4=(CIN, COUT),
        gain_sum=(1, NORMS), shift_sum=(1, NORMS), loss_sum=(1, 1))
    r0, s0, e0, p0 = ((w, vmem) for w in current)
    r1, s1, e1, p1 = ((w, vmem) for w in lagged)
    gains, shifts, gains1, shifts1 = ((v, vmem) for v in vectors)
    inputs = dict(
        big_hbm=(big, hbm), small_hbm=(small, hbm), key_hbm=(key, hbm), counts=(counts, smem), mask=(mask, smem),
        r0=r0, s0=s0, e0=e0, p0=p0, r1=r1, s1=s1, e1=e1, p1=p1, gains=gains, shifts=shifts, gains1=gains1, shifts1=shifts1)
    outputs = dict(
        big_out=(jax.ShapeDtypeStruct(big.shape, bf16), hbm), small_out=(jax.ShapeDtypeStruct(small.shape, bf16), hbm))
    if own:
        outputs |= dict(packed=(jax.ShapeDtypeStruct((sum(JOB_ROWS), 128), f32), vmem))
    else:
        outputs |= {n: (jax.ShapeDtypeStruct(shape, f32), vmem) for n, shape in totals.items()}

    def buf(dtype, *shape):
        return pltpu.VMEM(shape, dtype)

    def dma(*shape):
        return pltpu.SemaphoreType.DMA(shape)

    scratch = dict(
        field=buf(bf16, rows + 2 * micros * one.area, CIN),
        a1=buf(f32, rows, 128), slope1=buf(bf16, rows, 128),
        planes_big=buf(bf16, 2, one.count, one.half + 1, one.wide, 384),
        planes_small=buf(bf16, 2, two.count, two.half + 1, two.wide, 384),
        a2=buf(f32, outs, 128), thin=buf(bf16, 2 * outs, 128), even=buf(bf16, outs, CIN),
        wide=buf(f32, 2 * BLOCKS * outs, 128), slope3=buf(bf16, BLOCKS * outs, 128),
        back_big=buf(bf16, one.count, one.half + 1, one.wide, 256),
        back_small=buf(bf16, two.count, two.half + 1, two.wide, 256),
        gy2=buf(f32, outs + 16, 128), stage_big=buf(f32, 2, 2, 80, 128), stage_small=buf(f32, 2, 2, 48, 128),
        wide_stage=buf(f32, 8, SIDE, 128), dense_stage=buf(f32, 2, one.out_area, 128), raised=buf(f32, 8, SIDE, 128),
        d3=buf(bf16, two.count * two.out_area, COUT), dp=buf(bf16, two.count * two.out_area, COUT),
        w1t=buf(bf16, CMID, CIN), w3t=buf(bf16, COUT, CMID), w4t=buf(bf16, COUT, CIN),
        wt0=buf(bf16, 256, 256), wt1=buf(bf16, 512, 256), sums=buf(f32, 18, 8, 128), vec=buf(f32, 80, 128),
        rows_e=buf(f32, 4, BLOCKS, crops, 128), rows_c=buf(f32, 2, BLOCKS, crops, 128),
        keys=buf(f32, devices * 16, 128), embed=buf(f32, 16, 128),
        moved=[[buf(f32, 1 << width, n, 128) for width in widths] for _ in range(micros) for n in TURN_ROWS],
        key_load=dma(2 * micros), query_load=dma(micros, 2), store=dma(micros, images + 1),
        move_send=dma(3 * micros, 2, 1 << widths[0]), move_recv=dma(3 * micros, 2, 1 << widths[0]),
        key_send=dma(micros, devices), key_recv=dma(micros, devices),
    )
    first, second, third, fourth = (buf(bf16, *shape) for shape in weights)
    scratch |= dict(w1q=first, w2q=second, w3q=third, w4q=fourth, w1k=first, w2k=second, w3k=third, w4k=fourth)
    wires = (bf16, bf16, f32, f32)
    if own:
        scratch |= {n: buf(f32, *shape) for n, shape in totals.items()}
        scratch |= dict(
            sent=buf(bf16, 2, PACK, 128), gathered=buf(bf16, 2, 2, 4, 4, PACK, 128),
            parts=[buf(f32, 2, chips, n, 128) for n in JOB_ROWS], arrived=[buf(f32, chips, n, 128) for n in JOB_ROWS],
            outward=[buf(t, chips, n, 128) for n, t in zip(JOB_ROWS, wires)],
            inward=[buf(t, chips, n, 128) for n, t in zip(JOB_ROWS, wires)],
            gather_send=dma(2, 3, 3), gather_recv=dma(2, 3, 3), core_send=dma(4), core_recv=dma(4),
            row_send=dma(4, chips), row_recv=dma(4, chips),
        )
    names = list(inputs) + list(outputs) + list(scratch)
    out = pl.pallas_call(
        functools.partial(step_kernel, axes, own, slots, names),
        out_shape=[shape for shape, _ in outputs.values()],
        in_specs=[spec for _, spec in inputs.values()],
        out_specs=[spec for _, spec in outputs.values()],
        scratch_shapes=list(scratch.values()),
        compiler_params=pltpu.CompilerParams(vmem_limit_bytes=63 * 2**20, collective_id=0, has_side_effects=True),
        name="step",
    )(*[array for array, _ in inputs.values()])
    return types.SimpleNamespace(**dict(zip(outputs, out)))


def finish_kernel(packed, loss, reduce_out, spatial_out, expand_out, shortcut_out, gains, shifts):
    reduce_out[0:8] = packed[120:128, 0:64]
    reduce_out[8:16] = packed[120:128, 64:128]
    rows = jnp.concatenate([packed[48:88], jnp.zeros((88, 128), f32)], axis=0).T
    spatial_out[...] = jnp.concatenate([rows[0:64, 0:40], rows[64:128, 0:32]], axis=1)
    for block in range(2):
        lanes = slice(block * 128, (block + 1) * 128)
        expand_out[:, lanes] = packed[block * 8 : block * 8 + 8]
        shortcut_out[:, lanes] = packed[16 + block * 16 : 32 + block * 16]
    for row in range(NORMS // 128):
        gains[pl.ds(row * 128, 128)] = packed[96 + row]
        shifts[pl.ds(row * 128, 128)] = packed[108 + row]
    loss[...] = packed[106:107, 0:1]


def finish_pass(packed):
    vmem = pl.BlockSpec(memory_space=pltpu.VMEM)
    shapes = [(1, 1), (16, 64), (64, 72), (8, 256), (16, 256), (NORMS,), (NORMS,)]
    return pl.pallas_call(
        finish_kernel,
        out_shape=[jax.ShapeDtypeStruct(shape, f32) for shape in shapes],
        in_specs=[vmem],
        out_specs=[vmem] * 7,
        name="finish",
    )(packed)


def gather_weights(shards):
    rows = [lax.all_gather(part, "dp", axis=0, tiled=True) for part in shards]
    return [lax.all_gather(part, "fsdp", axis=1, tiled=True) for part in rows]


def per_device(axes, *args):
    query_global, small_crop_query, small_count, key_global, shuffle_mask = args[:5]
    current, lagged = args[5:9], args[11:15]
    vectors = (args[9], args[10], args[15], args[16])
    micros = query_global.shape[0]
    slots = small_crop_query.shape[2]
    chips, cores = axes
    own = chips == 16 and cores == 2
    if own:
        current = [w.T if i == 1 else w for i, w in enumerate(current)]
        lagged = [w.T if i == 1 else w for i, w in enumerate(lagged)]
    else:
        fresh = [MOMENTUM * old + (1.0 - MOMENTUM) * new for old, new in zip(lagged, current)]
        current = gather_weights([w.astype(bf16) for w in current])
        lagged = gather_weights([w.astype(bf16) for w in fresh])
    out = step_pass(
        axes, own, slots, query_global.reshape(micros, -1, CIN), small_crop_query.reshape(micros, -1, CIN),
        key_global.reshape(micros, -1, CIN), small_count, shuffle_mask, current, lagged, vectors,
    )
    fields = (out.big_out.reshape(query_global.shape), out.small_out.reshape(small_crop_query.shape))
    if own:
        loss, first, second, third, fourth, gains_grad, shifts_grad = finish_pass(out.packed)
        return (loss.reshape(()), *fields, first, second.T, third, fourth, gains_grad, shifts_grad)
    totals = (out.g1.T, out.g2.T, out.g3, out.g4)
    summed = lax.psum_scatter(totals, "dp", scatter_dimension=0, tiled=True)
    owned = lax.psum_scatter(summed, "fsdp", scatter_dimension=1, tiled=True)
    sums = lax.psum((out.loss_sum, out.gain_sum, out.shift_sum), ("dp", "fsdp"))
    return (sums[0].reshape(()), *fields, *owned, sums[1].reshape(NORMS), sums[2].reshape(NORMS))


def solution(mesh):
    whole, split = P(), P("dp", "fsdp")
    images, crops = P(None, ("dp", "fsdp"), None, None, None), P(None, ("dp", "fsdp"), None, None, None, None)
    axes = (mesh.shape["dp"], mesh.shape["fsdp"])
    return jax.shard_map(
        functools.partial(per_device, axes),
        mesh=mesh,
        in_specs=(images, crops, P(None, ("dp", "fsdp")), images, whole)
        + (split,) * 4 + (whole,) * 2 + (split,) * 4 + (whole,) * 2,
        out_specs=(whole, images, crops) + (split,) * 4 + (whole,) * 2,
        check_vma=False,
    )
```

```python
import functools
import types
import jax
import jax.numpy as jnp
from jax import lax
from jax.experimental import pallas as pl
from jax.experimental.pallas import tpu as pltpu
from jax.sharding import PartitionSpec as P

f32, bf16 = jnp.float32, jnp.bfloat16
CIN, CMID, COUT, NORMS = 256, 128, 512, 1280
SIDE, SMALL = 56, 24
BLOCKS = COUT // 128
TEMP, NORM_EPS, UNIT_EPS = 0.2, 1e-05, 1e-06
ROOT_HALF = 0.7071067811865476
DENSITY = 0.3989422804014327


class Field:
    def __init__(self, count, side, row, out_row, ahead):
        self.count, self.side, self.row, self.out_row = count, side, row, out_row
        self.ahead = ahead
        self.half = side // 2
        self.wide = -(-self.half // 16) * 16
        self.area, self.out_area = side * side, (side // 2) ** 2


def field_pair(images, slots):
    big = Field(images, SIDE, 0, 0, 0)
    small = Field(images * slots, SMALL, images * big.area, images * big.out_area, images)
    return big, small


def at(start, size, align=16):
    if isinstance(start, int):
        return pl.ds(start, size)
    return pl.ds(pl.multiple_of(start, align), size)


def folded(x):
    return x.reshape(x.shape[0] // 8, 8, x.shape[1]).sum(0)


def dot(a, b):
    return jnp.dot(a, b, preferred_element_type=f32)


def dot_rows(a, b):
    return lax.dot_general(a, b, (((0,), (0,)), ((), ())), preferred_element_type=f32)


def gelu_pair(v):
    share = 0.5 + 0.5 * lax.erf(v * ROOT_HALF)
    return v * share, share + v * (DENSITY * jnp.exp(v * v * -0.5))


def gelu_only(v):
    return v * (0.5 + 0.5 * lax.erf(v * ROOT_HALF))


MOMENTUM = 0.999
MESH = pl.DeviceIdType.MESH
PACK = 96
QUICK = 2
JOB_ROWS = (48, 48, 24, 8)
TURN_ROWS = (8, 24, 16)


def line(vector, start):
    return vector[pl.ds(start, 128)].reshape(1, 128)


def two_parts(x):
    high = x.astype(bf16)
    return high, (x - high.astype(f32)).astype(bf16)


def moments(ref, start, size, step, pivot):
    total = jnp.zeros((8, 128), f32)
    square = jnp.zeros((8, 128), f32)
    for k in range(size // step):
        x = ref[at(start + k * step, step, 8)] - pivot
        total += folded(x)
        square += folded(x * x)
    return total, square


def closed(total, square, pivot, count):
    off = total.sum(0, keepdims=True) / count
    spread = jnp.maximum(square.sum(0, keepdims=True) / count - off * off, 0.0)
    return pivot + off, lax.rsqrt(spread + NORM_EPS)


def patches(planes, field, first, crops):
    size = crops * field.half * field.wide
    here = pl.ds(first, crops)
    above = planes[1, here, 0 : field.half].reshape(size, 3 * CMID)
    level = planes[0, here, 0 : field.half].reshape(size, 3 * CMID)
    below = planes[1, here, 1 : field.half + 1].reshape(size, 3 * CMID)
    return jnp.concatenate([above, level, below], axis=1)


def split_planes(hidden, stage, planes, field, crop, row, slot):
    side, wide = field.side, field.wide
    for odd in range(2):
        stage[slot, odd, 8 : 8 + side] = hidden[odd * side : (odd + 1) * side]
    for odd in range(2):
        for tap in range(3):
            column = stage[slot, odd, pl.ds(7 + tap, wide, stride=2)]
            planes[odd, crop, row + odd, :, tap * CMID : (tap + 1) * CMID] = column.astype(bf16)


def even_cells(source, base, field, wide_stage, dense_stage, put):
    side, half = field.side, field.half
    for y in range(half):
        for block in range(CIN // 128):
            slot = y % 4 * 2 + block
            x = source[at(base + y * 2 * side, 2 * side), block * 128 : (block + 1) * 128]
            wide_stage[slot, 0:side] = x.astype(f32)[0:side]
            dense_stage[block, y * half : (y + 1) * half] = wide_stage[slot, pl.ds(0, half, stride=2)]
    for block in range(CIN // 128):
        put(block, dense_stage[block, 0 : field.out_area].astype(bf16))


def flipped(index, mask):
    bit = 1
    while bit <= mask:
        if mask & bit:
            index = index + bit * (1 - 2 * lax.rem(lax.div(index, bit), 2))
        bit *= 2
    return index


def side_by_side(top, bottom, core):
    left = lax.broadcasted_iota(jnp.int32, top.shape, 1) < 64
    if core == 0:
        return jnp.where(left, top, pltpu.roll(bottom, 64, 1))
    return jnp.where(left, pltpu.roll(top, 64, 1), bottom)


def packed_shards(shards, store, which):
    first, second, third, fourth = shards
    zero = jnp.zeros
    second = jnp.concatenate([second, zero((second.shape[0], 56), f32)], axis=1)
    second = jnp.concatenate([second, zero((64, 128), f32)], axis=0).T[0:80, 0:64]
    rows = [jnp.concatenate([first[0:8], first[8:16]], axis=1), jnp.concatenate([second[0:40], second[40:80]], axis=1)]
    rows += [third[:, 0:128], third[:, 128:256], fourth[:, 0:128], fourth[:, 128:256]]
    store[which] = jnp.concatenate(rows, axis=0).astype(bf16)


def unpacked(gathered, which, chips, weights, stage):
    w1, w2, w3, w4 = weights

    def turn(i, _):
        z, xy = lax.div(i, 4), lax.rem(i, 4)
        ours = [gathered[which, core, xy, z] for core in range(2)]
        first, second = (rows[0:48].astype(f32) for rows in ours)
        left = lax.broadcasted_iota(jnp.int32, (48, 128), 1) < 64
        top = jnp.where(left, first, pltpu.roll(second, 64, 1))
        bottom = jnp.where(left, pltpu.roll(first, 64, 1), second)
        w1[at(i * 16, 16)] = jnp.concatenate([top[0:8], bottom[0:8]], axis=0).astype(bf16)
        stage[at(i * 72, 40, 8)] = top[8:48]
        stage[at(i * 72 + 40, 32, 8)] = bottom[8:40]
        for block in range(BLOCKS):
            start = 64 + block % 2 * 16
            w4[at(i * 16, 16), block * 128 : (block + 1) * 128] = ours[block // 2][start : start + 16]
        return 0

    lax.fori_loop(0, chips, turn, 0)
    w2[...] = stage[0 : 9 * CMID].astype(bf16)

    def pairs(i, _):
        z, xy = lax.div(i, 2), lax.rem(i, 2) * 2
        for block in range(BLOCKS):
            rows = slice(block % 2 * 8, block % 2 * 8 + 8)
            both = [gathered[which, block // 2, xy + k, z, 48:64].astype(f32)[rows] for k in range(2)]
            w3[at(i * 16, 16), block * 128 : (block + 1) * 128] = jnp.concatenate(both, axis=0).astype(bf16)
        return 0

    lax.fori_loop(0, chips // 2, pairs, 0)


def unpacked_reduce(quick, chips, key_weight, query_weight):
    for i in range(chips):
        first, second = (quick[core, i % 4, i // 4].astype(f32) for core in range(2))
        left = lax.broadcasted_iota(jnp.int32, (16, 128), 1) < 64
        top = jnp.where(left, first, pltpu.roll(second, 64, 1))
        bottom = jnp.where(left, pltpu.roll(first, 64, 1), second)
        for k, weight in enumerate((key_weight, query_weight)):
            rows = slice(k * 8, k * 8 + 8)
            weight[i * 16 : (i + 1) * 16] = jnp.concatenate([top[rows], bottom[rows]], axis=0).astype(bf16)


def stage_widths(devices):
    bits = devices.bit_length() - 1
    return (bits + 1) // 2, bits // 2


def step_kernel(axes, own, slots, names, *refs):
    r = types.SimpleNamespace(**dict(zip(names, refs)))
    chips, cores = axes
    devices = chips * cores
    widths = stage_widths(devices)
    shifts_of = (0, widths[0])
    counts, mask = r.counts, r.mask
    micros, images = counts.shape
    fields = field_pair(images, slots)
    big, small = fields
    crops = images * (1 + slots)
    field_rows = small.row + small.count * small.area
    outs = small.out_row + small.count * small.out_area
    chip, core = lax.axis_index("dp"), lax.axis_index("fsdp")
    me = chip * cores + core
    xy, z = lax.rem(chip, 4), lax.div(chip, 4)
    field, a1, slope1, a2, even, wide, slope3 = (r.field, r.a1, r.slope1, r.a2, r.even, r.wide, r.slope3)
    thin, gy2, vec, sums, keys = (r.thin, r.gy2, r.vec, r.sums, r.keys)
    planes_of = {0: r.planes_big, images: r.planes_small}
    back_of = {0: r.back_big, images: r.back_small}
    stage_of = {0: r.stage_big, images: r.stage_small}
    wide_stage, dense_stage = r.wide_stage, r.dense_stage
    wq = [r.w1q, r.w2q, r.w3q, r.w4q]
    wk = [r.w1k, r.w2k, r.w3k, r.w4k]
    grads = [r.g1, r.g2, r.g3, r.g4]
    gains, shifts, gains1, shifts1 = (r.gains, r.shifts, r.gains1, r.shifts1)
    gain_sum, shift_sum, loss_sum = r.gain_sum, r.shift_sum, r.loss_sum
    A3, AP, H2, SLOPE2 = 0, BLOCKS * outs, 0, outs

    def place(device):
        return (lax.div(device, cores), lax.rem(device, cores))

    def remote(source, target, send, receive, device):
        return pltpu.make_async_remote_copy(
            src_ref=source, dst_ref=target, send_sem=send, recv_sem=receive, device_id=device, device_id_type=MESH)

    def repeat(first, last, body):
        lax.fori_loop(first, last, lambda k, _: (body(k), 0)[1], 0)

    key_base = field_rows
    key_loads = [
        pltpu.make_async_copy(
            r.key_hbm.at[i // 2, pl.ds(i % 2 * big.area, big.area)],
            field.at[pl.ds(key_base + i * big.area, big.area)], r.key_load.at[i])
        for i in range(2 * micros)
    ]

    def query_loads(m):
        return [
            pltpu.make_async_copy(
                r.big_hbm.at[m], field.at[pl.ds(m * field_rows, small.row)], r.query_load.at[m, 0]),
            pltpu.make_async_copy(
                r.small_hbm.at[m], field.at[pl.ds(m * field_rows + small.row, field_rows - small.row)],
                r.query_load.at[m, 1]),
        ]

    def store_big(m, c):
        return pltpu.make_async_copy(
            field.at[pl.ds(m * field_rows + c * big.area, big.area)],
            r.big_out.at[m, pl.ds(c * big.area, big.area)], r.store.at[m, c])

    def store_small(m):
        return pltpu.make_async_copy(
            field.at[pl.ds(m * field_rows + small.row, field_rows - small.row)], r.small_out.at[m],
            r.store.at[m, images])

    def partner(flip):
        return place(flipped(me, flip))

    def gather_copies(which, stage):
        whole = r.quick if which == QUICK else r.gathered.at[which]
        if stage == 0:
            here = whole.at[core, xy, z]
            flips = [8 * k for k in range(1, chips // 4)]
        elif stage == 1:
            here = whole.at[core, xy]
            flips = [2 * k for k in range(1, 4)]
        else:
            here = whole.at[core]
            flips = [1]
        return [
            remote(here, here, r.gather_send.at[which, stage, k], r.gather_recv.at[which, stage, k], partner(flip))
            for k, flip in enumerate(flips)
        ]

    def gather_start(which, stage):
        for copy in gather_copies(which, stage):
            copy.start()

    def gather_end(which, stage):
        for copy in gather_copies(which, stage):
            copy.wait()

    moved = r.moved

    def exchange_copies(m, turn, stage):
        ref, which = moved[m * 3 + turn][stage], m * 3 + turn
        return [
            remote(
                ref.at[0], ref.at[k], r.move_send.at[which, stage, k], r.move_recv.at[which, stage, k],
                partner(k << shifts_of[stage]))
            for k in range(1, 1 << widths[stage])
        ]

    def picked(m, stage):
        return lax.rem(lax.div(jnp.bitwise_xor(mask[m, 0], mask[m, 1]), 1 << shifts_of[stage]), 1 << widths[stage])

    def exchange_start(m, turn):
        for copy in exchange_copies(m, turn, 0):
            copy.start()

    def exchange_next(m, turn):
        for copy in exchange_copies(m, turn, 0):
            copy.wait()
        first, second = moved[m * 3 + turn]
        second[0] = first[picked(m, 0)]
        for copy in exchange_copies(m, turn, 1):
            copy.start()

    def exchange_end(m, turn):
        for copy in exchange_copies(m, turn, 1):
            copy.wait()

    def put_moments(m, turn, row, start, size, step):
        pivot = folded(wide[at(start, step, 8)]).sum(0, keepdims=True) / step
        total, square = moments(wide, start, size, step, pivot)
        off = total.sum(0, keepdims=True) / size
        moved[m * 3 + turn][0][0, pl.ds(row, 1)] = pivot + off
        moved[m * 3 + turn][0][0, pl.ds(row + 1, 1)] = jnp.maximum(square.sum(0, keepdims=True) - off * off * size, 0.0)

    def combined(m, turn, row, other, count):
        pick = picked(m, 1)
        mean, spread = moved[m * 3 + turn][0][0, pl.ds(row, 1)], moved[m * 3 + turn][0][0, pl.ds(row + 1, 1)]
        mean2, spread2 = moved[m * 3 + turn][1][pick, pl.ds(other, 1)], moved[m * 3 + turn][1][pick, pl.ds(other + 1, 1)]
        apart = mean - mean2
        variance = (spread + spread2 + apart * apart * (count * 0.5)) / (2.0 * count)
        return (mean + mean2) * 0.5, lax.rsqrt(variance + NORM_EPS)

    def affine(group, start):
        mean, root = group
        new_gain = MOMENTUM * line(gains1, start) + (1.0 - MOMENTUM) * line(gains, start)
        new_shift = MOMENTUM * line(shifts1, start) + (1.0 - MOMENTUM) * line(shifts, start)
        scale = root * new_gain
        return scale, new_shift - mean * scale

    area, out_area = float(big.area), float(big.out_area)
    first_row = BLOCKS * outs
    spare = 2 * big.area

    def key_even(i):
        def put(block, value):
            slope3[at((i * 2 + block) * big.out_area, big.out_area)] = value

        even_cells(field, key_base + i * big.area, big, wide_stage, dense_stage, put)

    def key_side(i, start):
        cells = [slope3[at((i * 2 + block) * big.out_area, big.out_area)] for block in range(2)]
        value = dot(jnp.concatenate(cells, axis=1), wk[3][...])
        for block in range(BLOCKS):
            wide[at(start + block * big.out_area, big.out_area)] = value[:, block * 128 : (block + 1) * 128]

    def key_third(m, c, start):
        value = dot(thin[at(m * outs + c * big.out_area, big.out_area)], wk[2][...])
        for block in range(BLOCKS):
            wide[at(start + block * big.out_area, big.out_area)] = value[:, block * 128 : (block + 1) * 128]

    def key_a(m, c):
        start = m * first_row + c * big.area
        wide[at(start, big.area)] = dot(field[at(key_base + (2 * m + c) * big.area, big.area)], wk[0][...])
        put_moments(m, 0, c * 2, start, big.area, 112)

    def key_b(m, c):
        scale, bias = affine(combined(m, 0, c * 2, (1 - c) * 2, area), 0)

        def rows_of(y):
            for k in range(4):
                row = y * 4 + k
                v = wide[at(m * first_row + c * big.area + row * 2 * SIDE, 2 * SIDE)] * scale + bias
                split_planes(gelu_only(v), stage_of[0], planes_of[0], big, c, row, k % 2)

        repeat(0, big.half // 4, rows_of)
        value = dot(patches(planes_of[0], big, c, 1), wk[1][...])
        start = m * first_row + spare + c * big.out_area
        for k in range(big.half):
            wide[pl.ds(start + k * big.half, big.half)] = value[k * big.wide : k * big.wide + big.half]
        put_moments(m, 1, c * 2, start, big.out_area, 112)
        start = m * first_row + c * big.area
        key_side(2 * m + c, start)
        for block in range(BLOCKS):
            put_moments(m, 1, 8 + (c * BLOCKS + block) * 2, start + block * big.out_area, big.out_area, 112)

    def key_c(m, c):
        scale, bias = affine(combined(m, 1, c * 2, (1 - c) * 2, out_area), CMID)
        for k in range(big.out_area // 112):
            v = wide[at(m * first_row + spare + c * big.out_area + k * 112, 112)] * scale + bias
            thin[at(m * outs + c * big.out_area + k * 112, 112)] = gelu_only(v).astype(bf16)
        start = m * first_row + c * BLOCKS * big.out_area
        key_third(m, c, start)
        for block in range(BLOCKS):
            put_moments(m, 2, (c * BLOCKS + block) * 2, start + block * big.out_area, big.out_area, 112)

    def key_d(m, c):
        start = m * first_row + c * BLOCKS * big.out_area
        side = m * first_row + spare
        key_side(2 * m + c, side)
        parts = []
        for block in range(BLOCKS):
            lanes = 2 * CMID + block * 128
            row, other = (c * BLOCKS + block) * 2, ((1 - c) * BLOCKS + block) * 2
            scale3, bias3 = affine(combined(m, 2, row, other, out_area), lanes)
            scale4, bias4 = affine(combined(m, 1, 8 + row, 8 + other, out_area), lanes + COUT)
            bias = bias3 + bias4
            e = jnp.zeros((8, 128), f32)
            for k in range(big.out_area // 112):
                x3 = wide[at(start + block * big.out_area + k * 112, 112)]
                x4 = wide[at(side + block * big.out_area + k * 112, 112)]
                e += folded(gelu_only(x3 * scale3 + x4 * scale4 + bias))
            parts.append(e.sum(0, keepdims=True) / out_area)
        length = sum(jnp.sum(part * part, axis=1, keepdims=True) for part in parts)
        inverse = lax.rsqrt(length + UNIT_EPS)
        for block in range(BLOCKS):
            r.embed[pl.ds(m * 8 + c * BLOCKS + block, 1)] = parts[block] * inverse

    def key_copy(m, k):
        mine = keys.at[pl.ds(pl.multiple_of((m * devices + me) * 8, 8), 8)]
        return remote(
            r.embed.at[pl.ds(m * 8, 8)], mine, r.key_send.at[m, k], r.key_recv.at[m, k], place(lax.rem(me + k, devices)))

    def share_start(m):
        keys[at((m * devices + me) * 8, 8, 8)] = r.embed[m * 8 : (m + 1) * 8]
        repeat(1, devices, lambda k: key_copy(m, k).start())

    def share_end(m):
        repeat(1, devices, lambda k: key_copy(m, k).wait())

    def core_copy(job):
        return remote(r.parts[job].at[1 - core], r.arrived[job], r.core_send.at[job], r.core_recv.at[job], partner(1))

    def row_copy(job, target, source):
        return remote(
            r.outward[job].at[target], r.inward[job].at[source], r.row_send.at[job, target], r.row_recv.at[job, source],
            (target, core))

    def job_send(job):
        core_copy(job).wait()

        for k in range(1, chips):
            target = lax.rem(chip + k, chips)
            value = r.parts[job][core, target] + r.arrived[job][target]
            r.outward[job][target] = value.astype(r.outward[job].dtype)
            row_copy(job, target, chip).start()

    def job_end(job):
        total = r.parts[job][core, chip] + r.arrived[job][chip]
        for k in range(1, chips):
            row_copy(job, chip, lax.rem(chip + k, chips)).wait_recv()
        for k in range(1, chips):
            total += r.inward[job][lax.rem(chip + k, chips)].astype(f32)
        start = sum(JOB_ROWS[:job])
        r.packed[start : start + JOB_ROWS[job]] = total
        for k in range(1, chips):
            row_copy(job, lax.rem(chip + k, chips), chip).wait_send()

    def fill_head():
        part, third, fourth = r.parts[0], grads[2], grads[3]

        def turn(i):
            for block in range(BLOCKS):
                half, row = block // 2, block % 2
                lanes = slice(block * 128, (block + 1) * 128)
                part[half, i, row * 8 : row * 8 + 8] = third[at(i * 8, 8, 8), lanes]
                part[half, i, 16 + row * 16 : 32 + row * 16] = fourth[at(i * 16, 16), lanes]

        for i in range(chips):
            turn(i)
        core_copy(0).start()

    def fill_spatial():
        part = r.parts[1]
        for tile in range(9):
            lanes = slice(tile * 128, (tile + 1) * 128)
            gy2[lanes] = grads[1][:, lanes].T
        filler = jnp.zeros((8, 128), f32)

        def turn(i):
            top = gy2[at(i * 72, 40, 8)]
            bottom = jnp.concatenate([gy2[at(i * 72 + 40, 32, 8)], filler], axis=0)
            for half in range(2):
                part[half, i, 0:40] = side_by_side(top, bottom, half)
                part[half, i, 40:48] = filler

        for i in range(chips):
            turn(i)
        core_copy(1).start()

    def fill_sums():
        part = r.parts[2]
        column = lax.broadcasted_iota(jnp.int32, (1, 128), 1)
        filler = jnp.zeros((1, 128), f32)
        rows = [gain_sum[:, k * 128 : (k + 1) * 128] for k in range(10)]
        rows += [jnp.where(column == 0, loss_sum[...], 0.0), filler]
        rows += [shift_sum[:, k * 128 : (k + 1) * 128] for k in range(10)] + [filler, filler]
        rows = jnp.concatenate(rows, axis=0)

        def turn(i):
            for half in range(2):
                part[half, i] = rows

        for i in range(chips):
            turn(i)
        core_copy(2).start()

    def fill_reduce():
        part = r.parts[3]
        for tile in range(2):
            lanes = slice(tile * 128, (tile + 1) * 128)
            gy2[lanes] = grads[0][:, lanes].T

        def turn(i):
            for half in range(2):
                part[half, i] = side_by_side(gy2[at(i * 16, 8, 8)], gy2[at(i * 16 + 8, 8, 8)], half)

        for i in range(chips):
            turn(i)
        core_copy(3).start()

    for load in query_loads(0) + key_loads:
        load.start()
    barrier = pltpu.get_barrier_semaphore()
    repeat(1, devices, lambda k: pl.semaphore_signal(
        barrier, inc=1, device_id=place(lax.rem(me + k, devices)), device_id_type=MESH))
    if own:
        current = [r.r0[...], r.s0[...], r.e0[...], r.p0[...]]
        lagged = [r.r1[...], r.s1[...], r.e1[...], r.p1[...]]
        packed_shards([MOMENTUM * old + (1.0 - MOMENTUM) * new for old, new in zip(lagged, current)], r.sent, 0)
        packed_shards(current, r.sent, 1)
        for which in range(2):
            r.gathered[which, core, xy, z] = r.sent[which]
        r.quick[core, xy, z] = jnp.concatenate([r.sent[k, 0:16].astype(f32)[0:8] for k in range(2)], axis=0).astype(bf16)
    else:
        for shard, w in zip((r.r0, r.s0, r.e0, r.p0, r.r1, r.s1, r.e1, r.p1), wq + wk):
            w[...] = shard[...]
    if devices > 1:
        pl.semaphore_wait(barrier, devices - 1)
    if own:
        gather_start(QUICK, 0)
    for ref in list(planes_of.values()) + list(back_of.values()) + list(stage_of.values()) + grads + [
        r.raised, gain_sum, shift_sum, loss_sum, gy2] + [pair[0] for pair in moved]:
        ref[...] = jnp.zeros_like(ref)
    if own:
        gather_end(QUICK, 0)
        gather_start(QUICK, 1)
        gather_start(0, 0)

    def micro_step(m):
        opening, closing = m == 0, m == micros - 1
        base = m * field_rows
        w1, w2, w3, w4 = wq
        w1t, w3t, w4t, wt0, wt1 = (r.w1t, r.w3t, r.w4t, r.wt0, r.wt1)
        alive_count = sum(counts[m, i] for i in range(images)).astype(f32)
        count1 = images * big.area + small.area * alive_count
        count2 = images * big.out_area + small.out_area * alive_count

        def living(kind, crop):
            if kind is big:
                return jnp.float32(1.0)
            return jnp.where(lax.rem(crop, slots) < counts[m, lax.div(crop, slots)], 1.0, 0.0)

        def step_of(kind):
            return 112 if kind is big else 144

        def over_big(body, *hooks):
            def turn(c):
                body(big, c, 1)
                for k, (when, hook) in enumerate(hooks):

                    @pl.when(jnp.logical_and(when, c == k))
                    def _():
                        hook()

            repeat(0, big.count, turn)

        def over_small(body):
            body(small, 0, small.count)

        def add_moments(ref, offset, kind, first, count, row0, size, row, where, opener):
            start = offset + row0 + first * size
            if kind is big:

                @pl.when(first == 0)
                def _():
                    vec[row : row + 1] = folded(ref[at(start, opener, 8)]).sum(0, keepdims=True) / opener

            for c in range(count):
                total, square = moments(ref, start + c * size, size, step_of(kind), vec[row : row + 1])
                alive = living(kind, first + c)
                sums[where] += total * alive
                sums[where + 1] += square * alive

        for load in query_loads(m):
            load.wait()

        def even_batch(kind, first, count):
            for c in range(count):
                start = kind.out_row + (first + c) * kind.out_area

                def put(block, value):
                    even[at(start, kind.out_area), block * 128 : (block + 1) * 128] = value

                even_cells(field, base + kind.row + (first + c) * kind.area, kind, wide_stage, dense_stage, put)

        over_big(even_batch)
        over_small(even_batch)

        @pl.when(opening)
        def _():
            if own:
                gather_end(QUICK, 1)
                gather_start(QUICK, 2)
                gather_end(0, 0)
                gather_start(0, 1)
                gather_start(1, 0)
            for load in key_loads:
                load.wait()
            repeat(0, 2 * micros, key_even)
            if own:
                gather_end(QUICK, 2)
                unpacked_reduce(r.quick, chips, wk[0], wq[0])
            repeat(0, 2, lambda c: key_a(0, c))
            exchange_start(0, 0)
            if own:
                gather_end(0, 1)
                gather_start(0, 2)
                gather_end(1, 0)
                gather_start(1, 1)
            repeat(0, 2, lambda c: key_a(1, c))
            exchange_start(1, 0)
            for load in query_loads(1):
                load.start()

        def prepare_weights():
            if own:
                gather_end(1, 2)
                unpacked(r.gathered, 1, chips, wq, gy2)
            w1t[...] = w1[...].T
            w3t[...] = w3[...].T
            w4t[...] = w4[...].T
            wt0[...] = jnp.zeros_like(wt0)
            wt1[...] = jnp.zeros_like(wt1)

            def tap(ky, kx):
                start = (3 * ky + kx) * CMID
                return w2[start : start + CMID, :].T

            wt0[0:128, 0:128] = tap(1, 1)
            wt0[0:128, 128:256] = tap(1, 2)
            wt0[128:256, 128:256] = tap(1, 0)
            wt1[0:128, 0:128] = tap(2, 1)
            wt1[0:128, 128:256] = tap(2, 2)
            wt1[128:256, 128:256] = tap(2, 0)
            wt1[256:384, 0:128] = tap(0, 1)
            wt1[256:384, 128:256] = tap(0, 2)
            wt1[384:512, 128:256] = tap(0, 0)

        sums[...] = jnp.zeros_like(sums)

        def reduce_batch(kind, first, count):
            start = kind.row + first * kind.area
            size = count * kind.area
            a1[at(start, size)] = dot(field[at(base + start, size)], w1[...])
            add_moments(a1, 0, kind, first, count, kind.row, kind.area, 0, 0, 784)

        over_big(reduce_batch, (opening, lambda: exchange_next(0, 0)), (opening, lambda: exchange_next(1, 0)))
        over_small(reduce_batch)
        mean1, root1 = closed(sums[0], sums[1], vec[0:1], count1)
        scale1 = root1 * line(gains, 0)
        bias1 = line(shifts, 0) - mean1 * scale1
        vec[1:2], vec[2:3], vec[3:4], vec[4:5] = mean1, root1, scale1, bias1

        @pl.when(opening)
        def _():
            if own:
                gather_end(0, 2)
                unpacked(r.gathered, 0, chips, wk, gy2)
                gather_end(1, 1)
                gather_start(1, 2)
            for k in range(2):
                exchange_end(k, 0)
                repeat(0, 2, lambda c: key_b(k, c))
                exchange_start(k, 1)
            prepare_weights()

        sums[...] = jnp.zeros_like(sums)

        def hidden_batch(kind, first, count):
            scale, bias = vec[3:4], vec[4:5]
            for c in range(count):
                for k in range(kind.half):
                    start = kind.row + (first + c) * kind.area + k * 2 * kind.side
                    v = a1[at(start, 2 * kind.side)] * scale + bias
                    hidden, slope = gelu_pair(v)
                    slope1[at(start, 2 * kind.side)] = slope.astype(bf16)
                    split_planes(hidden, stage_of[kind.ahead], planes_of[kind.ahead], kind, first + c, k, k % 2)

        over_big(hidden_batch, (opening, lambda: exchange_next(0, 1)), (opening, lambda: exchange_next(1, 1)))
        over_small(hidden_batch)

        @pl.when(opening)
        def _():
            for k in range(2):
                exchange_end(k, 1)
                repeat(0, 2, lambda c: key_c(k, c))
                exchange_start(k, 2)

        def spatial_batch(kind, first, count):
            half, lanes = kind.half, kind.wide
            value = dot(patches(planes_of[kind.ahead], kind, first, count), w2[...])
            start = kind.out_row + first * kind.out_area
            for k in range(count * half):
                a2[pl.ds(start + k * half, half)] = value[k * lanes : k * lanes + half]
            add_moments(a2, 0, kind, first, count, kind.out_row, kind.out_area, 0, 16, 784)

        over_big(spatial_batch, (opening, lambda: exchange_next(0, 2)), (opening, lambda: exchange_next(1, 2)))
        over_small(spatial_batch)
        mean2, root2 = closed(sums[16], sums[17], vec[0:1], count2)
        scale2 = root2 * line(gains, CMID)
        bias2 = line(shifts, CMID) - mean2 * scale2
        vec[5:6], vec[6:7], vec[7:8], vec[8:9] = mean2, root2, scale2, bias2

        @pl.when(opening)
        def _():
            for k in range(2):
                exchange_end(k, 2)
                repeat(0, 2, lambda c: key_d(k, c))
                share_start(k)

        def head_product(which, source, weight, kind, first, count):
            start = kind.out_row + first * kind.out_area
            size = count * kind.out_area
            value = dot(source, weight[...])
            for block in range(BLOCKS):
                offset = (which * BLOCKS + block) * outs
                wide[at(offset + start, size)] = value[:, block * 128 : (block + 1) * 128]
            for block in range(BLOCKS):
                offset = (which * BLOCKS + block) * outs
                add_moments(
                    wide, offset, kind, first, count, kind.out_row, kind.out_area,
                    16 + which * 4 + block, which * 8 + block * 2, 784)

        def expand_batch(kind, first, count):
            start = kind.out_row + first * kind.out_area
            size, step = count * kind.out_area, step_of(kind)
            scale, bias = vec[7:8], vec[8:9]
            head_product(1, even[at(start, size)], w4, kind, first, count)
            for k in range(size // step):
                hidden, slope = gelu_pair(a2[at(start + k * step, step)] * scale + bias)
                thin[at(H2 + start + k * step, step)] = hidden.astype(bf16)
                thin[at(SLOPE2 + start + k * step, step)] = slope.astype(bf16)
            head_product(0, thin[at(H2 + start, size)], w3, kind, first, count)

        over_big(expand_batch)
        over_small(expand_batch)
        for which in range(2):
            for block in range(BLOCKS):
                row = which * 4 + block
                where = which * 8 + block * 2
                lanes = 2 * CMID + row * 128
                mean, root = closed(sums[where], sums[where + 1], vec[16 + row : 17 + row], count2)
                scale = root * line(gains, lanes)
                bias = line(shifts, lanes) - mean * scale
                vec[24 + row : 25 + row], vec[32 + row : 33 + row] = mean, root
                vec[40 + row : 41 + row] = scale
                if which == 0:
                    vec[48 + block : 49 + block] = bias
                else:
                    vec[48 + block : 49 + block] += bias

        rows_e, rows_c = r.rows_e, r.rows_c

        def embed_batch(kind, first, count):
            step = step_of(kind)
            for c in range(count):
                start = kind.out_row + (first + c) * kind.out_area
                for block in range(BLOCKS):
                    mean3, mean4 = vec[24 + block : 25 + block], vec[28 + block : 29 + block]
                    scale3, scale4 = vec[40 + block : 41 + block], vec[44 + block : 45 + block]
                    bias = vec[48 + block : 49 + block]
                    zero = jnp.zeros((8, 128), f32)
                    e, s0, s3, s4 = zero, zero, zero, zero
                    for k in range(kind.out_area // step):
                        inside = block * outs + start + k * step
                        x3, x4 = wide[at(A3 + inside, step)], wide[at(AP + inside, step)]
                        value, slope = gelu_pair(x3 * scale3 + x4 * scale4 + bias)
                        slope3[at(inside, step)] = slope.astype(bf16)
                        e += folded(value)
                        s0 += folded(slope)
                        s3 += folded(slope * (x3 - mean3))
                        s4 += folded(slope * (x4 - mean4))
                    row = kind.ahead + first + c
                    for which, value in enumerate((e / kind.out_area, s0, s3, s4)):
                        rows_e[which, block, pl.ds(row, 1)] = value.sum(0, keepdims=True)

        over_big(embed_batch)
        over_small(embed_batch)

        share_end(m)

        def joined(which):
            return jnp.concatenate([rows_e[which, block] for block in range(BLOCKS)], axis=1)

        e = joined(0)
        inverse = lax.rsqrt(jnp.sum(e * e, axis=-1, keepdims=True) + UNIT_EPS)
        row = lax.broadcasted_iota(jnp.int32, (crops, 1), 0)
        owner = jnp.zeros((crops, 1), jnp.int32)
        live = jnp.where(row < images, 1.0, 0.0)
        for i in range(images):
            owner = jnp.where(row == i, i, owner)
            for slot in range(slots):
                here = row == images + i * slots + slot
                owner = jnp.where(here, i, owner)
                live = jnp.where(here, jnp.where(slot < counts[m, i], 1.0, 0.0), live)
        key_rows = [
            jnp.concatenate(
                [keys[pl.ds(m * devices * 8 + c * BLOCKS + block, devices, stride=8)] for c in range(images)], axis=0)
            for block in range(BLOCKS)
        ]
        key_high, key_low = two_parts(jnp.concatenate(key_rows, axis=1))
        logits = lax.dot_general(
            jnp.concatenate(two_parts(e * inverse), axis=0), jnp.concatenate([key_high, key_low], axis=0),
            (((1,), (1,)), ((), ())), preferred_element_type=f32)
        count = devices * images
        logits = logits[0:crops] + logits[crops:]
        logits = (logits[:, 0:count] + logits[:, count:]) / TEMP
        top = jnp.max(logits, axis=-1, keepdims=True)
        powers = jnp.exp(logits - top)
        total = jnp.sum(powers, axis=-1, keepdims=True)
        column = lax.broadcasted_iota(jnp.int32, logits.shape, 1)
        mine = column == owner * devices + me
        chosen = jnp.sum(jnp.where(mine, logits, 0.0), axis=-1, keepdims=True)
        ce = (top + jnp.log(total) - chosen) * live
        loss_sum[...] += jnp.sum(ce, axis=0, keepdims=True)
        toward = (powers / total - jnp.where(mine, 1.0, 0.0)) * (live / TEMP)
        back = dot(jnp.concatenate(two_parts(toward), axis=0), jnp.concatenate([key_high, key_low], axis=1))
        back = back[0:crops] + back[crops:]
        back = back[:, 0:COUT] + back[:, COUT:]
        de = inverse * back - e * (inverse * inverse * inverse * jnp.sum(e * back, axis=-1, keepdims=True))
        de = de * jnp.where(row < images, 1.0 / big.out_area, 1.0 / small.out_area)
        sum0 = jnp.sum(de * joined(1), axis=0, keepdims=True)
        for which in range(2):
            reach = jnp.sum(de * joined(2 + which), axis=0, keepdims=True)
            for block in range(BLOCKS):
                row = which * 4 + block
                here = slice(block * 128, (block + 1) * 128)
                lanes = slice(2 * CMID + row * 128, 2 * CMID + (row + 1) * 128)
                mean, root, scale = vec[24 + row : 25 + row], vec[32 + row : 33 + row], vec[40 + row : 41 + row]
                along = reach[:, here] * root
                gain_sum[:, lanes] += along
                shift_sum[:, lanes] += sum0[:, here]
                tilt = scale * root * along / count2
                vec[52 + row : 53 + row] = tilt
                vec[60 + row : 61 + row] = scale * sum0[:, here] / count2 - tilt * mean
                rows_c[which, block] = de[:, here] * scale

        sums[...] = jnp.zeros_like(sums)
        d3, dp = r.d3, r.dp

        def head_back(kind, first, count):
            start = kind.out_row + first * kind.out_area
            size, step = count * kind.out_area, step_of(kind)
            for which, store in ((0, d3), (1, dp)):
                for block in range(BLOCKS):
                    lanes = slice(block * 128, (block + 1) * 128)
                    where = which * 4 + block
                    for c in range(count):
                        rise = rows_c[which, block, pl.ds(kind.ahead + first + c, 1)]
                        alive = living(kind, first + c)
                        tilt, level = vec[52 + where : 53 + where] * alive, vec[60 + where : 61 + where] * alive
                        for k in range(kind.out_area // step):
                            inside = c * kind.out_area + k * step
                            here = block * outs + start + inside
                            x = wide[at(which * BLOCKS * outs + here, step)]
                            grad = slope3[at(here, step)].astype(f32) * rise - (x * tilt + level)
                            store[inside : inside + step, lanes] = grad.astype(bf16)
            grad3, gradp = d3[0:size], dp[0:size]
            gy2[at(start, size)] = dot(grad3, w3t[...])
            gradient = dot(gradp, w4t[...])
            for block in range(2):
                wide[at(AP + block * outs + start, size)] = gradient[:, block * 128 : (block + 1) * 128]
            grads[2][...] += dot_rows(thin[at(H2 + start, size)], grad3)
            grads[3][...] += dot_rows(even[at(start, size)], gradp)
            mean = vec[5:6]
            level, reach = jnp.zeros((8, 128), f32), jnp.zeros((8, 128), f32)
            for k in range(size // step):
                here = at(start + k * step, step)
                gy = gy2[here] * thin[at(SLOPE2 + start + k * step, step)].astype(f32)
                gy2[here] = gy
                level += folded(gy)
                reach += folded(gy * (a2[here] - mean))
            sums[0] += level
            sums[1] += reach

        over_big(head_back)
        over_small(head_back)

        if own:

            @pl.when(closing)
            def _():
                fill_head()

        def norm_back(where, lanes, count):
            mean, root, scale = vec[where : where + 1], vec[where + 1 : where + 2], vec[where + 2 : where + 3]
            level = sums[0].sum(0, keepdims=True)
            along = sums[1].sum(0, keepdims=True) * root
            gain_sum[:, lanes] += along
            shift_sum[:, lanes] += level
            tilt = scale * root * along / count
            vec[68:69] = scale
            vec[69:70] = tilt
            vec[70:71] = scale * level / count - tilt * mean

        norm_back(5, slice(CMID, 2 * CMID), count2)
        sums[...] = jnp.zeros_like(sums)

        def spatial_back(kind, first, count):
            half, lanes, side, step = kind.half, kind.wide, kind.side, step_of(kind)
            out_start = kind.out_row + first * kind.out_area
            for c in range(count):
                alive = living(kind, first + c)
                tilt, level = vec[69:70] * alive, vec[70:71] * alive
                for k in range(kind.out_area // step):
                    here = at(out_start + c * kind.out_area + k * step, step)
                    gy2[here] = gy2[here] * vec[68:69] - (a2[here] * tilt + level)
            column = lax.broadcasted_iota(jnp.int32, (lanes, 128), 0)
            store = back_of[kind.ahead]
            for k in range(count * half):
                here = jnp.where(column < half, gy2[pl.ds(out_start + k * half, lanes)], 0.0)
                following = jnp.where(column < half - 1, gy2[pl.ds(out_start + k * half + 1, lanes)], 0.0)
                store[first + k // half, k % half, :, 0:128] = here.astype(bf16)
                store[first + k // half, k % half, :, 128:256] = following.astype(bf16)
            size = count * half * lanes
            near = store[pl.ds(first, count), 0:half].reshape(size, 256)
            beyond = store[pl.ds(first, count), 1 : half + 1].reshape(size, 256)
            upper_rows = dot(near, wt0[...])
            lower_rows = dot(jnp.concatenate([near, beyond], axis=1), wt1[...])
            start = kind.row + first * kind.area
            for k in range(count * half):
                here = slice(k * lanes, k * lanes + half)
                row = start + k * 2 * side
                for odd, value in ((0, upper_rows), (1, lower_rows)):
                    wide[pl.ds(row + odd * side, half, stride=2)] = value[here, 0:128]
                    wide[pl.ds(row + odd * side + 1, half, stride=2)] = value[here, 128:256]
            grads[1][...] += dot_rows(near[:, 0:128], patches(planes_of[kind.ahead], kind, first, count))
            mean = vec[1:2]
            level, reach = jnp.zeros((8, 128), f32), jnp.zeros((8, 128), f32)
            for k in range(count * kind.area // step):
                here = at(start + k * step, step)
                gy = wide[here] * slope1[here].astype(f32)
                wide[here] = gy
                level += folded(gy)
                reach += folded(gy * (a1[here] - mean))
            sums[0] += level
            sums[1] += reach

        def job_hooks(*jobs):
            def sends(some):
                return lambda: [job_send(job) for job in some]

            return [(closing, sends(some)) for some in jobs] if own else []

        over_big(spatial_back, *job_hooks((0,)))
        over_small(spatial_back)
        norm_back(1, slice(0, CMID), count1)

        if own:

            @pl.when(closing)
            def _():
                fill_spatial()
                fill_sums()

        def reduce_back(kind, first, count):
            step = step_of(kind)
            size = count * kind.area
            start = kind.row + first * kind.area
            rise = vec[68:69]
            for c in range(count):
                alive = living(kind, first + c)
                tilt, level = vec[69:70] * alive, vec[70:71] * alive
                for k in range(kind.area // step):
                    here = at(start + c * kind.area + k * step, step)
                    grad = wide[here] * rise - (a1[here] * tilt + level)
                    slope1[here] = grad.astype(bf16)
            grads[0][...] += dot_rows(slope1[at(start, size)], field[at(base + start, size)])

        over_big(reduce_back, *job_hooks((1,), (2,)))
        over_small(reduce_back)

        if own:

            @pl.when(closing)
            def _():
                fill_reduce()
                job_end(0)

        raised = r.raised

        def field_back(kind, first, count):
            half, side = kind.half, kind.side
            size = count * kind.area
            start = kind.row + first * kind.area
            whole = dot(slope1[at(start, size)], w1t[...])
            out_start = kind.out_row + first * kind.out_area
            for k in range(count * half):
                row = k * 2 * side
                for block in range(2):
                    lanes = slice(block * 128, (block + 1) * 128)
                    slot = k % 4 * 2 + block
                    raised[slot, pl.ds(0, half, stride=2)] = wide[pl.ds(AP + block * outs + out_start + k * half, half)]
                    top_row = whole[row : row + side, lanes] + raised[slot, 0:side]
                    both = jnp.concatenate([top_row, whole[row + side : row + 2 * side, lanes]], axis=0)
                    field[at(base + start + row, 2 * side), lanes] = both.astype(bf16)
            if kind is big:
                store_big(m, first).start()
            else:
                store_small(m).start()

        over_big(field_back, *job_hooks((), (3,)))
        over_small(field_back)

    repeat(0, micros, micro_step)
    if own:
        for job in range(1, 4):
            job_end(job)
    for m in range(micros):
        for c in range(images):
            store_big(m, c).wait()
        store_small(m).wait()


def step_pass(axes, own, slots, big, small, key, counts, mask, current, lagged, vectors):
    chips, cores = axes
    devices = chips * cores
    widths = stage_widths(devices)
    micros, images = counts.shape
    one, two = field_pair(images, slots)
    rows = two.row + two.count * two.area
    outs = two.out_row + two.count * two.out_area
    crops = images * (1 + slots)
    vmem = pl.BlockSpec(memory_space=pltpu.VMEM)
    smem = pl.BlockSpec(memory_space=pltpu.SMEM)
    hbm = pl.BlockSpec(memory_space=pl.ANY)
    weights = [(CIN, CMID), (9 * CMID, CMID), (CMID, COUT), (CIN, COUT)]
    totals = dict(
        g1=(CMID, CIN), g2=(CMID, 9 * CMID), g3=(CMID, COUT), g4=(CIN, COUT),
        gain_sum=(1, NORMS), shift_sum=(1, NORMS), loss_sum=(1, 1))
    r0, s0, e0, p0 = ((w, vmem) for w in current)
    r1, s1, e1, p1 = ((w, vmem) for w in lagged)
    gains, shifts, gains1, shifts1 = ((v, vmem) for v in vectors)
    inputs = dict(
        big_hbm=(big, hbm), small_hbm=(small, hbm), key_hbm=(key, hbm), counts=(counts, smem), mask=(mask, smem),
        r0=r0, s0=s0, e0=e0, p0=p0, r1=r1, s1=s1, e1=e1, p1=p1, gains=gains, shifts=shifts, gains1=gains1, shifts1=shifts1)
    outputs = dict(
        big_out=(jax.ShapeDtypeStruct(big.shape, bf16), hbm), small_out=(jax.ShapeDtypeStruct(small.shape, bf16), hbm))
    if own:
        outputs |= dict(packed=(jax.ShapeDtypeStruct((sum(JOB_ROWS), 128), f32), vmem))
    else:
        outputs |= {n: (jax.ShapeDtypeStruct(shape, f32), vmem) for n, shape in totals.items()}

    def buf(dtype, *shape):
        return pltpu.VMEM(shape, dtype)

    def dma(*shape):
        return pltpu.SemaphoreType.DMA(shape)

    scratch = dict(
        field=buf(bf16, rows + 2 * micros * one.area, CIN),
        a1=buf(f32, rows, 128), slope1=buf(bf16, rows, 128),
        planes_big=buf(bf16, 2, one.count, one.half + 1, one.wide, 384),
        planes_small=buf(bf16, 2, two.count, two.half + 1, two.wide, 384),
        a2=buf(f32, outs, 128), thin=buf(bf16, 2 * outs, 128), even=buf(bf16, outs, CIN),
        wide=buf(f32, 2 * BLOCKS * outs, 128), slope3=buf(bf16, BLOCKS * outs, 128),
        back_big=buf(bf16, one.count, one.half + 1, one.wide, 256),
        back_small=buf(bf16, two.count, two.half + 1, two.wide, 256),
        gy2=buf(f32, outs + 16, 128), stage_big=buf(f32, 2, 2, 80, 128), stage_small=buf(f32, 2, 2, 48, 128),
        wide_stage=buf(f32, 8, SIDE, 128), dense_stage=buf(f32, 2, one.out_area, 128), raised=buf(f32, 8, SIDE, 128),
        d3=buf(bf16, two.count * two.out_area, COUT), dp=buf(bf16, two.count * two.out_area, COUT),
        w1t=buf(bf16, CMID, CIN), w3t=buf(bf16, COUT, CMID), w4t=buf(bf16, COUT, CIN),
        wt0=buf(bf16, 256, 256), wt1=buf(bf16, 512, 256), sums=buf(f32, 18, 8, 128), vec=buf(f32, 80, 128),
        rows_e=buf(f32, 4, BLOCKS, crops, 128), rows_c=buf(f32, 2, BLOCKS, crops, 128),
        keys=buf(f32, devices * 16, 128), embed=buf(f32, 16, 128),
        moved=[[buf(f32, 1 << width, n, 128) for width in widths] for _ in range(micros) for n in TURN_ROWS],
        key_load=dma(2 * micros), query_load=dma(micros, 2), store=dma(micros, images + 1),
        move_send=dma(3 * micros, 2, 1 << widths[0]), move_recv=dma(3 * micros, 2, 1 << widths[0]),
        key_send=dma(micros, devices), key_recv=dma(micros, devices),
    )
    first, second, third, fourth = (buf(bf16, *shape) for shape in weights)
    scratch |= dict(w1q=first, w2q=second, w3q=third, w4q=fourth, w1k=first, w2k=second, w3k=third, w4k=fourth)
    wires = (bf16, bf16, f32, f32)
    if own:
        scratch |= {n: buf(f32, *shape) for n, shape in totals.items()}
        scratch |= dict(
            sent=buf(bf16, 2, PACK, 128), gathered=buf(bf16, 2, 2, 4, 4, PACK, 128), quick=buf(bf16, 2, 4, 4, 16, 128),
            parts=[buf(f32, 2, chips, n, 128) for n in JOB_ROWS], arrived=[buf(f32, chips, n, 128) for n in JOB_ROWS],
            outward=[buf(t, chips, n, 128) for n, t in zip(JOB_ROWS, wires)],
            inward=[buf(t, chips, n, 128) for n, t in zip(JOB_ROWS, wires)],
            gather_send=dma(3, 3, 3), gather_recv=dma(3, 3, 3), core_send=dma(4), core_recv=dma(4),
            row_send=dma(4, chips), row_recv=dma(4, chips),
        )
    names = list(inputs) + list(outputs) + list(scratch)
    out = pl.pallas_call(
        functools.partial(step_kernel, axes, own, slots, names),
        out_shape=[shape for shape, _ in outputs.values()],
        in_specs=[spec for _, spec in inputs.values()],
        out_specs=[spec for _, spec in outputs.values()],
        scratch_shapes=list(scratch.values()),
        compiler_params=pltpu.CompilerParams(vmem_limit_bytes=63 * 2**20, collective_id=0, has_side_effects=True),
        name="step",
    )(*[array for array, _ in inputs.values()])
    return types.SimpleNamespace(**dict(zip(outputs, out)))


def finish_kernel(packed, loss, reduce_out, spatial_out, expand_out, shortcut_out, gains, shifts):
    reduce_out[0:8] = packed[120:128, 0:64]
    reduce_out[8:16] = packed[120:128, 64:128]
    rows = jnp.concatenate([packed[48:88], jnp.zeros((88, 128), f32)], axis=0).T
    spatial_out[...] = jnp.concatenate([rows[0:64, 0:40], rows[64:128, 0:32]], axis=1)
    for block in range(2):
        lanes = slice(block * 128, (block + 1) * 128)
        expand_out[:, lanes] = packed[block * 8 : block * 8 + 8]
        shortcut_out[:, lanes] = packed[16 + block * 16 : 32 + block * 16]
    for row in range(NORMS // 128):
        gains[pl.ds(row * 128, 128)] = packed[96 + row]
        shifts[pl.ds(row * 128, 128)] = packed[108 + row]
    loss[...] = packed[106:107, 0:1]


def finish_pass(packed):
    vmem = pl.BlockSpec(memory_space=pltpu.VMEM)
    shapes = [(1, 1), (16, 64), (64, 72), (8, 256), (16, 256), (NORMS,), (NORMS,)]
    return pl.pallas_call(
        finish_kernel,
        out_shape=[jax.ShapeDtypeStruct(shape, f32) for shape in shapes],
        in_specs=[vmem],
        out_specs=[vmem] * 7,
        name="finish",
    )(packed)


def gather_weights(shards):
    rows = [lax.all_gather(part, "dp", axis=0, tiled=True) for part in shards]
    return [lax.all_gather(part, "fsdp", axis=1, tiled=True) for part in rows]


def per_device(axes, *args):
    query_global, small_crop_query, small_count, key_global, shuffle_mask = args[:5]
    current, lagged = args[5:9], args[11:15]
    vectors = (args[9], args[10], args[15], args[16])
    micros = query_global.shape[0]
    slots = small_crop_query.shape[2]
    chips, cores = axes
    own = chips == 16 and cores == 2
    if own:
        current = [w.T if i == 1 else w for i, w in enumerate(current)]
        lagged = [w.T if i == 1 else w for i, w in enumerate(lagged)]
    else:
        fresh = [MOMENTUM * old + (1.0 - MOMENTUM) * new for old, new in zip(lagged, current)]
        current = gather_weights([w.astype(bf16) for w in current])
        lagged = gather_weights([w.astype(bf16) for w in fresh])
    out = step_pass(
        axes, own, slots, query_global.reshape(micros, -1, CIN), small_crop_query.reshape(micros, -1, CIN),
        key_global.reshape(micros, -1, CIN), small_count, shuffle_mask, current, lagged, vectors,
    )
    fields = (out.big_out.reshape(query_global.shape), out.small_out.reshape(small_crop_query.shape))
    if own:
        loss, first, second, third, fourth, gains_grad, shifts_grad = finish_pass(out.packed)
        return (loss.reshape(()), *fields, first, second.T, third, fourth, gains_grad, shifts_grad)
    totals = (out.g1.T, out.g2.T, out.g3, out.g4)
    summed = lax.psum_scatter(totals, "dp", scatter_dimension=0, tiled=True)
    owned = lax.psum_scatter(summed, "fsdp", scatter_dimension=1, tiled=True)
    sums = lax.psum((out.loss_sum, out.gain_sum, out.shift_sum), ("dp", "fsdp"))
    return (sums[0].reshape(()), *fields, *owned, sums[1].reshape(NORMS), sums[2].reshape(NORMS))


def solution(mesh):
    whole, split = P(), P("dp", "fsdp")
    images, crops = P(None, ("dp", "fsdp"), None, None, None), P(None, ("dp", "fsdp"), None, None, None, None)
    axes = (mesh.shape["dp"], mesh.shape["fsdp"])
    return jax.shard_map(
        functools.partial(per_device, axes),
        mesh=mesh,
        in_specs=(images, crops, P(None, ("dp", "fsdp")), images, whole)
        + (split,) * 4 + (whole,) * 2 + (split,) * 4 + (whole,) * 2,
        out_specs=(whole, images, crops) + (split,) * 4 + (whole,) * 2,
        check_vma=False,
    )
```

```python
import functools
import types
import jax
import jax.numpy as jnp
from jax import lax
from jax.experimental import pallas as pl
from jax.experimental.pallas import tpu as pltpu
from jax.sharding import PartitionSpec as P

f32, bf16 = jnp.float32, jnp.bfloat16
CIN, CMID, COUT, NORMS = 256, 128, 512, 1280
SIDE, SMALL = 56, 24
BLOCKS = COUT // 128
TEMP, NORM_EPS, UNIT_EPS = 0.2, 1e-05, 1e-06
ROOT_HALF = 0.7071067811865476
DENSITY = 0.3989422804014327


class Field:
    def __init__(self, count, side, row, out_row, ahead):
        self.count, self.side, self.row, self.out_row = count, side, row, out_row
        self.ahead = ahead
        self.half = side // 2
        self.wide = -(-self.half // 16) * 16
        self.area, self.out_area = side * side, (side // 2) ** 2


def field_pair(images, slots):
    big = Field(images, SIDE, 0, 0, 0)
    small = Field(images * slots, SMALL, images * big.area, images * big.out_area, images)
    return big, small


def at(start, size, align=16):
    if isinstance(start, int):
        return pl.ds(start, size)
    return pl.ds(pl.multiple_of(start, align), size)


def folded(x):
    return x.reshape(x.shape[0] // 8, 8, x.shape[1]).sum(0)


def dot(a, b):
    return jnp.dot(a, b, preferred_element_type=f32)


def dot_rows(a, b):
    return lax.dot_general(a, b, (((0,), (0,)), ((), ())), preferred_element_type=f32)


def gelu_pair(v):
    share = 0.5 + 0.5 * lax.erf(v * ROOT_HALF)
    return v * share, share + v * (DENSITY * jnp.exp(v * v * -0.5))


def gelu_only(v):
    return v * (0.5 + 0.5 * lax.erf(v * ROOT_HALF))


MOMENTUM = 0.999
MESH = pl.DeviceIdType.MESH
PACK = 96
JOB_ROWS = (48, 48, 24, 8)
TURN_ROWS = (24, 8, 16)


def line(vector, start):
    return vector[pl.ds(start, 128)].reshape(1, 128)


def two_parts(x):
    high = x.astype(bf16)
    return high, (x - high.astype(f32)).astype(bf16)


def moments(ref, start, size, step, pivot):
    total = jnp.zeros((8, 128), f32)
    square = jnp.zeros((8, 128), f32)
    for k in range(size // step):
        x = ref[at(start + k * step, step, 8)] - pivot
        total += folded(x)
        square += folded(x * x)
    return total, square


def closed(total, square, pivot, count):
    off = total.sum(0, keepdims=True) / count
    spread = jnp.maximum(square.sum(0, keepdims=True) / count - off * off, 0.0)
    return pivot + off, lax.rsqrt(spread + NORM_EPS)


def patches(planes, field, first, crops):
    size = crops * field.half * field.wide
    here = pl.ds(first, crops)
    above = planes[1, here, 0 : field.half].reshape(size, 3 * CMID)
    level = planes[0, here, 0 : field.half].reshape(size, 3 * CMID)
    below = planes[1, here, 1 : field.half + 1].reshape(size, 3 * CMID)
    return jnp.concatenate([above, level, below], axis=1)


def split_planes(hidden, stage, planes, field, crop, row, slot):
    side, wide = field.side, field.wide
    for odd in range(2):
        stage[slot, odd, 8 : 8 + side] = hidden[odd * side : (odd + 1) * side]
    for odd in range(2):
        for tap in range(3):
            column = stage[slot, odd, pl.ds(7 + tap, wide, stride=2)]
            planes[odd, crop, row + odd, :, tap * CMID : (tap + 1) * CMID] = column.astype(bf16)


def even_cells(source, base, field, wide_stage, dense_stage, put):
    side, half = field.side, field.half
    for y in range(half):
        for block in range(CIN // 128):
            slot = y % 4 * 2 + block
            x = source[at(base + y * 2 * side, 2 * side), block * 128 : (block + 1) * 128]
            wide_stage[slot, 0:side] = x.astype(f32)[0:side]
            dense_stage[block, y * half : (y + 1) * half] = wide_stage[slot, pl.ds(0, half, stride=2)]
    for block in range(CIN // 128):
        put(block, dense_stage[block, 0 : field.out_area].astype(bf16))


def flipped(index, mask):
    bit = 1
    while bit <= mask:
        if mask & bit:
            index = index + bit * (1 - 2 * lax.rem(lax.div(index, bit), 2))
        bit *= 2
    return index


def side_by_side(top, bottom, core):
    left = lax.broadcasted_iota(jnp.int32, top.shape, 1) < 64
    if core == 0:
        return jnp.where(left, top, pltpu.roll(bottom, 64, 1))
    return jnp.where(left, pltpu.roll(top, 64, 1), bottom)


def packed_shards(shards, store, which):
    first, second, third, fourth = shards
    zero = jnp.zeros
    second = jnp.concatenate([second, zero((second.shape[0], 56), f32)], axis=1)
    second = jnp.concatenate([second, zero((64, 128), f32)], axis=0).T[0:80, 0:64]
    rows = [jnp.concatenate([first[0:8], first[8:16]], axis=1), jnp.concatenate([second[0:40], second[40:80]], axis=1)]
    rows += [third[:, 0:128], third[:, 128:256], fourth[:, 0:128], fourth[:, 128:256]]
    store[which] = jnp.concatenate(rows, axis=0).astype(bf16)


def unpacked(gathered, which, chips, weights, stage):
    w1, w2, w3, w4 = weights

    def turn(i, _):
        z, xy = lax.div(i, 4), lax.rem(i, 4)
        ours = [gathered[which, core, xy, z] for core in range(2)]
        first, second = (rows[0:48].astype(f32) for rows in ours)
        left = lax.broadcasted_iota(jnp.int32, (48, 128), 1) < 64
        top = jnp.where(left, first, pltpu.roll(second, 64, 1))
        bottom = jnp.where(left, pltpu.roll(first, 64, 1), second)
        w1[at(i * 16, 16)] = jnp.concatenate([top[0:8], bottom[0:8]], axis=0).astype(bf16)
        stage[at(i * 72, 40, 8)] = top[8:48]
        stage[at(i * 72 + 40, 32, 8)] = bottom[8:40]
        for block in range(BLOCKS):
            start = 64 + block % 2 * 16
            w4[at(i * 16, 16), block * 128 : (block + 1) * 128] = ours[block // 2][start : start + 16]
        return 0

    lax.fori_loop(0, chips, turn, 0)
    w2[...] = stage[0 : 9 * CMID].astype(bf16)

    def pairs(i, _):
        z, xy = lax.div(i, 2), lax.rem(i, 2) * 2
        for block in range(BLOCKS):
            rows = slice(block % 2 * 8, block % 2 * 8 + 8)
            both = [gathered[which, block // 2, xy + k, z, 48:64].astype(f32)[rows] for k in range(2)]
            w3[at(i * 16, 16), block * 128 : (block + 1) * 128] = jnp.concatenate(both, axis=0).astype(bf16)
        return 0

    lax.fori_loop(0, chips // 2, pairs, 0)


def stage_widths(devices):
    bits = devices.bit_length() - 1
    return (bits + 1) // 2, bits // 2


def step_kernel(axes, own, slots, names, *refs):
    r = types.SimpleNamespace(**dict(zip(names, refs)))
    chips, cores = axes
    devices = chips * cores
    widths = stage_widths(devices)
    shifts_of = (0, widths[0])
    counts, mask = r.counts, r.mask
    micros, images = counts.shape
    fields = field_pair(images, slots)
    big, small = fields
    crops = images * (1 + slots)
    field_rows = small.row + small.count * small.area
    outs = small.out_row + small.count * small.out_area
    chip, core = lax.axis_index("dp"), lax.axis_index("fsdp")
    me = chip * cores + core
    xy, z = lax.rem(chip, 4), lax.div(chip, 4)
    field, a1, slope1, a2, even, wide, slope3 = (r.field, r.a1, r.slope1, r.a2, r.even, r.wide, r.slope3)
    thin, gy2, vec, sums, keys = (r.thin, r.gy2, r.vec, r.sums, r.keys)
    planes_of = {0: r.planes_big, images: r.planes_small}
    back_of = {0: r.back_big, images: r.back_small}
    stage_of = {0: r.stage_big, images: r.stage_small}
    wide_stage, dense_stage = r.wide_stage, r.dense_stage
    wq = [r.w1q, r.w2q, r.w3q, r.w4q]
    wk = [r.w1k, r.w2k, r.w3k, r.w4k]
    grads = [r.g1, r.g2, r.g3, r.g4]
    gains, shifts, gains1, shifts1 = (r.gains, r.shifts, r.gains1, r.shifts1)
    gain_sum, shift_sum, loss_sum = r.gain_sum, r.shift_sum, r.loss_sum
    A3, AP, H2, SLOPE2 = 0, BLOCKS * outs, 0, outs

    def place(device):
        return (lax.div(device, cores), lax.rem(device, cores))

    def remote(source, target, send, receive, device):
        return pltpu.make_async_remote_copy(
            src_ref=source, dst_ref=target, send_sem=send, recv_sem=receive, device_id=device, device_id_type=MESH)

    def repeat(first, last, body):
        lax.fori_loop(first, last, lambda k, _: (body(k), 0)[1], 0)

    key_base = field_rows
    key_loads = [
        pltpu.make_async_copy(
            r.key_hbm.at[i // 2, pl.ds(i % 2 * big.area, big.area)],
            field.at[pl.ds(key_base + i * big.area, big.area)], r.key_load.at[i])
        for i in range(2 * micros)
    ]

    def query_loads(m):
        return [
            pltpu.make_async_copy(
                r.big_hbm.at[m], field.at[pl.ds(m * field_rows, small.row)], r.query_load.at[m, 0]),
            pltpu.make_async_copy(
                r.small_hbm.at[m], field.at[pl.ds(m * field_rows + small.row, field_rows - small.row)],
                r.query_load.at[m, 1]),
        ]

    def field_stores(m):
        return [
            pltpu.make_async_copy(slope1.at[pl.ds(0, small.row)], r.da_big.at[m], r.store.at[m, 0]),
            pltpu.make_async_copy(slope1.at[pl.ds(small.row, field_rows - small.row)], r.da_small.at[m], r.store.at[m, 1]),
        ]

    def even_stores(m):
        return [
            pltpu.make_async_copy(even.at[pl.ds(0, small.out_row)], r.even_big.at[m], r.store.at[m, 2]),
            pltpu.make_async_copy(even.at[pl.ds(small.out_row, outs - small.out_row)], r.even_small.at[m], r.store.at[m, 3]),
        ]

    def settle(copies):
        for copy in copies:
            copy.wait()

    def partner(flip):
        return place(flipped(me, flip))

    def gather_copies(which, stage):
        if stage == 0:
            here = r.gathered.at[which, core, xy, z]
            flips = [8 * k for k in range(1, chips // 4)]
        elif stage == 1:
            here = r.gathered.at[which, core, xy]
            flips = [2 * k for k in range(1, 4)]
        else:
            here = r.gathered.at[which, core]
            flips = [1]
        return [
            remote(here, here, r.gather_send.at[which, stage, k], r.gather_recv.at[which, stage, k], partner(flip))
            for k, flip in enumerate(flips)
        ]

    def gather_start(which, stage):
        for copy in gather_copies(which, stage):
            copy.start()

    def gather_end(which, stage):
        for copy in gather_copies(which, stage):
            copy.wait()

    moved = r.moved

    def exchange_copies(m, turn, stage):
        ref, which = moved[m * 3 + turn][stage], m * 3 + turn
        return [
            remote(
                ref.at[0], ref.at[k], r.move_send.at[which, stage, k], r.move_recv.at[which, stage, k],
                partner(k << shifts_of[stage]))
            for k in range(1, 1 << widths[stage])
        ]

    def picked(m, stage):
        return lax.rem(lax.div(jnp.bitwise_xor(mask[m, 0], mask[m, 1]), 1 << shifts_of[stage]), 1 << widths[stage])

    def exchange_start(m, turn):
        for copy in exchange_copies(m, turn, 0):
            copy.start()

    def exchange_next(m, turn):
        for copy in exchange_copies(m, turn, 0):
            copy.wait()
        first, second = moved[m * 3 + turn]
        second[0] = first[picked(m, 0)]
        for copy in exchange_copies(m, turn, 1):
            copy.start()

    def exchange_end(m, turn):
        for copy in exchange_copies(m, turn, 1):
            copy.wait()

    def put_moments(m, turn, row, start, size, step):
        pivot = folded(wide[at(start, step, 8)]).sum(0, keepdims=True) / step
        total, square = moments(wide, start, size, step, pivot)
        off = total.sum(0, keepdims=True) / size
        moved[m * 3 + turn][0][0, pl.ds(row, 1)] = pivot + off
        moved[m * 3 + turn][0][0, pl.ds(row + 1, 1)] = jnp.maximum(square.sum(0, keepdims=True) - off * off * size, 0.0)

    def combined(m, turn, row, other, count):
        pick = picked(m, 1)
        mean, spread = moved[m * 3 + turn][0][0, pl.ds(row, 1)], moved[m * 3 + turn][0][0, pl.ds(row + 1, 1)]
        mean2, spread2 = moved[m * 3 + turn][1][pick, pl.ds(other, 1)], moved[m * 3 + turn][1][pick, pl.ds(other + 1, 1)]
        apart = mean - mean2
        variance = (spread + spread2 + apart * apart * (count * 0.5)) / (2.0 * count)
        return (mean + mean2) * 0.5, lax.rsqrt(variance + NORM_EPS)

    def affine(group, start):
        mean, root = group
        new_gain = MOMENTUM * line(gains1, start) + (1.0 - MOMENTUM) * line(gains, start)
        new_shift = MOMENTUM * line(shifts1, start) + (1.0 - MOMENTUM) * line(shifts, start)
        scale = root * new_gain
        return scale, new_shift - mean * scale

    area, out_area = float(big.area), float(big.out_area)
    first_row = BLOCKS * outs
    spare = 2 * big.area

    def key_even(i):
        def put(block, value):
            slope3[at((i * 2 + block) * big.out_area, big.out_area)] = value

        even_cells(field, key_base + i * big.area, big, wide_stage, dense_stage, put)

    def key_side(i, start):
        cells = [slope3[at((i * 2 + block) * big.out_area, big.out_area)] for block in range(2)]
        value = dot(jnp.concatenate(cells, axis=1), wk[3][...])
        for block in range(BLOCKS):
            wide[at(start + block * big.out_area, big.out_area)] = value[:, block * 128 : (block + 1) * 128]

    def key_third(m, c, start):
        value = dot(thin[at(m * outs + c * big.out_area, big.out_area)], wk[2][...])
        for block in range(BLOCKS):
            wide[at(start + block * big.out_area, big.out_area)] = value[:, block * 128 : (block + 1) * 128]

    def key_a(m, c):
        start = m * first_row + c * big.area
        wide[at(start, big.area)] = dot(field[at(key_base + (2 * m + c) * big.area, big.area)], wk[0][...])
        put_moments(m, 0, c * 2, start, big.area, 112)
        start = m * first_row + spare
        key_side(2 * m + c, start)
        for block in range(BLOCKS):
            put_moments(m, 0, 8 + (c * BLOCKS + block) * 2, start + block * big.out_area, big.out_area, 112)

    def key_b(m, c):
        scale, bias = affine(combined(m, 0, c * 2, (1 - c) * 2, area), 0)

        def rows_of(y):
            for k in range(4):
                row = y * 4 + k
                v = wide[at(m * first_row + c * big.area + row * 2 * SIDE, 2 * SIDE)] * scale + bias
                split_planes(gelu_only(v), stage_of[0], planes_of[0], big, c, row, k % 2)

        repeat(0, big.half // 4, rows_of)
        value = dot(patches(planes_of[0], big, c, 1), wk[1][...])
        start = m * first_row + spare + c * big.out_area
        for k in range(big.half):
            wide[pl.ds(start + k * big.half, big.half)] = value[k * big.wide : k * big.wide + big.half]
        put_moments(m, 1, c * 2, start, big.out_area, 112)

    def key_c(m, c):
        scale, bias = affine(combined(m, 1, c * 2, (1 - c) * 2, out_area), CMID)
        for k in range(big.out_area // 112):
            v = wide[at(m * first_row + spare + c * big.out_area + k * 112, 112)] * scale + bias
            thin[at(m * outs + c * big.out_area + k * 112, 112)] = gelu_only(v).astype(bf16)
        start = m * first_row + c * BLOCKS * big.out_area
        key_third(m, c, start)
        for block in range(BLOCKS):
            put_moments(m, 2, (c * BLOCKS + block) * 2, start + block * big.out_area, big.out_area, 112)

    def key_d(m, c):
        start = m * first_row + c * BLOCKS * big.out_area
        side = m * first_row + spare
        key_side(2 * m + c, side)
        parts = []
        for block in range(BLOCKS):
            lanes = 2 * CMID + block * 128
            row, other = (c * BLOCKS + block) * 2, ((1 - c) * BLOCKS + block) * 2
            scale3, bias3 = affine(combined(m, 2, row, other, out_area), lanes)
            scale4, bias4 = affine(combined(m, 0, 8 + row, 8 + other, out_area), lanes + COUT)
            bias = bias3 + bias4
            e = jnp.zeros((8, 128), f32)
            for k in range(big.out_area // 112):
                x3 = wide[at(start + block * big.out_area + k * 112, 112)]
                x4 = wide[at(side + block * big.out_area + k * 112, 112)]
                e += folded(gelu_only(x3 * scale3 + x4 * scale4 + bias))
            parts.append(e.sum(0, keepdims=True) / out_area)
        length = sum(jnp.sum(part * part, axis=1, keepdims=True) for part in parts)
        inverse = lax.rsqrt(length + UNIT_EPS)
        for block in range(BLOCKS):
            r.embed[pl.ds(m * 8 + c * BLOCKS + block, 1)] = parts[block] * inverse

    def key_copy(m, k):
        mine = keys.at[pl.ds(pl.multiple_of((m * devices + me) * 8, 8), 8)]
        return remote(
            r.embed.at[pl.ds(m * 8, 8)], mine, r.key_send.at[m, k], r.key_recv.at[m, k], place(lax.rem(me + k, devices)))

    def share_start(m):
        keys[at((m * devices + me) * 8, 8, 8)] = r.embed[m * 8 : (m + 1) * 8]
        repeat(1, devices, lambda k: key_copy(m, k).start())

    def share_end(m):
        repeat(1, devices, lambda k: key_copy(m, k).wait())

    def core_copy(job):
        return remote(r.parts[job].at[1 - core], r.arrived[job], r.core_send.at[job], r.core_recv.at[job], partner(1))

    def row_copy(job, target, source):
        return remote(
            r.outward[job].at[target], r.inward[job].at[source], r.row_send.at[job, target], r.row_recv.at[job, source],
            (target, core))

    def job_send(job):
        core_copy(job).wait()

        for k in range(1, chips):
            target = lax.rem(chip + k, chips)
            value = r.parts[job][core, target] + r.arrived[job][target]
            r.outward[job][target] = value.astype(r.outward[job].dtype)
            row_copy(job, target, chip).start()

    def job_end(job):
        total = r.parts[job][core, chip] + r.arrived[job][chip]
        for k in range(1, chips):
            row_copy(job, chip, lax.rem(chip + k, chips)).wait_recv()
        for k in range(1, chips):
            total += r.inward[job][lax.rem(chip + k, chips)].astype(f32)
        start = sum(JOB_ROWS[:job])
        r.packed[start : start + JOB_ROWS[job]] = total
        for k in range(1, chips):
            row_copy(job, lax.rem(chip + k, chips), chip).wait_send()

    def fill_head():
        part, third, fourth = r.parts[0], grads[2], grads[3]

        def turn(i):
            for block in range(BLOCKS):
                half, row = block // 2, block % 2
                lanes = slice(block * 128, (block + 1) * 128)
                part[half, i, row * 8 : row * 8 + 8] = third[at(i * 8, 8, 8), lanes]
                part[half, i, 16 + row * 16 : 32 + row * 16] = fourth[at(i * 16, 16), lanes]

        for i in range(chips):
            turn(i)
        core_copy(0).start()

    def fill_spatial():
        part = r.parts[1]
        for tile in range(9):
            lanes = slice(tile * 128, (tile + 1) * 128)
            gy2[lanes] = grads[1][:, lanes].T
        filler = jnp.zeros((8, 128), f32)

        def turn(i):
            top = gy2[at(i * 72, 40, 8)]
            bottom = jnp.concatenate([gy2[at(i * 72 + 40, 32, 8)], filler], axis=0)
            for half in range(2):
                part[half, i, 0:40] = side_by_side(top, bottom, half)
                part[half, i, 40:48] = filler

        for i in range(chips):
            turn(i)
        core_copy(1).start()

    def fill_sums():
        part = r.parts[2]
        column = lax.broadcasted_iota(jnp.int32, (1, 128), 1)
        filler = jnp.zeros((1, 128), f32)
        rows = [gain_sum[:, k * 128 : (k + 1) * 128] for k in range(10)]
        rows += [jnp.where(column == 0, loss_sum[...], 0.0), filler]
        rows += [shift_sum[:, k * 128 : (k + 1) * 128] for k in range(10)] + [filler, filler]
        rows = jnp.concatenate(rows, axis=0)

        def turn(i):
            for half in range(2):
                part[half, i] = rows

        for i in range(chips):
            turn(i)
        core_copy(2).start()

    def fill_reduce():
        part = r.parts[3]
        for tile in range(2):
            lanes = slice(tile * 128, (tile + 1) * 128)
            gy2[lanes] = grads[0][:, lanes].T

        def turn(i):
            for half in range(2):
                part[half, i] = side_by_side(gy2[at(i * 16, 8, 8)], gy2[at(i * 16 + 8, 8, 8)], half)

        for i in range(chips):
            turn(i)
        core_copy(3).start()

    for load in query_loads(0) + key_loads:
        load.start()
    barrier = pltpu.get_barrier_semaphore()
    repeat(1, devices, lambda k: pl.semaphore_signal(
        barrier, inc=1, device_id=place(lax.rem(me + k, devices)), device_id_type=MESH))
    if own:
        current = [r.r0[...], r.s0[...], r.e0[...], r.p0[...]]
        lagged = [r.r1[...], r.s1[...], r.e1[...], r.p1[...]]
        packed_shards([MOMENTUM * old + (1.0 - MOMENTUM) * new for old, new in zip(lagged, current)], r.sent, 0)
        packed_shards(current, r.sent, 1)
        for which in range(2):
            r.gathered[which, core, xy, z] = r.sent[which]
    else:
        for shard, w in zip((r.r0, r.s0, r.e0, r.p0, r.r1, r.s1, r.e1, r.p1), wq + wk):
            w[...] = shard[...]
    if devices > 1:
        pl.semaphore_wait(barrier, devices - 1)
    if own:
        gather_start(0, 0)
    for ref in list(planes_of.values()) + list(back_of.values()) + list(stage_of.values()) + grads + [
        gain_sum, shift_sum, loss_sum, gy2] + [pair[0] for pair in moved]:
        ref[...] = jnp.zeros_like(ref)
    if own:
        gather_end(0, 0)
        gather_start(0, 1)
        gather_start(1, 0)

    def micro_step(m):
        opening, closing = m == 0, m == micros - 1
        base = m * field_rows
        w1, w2, w3, w4 = wq
        w3t, w4t, wt0, wt1 = (r.w3t, r.w4t, r.wt0, r.wt1)
        alive_count = sum(counts[m, i] for i in range(images)).astype(f32)
        count1 = images * big.area + small.area * alive_count
        count2 = images * big.out_area + small.out_area * alive_count

        def living(kind, crop):
            if kind is big:
                return jnp.float32(1.0)
            return jnp.where(lax.rem(crop, slots) < counts[m, lax.div(crop, slots)], 1.0, 0.0)

        def step_of(kind):
            return 112 if kind is big else 144

        def over_big(body, *hooks):
            def turn(c):
                body(big, c, 1)
                for k, (when, hook) in enumerate(hooks):

                    @pl.when(jnp.logical_and(when, c == k))
                    def _():
                        hook()

            repeat(0, big.count, turn)

        def over_small(body):
            body(small, 0, small.count)

        def add_moments(ref, offset, kind, first, count, row0, size, row, where, opener):
            start = offset + row0 + first * size
            if kind is big:

                @pl.when(first == 0)
                def _():
                    vec[row : row + 1] = folded(ref[at(start, opener, 8)]).sum(0, keepdims=True) / opener

            for c in range(count):
                total, square = moments(ref, start + c * size, size, step_of(kind), vec[row : row + 1])
                alive = living(kind, first + c)
                sums[where] += total * alive
                sums[where + 1] += square * alive

        for load in query_loads(m):
            load.wait()

        def even_batch(kind, first, count):
            for c in range(count):
                start = kind.out_row + (first + c) * kind.out_area

                def put(block, value):
                    even[at(start, kind.out_area), block * 128 : (block + 1) * 128] = value

                even_cells(field, base + kind.row + (first + c) * kind.area, kind, wide_stage, dense_stage, put)

        @pl.when(m > 0)
        def _():
            settle(even_stores(m - 1))

        over_big(even_batch)
        over_small(even_batch)

        @pl.when(opening)
        def _():
            for load in key_loads:
                load.wait()
            repeat(0, 2 * micros, key_even)
            if own:
                gather_end(0, 1)
                gather_start(0, 2)
                gather_end(1, 0)
                gather_start(1, 1)
                gather_end(0, 2)
                unpacked(r.gathered, 0, chips, wk, gy2)
            repeat(0, 2, lambda c: key_a(0, c))
            exchange_start(0, 0)
            if own:
                gather_end(1, 1)
                gather_start(1, 2)
            repeat(0, 2, lambda c: key_a(1, c))
            exchange_start(1, 0)
            for load in query_loads(1):
                load.start()
            if own:
                gather_end(1, 2)
                unpacked(r.gathered, 1, chips, wq, gy2)
            w3t[...] = w3[...].T
            w4t[...] = w4[...].T
            wt0[...] = jnp.zeros_like(wt0)
            wt1[...] = jnp.zeros_like(wt1)

            def tap(ky, kx):
                start = (3 * ky + kx) * CMID
                return w2[start : start + CMID, :].T

            wt0[0:128, 0:128] = tap(1, 1)
            wt0[0:128, 128:256] = tap(1, 2)
            wt0[128:256, 128:256] = tap(1, 0)
            wt1[0:128, 0:128] = tap(2, 1)
            wt1[0:128, 128:256] = tap(2, 2)
            wt1[128:256, 128:256] = tap(2, 0)
            wt1[256:384, 0:128] = tap(0, 1)
            wt1[256:384, 128:256] = tap(0, 2)
            wt1[384:512, 128:256] = tap(0, 0)

        sums[...] = jnp.zeros_like(sums)

        def reduce_batch(kind, first, count):
            start = kind.row + first * kind.area
            size = count * kind.area
            a1[at(start, size)] = dot(field[at(base + start, size)], w1[...])
            add_moments(a1, 0, kind, first, count, kind.row, kind.area, 0, 0, 784)

        over_big(reduce_batch, (opening, lambda: exchange_next(0, 0)), (opening, lambda: exchange_next(1, 0)))
        over_small(reduce_batch)
        mean1, root1 = closed(sums[0], sums[1], vec[0:1], count1)
        scale1 = root1 * line(gains, 0)
        bias1 = line(shifts, 0) - mean1 * scale1
        vec[1:2], vec[2:3], vec[3:4], vec[4:5] = mean1, root1, scale1, bias1

        @pl.when(opening)
        def _():
            for k in range(2):
                exchange_end(k, 0)
                repeat(0, 2, lambda c: key_b(k, c))
                exchange_start(k, 1)

        sums[...] = jnp.zeros_like(sums)

        @pl.when(m > 0)
        def _():
            settle(field_stores(m - 1))

        def hidden_batch(kind, first, count):
            scale, bias = vec[3:4], vec[4:5]
            for c in range(count):
                for k in range(kind.half):
                    start = kind.row + (first + c) * kind.area + k * 2 * kind.side
                    v = a1[at(start, 2 * kind.side)] * scale + bias
                    hidden, slope = gelu_pair(v)
                    slope1[at(start, 2 * kind.side)] = slope.astype(bf16)
                    split_planes(hidden, stage_of[kind.ahead], planes_of[kind.ahead], kind, first + c, k, k % 2)

        over_big(hidden_batch, (opening, lambda: exchange_next(0, 1)), (opening, lambda: exchange_next(1, 1)))
        over_small(hidden_batch)

        @pl.when(opening)
        def _():
            for k in range(2):
                exchange_end(k, 1)
                repeat(0, 2, lambda c: key_c(k, c))
                exchange_start(k, 2)

        def spatial_batch(kind, first, count):
            half, lanes = kind.half, kind.wide
            value = dot(patches(planes_of[kind.ahead], kind, first, count), w2[...])
            start = kind.out_row + first * kind.out_area
            for k in range(count * half):
                a2[pl.ds(start + k * half, half)] = value[k * lanes : k * lanes + half]
            add_moments(a2, 0, kind, first, count, kind.out_row, kind.out_area, 0, 16, 784)

        over_big(spatial_batch, (opening, lambda: exchange_next(0, 2)), (opening, lambda: exchange_next(1, 2)))
        over_small(spatial_batch)
        mean2, root2 = closed(sums[16], sums[17], vec[0:1], count2)
        scale2 = root2 * line(gains, CMID)
        bias2 = line(shifts, CMID) - mean2 * scale2
        vec[5:6], vec[6:7], vec[7:8], vec[8:9] = mean2, root2, scale2, bias2

        @pl.when(opening)
        def _():
            for k in range(2):
                exchange_end(k, 2)
                repeat(0, 2, lambda c: key_d(k, c))
                share_start(k)

        def head_product(which, source, weight, kind, first, count):
            start = kind.out_row + first * kind.out_area
            size = count * kind.out_area
            value = dot(source, weight[...])
            for block in range(BLOCKS):
                offset = (which * BLOCKS + block) * outs
                wide[at(offset + start, size)] = value[:, block * 128 : (block + 1) * 128]
            for block in range(BLOCKS):
                offset = (which * BLOCKS + block) * outs
                add_moments(
                    wide, offset, kind, first, count, kind.out_row, kind.out_area,
                    16 + which * 4 + block, which * 8 + block * 2, 784)

        def expand_batch(kind, first, count):
            start = kind.out_row + first * kind.out_area
            size, step = count * kind.out_area, step_of(kind)
            scale, bias = vec[7:8], vec[8:9]
            head_product(1, even[at(start, size)], w4, kind, first, count)
            for k in range(size // step):
                hidden, slope = gelu_pair(a2[at(start + k * step, step)] * scale + bias)
                thin[at(H2 + start + k * step, step)] = hidden.astype(bf16)
                thin[at(SLOPE2 + start + k * step, step)] = slope.astype(bf16)
            head_product(0, thin[at(H2 + start, size)], w3, kind, first, count)

        over_big(expand_batch)
        over_small(expand_batch)
        for which in range(2):
            for block in range(BLOCKS):
                row = which * 4 + block
                where = which * 8 + block * 2
                lanes = 2 * CMID + row * 128
                mean, root = closed(sums[where], sums[where + 1], vec[16 + row : 17 + row], count2)
                scale = root * line(gains, lanes)
                bias = line(shifts, lanes) - mean * scale
                vec[24 + row : 25 + row], vec[32 + row : 33 + row] = mean, root
                vec[40 + row : 41 + row] = scale
                if which == 0:
                    vec[48 + block : 49 + block] = bias
                else:
                    vec[48 + block : 49 + block] += bias

        rows_e, rows_c = r.rows_e, r.rows_c

        def embed_batch(kind, first, count):
            step = step_of(kind)
            for c in range(count):
                start = kind.out_row + (first + c) * kind.out_area
                for block in range(BLOCKS):
                    mean3, mean4 = vec[24 + block : 25 + block], vec[28 + block : 29 + block]
                    scale3, scale4 = vec[40 + block : 41 + block], vec[44 + block : 45 + block]
                    bias = vec[48 + block : 49 + block]
                    zero = jnp.zeros((8, 128), f32)
                    e, s0, s3, s4 = zero, zero, zero, zero
                    for k in range(kind.out_area // step):
                        inside = block * outs + start + k * step
                        x3, x4 = wide[at(A3 + inside, step)], wide[at(AP + inside, step)]
                        value, slope = gelu_pair(x3 * scale3 + x4 * scale4 + bias)
                        slope3[at(inside, step)] = slope.astype(bf16)
                        e += folded(value)
                        s0 += folded(slope)
                        s3 += folded(slope * (x3 - mean3))
                        s4 += folded(slope * (x4 - mean4))
                    row = kind.ahead + first + c
                    for which, value in enumerate((e / kind.out_area, s0, s3, s4)):
                        rows_e[which, block, pl.ds(row, 1)] = value.sum(0, keepdims=True)

        over_big(embed_batch)
        over_small(embed_batch)

        share_end(m)

        def joined(which):
            return jnp.concatenate([rows_e[which, block] for block in range(BLOCKS)], axis=1)

        e = joined(0)
        inverse = lax.rsqrt(jnp.sum(e * e, axis=-1, keepdims=True) + UNIT_EPS)
        row = lax.broadcasted_iota(jnp.int32, (crops, 1), 0)
        owner = jnp.zeros((crops, 1), jnp.int32)
        live = jnp.where(row < images, 1.0, 0.0)
        for i in range(images):
            owner = jnp.where(row == i, i, owner)
            for slot in range(slots):
                here = row == images + i * slots + slot
                owner = jnp.where(here, i, owner)
                live = jnp.where(here, jnp.where(slot < counts[m, i], 1.0, 0.0), live)
        key_rows = [
            jnp.concatenate(
                [keys[pl.ds(m * devices * 8 + c * BLOCKS + block, devices, stride=8)] for c in range(images)], axis=0)
            for block in range(BLOCKS)
        ]
        key_high, key_low = two_parts(jnp.concatenate(key_rows, axis=1))
        logits = lax.dot_general(
            jnp.concatenate(two_parts(e * inverse), axis=0), jnp.concatenate([key_high, key_low], axis=0),
            (((1,), (1,)), ((), ())), preferred_element_type=f32)
        count = devices * images
        logits = logits[0:crops] + logits[crops:]
        logits = (logits[:, 0:count] + logits[:, count:]) / TEMP
        top = jnp.max(logits, axis=-1, keepdims=True)
        powers = jnp.exp(logits - top)
        total = jnp.sum(powers, axis=-1, keepdims=True)
        column = lax.broadcasted_iota(jnp.int32, logits.shape, 1)
        mine = column == owner * devices + me
        chosen = jnp.sum(jnp.where(mine, logits, 0.0), axis=-1, keepdims=True)
        ce = (top + jnp.log(total) - chosen) * live
        loss_sum[...] += jnp.sum(ce, axis=0, keepdims=True)
        toward = (powers / total - jnp.where(mine, 1.0, 0.0)) * (live / TEMP)
        back = dot(jnp.concatenate(two_parts(toward), axis=0), jnp.concatenate([key_high, key_low], axis=1))
        back = back[0:crops] + back[crops:]
        back = back[:, 0:COUT] + back[:, COUT:]
        de = inverse * back - e * (inverse * inverse * inverse * jnp.sum(e * back, axis=-1, keepdims=True))
        de = de * jnp.where(row < images, 1.0 / big.out_area, 1.0 / small.out_area)
        sum0 = jnp.sum(de * joined(1), axis=0, keepdims=True)
        for which in range(2):
            reach = jnp.sum(de * joined(2 + which), axis=0, keepdims=True)
            for block in range(BLOCKS):
                row = which * 4 + block
                here = slice(block * 128, (block + 1) * 128)
                lanes = slice(2 * CMID + row * 128, 2 * CMID + (row + 1) * 128)
                mean, root, scale = vec[24 + row : 25 + row], vec[32 + row : 33 + row], vec[40 + row : 41 + row]
                along = reach[:, here] * root
                gain_sum[:, lanes] += along
                shift_sum[:, lanes] += sum0[:, here]
                tilt = scale * root * along / count2
                vec[52 + row : 53 + row] = tilt
                vec[60 + row : 61 + row] = scale * sum0[:, here] / count2 - tilt * mean
                rows_c[which, block] = de[:, here] * scale

        sums[...] = jnp.zeros_like(sums)
        d3, dp = r.d3, r.dp

        def head_back(kind, first, count):
            start = kind.out_row + first * kind.out_area
            size, step = count * kind.out_area, step_of(kind)
            for which, store in ((0, d3), (1, dp)):
                for block in range(BLOCKS):
                    lanes = slice(block * 128, (block + 1) * 128)
                    where = which * 4 + block
                    for c in range(count):
                        rise = rows_c[which, block, pl.ds(kind.ahead + first + c, 1)]
                        alive = living(kind, first + c)
                        tilt, level = vec[52 + where : 53 + where] * alive, vec[60 + where : 61 + where] * alive
                        for k in range(kind.out_area // step):
                            inside = c * kind.out_area + k * step
                            here = block * outs + start + inside
                            x = wide[at(which * BLOCKS * outs + here, step)]
                            grad = slope3[at(here, step)].astype(f32) * rise - (x * tilt + level)
                            store[inside : inside + step, lanes] = grad.astype(bf16)
            grad3, gradp = d3[0:size], dp[0:size]
            gy2[at(start, size)] = dot(grad3, w3t[...])
            gradient = dot(gradp, w4t[...])
            grads[2][...] += dot_rows(thin[at(H2 + start, size)], grad3)
            grads[3][...] += dot_rows(even[at(start, size)], gradp)
            even[at(start, size)] = gradient.astype(bf16)
            mean = vec[5:6]
            level, reach = jnp.zeros((8, 128), f32), jnp.zeros((8, 128), f32)
            for k in range(size // step):
                here = at(start + k * step, step)
                gy = gy2[here] * thin[at(SLOPE2 + start + k * step, step)].astype(f32)
                gy2[here] = gy
                level += folded(gy)
                reach += folded(gy * (a2[here] - mean))
            sums[0] += level
            sums[1] += reach

        over_big(head_back)
        over_small(head_back)
        for copy in even_stores(m):
            copy.start()

        if own:

            @pl.when(closing)
            def _():
                fill_head()

        def norm_back(where, lanes, count):
            mean, root, scale = vec[where : where + 1], vec[where + 1 : where + 2], vec[where + 2 : where + 3]
            level = sums[0].sum(0, keepdims=True)
            along = sums[1].sum(0, keepdims=True) * root
            gain_sum[:, lanes] += along
            shift_sum[:, lanes] += level
            tilt = scale * root * along / count
            vec[68:69] = scale
            vec[69:70] = tilt
            vec[70:71] = scale * level / count - tilt * mean

        norm_back(5, slice(CMID, 2 * CMID), count2)
        sums[...] = jnp.zeros_like(sums)

        def spatial_back(kind, first, count):
            half, lanes, side, step = kind.half, kind.wide, kind.side, step_of(kind)
            out_start = kind.out_row + first * kind.out_area
            for c in range(count):
                alive = living(kind, first + c)
                tilt, level = vec[69:70] * alive, vec[70:71] * alive
                for k in range(kind.out_area // step):
                    here = at(out_start + c * kind.out_area + k * step, step)
                    gy2[here] = gy2[here] * vec[68:69] - (a2[here] * tilt + level)
            column = lax.broadcasted_iota(jnp.int32, (lanes, 128), 0)
            store = back_of[kind.ahead]
            for k in range(count * half):
                here = jnp.where(column < half, gy2[pl.ds(out_start + k * half, lanes)], 0.0)
                following = jnp.where(column < half - 1, gy2[pl.ds(out_start + k * half + 1, lanes)], 0.0)
                store[first + k // half, k % half, :, 0:128] = here.astype(bf16)
                store[first + k // half, k % half, :, 128:256] = following.astype(bf16)
            size = count * half * lanes
            near = store[pl.ds(first, count), 0:half].reshape(size, 256)
            beyond = store[pl.ds(first, count), 1 : half + 1].reshape(size, 256)
            upper_rows = dot(near, wt0[...])
            lower_rows = dot(jnp.concatenate([near, beyond], axis=1), wt1[...])
            start = kind.row + first * kind.area
            for k in range(count * half):
                here = slice(k * lanes, k * lanes + half)
                row = start + k * 2 * side
                for odd, value in ((0, upper_rows), (1, lower_rows)):
                    wide[pl.ds(row + odd * side, half, stride=2)] = value[here, 0:128]
                    wide[pl.ds(row + odd * side + 1, half, stride=2)] = value[here, 128:256]
            grads[1][...] += dot_rows(near[:, 0:128], patches(planes_of[kind.ahead], kind, first, count))
            mean = vec[1:2]
            level, reach = jnp.zeros((8, 128), f32), jnp.zeros((8, 128), f32)
            for k in range(count * kind.area // step):
                here = at(start + k * step, step)
                gy = wide[here] * slope1[here].astype(f32)
                wide[here] = gy
                level += folded(gy)
                reach += folded(gy * (a1[here] - mean))
            sums[0] += level
            sums[1] += reach

        def job_hooks(*jobs):
            def sends(some):
                return lambda: [job_send(job) for job in some]

            return [(closing, sends(some)) for some in jobs] if own else []

        over_big(spatial_back, *job_hooks((0,)))
        over_small(spatial_back)
        norm_back(1, slice(0, CMID), count1)

        if own:

            @pl.when(closing)
            def _():
                fill_spatial()
                fill_sums()

        def reduce_back(kind, first, count):
            step = step_of(kind)
            size = count * kind.area
            start = kind.row + first * kind.area
            rise = vec[68:69]
            for c in range(count):
                alive = living(kind, first + c)
                tilt, level = vec[69:70] * alive, vec[70:71] * alive
                for k in range(kind.area // step):
                    here = at(start + c * kind.area + k * step, step)
                    grad = wide[here] * rise - (a1[here] * tilt + level)
                    slope1[here] = grad.astype(bf16)
            grads[0][...] += dot_rows(slope1[at(start, size)], field[at(base + start, size)])

        over_big(reduce_back, *job_hooks((1,), (2,)))
        over_small(reduce_back)

        for copy in field_stores(m):
            copy.start()

    repeat(0, micros, micro_step)
    if own:
        fill_reduce()
        job_end(0)
        job_send(3)
        for job in range(1, 4):
            job_end(job)
    settle(even_stores(micros - 1))
    settle(field_stores(micros - 1))


def step_pass(axes, own, slots, big, small, key, counts, mask, current, lagged, vectors):
    chips, cores = axes
    devices = chips * cores
    widths = stage_widths(devices)
    micros, images = counts.shape
    one, two = field_pair(images, slots)
    rows = two.row + two.count * two.area
    outs = two.out_row + two.count * two.out_area
    crops = images * (1 + slots)
    vmem = pl.BlockSpec(memory_space=pltpu.VMEM)
    smem = pl.BlockSpec(memory_space=pltpu.SMEM)
    hbm = pl.BlockSpec(memory_space=pl.ANY)
    weights = [(CIN, CMID), (9 * CMID, CMID), (CMID, COUT), (CIN, COUT)]
    totals = dict(
        g1=(CMID, CIN), g2=(CMID, 9 * CMID), g3=(CMID, COUT), g4=(CIN, COUT),
        gain_sum=(1, NORMS), shift_sum=(1, NORMS), loss_sum=(1, 1))
    r0, s0, e0, p0 = ((w, vmem) for w in current)
    r1, s1, e1, p1 = ((w, vmem) for w in lagged)
    gains, shifts, gains1, shifts1 = ((v, vmem) for v in vectors)
    inputs = dict(
        big_hbm=(big, hbm), small_hbm=(small, hbm), key_hbm=(key, hbm), counts=(counts, smem), mask=(mask, smem),
        r0=r0, s0=s0, e0=e0, p0=p0, r1=r1, s1=s1, e1=e1, p1=p1, gains=gains, shifts=shifts, gains1=gains1, shifts1=shifts1)
    outputs = dict(
        da_big=(jax.ShapeDtypeStruct((micros, two.row, CMID), bf16), hbm),
        da_small=(jax.ShapeDtypeStruct((micros, rows - two.row, CMID), bf16), hbm),
        even_big=(jax.ShapeDtypeStruct((micros, two.out_row, CIN), bf16), hbm),
        even_small=(jax.ShapeDtypeStruct((micros, outs - two.out_row, CIN), bf16), hbm),
        w1q=(jax.ShapeDtypeStruct((CIN, CMID), bf16), vmem))
    if own:
        outputs |= dict(packed=(jax.ShapeDtypeStruct((sum(JOB_ROWS), 128), f32), vmem))
    else:
        outputs |= {n: (jax.ShapeDtypeStruct(shape, f32), vmem) for n, shape in totals.items()}

    def buf(dtype, *shape):
        return pltpu.VMEM(shape, dtype)

    def dma(*shape):
        return pltpu.SemaphoreType.DMA(shape)

    scratch = dict(
        field=buf(bf16, rows + 2 * micros * one.area, CIN),
        a1=buf(f32, rows, 128), slope1=buf(bf16, rows, 128),
        planes_big=buf(bf16, 2, one.count, one.half + 1, one.wide, 384),
        planes_small=buf(bf16, 2, two.count, two.half + 1, two.wide, 384),
        a2=buf(f32, outs, 128), thin=buf(bf16, 2 * outs, 128), even=buf(bf16, outs, CIN),
        wide=buf(f32, 2 * BLOCKS * outs, 128), slope3=buf(bf16, BLOCKS * outs, 128),
        back_big=buf(bf16, one.count, one.half + 1, one.wide, 256),
        back_small=buf(bf16, two.count, two.half + 1, two.wide, 256),
        gy2=buf(f32, outs + 16, 128), stage_big=buf(f32, 2, 2, 80, 128), stage_small=buf(f32, 2, 2, 48, 128),
        wide_stage=buf(f32, 8, SIDE, 128), dense_stage=buf(f32, 2, one.out_area, 128),
        d3=buf(bf16, two.count * two.out_area, COUT), dp=buf(bf16, two.count * two.out_area, COUT),
        w3t=buf(bf16, COUT, CMID), w4t=buf(bf16, COUT, CIN),
        wt0=buf(bf16, 256, 256), wt1=buf(bf16, 512, 256), sums=buf(f32, 18, 8, 128), vec=buf(f32, 80, 128),
        rows_e=buf(f32, 4, BLOCKS, crops, 128), rows_c=buf(f32, 2, BLOCKS, crops, 128),
        keys=buf(f32, devices * 16, 128), embed=buf(f32, 16, 128),
        moved=[[buf(f32, 1 << width, n, 128) for width in widths] for _ in range(micros) for n in TURN_ROWS],
        key_load=dma(2 * micros), query_load=dma(micros, 2), store=dma(micros, 4),
        move_send=dma(3 * micros, 2, 1 << widths[0]), move_recv=dma(3 * micros, 2, 1 << widths[0]),
        key_send=dma(micros, devices), key_recv=dma(micros, devices),
    )
    first, second, third, fourth = (buf(bf16, *shape) for shape in weights)
    scratch |= dict(w2q=second, w3q=third, w4q=fourth, w1k=first, w2k=second, w3k=third, w4k=fourth)
    wires = (bf16, bf16, f32, f32)
    if own:
        scratch |= {n: buf(f32, *shape) for n, shape in totals.items()}
        scratch |= dict(
            sent=buf(bf16, 2, PACK, 128), gathered=buf(bf16, 2, 2, 4, 4, PACK, 128),
            parts=[buf(f32, 2, chips, n, 128) for n in JOB_ROWS], arrived=[buf(f32, chips, n, 128) for n in JOB_ROWS],
            outward=[buf(t, chips, n, 128) for n, t in zip(JOB_ROWS, wires)],
            inward=[buf(t, chips, n, 128) for n, t in zip(JOB_ROWS, wires)],
            gather_send=dma(2, 3, 3), gather_recv=dma(2, 3, 3), core_send=dma(4), core_recv=dma(4),
            row_send=dma(4, chips), row_recv=dma(4, chips),
        )
    names = list(inputs) + list(outputs) + list(scratch)
    out = pl.pallas_call(
        functools.partial(step_kernel, axes, own, slots, names),
        out_shape=[shape for shape, _ in outputs.values()],
        in_specs=[spec for _, spec in inputs.values()],
        out_specs=[spec for _, spec in outputs.values()],
        scratch_shapes=list(scratch.values()),
        compiler_params=pltpu.CompilerParams(vmem_limit_bytes=63 * 2**20, collective_id=0, has_side_effects=True),
        name="step",
    )(*[array for array, _ in inputs.values()])
    return types.SimpleNamespace(**dict(zip(outputs, out)))


def write_sums(packed, loss, reduce_out, spatial_out, expand_out, shortcut_out, gains, shifts):
    reduce_out[0:8] = packed[120:128, 0:64]
    reduce_out[8:16] = packed[120:128, 64:128]
    rows = jnp.concatenate([packed[48:88], jnp.zeros((88, 128), f32)], axis=0).T
    spatial_out[...] = jnp.concatenate([rows[0:64, 0:40], rows[64:128, 0:32]], axis=1)
    for block in range(2):
        lanes = slice(block * 128, (block + 1) * 128)
        expand_out[:, lanes] = packed[block * 8 : block * 8 + 8]
        shortcut_out[:, lanes] = packed[16 + block * 16 : 32 + block * 16]
    for row in range(NORMS // 128):
        gains[pl.ds(row * 128, 128)] = packed[96 + row]
        shifts[pl.ds(row * 128, 128)] = packed[108 + row]
    loss[...] = packed[106:107, 0:1]


def field_kernel(own, fields, da_big, da_small, even_big, even_small, weight, *refs):
    big, small = fields
    packed, refs = (refs[0], refs[1:]) if own else (None, refs)
    big_out, small_out = refs[:2]
    raised, cells = refs[-2:]
    part = pl.program_id(1)

    @pl.when(jnp.logical_and(pl.program_id(0) == 0, part == 0))
    def _():
        raised[...] = jnp.zeros_like(raised)
        if own:
            write_sums(packed, *refs[2:-2])

    def gradient(kind, count, da, shortcut, out):
        half, side = kind.half, kind.side
        whole = lax.dot_general(da[...], weight[...], (((1,), (1,)), ((), ())), preferred_element_type=f32)
        for block in range(2):
            lanes = slice(block * 128, (block + 1) * 128)
            cells[block, 0 : count * kind.out_area] = shortcut[:, lanes].astype(f32)
        for k in range(count * half):
            row = k * 2 * side
            for block in range(2):
                lanes = slice(block * 128, (block + 1) * 128)
                slot = k % 4 * 2 + block
                raised[slot, pl.ds(0, half, stride=2)] = cells[block, k * half : (k + 1) * half]
                upper = whole[row : row + side, lanes] + raised[slot, 0:side]
                both = jnp.concatenate([upper, whole[row + side : row + 2 * side, lanes]], axis=0)
                out[row : row + 2 * side, lanes] = both.astype(bf16)

    @pl.when(part < big.count)
    def _():
        gradient(big, 1, da_big, even_big, big_out)

    @pl.when(part >= big.count)
    def _():
        gradient(small, small.count // 2, da_small, even_small, small_out)


def field_pass(own, slots, images, step):
    micros = step.da_big.shape[0]
    fields = field_pair(images, slots)
    big, small = fields
    pair = small.count // 2
    whole = pl.BlockSpec(memory_space=pltpu.VMEM)

    def large(rows, lanes):
        return pl.BlockSpec((None, rows, lanes), lambda m, j: (m, jnp.minimum(j, big.count - 1), 0))

    def little(rows, lanes):
        return pl.BlockSpec((None, rows, lanes), lambda m, j: (m, jnp.maximum(j - big.count, 0), 0))

    outs = [jax.ShapeDtypeStruct((micros, big.count * big.area, CIN), bf16), jax.ShapeDtypeStruct((micros, small.count * small.area, CIN), bf16)]
    sums = [(1, 1), (16, 64), (64, 72), (8, 256), (16, 256), (NORMS,), (NORMS,)] if own else []
    return pl.pallas_call(
        functools.partial(field_kernel, own, fields),
        grid=(micros, big.count + 2),
        out_shape=outs + [jax.ShapeDtypeStruct(shape, f32) for shape in sums],
        in_specs=[
            large(big.area, CMID), little(pair * small.area, CMID), large(big.out_area, CIN),
            little(pair * small.out_area, CIN), whole,
        ] + [whole] * own,
        out_specs=[large(big.area, CIN), little(pair * small.area, CIN)] + [whole] * len(sums),
        scratch_shapes=[pltpu.VMEM((8, SIDE, 128), f32), pltpu.VMEM((2, pair * small.out_area if pair * small.out_area > big.out_area else big.out_area, 128), f32)],
        compiler_params=pltpu.CompilerParams(vmem_limit_bytes=58 * 2**20, dimension_semantics=("arbitrary", "arbitrary")),
        name="field",
    )(step.da_big, step.da_small, step.even_big, step.even_small, step.w1q, *([step.packed] if own else []))


def gather_weights(shards):
    rows = [lax.all_gather(part, "dp", axis=0, tiled=True) for part in shards]
    return [lax.all_gather(part, "fsdp", axis=1, tiled=True) for part in rows]


def per_device(axes, *args):
    query_global, small_crop_query, small_count, key_global, shuffle_mask = args[:5]
    current, lagged = args[5:9], args[11:15]
    vectors = (args[9], args[10], args[15], args[16])
    micros = query_global.shape[0]
    slots = small_crop_query.shape[2]
    chips, cores = axes
    own = chips == 16 and cores == 2
    if own:
        current = [w.T if i == 1 else w for i, w in enumerate(current)]
        lagged = [w.T if i == 1 else w for i, w in enumerate(lagged)]
    else:
        fresh = [MOMENTUM * old + (1.0 - MOMENTUM) * new for old, new in zip(lagged, current)]
        current = gather_weights([w.astype(bf16) for w in current])
        lagged = gather_weights([w.astype(bf16) for w in fresh])
    out = step_pass(
        axes, own, slots, query_global.reshape(micros, -1, CIN), small_crop_query.reshape(micros, -1, CIN),
        key_global.reshape(micros, -1, CIN), small_count, shuffle_mask, current, lagged, vectors,
    )
    big_out, small_out, *sums = field_pass(own, slots, query_global.shape[1], out)
    fields = (big_out.reshape(query_global.shape), small_out.reshape(small_crop_query.shape))
    if own:
        loss, first, second, third, fourth, gains_grad, shifts_grad = sums
        return (loss.reshape(()), *fields, first, second.T, third, fourth, gains_grad, shifts_grad)
    totals = (out.g1.T, out.g2.T, out.g3, out.g4)
    summed = lax.psum_scatter(totals, "dp", scatter_dimension=0, tiled=True)
    owned = lax.psum_scatter(summed, "fsdp", scatter_dimension=1, tiled=True)
    sums = lax.psum((out.loss_sum, out.gain_sum, out.shift_sum), ("dp", "fsdp"))
    return (sums[0].reshape(()), *fields, *owned, sums[1].reshape(NORMS), sums[2].reshape(NORMS))


def solution(mesh):
    whole, split = P(), P("dp", "fsdp")
    images, crops = P(None, ("dp", "fsdp"), None, None, None), P(None, ("dp", "fsdp"), None, None, None, None)
    axes = (mesh.shape["dp"], mesh.shape["fsdp"])
    return jax.shard_map(
        functools.partial(per_device, axes),
        mesh=mesh,
        in_specs=(images, crops, P(None, ("dp", "fsdp")), images, whole)
        + (split,) * 4 + (whole,) * 2 + (split,) * 4 + (whole,) * 2,
        out_specs=(whole, images, crops) + (split,) * 4 + (whole,) * 2,
        check_vma=False,
    )
```

```python
import functools
import types
import jax
import jax.numpy as jnp
from jax import lax
from jax.experimental import pallas as pl
from jax.experimental.pallas import tpu as pltpu
from jax.sharding import PartitionSpec as P

f32, bf16 = jnp.float32, jnp.bfloat16
CIN, CMID, COUT, NORMS = 256, 128, 512, 1280
SIDE, SMALL = 56, 24
BLOCKS = COUT // 128
TEMP, NORM_EPS, UNIT_EPS = 0.2, 1e-05, 1e-06
ROOT_HALF = 0.7071067811865476
DENSITY = 0.3989422804014327


class Field:
    def __init__(self, count, side, row, out_row, ahead):
        self.count, self.side, self.row, self.out_row = count, side, row, out_row
        self.ahead = ahead
        self.half = side // 2
        self.wide = -(-self.half // 16) * 16
        self.area, self.out_area = side * side, (side // 2) ** 2


def field_pair(images, slots):
    big = Field(images, SIDE, 0, 0, 0)
    small = Field(images * slots, SMALL, images * big.area, images * big.out_area, images)
    return big, small


def at(start, size, align=16):
    if isinstance(start, int):
        return pl.ds(start, size)
    return pl.ds(pl.multiple_of(start, align), size)


def folded(x):
    return x.reshape(x.shape[0] // 8, 8, x.shape[1]).sum(0)


def dot(a, b):
    return jnp.dot(a, b, preferred_element_type=f32)


def dot_rows(a, b):
    return lax.dot_general(a, b, (((0,), (0,)), ((), ())), preferred_element_type=f32)


def gelu_pair(v):
    share = 0.5 + 0.5 * lax.erf(v * ROOT_HALF)
    return v * share, share + v * (DENSITY * jnp.exp(v * v * -0.5))


def gelu_only(v):
    return v * (0.5 + 0.5 * lax.erf(v * ROOT_HALF))


MOMENTUM = 0.999
MESH = pl.DeviceIdType.MESH
PACK = 96
JOB_ROWS = (48, 48, 24, 8)
TURN_ROWS = (24, 8, 16)


def line(vector, start):
    return vector[pl.ds(start, 128)].reshape(1, 128)


def two_parts(x):
    high = x.astype(bf16)
    return high, (x - high.astype(f32)).astype(bf16)


def moments(ref, start, size, step, pivot):
    total = jnp.zeros((8, 128), f32)
    square = jnp.zeros((8, 128), f32)
    for k in range(size // step):
        x = ref[at(start + k * step, step, 8)] - pivot
        total += folded(x)
        square += folded(x * x)
    return total, square


def closed(total, square, pivot, count):
    off = total.sum(0, keepdims=True) / count
    spread = jnp.maximum(square.sum(0, keepdims=True) / count - off * off, 0.0)
    return pivot + off, lax.rsqrt(spread + NORM_EPS)


def patches(planes, field, first, crops):
    size = crops * field.half * field.wide
    here = pl.ds(first, crops)
    above = planes[1, here, 0 : field.half].reshape(size, 3 * CMID)
    level = planes[0, here, 0 : field.half].reshape(size, 3 * CMID)
    below = planes[1, here, 1 : field.half + 1].reshape(size, 3 * CMID)
    return jnp.concatenate([above, level, below], axis=1)


def split_planes(hidden, stage, planes, field, crop, row, slot):
    side, wide = field.side, field.wide
    for odd in range(2):
        stage[slot, odd, 8 : 8 + side] = hidden[odd * side : (odd + 1) * side]
    for odd in range(2):
        for tap in range(3):
            column = stage[slot, odd, pl.ds(7 + tap, wide, stride=2)]
            planes[odd, crop, row + odd, :, tap * CMID : (tap + 1) * CMID] = column.astype(bf16)


def even_cells(source, base, field, wide_stage, dense_stage, put):
    side, half = field.side, field.half
    for y in range(half):
        for block in range(CIN // 128):
            slot = y % 4 * 2 + block
            x = source[at(base + y * 2 * side, 2 * side), block * 128 : (block + 1) * 128]
            wide_stage[slot, 0:side] = x.astype(f32)[0:side]
            dense_stage[block, y * half : (y + 1) * half] = wide_stage[slot, pl.ds(0, half, stride=2)]
    for block in range(CIN // 128):
        put(block, dense_stage[block, 0 : field.out_area].astype(bf16))


def flipped(index, mask):
    bit = 1
    while bit <= mask:
        if mask & bit:
            index = index + bit * (1 - 2 * lax.rem(lax.div(index, bit), 2))
        bit *= 2
    return index


def side_by_side(top, bottom, core):
    left = lax.broadcasted_iota(jnp.int32, top.shape, 1) < 64
    if core == 0:
        return jnp.where(left, top, pltpu.roll(bottom, 64, 1))
    return jnp.where(left, pltpu.roll(top, 64, 1), bottom)


def packed_shards(shards, store, which):
    first, second, third, fourth = shards
    zero = jnp.zeros
    second = jnp.concatenate([second, zero((second.shape[0], 56), f32)], axis=1)
    second = jnp.concatenate([second, zero((64, 128), f32)], axis=0).T[0:80, 0:64]
    rows = [jnp.concatenate([first[0:8], first[8:16]], axis=1), jnp.concatenate([second[0:40], second[40:80]], axis=1)]
    rows += [third[:, 0:128], third[:, 128:256], fourth[:, 0:128], fourth[:, 128:256]]
    store[which] = jnp.concatenate(rows, axis=0).astype(bf16)


def unpacked(gathered, which, chips, weights, stage):
    w1, w2, w3, w4 = weights

    def turn(i, _):
        z, xy = lax.div(i, 4), lax.rem(i, 4)
        ours = [gathered[which, core, xy, z] for core in range(2)]
        first, second = (rows[0:48].astype(f32) for rows in ours)
        left = lax.broadcasted_iota(jnp.int32, (48, 128), 1) < 64
        top = jnp.where(left, first, pltpu.roll(second, 64, 1))
        bottom = jnp.where(left, pltpu.roll(first, 64, 1), second)
        w1[at(i * 16, 16)] = jnp.concatenate([top[0:8], bottom[0:8]], axis=0).astype(bf16)
        stage[at(i * 72, 40, 8)] = top[8:48]
        stage[at(i * 72 + 40, 32, 8)] = bottom[8:40]
        for block in range(BLOCKS):
            start = 64 + block % 2 * 16
            w4[at(i * 16, 16), block * 128 : (block + 1) * 128] = ours[block // 2][start : start + 16]
        return 0

    lax.fori_loop(0, chips, turn, 0)
    w2[...] = stage[0 : 9 * CMID].astype(bf16)

    def pairs(i, _):
        z, xy = lax.div(i, 2), lax.rem(i, 2) * 2
        for block in range(BLOCKS):
            rows = slice(block % 2 * 8, block % 2 * 8 + 8)
            both = [gathered[which, block // 2, xy + k, z, 48:64].astype(f32)[rows] for k in range(2)]
            w3[at(i * 16, 16), block * 128 : (block + 1) * 128] = jnp.concatenate(both, axis=0).astype(bf16)
        return 0

    lax.fori_loop(0, chips // 2, pairs, 0)


def stage_widths(devices):
    bits = devices.bit_length() - 1
    return (bits + 1) // 2, bits // 2


def step_kernel(axes, own, slots, names, *refs):
    r = types.SimpleNamespace(**dict(zip(names, refs)))
    chips, cores = axes
    devices = chips * cores
    widths = stage_widths(devices)
    shifts_of = (0, widths[0])
    counts, mask = r.counts, r.mask
    micros, images = counts.shape
    fields = field_pair(images, slots)
    big, small = fields
    crops = images * (1 + slots)
    field_rows = small.row + small.count * small.area
    outs = small.out_row + small.count * small.out_area
    chip, core = lax.axis_index("dp"), lax.axis_index("fsdp")
    me = chip * cores + core
    xy, z = lax.rem(chip, 4), lax.div(chip, 4)
    field, a1, slope1, a2, even, wide, slope3 = (r.field, r.a1, r.slope1, r.a2, r.even, r.wide, r.slope3)
    thin, gy2, vec, sums, keys = (r.thin, r.gy2, r.vec, r.sums, r.keys)
    planes_of = {0: r.planes_big, images: r.planes_small}
    back_of = {0: r.back_big, images: r.back_small}
    stage_of = {0: r.stage_big, images: r.stage_small}
    wide_stage, dense_stage = r.wide_stage, r.dense_stage
    wq = [r.w1q, r.w2q, r.w3q, r.w4q]
    wk = [r.w1k, r.w2k, r.w3k, r.w4k]
    grads = [r.g1, r.g2, r.g3, r.g4]
    gains, shifts, gains1, shifts1 = (r.gains, r.shifts, r.gains1, r.shifts1)
    gain_sum, shift_sum, loss_sum = r.gain_sum, r.shift_sum, r.loss_sum
    A3, AP, H2, SLOPE2 = 0, BLOCKS * outs, 0, outs

    def place(device):
        return (lax.div(device, cores), lax.rem(device, cores))

    def remote(source, target, send, receive, device):
        return pltpu.make_async_remote_copy(
            src_ref=source, dst_ref=target, send_sem=send, recv_sem=receive, device_id=device, device_id_type=MESH)

    def repeat(first, last, body):
        lax.fori_loop(first, last, lambda k, _: (body(k), 0)[1], 0)

    key_base = field_rows
    key_loads = [
        pltpu.make_async_copy(
            r.key_hbm.at[i // 2, pl.ds(i % 2 * big.area, big.area)],
            field.at[pl.ds(key_base + i * big.area, big.area)], r.key_load.at[i])
        for i in range(2 * micros)
    ]

    def query_loads(m):
        return [
            pltpu.make_async_copy(
                r.big_hbm.at[m], field.at[pl.ds(m * field_rows, small.row)], r.query_load.at[m, 0]),
            pltpu.make_async_copy(
                r.small_hbm.at[m], field.at[pl.ds(m * field_rows + small.row, field_rows - small.row)],
                r.query_load.at[m, 1]),
        ]

    def field_stores(m):
        return [
            pltpu.make_async_copy(slope1.at[pl.ds(0, small.row)], r.da_big.at[m], r.store.at[m, 0]),
            pltpu.make_async_copy(slope1.at[pl.ds(small.row, field_rows - small.row)], r.da_small.at[m], r.store.at[m, 1]),
        ]

    def even_stores(m):
        return [
            pltpu.make_async_copy(even.at[pl.ds(0, small.out_row)], r.even_big.at[m], r.store.at[m, 2]),
            pltpu.make_async_copy(even.at[pl.ds(small.out_row, outs - small.out_row)], r.even_small.at[m], r.store.at[m, 3]),
        ]

    def settle(copies):
        for copy in copies:
            copy.wait()

    def partner(flip):
        return place(flipped(me, flip))

    def gather_copies(which, stage):
        if stage == 0:
            here = r.gathered.at[which, core, xy, z]
            flips = [8 * k for k in range(1, chips // 4)]
        elif stage == 1:
            here = r.gathered.at[which, core, xy]
            flips = [2 * k for k in range(1, 4)]
        else:
            here = r.gathered.at[which, core]
            flips = [1]
        return [
            remote(here, here, r.gather_send.at[which, stage, k], r.gather_recv.at[which, stage, k], partner(flip))
            for k, flip in enumerate(flips)
        ]

    def gather_start(which, stage):
        for copy in gather_copies(which, stage):
            copy.start()

    def gather_end(which, stage):
        for copy in gather_copies(which, stage):
            copy.wait()

    moved = r.moved

    def exchange_copies(m, turn, stage):
        ref, which = moved[m * 3 + turn][stage], m * 3 + turn
        return [
            remote(
                ref.at[0], ref.at[k], r.move_send.at[which, stage, k], r.move_recv.at[which, stage, k],
                partner(k << shifts_of[stage]))
            for k in range(1, 1 << widths[stage])
        ]

    def picked(m, stage):
        return lax.rem(lax.div(jnp.bitwise_xor(mask[m, 0], mask[m, 1]), 1 << shifts_of[stage]), 1 << widths[stage])

    def exchange_start(m, turn):
        for copy in exchange_copies(m, turn, 0):
            copy.start()

    def exchange_next(m, turn):
        for copy in exchange_copies(m, turn, 0):
            copy.wait()
        first, second = moved[m * 3 + turn]
        second[0] = first[picked(m, 0)]
        for copy in exchange_copies(m, turn, 1):
            copy.start()

    def exchange_end(m, turn):
        for copy in exchange_copies(m, turn, 1):
            copy.wait()

    def put_moments(m, turn, row, start, size, step):
        pivot = folded(wide[at(start, step, 8)]).sum(0, keepdims=True) / step
        total, square = moments(wide, start, size, step, pivot)
        off = total.sum(0, keepdims=True) / size
        moved[m * 3 + turn][0][0, pl.ds(row, 1)] = pivot + off
        moved[m * 3 + turn][0][0, pl.ds(row + 1, 1)] = jnp.maximum(square.sum(0, keepdims=True) - off * off * size, 0.0)

    def combined(m, turn, row, other, count):
        pick = picked(m, 1)
        mean, spread = moved[m * 3 + turn][0][0, pl.ds(row, 1)], moved[m * 3 + turn][0][0, pl.ds(row + 1, 1)]
        mean2, spread2 = moved[m * 3 + turn][1][pick, pl.ds(other, 1)], moved[m * 3 + turn][1][pick, pl.ds(other + 1, 1)]
        apart = mean - mean2
        variance = (spread + spread2 + apart * apart * (count * 0.5)) / (2.0 * count)
        return (mean + mean2) * 0.5, lax.rsqrt(variance + NORM_EPS)

    def affine(group, start):
        mean, root = group
        new_gain = MOMENTUM * line(gains1, start) + (1.0 - MOMENTUM) * line(gains, start)
        new_shift = MOMENTUM * line(shifts1, start) + (1.0 - MOMENTUM) * line(shifts, start)
        scale = root * new_gain
        return scale, new_shift - mean * scale

    area, out_area = float(big.area), float(big.out_area)
    first_row = BLOCKS * outs
    spare = 2 * big.area

    def key_even(i):
        def put(block, value):
            slope3[at((i * 2 + block) * big.out_area, big.out_area)] = value

        even_cells(field, key_base + i * big.area, big, wide_stage, dense_stage, put)

    def key_side(i, start):
        cells = [slope3[at((i * 2 + block) * big.out_area, big.out_area)] for block in range(2)]
        value = dot(jnp.concatenate(cells, axis=1), wk[3][...])
        for block in range(BLOCKS):
            wide[at(start + block * big.out_area, big.out_area)] = value[:, block * 128 : (block + 1) * 128]

    def key_third(m, c, start):
        value = dot(thin[at(m * outs + c * big.out_area, big.out_area)], wk[2][...])
        for block in range(BLOCKS):
            wide[at(start + block * big.out_area, big.out_area)] = value[:, block * 128 : (block + 1) * 128]

    def key_a(m, c):
        start = m * first_row + c * big.area
        wide[at(start, big.area)] = dot(field[at(key_base + (2 * m + c) * big.area, big.area)], wk[0][...])
        put_moments(m, 0, c * 2, start, big.area, 112)
        start = m * first_row + spare
        key_side(2 * m + c, start)
        for block in range(BLOCKS):
            put_moments(m, 0, 8 + (c * BLOCKS + block) * 2, start + block * big.out_area, big.out_area, 112)

    def key_b(m, c):
        scale, bias = affine(combined(m, 0, c * 2, (1 - c) * 2, area), 0)

        def rows_of(y):
            for k in range(4):
                row = y * 4 + k
                v = wide[at(m * first_row + c * big.area + row * 2 * SIDE, 2 * SIDE)] * scale + bias
                split_planes(gelu_only(v), stage_of[0], planes_of[0], big, c, row, k % 2)

        repeat(0, big.half // 4, rows_of)
        value = dot(patches(planes_of[0], big, c, 1), wk[1][...])
        start = m * first_row + spare + c * big.out_area
        for k in range(big.half):
            wide[pl.ds(start + k * big.half, big.half)] = value[k * big.wide : k * big.wide + big.half]
        put_moments(m, 1, c * 2, start, big.out_area, 112)

    def key_c(m, c):
        scale, bias = affine(combined(m, 1, c * 2, (1 - c) * 2, out_area), CMID)
        for k in range(big.out_area // 112):
            v = wide[at(m * first_row + spare + c * big.out_area + k * 112, 112)] * scale + bias
            thin[at(m * outs + c * big.out_area + k * 112, 112)] = gelu_only(v).astype(bf16)
        start = m * first_row + c * BLOCKS * big.out_area
        key_third(m, c, start)
        for block in range(BLOCKS):
            put_moments(m, 2, (c * BLOCKS + block) * 2, start + block * big.out_area, big.out_area, 112)

    def key_d(m, c):
        start = m * first_row + c * BLOCKS * big.out_area
        side = m * first_row + spare
        key_side(2 * m + c, side)
        parts = []
        for block in range(BLOCKS):
            lanes = 2 * CMID + block * 128
            row, other = (c * BLOCKS + block) * 2, ((1 - c) * BLOCKS + block) * 2
            scale3, bias3 = affine(combined(m, 2, row, other, out_area), lanes)
            scale4, bias4 = affine(combined(m, 0, 8 + row, 8 + other, out_area), lanes + COUT)
            bias = bias3 + bias4
            e = jnp.zeros((8, 128), f32)
            for k in range(big.out_area // 112):
                x3 = wide[at(start + block * big.out_area + k * 112, 112)]
                x4 = wide[at(side + block * big.out_area + k * 112, 112)]
                e += folded(gelu_only(x3 * scale3 + x4 * scale4 + bias))
            parts.append(e.sum(0, keepdims=True) / out_area)
        length = sum(jnp.sum(part * part, axis=1, keepdims=True) for part in parts)
        inverse = lax.rsqrt(length + UNIT_EPS)
        for block in range(BLOCKS):
            r.embed[pl.ds(m * 8 + c * BLOCKS + block, 1)] = parts[block] * inverse

    def key_copy(m, k):
        mine = keys.at[pl.ds(pl.multiple_of((m * devices + me) * 8, 8), 8)]
        return remote(
            r.embed.at[pl.ds(m * 8, 8)], mine, r.key_send.at[m, k], r.key_recv.at[m, k], place(lax.rem(me + k, devices)))

    def share_start(m):
        keys[at((m * devices + me) * 8, 8, 8)] = r.embed[m * 8 : (m + 1) * 8]
        repeat(1, devices, lambda k: key_copy(m, k).start())

    def share_end(m):
        repeat(1, devices, lambda k: key_copy(m, k).wait())

    def core_copy(job):
        return remote(r.parts[job].at[1 - core], r.arrived[job], r.core_send.at[job], r.core_recv.at[job], partner(1))

    def row_copy(job, target, source):
        return remote(
            r.outward[job].at[target], r.inward[job].at[source], r.row_send.at[job, target], r.row_recv.at[job, source],
            (target, core))

    def job_send(job):
        core_copy(job).wait()

        for k in range(1, chips):
            target = lax.rem(chip + k, chips)
            value = r.parts[job][core, target] + r.arrived[job][target]
            r.outward[job][target] = value.astype(r.outward[job].dtype)
            row_copy(job, target, chip).start()

    def job_end(job):
        total = r.parts[job][core, chip] + r.arrived[job][chip]
        for k in range(1, chips):
            row_copy(job, chip, lax.rem(chip + k, chips)).wait_recv()
        for k in range(1, chips):
            total += r.inward[job][lax.rem(chip + k, chips)].astype(f32)
        start = sum(JOB_ROWS[:job])
        r.packed[start : start + JOB_ROWS[job]] = total
        for k in range(1, chips):
            row_copy(job, lax.rem(chip + k, chips), chip).wait_send()

    def fill_head():
        part, third, fourth = r.parts[0], grads[2], grads[3]

        def turn(i):
            for block in range(BLOCKS):
                half, row = block // 2, block % 2
                lanes = slice(block * 128, (block + 1) * 128)
                part[half, i, row * 8 : row * 8 + 8] = third[at(i * 8, 8, 8), lanes]
                part[half, i, 16 + row * 16 : 32 + row * 16] = fourth[at(i * 16, 16), lanes]

        for i in range(chips):
            turn(i)
        core_copy(0).start()

    def fill_spatial():
        part = r.parts[1]
        for tile in range(9):
            lanes = slice(tile * 128, (tile + 1) * 128)
            gy2[lanes] = grads[1][:, lanes].T
        filler = jnp.zeros((8, 128), f32)

        def turn(i):
            top = gy2[at(i * 72, 40, 8)]
            bottom = jnp.concatenate([gy2[at(i * 72 + 40, 32, 8)], filler], axis=0)
            for half in range(2):
                part[half, i, 0:40] = side_by_side(top, bottom, half)
                part[half, i, 40:48] = filler

        for i in range(chips):
            turn(i)
        core_copy(1).start()

    def fill_sums():
        part = r.parts[2]
        column = lax.broadcasted_iota(jnp.int32, (1, 128), 1)
        filler = jnp.zeros((1, 128), f32)
        rows = [gain_sum[:, k * 128 : (k + 1) * 128] for k in range(10)]
        rows += [jnp.where(column == 0, loss_sum[...], 0.0), filler]
        rows += [shift_sum[:, k * 128 : (k + 1) * 128] for k in range(10)] + [filler, filler]
        rows = jnp.concatenate(rows, axis=0)

        def turn(i):
            for half in range(2):
                part[half, i] = rows

        for i in range(chips):
            turn(i)
        core_copy(2).start()

    def fill_reduce():
        part = r.parts[3]
        for tile in range(2):
            lanes = slice(tile * 128, (tile + 1) * 128)
            gy2[lanes] = grads[0][:, lanes].T

        def turn(i):
            for half in range(2):
                part[half, i] = side_by_side(gy2[at(i * 16, 8, 8)], gy2[at(i * 16 + 8, 8, 8)], half)

        for i in range(chips):
            turn(i)
        core_copy(3).start()

    for load in query_loads(0) + key_loads:
        load.start()
    barrier = pltpu.get_barrier_semaphore()
    repeat(1, devices, lambda k: pl.semaphore_signal(
        barrier, inc=1, device_id=place(lax.rem(me + k, devices)), device_id_type=MESH))
    if own:
        current = [r.r0[...], r.s0[...], r.e0[...], r.p0[...]]
        lagged = [r.r1[...], r.s1[...], r.e1[...], r.p1[...]]
        packed_shards([MOMENTUM * old + (1.0 - MOMENTUM) * new for old, new in zip(lagged, current)], r.sent, 0)
        packed_shards(current, r.sent, 1)
        for which in range(2):
            r.gathered[which, core, xy, z] = r.sent[which]
    else:
        for shard, w in zip((r.r0, r.s0, r.e0, r.p0, r.r1, r.s1, r.e1, r.p1), wq + wk):
            w[...] = shard[...]
    if devices > 1:
        pl.semaphore_wait(barrier, devices - 1)
    if own:
        gather_start(0, 0)
    for ref in list(planes_of.values()) + list(back_of.values()) + list(stage_of.values()) + grads + [
        gain_sum, shift_sum, loss_sum, gy2] + [pair[0] for pair in moved]:
        ref[...] = jnp.zeros_like(ref)
    if own:
        gather_end(0, 0)
        gather_start(0, 1)
        gather_start(1, 0)

    def micro_step(m):
        opening, closing = m == 0, m == micros - 1
        base = m * field_rows
        w1, w2, w3, w4 = wq
        w3t, w4t, wt0, wt1 = (r.w3t, r.w4t, r.wt0, r.wt1)
        alive_count = sum(counts[m, i] for i in range(images)).astype(f32)
        count1 = images * big.area + small.area * alive_count
        count2 = images * big.out_area + small.out_area * alive_count

        def living(kind, crop):
            if kind is big:
                return jnp.float32(1.0)
            return jnp.where(lax.rem(crop, slots) < counts[m, lax.div(crop, slots)], 1.0, 0.0)

        def step_of(kind):
            return 112 if kind is big else 144

        def over_big(body, *hooks):
            def turn(c):
                body(big, c, 1)
                for k, (when, hook) in enumerate(hooks):

                    @pl.when(jnp.logical_and(when, c == k))
                    def _():
                        hook()

            repeat(0, big.count, turn)

        def over_small(body):
            body(small, 0, small.count)

        def add_moments(ref, offset, kind, first, count, row0, size, row, where, opener):
            start = offset + row0 + first * size
            if kind is big:

                @pl.when(first == 0)
                def _():
                    vec[row : row + 1] = folded(ref[at(start, opener, 8)]).sum(0, keepdims=True) / opener

            for c in range(count):
                total, square = moments(ref, start + c * size, size, step_of(kind), vec[row : row + 1])
                alive = living(kind, first + c)
                sums[where] += total * alive
                sums[where + 1] += square * alive

        for load in query_loads(m):
            load.wait()

        def even_batch(kind, first, count):
            for c in range(count):
                start = kind.out_row + (first + c) * kind.out_area

                def put(block, value):
                    even[at(start, kind.out_area), block * 128 : (block + 1) * 128] = value

                even_cells(field, base + kind.row + (first + c) * kind.area, kind, wide_stage, dense_stage, put)

        @pl.when(m > 0)
        def _():
            settle(even_stores(m - 1))

        over_big(even_batch)
        over_small(even_batch)

        @pl.when(opening)
        def _():
            for load in key_loads:
                load.wait()
            repeat(0, 2 * micros, key_even)
            if own:
                gather_end(0, 1)
                gather_start(0, 2)
                gather_end(1, 0)
                gather_start(1, 1)
                gather_end(0, 2)
                unpacked(r.gathered, 0, chips, wk, gy2)
            repeat(0, 2, lambda c: key_a(0, c))
            exchange_start(0, 0)
            if own:
                gather_end(1, 1)
                gather_start(1, 2)
            repeat(0, 2, lambda c: key_a(1, c))
            exchange_start(1, 0)
            for load in query_loads(1):
                load.start()
            if own:
                gather_end(1, 2)
                unpacked(r.gathered, 1, chips, wq, gy2)
            r.w1t[...] = w1[...].T
            w3t[...] = w3[...].T
            w4t[...] = w4[...].T
            wt0[...] = jnp.zeros_like(wt0)
            wt1[...] = jnp.zeros_like(wt1)

            def tap(ky, kx):
                start = (3 * ky + kx) * CMID
                return w2[start : start + CMID, :].T

            wt0[0:128, 0:128] = tap(1, 1)
            wt0[0:128, 128:256] = tap(1, 2)
            wt0[128:256, 128:256] = tap(1, 0)
            wt1[0:128, 0:128] = tap(2, 1)
            wt1[0:128, 128:256] = tap(2, 2)
            wt1[128:256, 128:256] = tap(2, 0)
            wt1[256:384, 0:128] = tap(0, 1)
            wt1[256:384, 128:256] = tap(0, 2)
            wt1[384:512, 128:256] = tap(0, 0)

        sums[...] = jnp.zeros_like(sums)

        def reduce_batch(kind, first, count):
            start = kind.row + first * kind.area
            size = count * kind.area
            a1[at(start, size)] = dot(field[at(base + start, size)], w1[...])
            add_moments(a1, 0, kind, first, count, kind.row, kind.area, 0, 0, 784)

        over_big(reduce_batch, (opening, lambda: exchange_next(0, 0)), (opening, lambda: exchange_next(1, 0)))
        over_small(reduce_batch)
        mean1, root1 = closed(sums[0], sums[1], vec[0:1], count1)
        scale1 = root1 * line(gains, 0)
        bias1 = line(shifts, 0) - mean1 * scale1
        vec[1:2], vec[2:3], vec[3:4], vec[4:5] = mean1, root1, scale1, bias1

        @pl.when(opening)
        def _():
            for k in range(2):
                exchange_end(k, 0)
                repeat(0, 2, lambda c: key_b(k, c))
                exchange_start(k, 1)

        sums[...] = jnp.zeros_like(sums)

        @pl.when(m > 0)
        def _():
            settle(field_stores(m - 1))

        def hidden_batch(kind, first, count):
            scale, bias = vec[3:4], vec[4:5]
            for c in range(count):
                for k in range(kind.half):
                    start = kind.row + (first + c) * kind.area + k * 2 * kind.side
                    v = a1[at(start, 2 * kind.side)] * scale + bias
                    hidden, slope = gelu_pair(v)
                    slope1[at(start, 2 * kind.side)] = slope.astype(bf16)
                    split_planes(hidden, stage_of[kind.ahead], planes_of[kind.ahead], kind, first + c, k, k % 2)

        over_big(hidden_batch, (opening, lambda: exchange_next(0, 1)), (opening, lambda: exchange_next(1, 1)))
        over_small(hidden_batch)

        @pl.when(opening)
        def _():
            for k in range(2):
                exchange_end(k, 1)
                repeat(0, 2, lambda c: key_c(k, c))
                exchange_start(k, 2)

        def spatial_batch(kind, first, count):
            half, lanes = kind.half, kind.wide
            value = dot(patches(planes_of[kind.ahead], kind, first, count), w2[...])
            start = kind.out_row + first * kind.out_area
            for k in range(count * half):
                a2[pl.ds(start + k * half, half)] = value[k * lanes : k * lanes + half]
            add_moments(a2, 0, kind, first, count, kind.out_row, kind.out_area, 0, 16, 784)

        over_big(spatial_batch, (opening, lambda: exchange_next(0, 2)), (opening, lambda: exchange_next(1, 2)))
        over_small(spatial_batch)
        mean2, root2 = closed(sums[16], sums[17], vec[0:1], count2)
        scale2 = root2 * line(gains, CMID)
        bias2 = line(shifts, CMID) - mean2 * scale2
        vec[5:6], vec[6:7], vec[7:8], vec[8:9] = mean2, root2, scale2, bias2

        @pl.when(opening)
        def _():
            for k in range(2):
                exchange_end(k, 2)
                repeat(0, 2, lambda c: key_d(k, c))
                share_start(k)

        def head_product(which, source, weight, kind, first, count):
            start = kind.out_row + first * kind.out_area
            size = count * kind.out_area
            value = dot(source, weight[...])
            for block in range(BLOCKS):
                offset = (which * BLOCKS + block) * outs
                wide[at(offset + start, size)] = value[:, block * 128 : (block + 1) * 128]
            for block in range(BLOCKS):
                offset = (which * BLOCKS + block) * outs
                add_moments(
                    wide, offset, kind, first, count, kind.out_row, kind.out_area,
                    16 + which * 4 + block, which * 8 + block * 2, 784)

        def expand_batch(kind, first, count):
            start = kind.out_row + first * kind.out_area
            size, step = count * kind.out_area, step_of(kind)
            scale, bias = vec[7:8], vec[8:9]
            head_product(1, even[at(start, size)], w4, kind, first, count)
            for k in range(size // step):
                hidden, slope = gelu_pair(a2[at(start + k * step, step)] * scale + bias)
                thin[at(H2 + start + k * step, step)] = hidden.astype(bf16)
                thin[at(SLOPE2 + start + k * step, step)] = slope.astype(bf16)
            head_product(0, thin[at(H2 + start, size)], w3, kind, first, count)

        over_big(expand_batch)
        over_small(expand_batch)
        for which in range(2):
            for block in range(BLOCKS):
                row = which * 4 + block
                where = which * 8 + block * 2
                lanes = 2 * CMID + row * 128
                mean, root = closed(sums[where], sums[where + 1], vec[16 + row : 17 + row], count2)
                scale = root * line(gains, lanes)
                bias = line(shifts, lanes) - mean * scale
                vec[24 + row : 25 + row], vec[32 + row : 33 + row] = mean, root
                vec[40 + row : 41 + row] = scale
                if which == 0:
                    vec[48 + block : 49 + block] = bias
                else:
                    vec[48 + block : 49 + block] += bias

        rows_e, rows_c = r.rows_e, r.rows_c

        def embed_batch(kind, first, count):
            step = step_of(kind)
            for c in range(count):
                start = kind.out_row + (first + c) * kind.out_area
                for block in range(BLOCKS):
                    mean3, mean4 = vec[24 + block : 25 + block], vec[28 + block : 29 + block]
                    scale3, scale4 = vec[40 + block : 41 + block], vec[44 + block : 45 + block]
                    bias = vec[48 + block : 49 + block]
                    zero = jnp.zeros((8, 128), f32)
                    e, s0, s3, s4 = zero, zero, zero, zero
                    for k in range(kind.out_area // step):
                        inside = block * outs + start + k * step
                        x3, x4 = wide[at(A3 + inside, step)], wide[at(AP + inside, step)]
                        value, slope = gelu_pair(x3 * scale3 + x4 * scale4 + bias)
                        slope3[at(inside, step)] = slope.astype(bf16)
                        e += folded(value)
                        s0 += folded(slope)
                        s3 += folded(slope * (x3 - mean3))
                        s4 += folded(slope * (x4 - mean4))
                    row = kind.ahead + first + c
                    for which, value in enumerate((e / kind.out_area, s0, s3, s4)):
                        rows_e[which, block, pl.ds(row, 1)] = value.sum(0, keepdims=True)

        over_big(embed_batch)
        over_small(embed_batch)

        share_end(m)

        def joined(which):
            return jnp.concatenate([rows_e[which, block] for block in range(BLOCKS)], axis=1)

        e = joined(0)
        inverse = lax.rsqrt(jnp.sum(e * e, axis=-1, keepdims=True) + UNIT_EPS)
        row = lax.broadcasted_iota(jnp.int32, (crops, 1), 0)
        owner = jnp.zeros((crops, 1), jnp.int32)
        live = jnp.where(row < images, 1.0, 0.0)
        for i in range(images):
            owner = jnp.where(row == i, i, owner)
            for slot in range(slots):
                here = row == images + i * slots + slot
                owner = jnp.where(here, i, owner)
                live = jnp.where(here, jnp.where(slot < counts[m, i], 1.0, 0.0), live)
        key_rows = [
            jnp.concatenate(
                [keys[pl.ds(m * devices * 8 + c * BLOCKS + block, devices, stride=8)] for c in range(images)], axis=0)
            for block in range(BLOCKS)
        ]
        key_high, key_low = two_parts(jnp.concatenate(key_rows, axis=1))
        logits = lax.dot_general(
            jnp.concatenate(two_parts(e * inverse), axis=0), jnp.concatenate([key_high, key_low], axis=0),
            (((1,), (1,)), ((), ())), preferred_element_type=f32)
        count = devices * images
        logits = logits[0:crops] + logits[crops:]
        logits = (logits[:, 0:count] + logits[:, count:]) / TEMP
        top = jnp.max(logits, axis=-1, keepdims=True)
        powers = jnp.exp(logits - top)
        total = jnp.sum(powers, axis=-1, keepdims=True)
        column = lax.broadcasted_iota(jnp.int32, logits.shape, 1)
        mine = column == owner * devices + me
        chosen = jnp.sum(jnp.where(mine, logits, 0.0), axis=-1, keepdims=True)
        ce = (top + jnp.log(total) - chosen) * live
        loss_sum[...] += jnp.sum(ce, axis=0, keepdims=True)
        toward = (powers / total - jnp.where(mine, 1.0, 0.0)) * (live / TEMP)
        back = dot(jnp.concatenate(two_parts(toward), axis=0), jnp.concatenate([key_high, key_low], axis=1))
        back = back[0:crops] + back[crops:]
        back = back[:, 0:COUT] + back[:, COUT:]
        de = inverse * back - e * (inverse * inverse * inverse * jnp.sum(e * back, axis=-1, keepdims=True))
        de = de * jnp.where(row < images, 1.0 / big.out_area, 1.0 / small.out_area)
        sum0 = jnp.sum(de * joined(1), axis=0, keepdims=True)
        for which in range(2):
            reach = jnp.sum(de * joined(2 + which), axis=0, keepdims=True)
            for block in range(BLOCKS):
                row = which * 4 + block
                here = slice(block * 128, (block + 1) * 128)
                lanes = slice(2 * CMID + row * 128, 2 * CMID + (row + 1) * 128)
                mean, root, scale = vec[24 + row : 25 + row], vec[32 + row : 33 + row], vec[40 + row : 41 + row]
                along = reach[:, here] * root
                gain_sum[:, lanes] += along
                shift_sum[:, lanes] += sum0[:, here]
                tilt = scale * root * along / count2
                vec[52 + row : 53 + row] = tilt
                vec[60 + row : 61 + row] = scale * sum0[:, here] / count2 - tilt * mean
                rows_c[which, block] = de[:, here] * scale

        sums[...] = jnp.zeros_like(sums)
        d3, dp = r.d3, r.dp

        def head_back(kind, first, count):
            start = kind.out_row + first * kind.out_area
            size, step = count * kind.out_area, step_of(kind)
            for which, store in ((0, d3), (1, dp)):
                for block in range(BLOCKS):
                    lanes = slice(block * 128, (block + 1) * 128)
                    where = which * 4 + block
                    for c in range(count):
                        rise = rows_c[which, block, pl.ds(kind.ahead + first + c, 1)]
                        alive = living(kind, first + c)
                        tilt, level = vec[52 + where : 53 + where] * alive, vec[60 + where : 61 + where] * alive
                        for k in range(kind.out_area // step):
                            inside = c * kind.out_area + k * step
                            here = block * outs + start + inside
                            x = wide[at(which * BLOCKS * outs + here, step)]
                            grad = slope3[at(here, step)].astype(f32) * rise - (x * tilt + level)
                            store[inside : inside + step, lanes] = grad.astype(bf16)
            grad3, gradp = d3[0:size], dp[0:size]
            gy2[at(start, size)] = dot(grad3, w3t[...])
            gradient = dot(gradp, w4t[...])
            grads[2][...] += dot_rows(thin[at(H2 + start, size)], grad3)
            grads[3][...] += dot_rows(even[at(start, size)], gradp)
            even[at(start, size)] = gradient.astype(bf16)
            mean = vec[5:6]
            level, reach = jnp.zeros((8, 128), f32), jnp.zeros((8, 128), f32)
            for k in range(size // step):
                here = at(start + k * step, step)
                gy = gy2[here] * thin[at(SLOPE2 + start + k * step, step)].astype(f32)
                gy2[here] = gy
                level += folded(gy)
                reach += folded(gy * (a2[here] - mean))
            sums[0] += level
            sums[1] += reach

        over_big(head_back)
        over_small(head_back)
        for copy in even_stores(m):
            copy.start()

        if own:

            @pl.when(closing)
            def _():
                fill_head()

        def norm_back(where, lanes, count):
            mean, root, scale = vec[where : where + 1], vec[where + 1 : where + 2], vec[where + 2 : where + 3]
            level = sums[0].sum(0, keepdims=True)
            along = sums[1].sum(0, keepdims=True) * root
            gain_sum[:, lanes] += along
            shift_sum[:, lanes] += level
            tilt = scale * root * along / count
            vec[68:69] = scale
            vec[69:70] = tilt
            vec[70:71] = scale * level / count - tilt * mean

        norm_back(5, slice(CMID, 2 * CMID), count2)
        sums[...] = jnp.zeros_like(sums)

        def spatial_back(kind, first, count):
            half, lanes, side, step = kind.half, kind.wide, kind.side, step_of(kind)
            out_start = kind.out_row + first * kind.out_area
            for c in range(count):
                alive = living(kind, first + c)
                tilt, level = vec[69:70] * alive, vec[70:71] * alive
                for k in range(kind.out_area // step):
                    here = at(out_start + c * kind.out_area + k * step, step)
                    gy2[here] = gy2[here] * vec[68:69] - (a2[here] * tilt + level)
            column = lax.broadcasted_iota(jnp.int32, (lanes, 128), 0)
            store = back_of[kind.ahead]
            for k in range(count * half):
                here = jnp.where(column < half, gy2[pl.ds(out_start + k * half, lanes)], 0.0)
                following = jnp.where(column < half - 1, gy2[pl.ds(out_start + k * half + 1, lanes)], 0.0)
                store[first + k // half, k % half, :, 0:128] = here.astype(bf16)
                store[first + k // half, k % half, :, 128:256] = following.astype(bf16)
            size = count * half * lanes
            near = store[pl.ds(first, count), 0:half].reshape(size, 256)
            beyond = store[pl.ds(first, count), 1 : half + 1].reshape(size, 256)
            upper_rows = dot(near, wt0[...])
            lower_rows = dot(jnp.concatenate([near, beyond], axis=1), wt1[...])
            start = kind.row + first * kind.area
            for k in range(count * half):
                here = slice(k * lanes, k * lanes + half)
                row = start + k * 2 * side
                for odd, value in ((0, upper_rows), (1, lower_rows)):
                    wide[pl.ds(row + odd * side, half, stride=2)] = value[here, 0:128]
                    wide[pl.ds(row + odd * side + 1, half, stride=2)] = value[here, 128:256]
            grads[1][...] += dot_rows(near[:, 0:128], patches(planes_of[kind.ahead], kind, first, count))
            mean = vec[1:2]
            level, reach = jnp.zeros((8, 128), f32), jnp.zeros((8, 128), f32)
            for k in range(count * kind.area // step):
                here = at(start + k * step, step)
                gy = wide[here] * slope1[here].astype(f32)
                wide[here] = gy
                level += folded(gy)
                reach += folded(gy * (a1[here] - mean))
            sums[0] += level
            sums[1] += reach

        def job_hooks(*jobs):
            def sends(some):
                return lambda: [job_send(job) for job in some]

            return [(closing, sends(some)) for some in jobs] if own else []

        over_big(spatial_back, *job_hooks((0,)))
        over_small(spatial_back)
        norm_back(1, slice(0, CMID), count1)

        if own:

            @pl.when(closing)
            def _():
                fill_spatial()
                fill_sums()

        def reduce_back(kind, first, count):
            step = step_of(kind)
            size = count * kind.area
            start = kind.row + first * kind.area
            rise = vec[68:69]
            for c in range(count):
                alive = living(kind, first + c)
                tilt, level = vec[69:70] * alive, vec[70:71] * alive
                for k in range(kind.area // step):
                    here = at(start + c * kind.area + k * step, step)
                    grad = wide[here] * rise - (a1[here] * tilt + level)
                    slope1[here] = grad.astype(bf16)
            grads[0][...] += dot_rows(slope1[at(start, size)], field[at(base + start, size)])

        over_big(reduce_back, *job_hooks((1,), (2,)))
        over_small(reduce_back)

        for copy in field_stores(m):
            copy.start()

    repeat(0, micros, micro_step)
    if own:
        fill_reduce()
        job_end(0)
        job_send(3)
        for job in range(1, 4):
            job_end(job)
    settle(even_stores(micros - 1))
    settle(field_stores(micros - 1))


def step_pass(axes, own, slots, big, small, key, counts, mask, current, lagged, vectors):
    chips, cores = axes
    devices = chips * cores
    widths = stage_widths(devices)
    micros, images = counts.shape
    one, two = field_pair(images, slots)
    rows = two.row + two.count * two.area
    outs = two.out_row + two.count * two.out_area
    crops = images * (1 + slots)
    vmem = pl.BlockSpec(memory_space=pltpu.VMEM)
    smem = pl.BlockSpec(memory_space=pltpu.SMEM)
    hbm = pl.BlockSpec(memory_space=pl.ANY)
    weights = [(CIN, CMID), (9 * CMID, CMID), (CMID, COUT), (CIN, COUT)]
    totals = dict(
        g1=(CMID, CIN), g2=(CMID, 9 * CMID), g3=(CMID, COUT), g4=(CIN, COUT),
        gain_sum=(1, NORMS), shift_sum=(1, NORMS), loss_sum=(1, 1))
    r0, s0, e0, p0 = ((w, vmem) for w in current)
    r1, s1, e1, p1 = ((w, vmem) for w in lagged)
    gains, shifts, gains1, shifts1 = ((v, vmem) for v in vectors)
    inputs = dict(
        big_hbm=(big, hbm), small_hbm=(small, hbm), key_hbm=(key, hbm), counts=(counts, smem), mask=(mask, smem),
        r0=r0, s0=s0, e0=e0, p0=p0, r1=r1, s1=s1, e1=e1, p1=p1, gains=gains, shifts=shifts, gains1=gains1, shifts1=shifts1)
    outputs = dict(
        da_big=(jax.ShapeDtypeStruct((micros, two.row, CMID), bf16), hbm),
        da_small=(jax.ShapeDtypeStruct((micros, rows - two.row, CMID), bf16), hbm),
        even_big=(jax.ShapeDtypeStruct((micros, two.out_row, CIN), bf16), hbm),
        even_small=(jax.ShapeDtypeStruct((micros, outs - two.out_row, CIN), bf16), hbm),
        w1t=(jax.ShapeDtypeStruct((CMID, CIN), bf16), vmem))
    if own:
        outputs |= dict(packed=(jax.ShapeDtypeStruct((sum(JOB_ROWS), 128), f32), vmem))
    else:
        outputs |= {n: (jax.ShapeDtypeStruct(shape, f32), vmem) for n, shape in totals.items()}

    def buf(dtype, *shape):
        return pltpu.VMEM(shape, dtype)

    def dma(*shape):
        return pltpu.SemaphoreType.DMA(shape)

    scratch = dict(
        field=buf(bf16, rows + 2 * micros * one.area, CIN),
        a1=buf(f32, rows, 128), slope1=buf(bf16, rows, 128),
        planes_big=buf(bf16, 2, one.count, one.half + 1, one.wide, 384),
        planes_small=buf(bf16, 2, two.count, two.half + 1, two.wide, 384),
        a2=buf(f32, outs, 128), thin=buf(bf16, 2 * outs, 128), even=buf(bf16, outs, CIN),
        wide=buf(f32, 2 * BLOCKS * outs, 128), slope3=buf(bf16, BLOCKS * outs, 128),
        back_big=buf(bf16, one.count, one.half + 1, one.wide, 256),
        back_small=buf(bf16, two.count, two.half + 1, two.wide, 256),
        gy2=buf(f32, outs + 16, 128), stage_big=buf(f32, 2, 2, 80, 128), stage_small=buf(f32, 2, 2, 48, 128),
        wide_stage=buf(f32, 8, SIDE, 128), dense_stage=buf(f32, 2, one.out_area, 128),
        d3=buf(bf16, two.count * two.out_area, COUT), dp=buf(bf16, two.count * two.out_area, COUT),
        w3t=buf(bf16, COUT, CMID), w4t=buf(bf16, COUT, CIN),
        wt0=buf(bf16, 256, 256), wt1=buf(bf16, 512, 256), sums=buf(f32, 18, 8, 128), vec=buf(f32, 80, 128),
        rows_e=buf(f32, 4, BLOCKS, crops, 128), rows_c=buf(f32, 2, BLOCKS, crops, 128),
        keys=buf(f32, devices * 16, 128), embed=buf(f32, 16, 128),
        moved=[[buf(f32, 1 << width, n, 128) for width in widths] for _ in range(micros) for n in TURN_ROWS],
        key_load=dma(2 * micros), query_load=dma(micros, 2), store=dma(micros, 4),
        move_send=dma(3 * micros, 2, 1 << widths[0]), move_recv=dma(3 * micros, 2, 1 << widths[0]),
        key_send=dma(micros, devices), key_recv=dma(micros, devices),
    )
    first, second, third, fourth = (buf(bf16, *shape) for shape in weights)
    scratch |= dict(w1q=first, w2q=second, w3q=third, w4q=fourth, w1k=first, w2k=second, w3k=third, w4k=fourth)
    wires = (bf16, bf16, f32, f32)
    if own:
        scratch |= {n: buf(f32, *shape) for n, shape in totals.items()}
        scratch |= dict(
            sent=buf(bf16, 2, PACK, 128), gathered=buf(bf16, 2, 2, 4, 4, PACK, 128),
            parts=[buf(f32, 2, chips, n, 128) for n in JOB_ROWS], arrived=[buf(f32, chips, n, 128) for n in JOB_ROWS],
            outward=[buf(t, chips, n, 128) for n, t in zip(JOB_ROWS, wires)],
            inward=[buf(t, chips, n, 128) for n, t in zip(JOB_ROWS, wires)],
            gather_send=dma(2, 3, 3), gather_recv=dma(2, 3, 3), core_send=dma(4), core_recv=dma(4),
            row_send=dma(4, chips), row_recv=dma(4, chips),
        )
    names = list(inputs) + list(outputs) + list(scratch)
    out = pl.pallas_call(
        functools.partial(step_kernel, axes, own, slots, names),
        out_shape=[shape for shape, _ in outputs.values()],
        in_specs=[spec for _, spec in inputs.values()],
        out_specs=[spec for _, spec in outputs.values()],
        scratch_shapes=list(scratch.values()),
        compiler_params=pltpu.CompilerParams(vmem_limit_bytes=63 * 2**20, collective_id=0, has_side_effects=True),
        name="step",
    )(*[array for array, _ in inputs.values()])
    return types.SimpleNamespace(**dict(zip(outputs, out)))


def write_sums(packed, loss, reduce_out, spatial_out, expand_out, shortcut_out, gains, shifts):
    reduce_out[0:8] = packed[120:128, 0:64]
    reduce_out[8:16] = packed[120:128, 64:128]
    rows = jnp.concatenate([packed[48:88], jnp.zeros((88, 128), f32)], axis=0).T
    spatial_out[...] = jnp.concatenate([rows[0:64, 0:40], rows[64:128, 0:32]], axis=1)
    for block in range(2):
        lanes = slice(block * 128, (block + 1) * 128)
        expand_out[:, lanes] = packed[block * 8 : block * 8 + 8]
        shortcut_out[:, lanes] = packed[16 + block * 16 : 32 + block * 16]
    for row in range(NORMS // 128):
        gains[pl.ds(row * 128, 128)] = packed[96 + row]
        shifts[pl.ds(row * 128, 128)] = packed[108 + row]
    loss[...] = packed[106:107, 0:1]


def field_kernel(own, fields, da_big, da_small, even_big, even_small, weight, *refs):
    big, small = fields
    packed, refs = (refs[0], refs[1:]) if own else (None, refs)
    big_out, small_out = refs[:2]
    raised, cells = refs[-2:]
    part = pl.program_id(1)

    @pl.when(jnp.logical_and(pl.program_id(0) == 0, part == 0))
    def _():
        raised[...] = jnp.zeros_like(raised)
        if own:
            write_sums(packed, *refs[2:-2])

    def gradient(kind, count, da, shortcut, out):
        half, side = kind.half, kind.side
        for block in range(2):
            lanes = slice(block * 128, (block + 1) * 128)
            cells[block, 0 : count * kind.out_area] = shortcut[:, lanes].astype(f32)
        pairs = 1 if kind is big else 3
        for first in range(0, count * half, pairs):
            whole = dot(da[first * 2 * side : (first + pairs) * 2 * side], weight[...])
            for k in range(pairs):
                row, line_of = k * 2 * side, first + k
                for block in range(2):
                    lanes = slice(block * 128, (block + 1) * 128)
                    slot = line_of % 4 * 2 + block
                    raised[slot, pl.ds(0, half, stride=2)] = cells[block, line_of * half : (line_of + 1) * half]
                    upper = whole[row : row + side, lanes] + raised[slot, 0:side]
                    both = jnp.concatenate([upper, whole[row + side : row + 2 * side, lanes]], axis=0)
                    out[line_of * 2 * side : (line_of + 1) * 2 * side, lanes] = both.astype(bf16)

    @pl.when(part < big.count)
    def _():
        gradient(big, 1, da_big, even_big, big_out)

    @pl.when(part >= big.count)
    def _():
        gradient(small, small.count // 2, da_small, even_small, small_out)


def field_pass(own, slots, images, step):
    micros = step.da_big.shape[0]
    fields = field_pair(images, slots)
    big, small = fields
    pair = small.count // 2
    whole = pl.BlockSpec(memory_space=pltpu.VMEM)

    def large(rows, lanes):
        return pl.BlockSpec((None, rows, lanes), lambda m, j: (m, jnp.minimum(j, big.count - 1), 0))

    def little(rows, lanes):
        return pl.BlockSpec((None, rows, lanes), lambda m, j: (m, jnp.maximum(j - big.count, 0), 0))

    outs = [jax.ShapeDtypeStruct((micros, big.count * big.area, CIN), bf16), jax.ShapeDtypeStruct((micros, small.count * small.area, CIN), bf16)]
    sums = [(1, 1), (16, 64), (64, 72), (8, 256), (16, 256), (NORMS,), (NORMS,)] if own else []
    return pl.pallas_call(
        functools.partial(field_kernel, own, fields),
        grid=(micros, big.count + 2),
        out_shape=outs + [jax.ShapeDtypeStruct(shape, f32) for shape in sums],
        in_specs=[
            large(big.area, CMID), little(pair * small.area, CMID), large(big.out_area, CIN),
            little(pair * small.out_area, CIN), whole,
        ] + [whole] * own,
        out_specs=[large(big.area, CIN), little(pair * small.area, CIN)] + [whole] * len(sums),
        scratch_shapes=[pltpu.VMEM((8, SIDE, 128), f32), pltpu.VMEM((2, pair * small.out_area if pair * small.out_area > big.out_area else big.out_area, 128), f32)],
        compiler_params=pltpu.CompilerParams(vmem_limit_bytes=58 * 2**20, dimension_semantics=("arbitrary", "arbitrary")),
        name="field",
    )(step.da_big, step.da_small, step.even_big, step.even_small, step.w1t, *([step.packed] if own else []))


def gather_weights(shards):
    rows = [lax.all_gather(part, "dp", axis=0, tiled=True) for part in shards]
    return [lax.all_gather(part, "fsdp", axis=1, tiled=True) for part in rows]


def per_device(axes, *args):
    query_global, small_crop_query, small_count, key_global, shuffle_mask = args[:5]
    current, lagged = args[5:9], args[11:15]
    vectors = (args[9], args[10], args[15], args[16])
    micros = query_global.shape[0]
    slots = small_crop_query.shape[2]
    chips, cores = axes
    own = chips == 16 and cores == 2
    if own:
        current = [w.T if i == 1 else w for i, w in enumerate(current)]
        lagged = [w.T if i == 1 else w for i, w in enumerate(lagged)]
    else:
        fresh = [MOMENTUM * old + (1.0 - MOMENTUM) * new for old, new in zip(lagged, current)]
        current = gather_weights([w.astype(bf16) for w in current])
        lagged = gather_weights([w.astype(bf16) for w in fresh])
    out = step_pass(
        axes, own, slots, query_global.reshape(micros, -1, CIN), small_crop_query.reshape(micros, -1, CIN),
        key_global.reshape(micros, -1, CIN), small_count, shuffle_mask, current, lagged, vectors,
    )
    big_out, small_out, *sums = field_pass(own, slots, query_global.shape[1], out)
    fields = (big_out.reshape(query_global.shape), small_out.reshape(small_crop_query.shape))
    if own:
        loss, first, second, third, fourth, gains_grad, shifts_grad = sums
        return (loss.reshape(()), *fields, first, second.T, third, fourth, gains_grad, shifts_grad)
    totals = (out.g1.T, out.g2.T, out.g3, out.g4)
    summed = lax.psum_scatter(totals, "dp", scatter_dimension=0, tiled=True)
    owned = lax.psum_scatter(summed, "fsdp", scatter_dimension=1, tiled=True)
    sums = lax.psum((out.loss_sum, out.gain_sum, out.shift_sum), ("dp", "fsdp"))
    return (sums[0].reshape(()), *fields, *owned, sums[1].reshape(NORMS), sums[2].reshape(NORMS))


def solution(mesh):
    whole, split = P(), P("dp", "fsdp")
    images, crops = P(None, ("dp", "fsdp"), None, None, None), P(None, ("dp", "fsdp"), None, None, None, None)
    axes = (mesh.shape["dp"], mesh.shape["fsdp"])
    return jax.shard_map(
        functools.partial(per_device, axes),
        mesh=mesh,
        in_specs=(images, crops, P(None, ("dp", "fsdp")), images, whole)
        + (split,) * 4 + (whole,) * 2 + (split,) * 4 + (whole,) * 2,
        out_specs=(whole, images, crops) + (split,) * 4 + (whole,) * 2,
        check_vma=False,
    )
```
